32 devices in a mesh: pipe: 4 (over y, x), dp: 8 (over z, core).
Axes of the slice: x: 2, y: 2, z: 4, core: 2. Of those that a mesh axis runs over, the one named last changes fastest.
Arguments:
- tokens: bfloat16 [2, 16, 32, 4096], P(None, 'dp'), may hold values from -6 to 6
- cotangents: bfloat16 [2, 16, 32, 4096], P(None, 'dp'), may hold values from -1 to 1
- starts: int32 [2, 16, 4], P(None, 'dp'), may hold values from 0 to 31, as said below
- counts: int32 [2, 16], P(None, 'dp'), may hold values from 1 to 4
- layer_gains: bfloat16 [4, 4096], P('pipe', 'dp'), may hold values from 0.5 to 1.5
- first_map: bfloat16 [4, 4096, 128], P('pipe', 'dp'), may hold values from -0.09375 to 0.09375
- second_map: bfloat16 [4, 128, 4096], P('pipe', None, 'dp'), may hold values from -0.5 to 0.5
Outputs:
- gain_grad: float32 [4, 4096], P('pipe', 'dp')
- first_grad: float32 [4, 4096, 128], P('pipe', 'dp')
- second_grad: float32 [4, 128, 4096], P('pipe', None, 'dp')
The draws below stay inside these ranges and needn't reach their ends.
Inputs may be any that keep to these rules, and one draw needn't show every extreme that they name: `starts`: each row begins with 0 and rises strictly; a micro-batch's documents begin at the first counts entries of its row, the later entries are not used.
All inputs are finite; a program needn't handle non-finite values.
Results may differ from the reference program's by a relative error of at most 0.03.
Values may be sent and summed in bfloat16 or wider, within the bound.
No kernel may reach another device: no remote copies, remote signals or barrier semaphores. Data moves between devices by JAX's collectives and lax.ppermute only.
A program may use at most 64 MiB of HBM per device.

```python
import jax
import jax.numpy as jnp
from jax import lax

D = 4096
HD = 128
RANK = 128
SEQ = 32
MB = 2
NDOC = 4
ROWS = 16
LAYERS = 4
N_DP = 8


def draw_starts(key, part):
    start_key = jax.random.fold_in(key, 7001)
    row_keys = jax.random.split(start_key, 2 * ROWS)

    def one_row(row_key):
        picked = jax.random.permutation(row_key, SEQ - 1)[:NDOC - 1].astype(jnp.int32) + 1
        return jnp.concatenate((jnp.zeros((1,), jnp.int32), jnp.sort(picked).astype(jnp.int32)))
    start_table = jax.vmap(one_row)(row_keys).reshape(2, ROWS, NDOC)
    return start_table.at[0, 0, NDOC - 1].set(SEQ - 1)


def draw_counts(key, part):
    count_key = jax.random.fold_in(key, 7002)
    count_table = jax.random.randint(count_key, (2, ROWS), 1, NDOC + 1).astype(jnp.int32)
    return count_table.at[0, 0].set(NDOC).at[1, 0].set(1)


def with_spikes(drawn, own_key, source, target, parts, factor):
    owner, partner = [(jnp.arange(drawn.shape[dim]) // (drawn.shape[dim] // parts)).reshape([-1 if axis == dim else 1 for axis in range(drawn.ndim)]) for dim in (source, target)]
    chosen = jax.random.permutation(own_key, parts)[partner]
    strong = (owner == chosen) | (owner == (partner + parts // 2) % parts)
    return jnp.where(strong, factor * drawn, drawn)


def block_levels(key, extent, cuts, low, high):
    def one(dim, blocks):
        steps = jax.random.uniform(jax.random.fold_in(jax.random.fold_in(key, 6), dim), (blocks,), jnp.float32, low / len(cuts), high / len(cuts))
        return jnp.repeat(jnp.exp(steps), extent[dim] // blocks).reshape((-1,) + (1,) * (len(extent) - dim - 1))

    level = one(*cuts[0])
    for cut in cuts[1:]:
        level = level * one(*cut)
    return level


def normal_values(own_key, shape, deviation, reach, cuts=(), kind=jnp.bfloat16):
    values = deviation * jax.random.normal(own_key, shape, jnp.float32)
    if cuts:
        values = values * block_levels(own_key, shape, cuts, -0.22, 0.18)
    return jnp.clip(values, -reach, reach).astype(kind)


def heavy_noise(stream_key, shape, scale, most, cuts, heavy, kind=jnp.bfloat16):
    drawn = scale * jax.random.normal(stream_key, shape, jnp.float32)
    if cuts:
        drawn = drawn * block_levels(stream_key, shape, cuts, -0.22, 0.18)
    return jnp.clip(with_spikes(drawn, jax.random.fold_in(stream_key, 3), *heavy), -most, most).astype(kind)


def setup_inputs(seed: int = 0) -> dict:
    streams_of = jax.random.split(jax.random.key(seed), 8)
    tokens = normal_values(streams_of[0], (2, ROWS, SEQ, D), 1.0, 6.0, ((1, 8),))
    cotangents = heavy_noise(streams_of[1], (2, ROWS, SEQ, D), 0.05, 1.0, ((1, 8),), (1, 3, 8, 2.0))
    starts = draw_starts(jax.random.fold_in(streams_of[7], 71), 0)
    counts = draw_counts(jax.random.fold_in(streams_of[7], 71), 0)
    layer_gains = jnp.clip(1.0 + 0.1 * jax.random.normal(streams_of[4], (LAYERS, D), jnp.float32), 0.5, 1.5).astype(jnp.bfloat16)
    first_map = normal_values(streams_of[5], (LAYERS, D, RANK), D ** -0.5, 0.09375, ((0, 4), (1, 8)))
    second_map = normal_values(streams_of[6], (LAYERS, RANK, D), RANK ** -0.5, 0.5, ((0, 4), (2, 8)))
    return dict(tokens=tokens, cotangents=cotangents, starts=starts, counts=counts, layer_gains=layer_gains, first_map=first_map, second_map=second_map)


def doc_allowed(row_starts, row_count, length):
    positions = jnp.arange(length, dtype=jnp.int32)
    entries = jnp.arange(row_starts.shape[0], dtype=jnp.int32)
    started = (row_starts[None, :] <= positions[:, None]) & (entries < row_count)[None, :]
    document = lax.optimization_barrier(jnp.sum(started.astype(jnp.int32), axis=1))
    matched = document[:, None] == document[None, :]
    return matched & (positions[None, :] <= positions[:, None])

def apply_layer(activation, gain_row, first_weight, second_weight, allowed):
    length = activation.shape[0]
    model_width = activation.shape[1]
    widened = activation.astype(jnp.float32)
    factor = lax.rsqrt(lax.optimization_barrier(jnp.mean(widened * widened, axis=1, keepdims=True)) + 1e-05)
    normed = (widened * factor * gain_row).astype(jnp.bfloat16)
    split_heads = normed.reshape(length, model_width // HD, HD)
    scores = jnp.einsum('qhd,khd->hqk', split_heads, split_heads, preferred_element_type=jnp.float32) / HD
    weights = jnp.where(allowed[None, :, :], jnp.exp(scores), 0.0)
    probabilities = (weights / lax.optimization_barrier(jnp.sum(weights, axis=2, keepdims=True))).astype(jnp.bfloat16)
    mixed_heads = jnp.einsum('hqk,khd->qhd', probabilities, split_heads, preferred_element_type=jnp.float32)
    mixed_heads = mixed_heads.reshape(length, model_width).astype(jnp.bfloat16)
    reduced = jnp.dot(mixed_heads, first_weight, preferred_element_type=jnp.float32).astype(jnp.bfloat16)
    return (widened + jnp.dot(reduced, second_weight, preferred_element_type=jnp.float32)).astype(jnp.bfloat16)

def layer_chain(gain_all, first_all, second_all, start_tokens, allowed):
    hidden_state = start_tokens
    for layer_index in range(LAYERS):
        hidden_state = apply_layer(hidden_state, gain_all[layer_index], first_all[layer_index], second_all[layer_index], allowed)
    return hidden_state

def reference(tokens, cotangents, starts, counts, layer_gains, first_map, second_map):
    group_total = 2 * N_DP
    token_groups = tokens.reshape(group_total, MB, SEQ, D)
    cot_groups = cotangents.reshape(group_total, MB, SEQ, D)
    start_groups = starts.reshape(group_total, MB, NDOC)
    count_groups = counts.reshape(group_total, MB)
    zero_sums = (jnp.zeros((LAYERS, D), jnp.float32), jnp.zeros((LAYERS, D, RANK), jnp.float32), jnp.zeros((LAYERS, RANK, D), jnp.float32))

    def add_group(running_totals, group_item):
        group_tokens, group_cots, group_starts, group_counts = group_item
        running_sums = zero_sums
        for micro_index in range(MB):
            allowed = doc_allowed(group_starts[micro_index], group_counts[micro_index], SEQ)
            start_tokens = group_tokens[micro_index]
            _, pullback = jax.vjp(lambda gain_in, first_in, second_in: layer_chain(gain_in, first_in, second_in, start_tokens, allowed), layer_gains, first_map, second_map)
            gradients = pullback(group_cots[micro_index])
            running_sums = tuple((current + gradient.astype(jnp.float32) for current, gradient in zip(running_sums, gradients)))
        rounded = tuple((lax.optimization_barrier(current.astype(jnp.bfloat16)).astype(jnp.float32) for current in running_sums))
        return (tuple((current + addition for current, addition in zip(running_totals, rounded))), None)
    totals, _ = lax.scan(add_group, zero_sums, (token_groups, cot_groups, start_groups, count_groups))
    return (totals[0], totals[1], totals[2])
```

```python
import functools

import jax
import jax.numpy as jnp
from jax import lax
from jax.experimental import pallas as pl
from jax.experimental.pallas import tpu as pltpu
from jax.sharding import Mesh, PartitionSpec as P

HD = 128
EPS = 1e-05
BF = jnp.bfloat16
F32 = jnp.float32
PARAMS = pltpu.CompilerParams(vmem_limit_bytes=48 * 1024 * 1024)


def dot(a, b):
    return jnp.dot(a, b, preferred_element_type=F32)


def dot_nt(a, b):
    return lax.dot_general(a, b, (((1,), (1,)), ((), ())), preferred_element_type=F32)


def dot_tn(a, b):
    return lax.dot_general(a, b, (((0,), (0,)), ((), ())), preferred_element_type=F32)


def two_parts(value):
    high = value.astype(BF)
    return high, (value - high.astype(F32)).astype(BF)


def vmem_specs(count):
    return [pl.BlockSpec(memory_space=pltpu.VMEM)] * count


def layer_spec(shape, layer):
    return pl.BlockSpec((1,) + shape[1:], lambda *_: (layer, 0, 0, 0))


def slice_rows(own):
    return 2 * own + 16


def pack_kernel(slots, live, starts, counts, tok, cot, gain, first, second, pay, weights):
    micro = pl.program_id(0)
    groups, length, width = pay.shape[0], tok.shape[1], tok.shape[2]
    local = width // groups
    own = first.shape[1]
    slot = slots[micro]
    widened = tok[0].astype(F32)
    mean = jnp.mean(widened * widened, axis=1, keepdims=True)
    mean_high, mean_low = two_parts(mean)
    position = lax.broadcasted_iota(jnp.int32, (length, HD), 0)
    document = jnp.zeros((length, HD), jnp.int32)
    for entry in range(starts.shape[1]):
        started = (starts[slot, entry] <= position) & (entry < counts[slot])
        document = document + started.astype(jnp.int32)
    lane = lax.broadcasted_iota(jnp.int32, (length, HD), 1)
    tail = jnp.where(
        lane == 0,
        document.astype(F32),
        jnp.where(lane == 1, mean_high.astype(F32), mean_low.astype(F32)),
    ).astype(BF)
    keep = live[micro] > 0
    for group in range(groups):
        part = slice(group * local, (group + 1) * local)
        pay[group, :, 0:local] = tok[0, :, part]
        cotangent = cot[0, :, part]
        pay[group, :, local : 2 * local] = jnp.where(keep, cotangent, jnp.zeros_like(cotangent))
        pay[group, :, 2 * local :] = tail

    @pl.when(micro == 0)
    def _():
        weights[0:own, :] = first[0]
        weights[own : 2 * own, :] = second[0].astype(F32).T.astype(BF)
        gains = [
            gain[0:1, head * HD : (head + 1) * HD].astype(F32) for head in range(own // HD)
        ]
        gains.append(jnp.zeros((16 - own // HD, HD), F32))
        weights[2 * own :, :] = jnp.concatenate(gains, axis=0).astype(BF)


def pack(slots, live, starts, counts, tokens, cotangents, gain, first, second, groups):
    micro_total, length, width = tokens.shape
    micro_local = slots.shape[0]
    own = first.shape[1]
    local = width // groups

    def picked(micro, slots, *_):
        return (slots[micro], 0, 0)

    whole = lambda shape: pl.BlockSpec(shape, lambda *_: (0,) * len(shape))
    return pl.pallas_call(
        pack_kernel,
        grid_spec=pltpu.PrefetchScalarGridSpec(
            num_scalar_prefetch=4,
            grid=(micro_local,),
            in_specs=[
                pl.BlockSpec((1, length, width), picked),
                pl.BlockSpec((1, length, width), picked),
                whole(gain.shape),
                whole(first.shape),
                whole(second.shape),
            ],
            out_specs=[
                pl.BlockSpec((groups, length, 2 * local + HD), lambda micro, *_: (0, micro, 0)),
                whole((slice_rows(own), HD)),
            ],
        ),
        out_shape=[
            jax.ShapeDtypeStruct((groups, micro_local * length, 2 * local + HD), BF),
            jax.ShapeDtypeStruct((slice_rows(own), HD), BF),
        ],
        compiler_params=PARAMS,
        name="pack",
    )(slots, live, starts, counts, tokens, cotangents, gain, first, second)


def head_gain(weights, head):
    own = (weights.shape[2] - 16) // 2
    per_slice = own // HD
    row = 2 * own + head % per_slice
    return weights[0, head // per_slice, row : row + 1, :].astype(F32)


def block_size(rows):
    return HD if rows % HD == 0 else rows


def to_rank(value, weights, at):
    own = (weights.shape[2] - 16) // 2
    total = None
    for side in range(weights.shape[1]):
        term = dot(value[:, side * own : (side + 1) * own], weights[0, side, at : at + own, :])
        total = term if total is None else total + term
    return total


def from_rank(value, weights, at, side):
    own = (weights.shape[2] - 16) // 2
    return dot_nt(value, weights[0, side, at : at + own, :])


def gram(weights):
    own = (weights.shape[2] - 16) // 2
    total = None
    for side in range(weights.shape[1]):
        part = weights[0, side, own : 2 * own, :]
        term = dot_tn(part, part)
        total = term if total is None else total + term
    return total


def attend(x, mean, weights, mask, probs, mixed):
    rows, local = x.shape
    size = block_size(rows)
    factor = lax.rsqrt(mean + EPS)
    for block in range(rows // size):
        span = slice(block * size, (block + 1) * size)
        allowed = mask[block] > 0
        for head in range(local // HD):
            part = slice(head * HD, (head + 1) * HD)
            normed = (x[span, part].astype(F32) * factor[span] * head_gain(weights, head)).astype(BF)
            scores = dot_nt(normed, normed) * (1.0 / HD)
            raw = jnp.where(allowed, jnp.exp(scores), 0.0)
            prob = (raw / jnp.sum(raw, axis=1, keepdims=True)).astype(BF)
            probs[block, head] = prob
            mixed[span, part] = dot(prob, normed).astype(BF)


def send_forward(x, weights, mixed, pay):
    rows = x.shape[0]
    own = (weights.shape[2] - 16) // 2
    pay[0:rows, :] = to_rank(mixed[...], weights, 0).astype(BF)
    pay[rows : 2 * rows, :] = to_rank(x[...], weights, own).astype(BF)
    pay[2 * rows : 2 * rows + HD, :] = gram(weights).astype(BF)


def total_of(pays, start, stop):
    total = pays[0][start:stop, :].astype(F32)
    for pay in pays[1:]:
        total = total + pay[start:stop, :].astype(F32)
    return total


def receive_forward(pays, x_before, mean_before, weights_before, width, x, mean, reduced, cross):
    rows, local = x_before.shape
    own = (weights_before.shape[2] - 16) // 2
    low_rank = total_of(pays, 0, rows).astype(BF)
    before = total_of(pays, rows, 2 * rows)
    high, low = two_parts(total_of(pays, 2 * rows, 2 * rows + HD))
    through = dot(low_rank, high) + dot(low_rank, low)
    wide = low_rank.astype(F32)
    change = jnp.sum(wide * (2.0 * before + through), axis=1, keepdims=True) / width
    new_mean = jnp.maximum(mean_before[:, 0:1] + change, 0.0)
    mean[...] = jnp.broadcast_to(new_mean, mean.shape)
    reduced[...] = low_rank
    cross[...] = before + through
    for side in range(weights_before.shape[1]):
        part = slice(side * own, (side + 1) * own)
        x[:, part] = (
            x_before[:, part].astype(F32) + from_rank(low_rank, weights_before, own, side)
        ).astype(BF)


def first_kernel(length, received, weights, x, cot, mask, mean, probs, mixed, pay):
    rows, local = x.shape
    size = block_size(rows)
    x[...] = received[:, 0:local]
    cot[...] = received[:, local : 2 * local]
    tail = received[:, 2 * local :].astype(F32)
    mean[...] = jnp.broadcast_to(tail[:, 1:2] + tail[:, 2:3], mean.shape)
    build_mask(tail[:, 0:1], mask, size, length)
    attend(x, mean[:, 0:1], weights, mask, probs, mixed)
    send_forward(x, weights, mixed, pay)


def build_mask(document, mask, size, length):
    query = lax.broadcasted_iota(jnp.int32, (size, size), 0)
    key = lax.broadcasted_iota(jnp.int32, (size, size), 1)
    for block in range(mask.shape[0]):
        by_query = jnp.broadcast_to(document[block * size : (block + 1) * size], (size, size))
        by_key = by_query.T
        allowed = (by_query == by_key) & (key <= query) & (query // length == key // length)
        mask[block] = allowed.astype(F32).astype(BF)


def middle_kernel(count, last, width, *refs):
    pays, refs = refs[:count], refs[count:]
    x_before, mean_before, mask, weights_before, weights = refs[:5]
    refs = refs[5:]
    if last:
        cot, weights_after = refs[:2]
        refs = refs[2:]
    x, mean, reduced, cross, probs, mixed, pay = refs
    receive_forward(
        pays, x_before, mean_before, weights_before, width, x, mean, reduced, cross
    )
    attend(x, mean[:, 0:1], weights, mask, probs, mixed)
    send_forward(x, weights, mixed, pay)
    if last:
        rows = x.shape[0]
        own = (weights.shape[2] - 16) // 2
        pay[2 * rows + HD :, :] = to_rank(cot[...], weights_after, own).astype(BF)


def layer_backward(
    dout, dred, x, mean, mask, weights, weights_before, probs, mixed, reduced, grads, carried, pay
):
    rows, local = x.shape
    size = block_size(rows)
    own = (weights.shape[2] - 16) // 2
    per_slice = own // HD
    rank = dred.shape[1]
    factor = lax.rsqrt(mean + EPS)
    first = dot_tn(dred, mixed[...]).astype(BF)
    for side in range(weights.shape[1]):
        grads[side, 0:rank, :] = first[:, side * own : (side + 1) * own]
    if reduced is not None:
        second = dot_tn(reduced, dout[...]).astype(BF)
        for side in range(weights.shape[1]):
            grads[side, rank : 2 * rank, :] = second[:, side * own : (side + 1) * own]
    back_mixed = [
        from_rank(dred, weights, 0, side).astype(BF) for side in range(weights.shape[1])
    ]
    gain_sums = [None] * (local // HD)
    for block in range(rows // size):
        span = slice(block * size, (block + 1) * size)
        scale = factor[span]
        norm_dot = jnp.zeros((size, HD), F32)
        for head in range(local // HD):
            part = slice(head * HD, (head + 1) * HD)
            side, inner = head // per_slice, (head % per_slice) * HD
            wide = x[span, part].astype(F32)
            gain = head_gain(weights, head)
            unit = wide * scale
            normed = (unit * gain).astype(BF)
            prob = probs[block, head]
            upstream = back_mixed[side][span, inner : inner + HD]
            back_prob = dot_nt(upstream, normed)
            prob_wide = prob.astype(F32)
            inner_sum = jnp.sum(back_prob * prob_wide, axis=1, keepdims=True)
            back_score = prob_wide * (back_prob - inner_sum) * (1.0 / HD)
            both = (back_score + back_score.T).astype(BF)
            back_normed = (dot_tn(prob, upstream) + dot(both, normed)).astype(BF).astype(F32)
            term = jnp.sum(back_normed * unit, axis=0, keepdims=True)
            gain_sums[head] = term if gain_sums[head] is None else gain_sums[head] + term
            if carried is not None:
                scaled = back_normed * gain
                norm_dot = norm_dot + scaled * wide
                carried[span, part] = (dout[span, part].astype(F32) + scaled * scale).astype(BF)
        if carried is not None:
            column = jnp.broadcast_to(jnp.sum(norm_dot, axis=1, keepdims=True), (size, size))
            line = column.T[0:1, :]
            high, low = two_parts(line)
            base = rows + 16 * block
            pay[base : base + 16, :] = jnp.concatenate(
                (high.astype(F32), low.astype(F32), jnp.zeros((14, size), F32)), axis=0
            ).astype(BF)
    zeros = jnp.zeros((15, HD), F32)
    for head in range(local // HD):
        side, inner = head // per_slice, (head % per_slice) * HD
        grads[side, 2 * rank : 2 * rank + 16, inner : inner + HD] = jnp.concatenate(
            (gain_sums[head], zeros), axis=0
        ).astype(BF)
    if carried is not None:
        pay[0:rows, :] = to_rank(carried[...], weights_before, own).astype(BF)


def turn_kernel(count, width, *refs):
    pays, refs = refs[:count], refs[count:]
    (x_before, mean_before, mask, weights_before, weights, cot) = refs[:6]
    (x, mean, reduced, cross, grads, carried, pay) = refs[6:13]
    probs, mixed = refs[13:]
    rows = x.shape[0]
    receive_forward(
        pays, x_before, mean_before, weights_before, width, x, mean, reduced, cross
    )
    attend(x, mean[:, 0:1], weights, mask, probs, mixed)
    dred = total_of(pays, 2 * rows + HD, 3 * rows + HD).astype(BF)
    layer_backward(
        cot, dred, x, mean[:, 0:1], mask, weights, weights_before, probs, mixed, None, grads,
        carried, pay,
    )
    pay[pay.shape[0] - rows :, :] = to_rank(mixed[...], weights, 0).astype(BF)


def back_kernel(count, after_turn, to_first, width, *refs):
    pays, refs = refs[:count], refs[count:]
    carried_after, x_after, mean_after, cross_after = refs[:4]
    x, mean, mask, weights = refs[4:8]
    refs = refs[8:]
    if not to_first:
        weights_before = refs[0]
        refs = refs[1:]
    else:
        weights_before = None
    probs, mixed, reduced = refs[:3]
    refs = refs[3:]
    if after_turn:
        cot, turn_grads = refs[:2]
        refs = refs[2:]
    else:
        refs = refs[1:]
    grads = refs[0]
    refs = refs[1:]
    if to_first:
        carried = pay = None
    else:
        carried, pay = refs[:2]
        refs = refs[2:]
    dout = refs[0]
    rows, local = x.shape
    size = block_size(rows)
    own = (weights.shape[2] - 16) // 2
    rank = reduced.shape[1]
    dred_parts = []
    for block in range(rows // size):
        span = slice(block * size, (block + 1) * size)
        base = rows + 16 * block
        lines = total_of(pays, base, base + 16)
        line = lines[0:1] + lines[1:2]
        column = jnp.broadcast_to(line, (size, size)).T
        factor = lax.rsqrt(mean_after[span, 0:1] + EPS)
        pull = column[:, 0:1] * (factor * factor * factor / width)
        dred_parts.append(
            (
                total_of(pays, block * size, (block + 1) * size) - cross_after[span, :] * pull
            ).astype(BF)
        )
        dout[span, :] = (
            carried_after[span, :].astype(F32) - x_after[span, :].astype(F32) * pull
        ).astype(BF)
    dred = dred_parts[0] if len(dred_parts) == 1 else jnp.concatenate(dred_parts, axis=0)
    if after_turn:
        last_reduced = total_of(pays, pays[0].shape[0] - rows, pays[0].shape[0]).astype(BF)
        second = dot_tn(last_reduced, cot[...]).astype(BF)
        for side in range(weights.shape[1]):
            grads[1, side, 0:rank, :] = turn_grads[side, 0:rank, :]
            grads[1, side, rank : 2 * rank, :] = second[:, side * own : (side + 1) * own]
            grads[1, side, 2 * rank :, :] = turn_grads[side, 2 * rank :, :]
    layer_backward(
        dout, dred, x, mean[:, 0:1], mask, weights, weights_before, probs, mixed, reduced[...],
        grads.at[0], carried, pay,
    )


def finish_kernel(parts, gain, first, second):
    rank = second.shape[1]
    total = parts[0].astype(F32)
    for index in range(1, parts.shape[0]):
        total = total + parts[index].astype(F32)
    first[0] = total[0:rank].T
    second[0] = total[rank : 2 * rank]
    gain[...] = total[2 * rank : 2 * rank + 1]


def per_device(tokens, cotangents, starts, counts, layer_gains, first_map, second_map):
    sections = lax.axis_size("pipe")
    groups = lax.axis_size("z")
    my_section = lax.axis_index("pipe")
    directions, micro_count, length, width = tokens.shape
    micro_total = directions * micro_count
    micro_local = -(-micro_total // sections)
    rows = groups * micro_local * length
    local = width // groups
    own = first_map.shape[1]
    rank = first_map.shape[2]
    heads = local // HD
    size = block_size(rows)
    blocks = rows // size
    sides = lax.axis_size("core")

    wanted = my_section * micro_local + jnp.arange(micro_local, dtype=jnp.int32)
    live = (wanted < micro_total).astype(jnp.int32)
    slots = jnp.minimum(wanted, micro_total - 1)
    payload, packed = pack(
        slots,
        live,
        starts.reshape(micro_total, -1),
        counts.reshape(micro_total),
        tokens.reshape(micro_total, length, width),
        cotangents.reshape(micro_total, length, width),
        layer_gains,
        first_map,
        second_map,
        groups,
    )
    received = lax.all_to_all(payload, "z", split_axis=0, concat_axis=0, tiled=True)
    received = received.reshape(rows, 2 * local + HD)
    weights = lax.all_gather(packed, ("pipe", "core"), axis=0, tiled=False)
    weights = weights.reshape(sections, sides, slice_rows(own), HD)

    def exchange(pay):
        pays = [pay]
        for shift in range(1, groups):
            pays.append(
                lax.ppermute(pay, "z", [(i, (i + shift) % groups) for i in range(groups)])
            )
        return pays

    def shaped(shape, kind=BF):
        return jax.ShapeDtypeStruct(shape, kind)

    wide_shape = shaped((rows, local))
    mean_shape = shaped((rows, HD), F32)
    rank_shape = shaped((rows, rank))
    cross_shape = shaped((rows, rank), F32)
    probs_shape = shaped((blocks, heads, size, size))
    grads_shape = (sides, 2 * rank + 16, own)
    forward_rows = 2 * rows + HD

    def call(kernel, operands, specs, outs, name, **more):
        return pl.pallas_call(
            kernel,
            grid=(1,),
            in_specs=specs,
            out_specs=more.pop("out_specs", None) or vmem_specs(len(outs)),
            out_shape=outs,
            compiler_params=PARAMS,
            name=name,
            **more,
        )(*operands)

    def layer_of(index):
        return layer_spec(weights.shape, index)

    x, cot, mask, mean, probs, mixed, pay = call(
        functools.partial(first_kernel, length),
        (received, weights),
        vmem_specs(1) + [layer_of(0)],
        [
            wide_shape,
            wide_shape,
            shaped((blocks, size, size)),
            mean_shape,
            probs_shape,
            wide_shape,
            shaped((forward_rows, HD)),
        ],
        "forward_first",
    )
    xs, means, reduceds, crosses = [x], [mean], [], [None]
    all_probs, all_mixed = [probs], [mixed]
    for layer in range(1, sections - 1):
        pays = exchange(pay)
        last = layer == sections - 2
        operands = (*pays, xs[-1], means[-1], mask, weights, weights)
        specs = vmem_specs(len(pays) + 3) + [layer_of(layer - 1), layer_of(layer)]
        if last:
            operands += (cot, weights)
            specs += vmem_specs(1) + [layer_of(layer + 1)]
        x, mean, reduced, cross, probs, mixed, pay = call(
            functools.partial(middle_kernel, len(pays), last, float(width)),
            operands,
            specs,
            [
                wide_shape,
                mean_shape,
                rank_shape,
                cross_shape,
                probs_shape,
                wide_shape,
                shaped((forward_rows + (rows if last else 0), HD)),
            ],
            "forward_middle",
        )
        xs.append(x)
        means.append(mean)
        reduceds.append(reduced)
        crosses.append(cross)
        all_probs.append(probs)
        all_mixed.append(mixed)

    pays = exchange(pay)
    top = sections - 1
    back_rows = rows + 16 * blocks
    x, mean, reduced, cross, turn_grads, carried, pay = call(
        functools.partial(turn_kernel, len(pays), float(width)),
        (*pays, xs[-1], means[-1], mask, weights, weights, cot),
        vmem_specs(len(pays) + 3) + [layer_of(top - 1), layer_of(top)] + vmem_specs(1),
        [
            wide_shape,
            mean_shape,
            rank_shape,
            cross_shape,
            shaped(grads_shape),
            wide_shape,
            shaped((back_rows + rows, HD)),
        ],
        "turn",
        scratch_shapes=[
            pltpu.VMEM(probs_shape.shape, BF),
            pltpu.VMEM(wide_shape.shape, BF),
        ],
    )
    xs.append(x)
    means.append(mean)
    reduceds.append(reduced)
    crosses.append(cross)

    grads = None
    for layer in range(top - 1, -1, -1):
        pays = exchange(pay)
        after_turn = layer == top - 1
        to_first = layer == 0
        operands = (
            *pays, carried, xs[layer + 1], means[layer + 1], crosses[layer + 1],
            xs[layer], means[layer], mask, weights,
        )
        specs = vmem_specs(len(pays) + 7) + [layer_of(layer)]
        if not to_first:
            operands += (weights,)
            specs += [layer_of(layer - 1)]
        operands += (all_probs[layer], all_mixed[layer], reduceds[layer])
        specs += vmem_specs(3)
        more = {}
        if after_turn:
            operands += (cot, turn_grads)
            specs += vmem_specs(2)
            block = (2,) + grads_shape
            place = layer // 2
        else:
            operands += (grads,)
            specs += [pl.BlockSpec(memory_space=pl.ANY)]
            more["input_output_aliases"] = {len(operands) - 1: 0}
            block = (1,) + grads_shape
            place = layer
        outs = [shaped((sections,) + grads_shape)]
        out_specs = [pl.BlockSpec(block, lambda *_, place=place: (place, 0, 0, 0))]
        if not to_first:
            outs += [wide_shape, shaped((back_rows, HD))]
            out_specs += vmem_specs(2)
        result = call(
            functools.partial(back_kernel, len(pays), after_turn, to_first, float(width)),
            operands,
            specs,
            outs,
            "backward",
            out_specs=out_specs,
            scratch_shapes=[pltpu.VMEM(wide_shape.shape, BF)],
            **more,
        )
        grads = result[0]
        if not to_first:
            carried, pay = result[1:]

    parts = lax.all_to_all(
        grads.reshape((sections * sides,) + grads_shape[1:]),
        ("pipe", "core"),
        split_axis=0,
        concat_axis=0,
        tiled=True,
    )
    gain_grad, first_grad, second_grad = call(
        finish_kernel,
        (parts,),
        vmem_specs(1),
        [
            shaped((1, own), F32),
            shaped((1, own, rank), F32),
            shaped((1, rank, own), F32),
        ],
        "finish",
    )
    return (gain_grad, first_grad, second_grad)


def solution(mesh):
    fine = Mesh(
        mesh.devices.reshape(mesh.shape["pipe"], mesh.shape["dp"] // 2, 2), ("pipe", "z", "core")
    )
    data = ("z", "core")
    in_specs = (
        P(None, data, None, None),
        P(None, data, None, None),
        P(None, data, None),
        P(None, data),
        P("pipe", data),
        P("pipe", data, None),
        P("pipe", None, data),
    )
    out_specs = (P("pipe", data), P("pipe", data, None), P("pipe", None, data))
    mapped = jax.shard_map(
        per_device, mesh=fine, in_specs=in_specs, out_specs=out_specs, check_vma=False
    )

    return mapped
```

```python
import functools

import jax
import jax.numpy as jnp
from jax import lax
from jax.experimental import pallas as pl
from jax.experimental.pallas import tpu as pltpu
from jax.sharding import Mesh, PartitionSpec as P

HD = 128
EPS = 1e-05
BF = jnp.bfloat16
F32 = jnp.float32
PARAMS = pltpu.CompilerParams(vmem_limit_bytes=48 * 1024 * 1024)


def dot(a, b):
    return jnp.dot(a, b, preferred_element_type=F32)


def dot_nt(a, b):
    return lax.dot_general(a, b, (((1,), (1,)), ((), ())), preferred_element_type=F32)


def dot_tn(a, b):
    return lax.dot_general(a, b, (((0,), (0,)), ((), ())), preferred_element_type=F32)


def two_parts(value):
    high = value.astype(BF)
    return high, (value - high.astype(F32)).astype(BF)


def vmem_specs(count):
    return [pl.BlockSpec(memory_space=pltpu.VMEM)] * count


def layer_spec(shape, layer):
    return pl.BlockSpec((1,) + shape[1:], lambda *_: (layer, 0, 0, 0))


def slice_rows(own):
    return 2 * own + 16


def pack_kernel(groups, micro_local, *refs):
    tokens, cotangents, starts, counts, gain, first, second = refs[:7]
    token_parts, cot_parts = refs[7 : 7 + groups], refs[7 + groups : 7 + 2 * groups]
    weights = refs[7 + 2 * groups]
    tok, cot, starts_in, counts_in, gain_in, second_in, sems = refs[8 + 2 * groups :]
    directions, micro_count, length, width = tokens.shape
    local = width // groups
    own = first.shape[1]
    section = lax.axis_index("pipe")
    group = lax.axis_index("z")
    picks = []
    copies = [
        pltpu.make_async_copy(second.at[0], second_in, sems.at[0]),
        pltpu.make_async_copy(gain, gain_in, sems.at[1]),
        pltpu.make_async_copy(first.at[0], weights.at[pl.ds(0, own)], sems.at[2]),
        pltpu.make_async_copy(starts, starts_in, sems.at[3]),
        pltpu.make_async_copy(counts, counts_in, sems.at[4]),
    ]
    for micro in range(micro_local):
        wanted = section * micro_local + micro
        slot = jnp.minimum(wanted, directions * micro_count - 1)
        direction, place = slot // micro_count, slot % micro_count
        picks.append((wanted < directions * micro_count, direction, place))
        rows = pl.ds(micro * length, length)
        copies.append(
            pltpu.make_async_copy(
                tokens.at[direction, place], tok.at[rows], sems.at[5 + 2 * micro]
            )
        )
        copies.append(
            pltpu.make_async_copy(
                cotangents.at[direction, place], cot.at[rows], sems.at[6 + 2 * micro]
            )
        )
    for copy in copies:
        copy.start()
    for copy in copies:
        copy.wait()
    weights[own : 2 * own, :] = second_in[...].astype(F32).T.astype(BF)
    gains = [gain_in[0:1, head * HD : (head + 1) * HD].astype(F32) for head in range(own // HD)]
    gains.append(jnp.zeros((16 - own // HD, HD), F32))
    weights[2 * own :, :] = jnp.concatenate(gains, axis=0).astype(BF)
    for micro, (keep, direction, place) in enumerate(picks):
        rows = slice(micro * length, (micro + 1) * length)
        widened = tok[rows, :].astype(F32)
        mean = jnp.mean(widened * widened, axis=1, keepdims=True)
        mean_high, mean_low = two_parts(mean)
        position = lax.broadcasted_iota(jnp.int32, (length, HD), 0)
        document = jnp.zeros((length, HD), jnp.int32)
        for entry in range(starts.shape[2]):
            begun = starts_in[direction, place, entry] <= position
            begun = begun & (entry < counts_in[direction, place])
            document = document + begun.astype(jnp.int32)
        lane = lax.broadcasted_iota(jnp.int32, (length, HD), 1)
        tail = jnp.where(
            lane == 0,
            document.astype(F32),
            jnp.where(lane == 1, mean_high.astype(F32), mean_low.astype(F32)),
        ).astype(BF)
        for shift in range(groups):
            start = pl.multiple_of(((group + shift) % groups) * local, local)
            token_parts[shift][rows, 0:local] = tok[rows, pl.ds(start, local)]
            token_parts[shift][rows, local:] = tail
            cotangent = cot[rows, pl.ds(start, local)]
            cot_parts[shift][rows, :] = jnp.where(keep, cotangent, jnp.zeros_like(cotangent))


def pack(tokens, cotangents, starts, counts, gain, first, second, groups, micro_local):
    length, width = tokens.shape[2:]
    own = first.shape[1]
    local = width // groups
    rows = micro_local * length
    shape = jax.ShapeDtypeStruct
    results = pl.pallas_call(
        functools.partial(pack_kernel, groups, micro_local),
        in_specs=[pl.BlockSpec(memory_space=pltpu.HBM)] * 7,
        out_specs=vmem_specs(2 * groups + 1),
        out_shape=[shape((rows, local + HD), BF)] * groups
        + [shape((rows, local), BF)] * groups
        + [shape((slice_rows(own), HD), BF)],
        scratch_shapes=[
            pltpu.VMEM((rows, width), BF),
            pltpu.VMEM((rows, width), BF),
            pltpu.SMEM(starts.shape, jnp.int32),
            pltpu.SMEM(counts.shape, jnp.int32),
            pltpu.VMEM(gain.shape, BF),
            pltpu.VMEM(second.shape[1:], BF),
            pltpu.SemaphoreType.DMA((5 + 2 * micro_local,)),
        ],
        compiler_params=PARAMS,
        name="pack",
    )(tokens, cotangents, starts, counts, gain, first, second)
    return results[:groups], results[groups : 2 * groups], results[2 * groups]


def head_gain(weights, head):
    own = (weights.shape[2] - 16) // 2
    per_slice = own // HD
    row = 2 * own + head % per_slice
    return weights[0, head // per_slice, row : row + 1, :].astype(F32)


def block_size(rows):
    return HD if rows % HD == 0 else rows


def to_rank(value, weights, at):
    own = (weights.shape[2] - 16) // 2
    total = None
    for side in range(weights.shape[1]):
        term = dot(value[:, side * own : (side + 1) * own], weights[0, side, at : at + own, :])
        total = term if total is None else total + term
    return total


def from_rank(value, weights, at, side):
    own = (weights.shape[2] - 16) // 2
    return dot_nt(value, weights[0, side, at : at + own, :])


def gram(weights):
    own = (weights.shape[2] - 16) // 2
    total = None
    for side in range(weights.shape[1]):
        part = weights[0, side, own : 2 * own, :]
        term = dot_tn(part, part)
        total = term if total is None else total + term
    return total


def attend(x, mean, weights, mask, probs, mixed):
    rows, local = x.shape
    size = block_size(rows)
    factor = lax.rsqrt(mean + EPS)
    for block in range(rows // size):
        span = slice(block * size, (block + 1) * size)
        allowed = mask[block] > 0
        for head in range(local // HD):
            part = slice(head * HD, (head + 1) * HD)
            normed = (x[span, part].astype(F32) * factor[span] * head_gain(weights, head)).astype(BF)
            scores = dot_nt(normed, normed) * (1.0 / HD)
            raw = jnp.where(allowed, jnp.exp(scores), 0.0)
            prob = (raw / jnp.sum(raw, axis=1, keepdims=True)).astype(BF)
            probs[block, head] = prob
            mixed[span, part] = dot(prob, normed).astype(BF)


def send_forward(x, weights, mixed, pay):
    rows = x.shape[0]
    own = (weights.shape[2] - 16) // 2
    pay[0:rows, :] = to_rank(mixed[...], weights, 0).astype(BF)
    pay[rows : 2 * rows, :] = to_rank(x[...], weights, own).astype(BF)
    pay[2 * rows : 2 * rows + HD, :] = gram(weights).astype(BF)


def total_of(pays, start, stop):
    total = pays[0][start:stop, :].astype(F32)
    for pay in pays[1:]:
        total = total + pay[start:stop, :].astype(F32)
    return total


def receive_forward(pays, x_before, mean_before, weights_before, width, x, mean, reduced, cross):
    rows, local = x_before.shape
    own = (weights_before.shape[2] - 16) // 2
    low_rank = total_of(pays, 0, rows).astype(BF)
    before = total_of(pays, rows, 2 * rows)
    high, low = two_parts(total_of(pays, 2 * rows, 2 * rows + HD))
    through = dot(low_rank, high) + dot(low_rank, low)
    wide = low_rank.astype(F32)
    change = jnp.sum(wide * (2.0 * before + through), axis=1, keepdims=True) / width
    new_mean = jnp.maximum(mean_before[:, 0:1] + change, 0.0)
    mean[...] = jnp.broadcast_to(new_mean, mean.shape)
    reduced[...] = low_rank
    cross[...] = before + through
    for side in range(weights_before.shape[1]):
        part = slice(side * own, (side + 1) * own)
        x[:, part] = (
            x_before[:, part].astype(F32) + from_rank(low_rank, weights_before, own, side)
        ).astype(BF)


def first_kernel(length, groups, sections, *refs):
    received, refs = refs[:groups], refs[groups:]
    mine, theirs = refs[:sections], refs[sections : 2 * sections]
    x, mask, mean, probs, mixed, pay, weights, tails, sems = refs[2 * sections :]
    section, core = lax.axis_index("pipe"), lax.axis_index("core")
    rows, local = x.shape
    size = block_size(rows)
    copies = []
    for distance in range(sections):
        layer = section ^ distance
        for parts, side in ((mine, core), (theirs, 1 - core)):
            copies.append(
                pltpu.make_async_copy(
                    parts[distance], weights.at[layer, side], sems.at[distance, side]
                )
            )
    for copy in copies:
        copy.start()
    place_rows(received, tails, slice(local, None))
    place_rows(received, x, slice(0, local))
    tail = tails[...].astype(F32)
    mean[...] = jnp.broadcast_to(tail[:, 1:2] + tail[:, 2:3], mean.shape)
    build_mask(tail[:, 0:1], mask, size, length)
    for copy in copies:
        copy.wait()
    attend(x, mean[:, 0:1], weights, mask, probs, mixed)
    send_forward(x, weights, mixed, pay)


def place_rows(received, target, columns):
    groups = len(received)
    rows = received[0].shape[0]
    for shift, part in enumerate(received):
        source = (lax.axis_index("z") + groups - shift) % groups
        target[pl.ds(pl.multiple_of(source * rows, rows), rows), :] = part[:, columns]


def build_mask(document, mask, size, length):
    query = lax.broadcasted_iota(jnp.int32, (size, size), 0)
    key = lax.broadcasted_iota(jnp.int32, (size, size), 1)
    for block in range(mask.shape[0]):
        by_query = jnp.broadcast_to(document[block * size : (block + 1) * size], (size, size))
        by_key = by_query.T
        allowed = (by_query == by_key) & (key <= query) & (query // length == key // length)
        mask[block] = allowed.astype(F32).astype(BF)


def middle_kernel(count, last, width, groups, *refs):
    pays, refs = refs[:count], refs[count:]
    x_before, mean_before, mask, weights_before, weights = refs[:5]
    refs = refs[5:]
    if last:
        received, weights_after = refs[:groups], refs[groups]
        refs = refs[groups + 1 :]
    x, mean, reduced, cross, probs, mixed, pay = refs[:7]
    receive_forward(
        pays, x_before, mean_before, weights_before, width, x, mean, reduced, cross
    )
    attend(x, mean[:, 0:1], weights, mask, probs, mixed)
    send_forward(x, weights, mixed, pay)
    if last:
        cot = refs[7]
        place_rows(received, cot, slice(None))
        rows = x.shape[0]
        own = (weights.shape[2] - 16) // 2
        pay[2 * rows + HD :, :] = to_rank(cot[...], weights_after, own).astype(BF)


def layer_backward(
    dout, dred, x, mean, mask, weights, weights_before, probs, mixed, reduced, grads, carried, pay
):
    rows, local = x.shape
    size = block_size(rows)
    own = (weights.shape[2] - 16) // 2
    per_slice = own // HD
    rank = dred.shape[1]
    factor = lax.rsqrt(mean + EPS)
    first = dot_tn(dred, mixed[...]).astype(BF)
    for side in range(weights.shape[1]):
        grads[side, 0:rank, :] = first[:, side * own : (side + 1) * own]
    if reduced is not None:
        second = dot_tn(reduced, dout[...]).astype(BF)
        for side in range(weights.shape[1]):
            grads[side, rank : 2 * rank, :] = second[:, side * own : (side + 1) * own]
    back_mixed = [
        from_rank(dred, weights, 0, side).astype(BF) for side in range(weights.shape[1])
    ]
    gain_sums = [None] * (local // HD)
    for block in range(rows // size):
        span = slice(block * size, (block + 1) * size)
        scale = factor[span]
        norm_dot = jnp.zeros((size, HD), F32)
        for head in range(local // HD):
            part = slice(head * HD, (head + 1) * HD)
            side, inner = head // per_slice, (head % per_slice) * HD
            wide = x[span, part].astype(F32)
            gain = head_gain(weights, head)
            unit = wide * scale
            normed = (unit * gain).astype(BF)
            prob = probs[block, head]
            upstream = back_mixed[side][span, inner : inner + HD]
            back_prob = dot_nt(upstream, normed)
            prob_wide = prob.astype(F32)
            inner_sum = jnp.sum(back_prob * prob_wide, axis=1, keepdims=True)
            back_score = prob_wide * (back_prob - inner_sum) * (1.0 / HD)
            both = (back_score + back_score.T).astype(BF)
            back_normed = (dot_tn(prob, upstream) + dot(both, normed)).astype(BF).astype(F32)
            term = jnp.sum(back_normed * unit, axis=0, keepdims=True)
            gain_sums[head] = term if gain_sums[head] is None else gain_sums[head] + term
            if carried is not None:
                scaled = back_normed * gain
                norm_dot = norm_dot + scaled * wide
                carried[span, part] = (dout[span, part].astype(F32) + scaled * scale).astype(BF)
        if carried is not None:
            column = jnp.broadcast_to(jnp.sum(norm_dot, axis=1, keepdims=True), (size, size))
            line = column.T[0:1, :]
            high, low = two_parts(line)
            base = rows + 16 * block
            pay[base : base + 16, :] = jnp.concatenate(
                (high.astype(F32), low.astype(F32), jnp.zeros((14, size), F32)), axis=0
            ).astype(BF)
    zeros = jnp.zeros((15, HD), F32)
    for head in range(local // HD):
        side, inner = head // per_slice, (head % per_slice) * HD
        grads[side, 2 * rank : 2 * rank + 16, inner : inner + HD] = jnp.concatenate(
            (gain_sums[head], zeros), axis=0
        ).astype(BF)
    if carried is not None:
        pay[0:rows, :] = to_rank(carried[...], weights_before, own).astype(BF)


def turn_kernel(count, width, *refs):
    pays, refs = refs[:count], refs[count:]
    (x_before, mean_before, mask, weights_before, weights, cot) = refs[:6]
    (x, mean, reduced, cross, grads, carried, pay) = refs[6:13]
    probs, mixed = refs[13:]
    rows = x.shape[0]
    receive_forward(
        pays, x_before, mean_before, weights_before, width, x, mean, reduced, cross
    )
    attend(x, mean[:, 0:1], weights, mask, probs, mixed)
    dred = total_of(pays, 2 * rows + HD, 3 * rows + HD).astype(BF)
    layer_backward(
        cot, dred, x, mean[:, 0:1], mask, weights, weights_before, probs, mixed, None, grads,
        carried, pay,
    )
    pay[pay.shape[0] - rows :, :] = to_rank(mixed[...], weights, 0).astype(BF)


def split_sides(grads, keep, send):
    core = lax.axis_index("core")
    keep[...] = grads[core]
    send[...] = grads[1 - core]


def back_kernel(count, after_turn, to_first, width, *refs):
    pays, refs = refs[:count], refs[count:]
    carried_after, x_after, mean_after, cross_after = refs[:4]
    x, mean, mask, weights = refs[4:8]
    refs = refs[8:]
    weights_before = carried = pay = None
    if not to_first:
        weights_before, refs = refs[0], refs[1:]
    probs, mixed, reduced = refs[:3]
    refs = refs[3:]
    if after_turn:
        cot, turn_grads = refs[:2]
        refs = refs[2:]
    keep, send = refs[:2]
    refs = refs[2:]
    if after_turn:
        last_keep, last_send = refs[:2]
        refs = refs[2:]
    if not to_first:
        carried, pay = refs[:2]
        refs = refs[2:]
    dout, grads = refs
    rows, local = x.shape
    size = block_size(rows)
    own = (weights.shape[2] - 16) // 2
    rank = reduced.shape[1]
    dred_parts = []
    for block in range(rows // size):
        span = slice(block * size, (block + 1) * size)
        base = rows + 16 * block
        lines = total_of(pays, base, base + 16)
        line = lines[0:1] + lines[1:2]
        column = jnp.broadcast_to(line, (size, size)).T
        factor = lax.rsqrt(mean_after[span, 0:1] + EPS)
        pull = column[:, 0:1] * (factor * factor * factor / width)
        dred_parts.append(
            (
                total_of(pays, block * size, (block + 1) * size) - cross_after[span, :] * pull
            ).astype(BF)
        )
        dout[span, :] = (
            carried_after[span, :].astype(F32) - x_after[span, :].astype(F32) * pull
        ).astype(BF)
    dred = dred_parts[0] if len(dred_parts) == 1 else jnp.concatenate(dred_parts, axis=0)
    if after_turn:
        last_reduced = total_of(pays, pays[0].shape[0] - rows, pays[0].shape[0]).astype(BF)
        second = dot_tn(last_reduced, cot[...]).astype(BF)
        for side in range(weights.shape[1]):
            grads[side, 0:rank, :] = turn_grads[side, 0:rank, :]
            grads[side, rank : 2 * rank, :] = second[:, side * own : (side + 1) * own]
            grads[side, 2 * rank :, :] = turn_grads[side, 2 * rank :, :]
        split_sides(grads, last_keep, last_send)
    layer_backward(
        dout, dred, x, mean[:, 0:1], mask, weights, weights_before, probs, mixed, reduced[...],
        grads, carried, pay,
    )
    split_sides(grads, keep, send)


def combine_kernel(sections, *refs):
    kept, swapped = refs[:sections], refs[sections : 2 * sections]
    outs, sums = refs[2 * sections : 3 * sections], refs[3 * sections]
    section = lax.axis_index("pipe")
    for layer in range(sections):
        sums[layer] = (kept[layer][...].astype(F32) + swapped[layer][...].astype(F32)).astype(BF)
    for distance in range(sections):
        outs[distance][...] = sums[section ^ distance]


def finish_kernel(sections, *refs):
    parts = refs[:sections]
    gain, first, second = refs[sections:]
    rank = second.shape[1]
    total = parts[0][...].astype(F32)
    for part in parts[1:]:
        total = total + part[...].astype(F32)
    first[0] = total[0:rank].T
    second[0] = total[rank : 2 * rank]
    gain[...] = total[2 * rank : 2 * rank + 1]


def per_device(tokens, cotangents, starts, counts, layer_gains, first_map, second_map):
    sections = lax.axis_size("pipe")
    groups = lax.axis_size("z")
    directions, micro_count, length, width = tokens.shape
    micro_local = -(-directions * micro_count // sections)
    rows = groups * micro_local * length
    local = width // groups
    own = first_map.shape[1]
    rank = first_map.shape[2]
    heads = local // HD
    size = block_size(rows)
    blocks = rows // size
    sides = lax.axis_size("core")
    top = sections - 1

    def shifted(value, shift):
        return lax.ppermute(value, "z", [(i, (i + shift) % groups) for i in range(groups)])

    def across(value, distance):
        return lax.ppermute(value, "pipe", [(i, i ^ distance) for i in range(sections)])

    def swapped(value):
        return lax.ppermute(value, "core", [(i, 1 - i) for i in range(sides)])

    def exchange(pay):
        return [pay] + [shifted(pay, shift) for shift in range(1, groups)]

    token_parts, cot_parts, packed = pack(
        tokens, cotangents, starts, counts, layer_gains, first_map, second_map, groups, micro_local
    )
    received = [token_parts[0]]
    received += [shifted(token_parts[shift], shift) for shift in range(1, groups)]
    mine = [packed] + [across(packed, distance) for distance in range(1, sections)]
    theirs = [swapped(part) for part in mine]
    cot_received = [cot_parts[0]]
    cot_received += [shifted(cot_parts[shift], shift) for shift in range(1, groups)]

    def shaped(shape, kind=BF):
        return jax.ShapeDtypeStruct(shape, kind)

    wide_shape = shaped((rows, local))
    mean_shape = shaped((rows, HD), F32)
    rank_shape = shaped((rows, rank))
    cross_shape = shaped((rows, rank), F32)
    probs_shape = shaped((blocks, heads, size, size))
    grads_shape = (sides, 2 * rank + 16, own)
    half_shape = shaped(grads_shape[1:])
    weights_shape = shaped((sections, sides, slice_rows(own), HD))
    forward_rows = 2 * rows + HD

    def call(kernel, operands, specs, outs, name, **more):
        return pl.pallas_call(
            kernel,
            grid=(1,),
            in_specs=specs,
            out_specs=vmem_specs(len(outs)),
            out_shape=outs,
            compiler_params=PARAMS,
            name=name,
            **more,
        )(*operands)

    def layer_of(index):
        return layer_spec(weights_shape.shape, index)

    x, mask, mean, probs, mixed, pay, weights = call(
        functools.partial(first_kernel, length, groups, sections),
        (*received, *mine, *theirs),
        vmem_specs(groups + 2 * sections),
        [
            wide_shape,
            shaped((blocks, size, size)),
            mean_shape,
            probs_shape,
            wide_shape,
            shaped((forward_rows, HD)),
            weights_shape,
        ],
        "forward_first",
        scratch_shapes=[
            pltpu.VMEM((rows, HD), BF),
            pltpu.SemaphoreType.DMA((sections, sides)),
        ],
    )
    xs, means, reduceds, crosses = [x], [mean], [], [None]
    all_probs, all_mixed = [probs], [mixed]
    for layer in range(1, top):
        pays = exchange(pay)
        last = layer == top - 1
        operands = (*pays, xs[-1], means[-1], mask, weights, weights)
        specs = vmem_specs(len(pays) + 3) + [layer_of(layer - 1), layer_of(layer)]
        outs = [
            wide_shape,
            mean_shape,
            rank_shape,
            cross_shape,
            probs_shape,
            wide_shape,
            shaped((forward_rows + (rows if last else 0), HD)),
        ]
        if last:
            operands += (*cot_received, weights)
            specs += vmem_specs(groups) + [layer_of(layer + 1)]
            outs += [wide_shape]
        x, mean, reduced, cross, probs, mixed, pay, *cots = call(
            functools.partial(middle_kernel, len(pays), last, float(width), groups),
            operands,
            specs,
            outs,
            "forward_middle",
        )
        xs.append(x)
        means.append(mean)
        reduceds.append(reduced)
        crosses.append(cross)
        all_probs.append(probs)
        all_mixed.append(mixed)
    cot = cots[0]

    pays = exchange(pay)
    back_rows = rows + 16 * blocks
    x, mean, reduced, cross, turn_grads, carried, pay = call(
        functools.partial(turn_kernel, len(pays), float(width)),
        (*pays, xs[-1], means[-1], mask, weights, weights, cot),
        vmem_specs(len(pays) + 3) + [layer_of(top - 1), layer_of(top)] + vmem_specs(1),
        [
            wide_shape,
            mean_shape,
            rank_shape,
            cross_shape,
            shaped(grads_shape),
            wide_shape,
            shaped((back_rows + rows, HD)),
        ],
        "turn",
        scratch_shapes=[
            pltpu.VMEM(probs_shape.shape, BF),
            pltpu.VMEM(wide_shape.shape, BF),
        ],
    )
    xs.append(x)
    means.append(mean)
    reduceds.append(reduced)
    crosses.append(cross)

    kept, taken = [None] * sections, [None] * sections
    for layer in range(top - 1, -1, -1):
        pays = exchange(pay)
        after_turn = layer == top - 1
        to_first = layer == 0
        operands = (
            *pays, carried, xs[layer + 1], means[layer + 1], crosses[layer + 1],
            xs[layer], means[layer], mask, weights,
        )
        specs = vmem_specs(len(pays) + 7) + [layer_of(layer)]
        if not to_first:
            operands += (weights,)
            specs += [layer_of(layer - 1)]
        operands += (all_probs[layer], all_mixed[layer], reduceds[layer])
        specs += vmem_specs(3)
        outs = [half_shape] * 2
        if after_turn:
            operands += (cot, turn_grads)
            specs += vmem_specs(2)
            outs += [half_shape] * 2
        if not to_first:
            outs += [wide_shape, shaped((back_rows, HD))]
        result = call(
            functools.partial(back_kernel, len(pays), after_turn, to_first, float(width)),
            operands,
            specs,
            outs,
            "backward",
            scratch_shapes=[pltpu.VMEM(wide_shape.shape, BF), pltpu.VMEM(grads_shape, BF)],
        )
        kept[layer], taken[layer] = result[0], swapped(result[1])
        if after_turn:
            kept[top], taken[top] = result[2], swapped(result[3])
        if not to_first:
            carried, pay = result[-2:]

    parts = call(
        functools.partial(combine_kernel, sections),
        (*kept, *taken),
        vmem_specs(2 * sections),
        [half_shape] * sections,
        "combine",
        scratch_shapes=[pltpu.VMEM((sections,) + grads_shape[1:], BF)],
    )
    arrived = [parts[0]] + [across(parts[distance], distance) for distance in range(1, sections)]
    gain_grad, first_grad, second_grad = call(
        functools.partial(finish_kernel, sections),
        arrived,
        vmem_specs(sections),
        [
            shaped((1, own), F32),
            shaped((1, own, rank), F32),
            shaped((1, rank, own), F32),
        ],
        "finish",
    )
    return (gain_grad, first_grad, second_grad)


def solution(mesh):
    fine = Mesh(
        mesh.devices.reshape(mesh.shape["pipe"], mesh.shape["dp"] // 2, 2), ("pipe", "z", "core")
    )
    data = ("z", "core")
    in_specs = (
        P(None, data, None, None),
        P(None, data, None, None),
        P(None, data, None),
        P(None, data),
        P("pipe", data),
        P("pipe", data, None),
        P("pipe", None, data),
    )
    out_specs = (P("pipe", data), P("pipe", data, None), P("pipe", None, data))
    mapped = jax.shard_map(
        per_device, mesh=fine, in_specs=in_specs, out_specs=out_specs, check_vma=False
    )

    return mapped
```

```python
import functools

import jax
import jax.numpy as jnp
from jax import lax
from jax.experimental import pallas as pl
from jax.experimental.pallas import tpu as pltpu
from jax.sharding import Mesh, PartitionSpec as P

HD = 128
EPS = 1e-05
BF = jnp.bfloat16
F32 = jnp.float32
PARAMS = pltpu.CompilerParams(vmem_limit_bytes=48 * 1024 * 1024)
PACK_PARAMS = pltpu.CompilerParams(vmem_limit_bytes=60 * 1024 * 1024)


def dot(a, b):
    return jnp.dot(a, b, preferred_element_type=F32)


def dot_nt(a, b):
    return lax.dot_general(a, b, (((1,), (1,)), ((), ())), preferred_element_type=F32)


def dot_tn(a, b):
    return lax.dot_general(a, b, (((0,), (0,)), ((), ())), preferred_element_type=F32)


def two_parts(value):
    high = value.astype(BF)
    return high, (value - high.astype(F32)).astype(BF)


def vmem_specs(count):
    return [pl.BlockSpec(memory_space=pltpu.VMEM)] * count


def layer_spec(shape, layer):
    return pl.BlockSpec((1,) + shape[1:], lambda *_: (layer, 0, 0, 0))


def slice_rows(own):
    return 2 * own + 16


def pack_kernel(groups, micro_local, *refs):
    tokens, cotangents, starts, counts, gain, first, second = refs[:7]
    parts, weights = refs[7 : 7 + groups], refs[7 + groups]
    tok, cot, starts_in, counts_in, gain_in, second_in, sems = refs[8 + groups :]
    directions, micro_count, length, width = tokens.shape
    local = width // groups
    own = first.shape[1]
    section = lax.axis_index("pipe")
    group = lax.axis_index("z")
    picks = []
    copies = [
        pltpu.make_async_copy(second.at[0], second_in, sems.at[0]),
        pltpu.make_async_copy(gain, gain_in, sems.at[1]),
        pltpu.make_async_copy(first.at[0], weights.at[pl.ds(0, own)], sems.at[2]),
        pltpu.make_async_copy(starts, starts_in, sems.at[3]),
        pltpu.make_async_copy(counts, counts_in, sems.at[4]),
    ]
    for micro in range(micro_local):
        wanted = section * micro_local + micro
        slot = jnp.minimum(wanted, directions * micro_count - 1)
        direction, place = slot // micro_count, slot % micro_count
        picks.append((wanted < directions * micro_count, direction, place))
        rows = pl.ds(micro * length, length)
        copies.append(
            pltpu.make_async_copy(
                tokens.at[direction, place], tok.at[rows], sems.at[5 + 2 * micro]
            )
        )
        copies.append(
            pltpu.make_async_copy(
                cotangents.at[direction, place], cot.at[rows], sems.at[6 + 2 * micro]
            )
        )
    for copy in copies:
        copy.start()
    for copy in copies:
        copy.wait()
    weights[own : 2 * own, :] = second_in[...].astype(F32).T.astype(BF)
    gains = [gain_in[0:1, head * HD : (head + 1) * HD].astype(F32) for head in range(own // HD)]
    gains.append(jnp.zeros((16 - own // HD, HD), F32))
    weights[2 * own :, :] = jnp.concatenate(gains, axis=0).astype(BF)
    for micro, (keep, direction, place) in enumerate(picks):
        rows = slice(micro * length, (micro + 1) * length)
        widened = tok[rows, :].astype(F32)
        mean = jnp.mean(widened * widened, axis=1, keepdims=True)
        mean_high, mean_low = two_parts(mean)
        position = lax.broadcasted_iota(jnp.int32, (length, HD), 0)
        document = jnp.zeros((length, HD), jnp.int32)
        for entry in range(starts.shape[2]):
            begun = starts_in[direction, place, entry] <= position
            begun = begun & (entry < counts_in[direction, place])
            document = document + begun.astype(jnp.int32)
        lane = lax.broadcasted_iota(jnp.int32, (length, HD), 1)
        tail = jnp.where(
            lane == 0,
            document.astype(F32),
            jnp.where(lane == 1, mean_high.astype(F32), mean_low.astype(F32)),
        ).astype(BF)
        for shift in range(groups):
            start = pl.multiple_of(((group + shift) % groups) * local, local)
            parts[shift][rows, 0:local] = tok[rows, pl.ds(start, local)]
            cotangent = cot[rows, pl.ds(start, local)]
            parts[shift][rows, local : 2 * local] = jnp.where(
                keep, cotangent, jnp.zeros_like(cotangent)
            )
            parts[shift][rows, 2 * local :] = tail


def pack(tokens, cotangents, starts, counts, gain, first, second, groups, micro_local):
    length, width = tokens.shape[2:]
    own = first.shape[1]
    local = width // groups
    rows = micro_local * length
    shape = jax.ShapeDtypeStruct
    results = pl.pallas_call(
        functools.partial(pack_kernel, groups, micro_local),
        in_specs=[pl.BlockSpec(memory_space=pltpu.HBM)] * 7,
        out_specs=vmem_specs(groups + 1),
        out_shape=[shape((rows, 2 * local + HD), BF)] * groups
        + [shape((slice_rows(own), HD), BF)],
        scratch_shapes=[
            pltpu.VMEM((rows, width), BF),
            pltpu.VMEM((rows, width), BF),
            pltpu.SMEM(starts.shape, jnp.int32),
            pltpu.SMEM(counts.shape, jnp.int32),
            pltpu.VMEM(gain.shape, BF),
            pltpu.VMEM(second.shape[1:], BF),
            pltpu.SemaphoreType.DMA((5 + 2 * micro_local,)),
        ],
        compiler_params=PACK_PARAMS,
        name="pack",
    )(tokens, cotangents, starts, counts, gain, first, second)
    return results[:groups], results[groups]


def head_gain(weights, head):
    own = (weights.shape[2] - 16) // 2
    per_slice = own // HD
    row = 2 * own + head % per_slice
    return weights[0, head // per_slice, row : row + 1, :].astype(F32)


def block_size(rows):
    return HD if rows % HD == 0 else rows


def to_rank(value, weights, at):
    own = (weights.shape[2] - 16) // 2
    total = None
    for side in range(weights.shape[1]):
        term = dot(value[:, side * own : (side + 1) * own], weights[0, side, at : at + own, :])
        total = term if total is None else total + term
    return total


def from_rank(value, weights, at, side):
    own = (weights.shape[2] - 16) // 2
    return dot_nt(value, weights[0, side, at : at + own, :])


def gram(weights):
    own = (weights.shape[2] - 16) // 2
    total = None
    for side in range(weights.shape[1]):
        part = weights[0, side, own : 2 * own, :]
        term = dot_tn(part, part)
        total = term if total is None else total + term
    return total


def attend(x, mean, weights, mask, probs, mixed):
    rows, local = x.shape
    size = block_size(rows)
    factor = lax.rsqrt(mean + EPS)
    for block in range(rows // size):
        span = slice(block * size, (block + 1) * size)
        allowed = mask[block] > 0
        for head in range(local // HD):
            part = slice(head * HD, (head + 1) * HD)
            normed = (x[span, part].astype(F32) * factor[span] * head_gain(weights, head)).astype(BF)
            scores = dot_nt(normed, normed) * (1.0 / HD)
            raw = jnp.where(allowed, jnp.exp(scores), 0.0)
            prob = (raw / jnp.sum(raw, axis=1, keepdims=True)).astype(BF)
            probs[block, head] = prob
            mixed[span, part] = dot(prob, normed).astype(BF)


def send_forward(x, weights, mixed, pay):
    rows = x.shape[0]
    own = (weights.shape[2] - 16) // 2
    pay[0:rows, :] = to_rank(mixed[...], weights, 0).astype(BF)
    pay[rows : 2 * rows, :] = to_rank(x[...], weights, own).astype(BF)
    pay[2 * rows : 2 * rows + HD, :] = gram(weights).astype(BF)


def total_of(pays, start, stop):
    total = pays[0][start:stop, :].astype(F32)
    for pay in pays[1:]:
        total = total + pay[start:stop, :].astype(F32)
    return total


def receive_forward(pays, x_before, mean_before, weights_before, width, x, mean, reduced, cross):
    rows, local = x_before.shape
    own = (weights_before.shape[2] - 16) // 2
    low_rank = total_of(pays, 0, rows).astype(BF)
    before = total_of(pays, rows, 2 * rows)
    high, low = two_parts(total_of(pays, 2 * rows, 2 * rows + HD))
    through = dot(low_rank, high) + dot(low_rank, low)
    wide = low_rank.astype(F32)
    change = jnp.sum(wide * (2.0 * before + through), axis=1, keepdims=True) / width
    new_mean = jnp.maximum(mean_before[:, 0:1] + change, 0.0)
    mean[...] = jnp.broadcast_to(new_mean, mean.shape)
    reduced[...] = low_rank
    cross[...] = before + through
    for side in range(weights_before.shape[1]):
        part = slice(side * own, (side + 1) * own)
        x[:, part] = (
            x_before[:, part].astype(F32) + from_rank(low_rank, weights_before, own, side)
        ).astype(BF)


def first_kernel(length, groups, sections, *refs):
    received, refs = refs[:groups], refs[groups:]
    mine, theirs = refs[:sections], refs[sections : 2 * sections]
    x, cot, mask, mean, probs, mixed, pay, weights, tails, sems = refs[2 * sections :]
    section, core = lax.axis_index("pipe"), lax.axis_index("core")
    rows, local = x.shape
    size = block_size(rows)
    copies = []
    for distance in range(sections):
        layer = section ^ distance
        for parts, side in ((mine, core), (theirs, 1 - core)):
            copies.append(
                pltpu.make_async_copy(
                    parts[distance], weights.at[layer, side], sems.at[distance, side]
                )
            )
    for copy in copies:
        copy.start()
    place_rows(received, tails, slice(2 * local, None))
    place_rows(received, x, slice(0, local))
    place_rows(received, cot, slice(local, 2 * local))
    tail = tails[...].astype(F32)
    mean[...] = jnp.broadcast_to(tail[:, 1:2] + tail[:, 2:3], mean.shape)
    build_mask(tail[:, 0:1], mask, size, length)
    for copy in copies:
        copy.wait()
    attend(x, mean[:, 0:1], weights, mask, probs, mixed)
    send_forward(x, weights, mixed, pay)


def place_rows(received, target, columns):
    groups = len(received)
    rows = received[0].shape[0]
    for shift, part in enumerate(received):
        source = (lax.axis_index("z") + groups - shift) % groups
        target[pl.ds(pl.multiple_of(source * rows, rows), rows), :] = part[:, columns]


def build_mask(document, mask, size, length):
    query = lax.broadcasted_iota(jnp.int32, (size, size), 0)
    key = lax.broadcasted_iota(jnp.int32, (size, size), 1)
    for block in range(mask.shape[0]):
        by_query = jnp.broadcast_to(document[block * size : (block + 1) * size], (size, size))
        by_key = by_query.T
        allowed = (by_query == by_key) & (key <= query) & (query // length == key // length)
        mask[block] = allowed.astype(F32).astype(BF)


def middle_kernel(count, last, width, *refs):
    pays, refs = refs[:count], refs[count:]
    x_before, mean_before, mask, weights_before, weights = refs[:5]
    refs = refs[5:]
    if last:
        cot, weights_after = refs[:2]
        refs = refs[2:]
    x, mean, reduced, cross, probs, mixed, pay = refs
    receive_forward(
        pays, x_before, mean_before, weights_before, width, x, mean, reduced, cross
    )
    attend(x, mean[:, 0:1], weights, mask, probs, mixed)
    send_forward(x, weights, mixed, pay)
    if last:
        rows = x.shape[0]
        own = (weights.shape[2] - 16) // 2
        pay[2 * rows + HD :, :] = to_rank(cot[...], weights_after, own).astype(BF)


def layer_backward(
    dout, dred, x, mean, mask, weights, weights_before, probs, mixed, reduced, grads, carried, pay
):
    rows, local = x.shape
    size = block_size(rows)
    own = (weights.shape[2] - 16) // 2
    per_slice = own // HD
    rank = dred.shape[1]
    factor = lax.rsqrt(mean + EPS)
    first = dot_tn(dred, mixed[...]).astype(BF)
    for side in range(weights.shape[1]):
        grads[side, 0:rank, :] = first[:, side * own : (side + 1) * own]
    if reduced is not None:
        second = dot_tn(reduced, dout[...]).astype(BF)
        for side in range(weights.shape[1]):
            grads[side, rank : 2 * rank, :] = second[:, side * own : (side + 1) * own]
    back_mixed = [
        from_rank(dred, weights, 0, side).astype(BF) for side in range(weights.shape[1])
    ]
    gain_sums = [None] * (local // HD)
    for block in range(rows // size):
        span = slice(block * size, (block + 1) * size)
        scale = factor[span]
        norm_dot = jnp.zeros((size, HD), F32)
        for head in range(local // HD):
            part = slice(head * HD, (head + 1) * HD)
            side, inner = head // per_slice, (head % per_slice) * HD
            wide = x[span, part].astype(F32)
            gain = head_gain(weights, head)
            unit = wide * scale
            normed = (unit * gain).astype(BF)
            prob = probs[block, head]
            upstream = back_mixed[side][span, inner : inner + HD]
            back_prob = dot_nt(upstream, normed)
            prob_wide = prob.astype(F32)
            inner_sum = jnp.sum(back_prob * prob_wide, axis=1, keepdims=True)
            back_score = prob_wide * (back_prob - inner_sum) * (1.0 / HD)
            both = (back_score + back_score.T).astype(BF)
            back_normed = (dot_tn(prob, upstream) + dot(both, normed)).astype(BF).astype(F32)
            term = jnp.sum(back_normed * unit, axis=0, keepdims=True)
            gain_sums[head] = term if gain_sums[head] is None else gain_sums[head] + term
            if carried is not None:
                scaled = back_normed * gain
                norm_dot = norm_dot + scaled * wide
                carried[span, part] = (dout[span, part].astype(F32) + scaled * scale).astype(BF)
        if carried is not None:
            column = jnp.broadcast_to(jnp.sum(norm_dot, axis=1, keepdims=True), (size, size))
            line = column.T[0:1, :]
            high, low = two_parts(line)
            base = rows + 16 * block
            pay[base : base + 16, :] = jnp.concatenate(
                (high.astype(F32), low.astype(F32), jnp.zeros((14, size), F32)), axis=0
            ).astype(BF)
    zeros = jnp.zeros((15, HD), F32)
    for head in range(local // HD):
        side, inner = head // per_slice, (head % per_slice) * HD
        grads[side, 2 * rank : 2 * rank + 16, inner : inner + HD] = jnp.concatenate(
            (gain_sums[head], zeros), axis=0
        ).astype(BF)
    if carried is not None:
        pay[0:rows, :] = to_rank(carried[...], weights_before, own).astype(BF)


def turn_kernel(count, width, *refs):
    pays, refs = refs[:count], refs[count:]
    (x_before, mean_before, mask, weights_before, weights, cot) = refs[:6]
    (x, mean, reduced, cross, grads, carried, pay) = refs[6:13]
    probs, mixed = refs[13:]
    rows = x.shape[0]
    receive_forward(
        pays, x_before, mean_before, weights_before, width, x, mean, reduced, cross
    )
    attend(x, mean[:, 0:1], weights, mask, probs, mixed)
    dred = total_of(pays, 2 * rows + HD, 3 * rows + HD).astype(BF)
    layer_backward(
        cot, dred, x, mean[:, 0:1], mask, weights, weights_before, probs, mixed, None, grads,
        carried, pay,
    )
    pay[pay.shape[0] - rows :, :] = to_rank(mixed[...], weights, 0).astype(BF)


def split_sides(grads, keep, send):
    core = lax.axis_index("core")
    keep[...] = grads[core]
    send[...] = grads[1 - core]


def back_kernel(count, after_turn, to_first, width, *refs):
    pays, refs = refs[:count], refs[count:]
    carried_after, x_after, mean_after, cross_after = refs[:4]
    x, mean, mask, weights = refs[4:8]
    refs = refs[8:]
    weights_before = carried = pay = None
    if not to_first:
        weights_before, refs = refs[0], refs[1:]
    probs, mixed, reduced = refs[:3]
    refs = refs[3:]
    if after_turn:
        cot, turn_grads = refs[:2]
        refs = refs[2:]
    keep, send = refs[:2]
    refs = refs[2:]
    if after_turn:
        last_keep, last_send = refs[:2]
        refs = refs[2:]
    if not to_first:
        carried, pay = refs[:2]
        refs = refs[2:]
    dout, grads = refs
    rows, local = x.shape
    size = block_size(rows)
    own = (weights.shape[2] - 16) // 2
    rank = reduced.shape[1]
    dred_parts = []
    for block in range(rows // size):
        span = slice(block * size, (block + 1) * size)
        base = rows + 16 * block
        lines = total_of(pays, base, base + 16)
        line = lines[0:1] + lines[1:2]
        column = jnp.broadcast_to(line, (size, size)).T
        factor = lax.rsqrt(mean_after[span, 0:1] + EPS)
        pull = column[:, 0:1] * (factor * factor * factor / width)
        dred_parts.append(
            (
                total_of(pays, block * size, (block + 1) * size) - cross_after[span, :] * pull
            ).astype(BF)
        )
        dout[span, :] = (
            carried_after[span, :].astype(F32) - x_after[span, :].astype(F32) * pull
        ).astype(BF)
    dred = dred_parts[0] if len(dred_parts) == 1 else jnp.concatenate(dred_parts, axis=0)
    if after_turn:
        last_reduced = total_of(pays, pays[0].shape[0] - rows, pays[0].shape[0]).astype(BF)
        second = dot_tn(last_reduced, cot[...]).astype(BF)
        for side in range(weights.shape[1]):
            grads[side, 0:rank, :] = turn_grads[side, 0:rank, :]
            grads[side, rank : 2 * rank, :] = second[:, side * own : (side + 1) * own]
            grads[side, 2 * rank :, :] = turn_grads[side, 2 * rank :, :]
        split_sides(grads, last_keep, last_send)
    layer_backward(
        dout, dred, x, mean[:, 0:1], mask, weights, weights_before, probs, mixed, reduced[...],
        grads, carried, pay,
    )
    split_sides(grads, keep, send)


def combine_kernel(sections, *refs):
    kept, swapped = refs[:sections], refs[sections : 2 * sections]
    outs, sums = refs[2 * sections : 3 * sections], refs[3 * sections]
    section = lax.axis_index("pipe")
    for layer in range(sections):
        sums[layer] = (kept[layer][...].astype(F32) + swapped[layer][...].astype(F32)).astype(BF)
    for distance in range(sections):
        outs[distance][...] = sums[section ^ distance]


def finish_kernel(sections, *refs):
    parts = refs[:sections]
    gain, first, second = refs[sections:]
    rank = second.shape[1]
    total = parts[0][...].astype(F32)
    for part in parts[1:]:
        total = total + part[...].astype(F32)
    first[0] = total[0:rank].T
    second[0] = total[rank : 2 * rank]
    gain[...] = total[2 * rank : 2 * rank + 1]


def per_device(tokens, cotangents, starts, counts, layer_gains, first_map, second_map):
    sections = lax.axis_size("pipe")
    groups = lax.axis_size("z")
    directions, micro_count, length, width = tokens.shape
    micro_local = -(-directions * micro_count // sections)
    rows = groups * micro_local * length
    local = width // groups
    own = first_map.shape[1]
    rank = first_map.shape[2]
    heads = local // HD
    size = block_size(rows)
    blocks = rows // size
    sides = lax.axis_size("core")
    top = sections - 1

    def shifted(value, shift):
        return lax.ppermute(value, "z", [(i, (i + shift) % groups) for i in range(groups)])

    def across(value, distance):
        return lax.ppermute(value, "pipe", [(i, i ^ distance) for i in range(sections)])

    def swapped(value):
        return lax.ppermute(value, "core", [(i, 1 - i) for i in range(sides)])

    def exchange(pay):
        return [pay] + [shifted(pay, shift) for shift in range(1, groups)]

    token_parts, packed = pack(
        tokens, cotangents, starts, counts, layer_gains, first_map, second_map, groups, micro_local
    )
    received = [token_parts[0]]
    received += [shifted(token_parts[shift], shift) for shift in range(1, groups)]
    mine = [packed] + [across(packed, distance) for distance in range(1, sections)]
    received, mine = lax.optimization_barrier((received, mine))
    theirs = [swapped(part) for part in mine]

    def shaped(shape, kind=BF):
        return jax.ShapeDtypeStruct(shape, kind)

    wide_shape = shaped((rows, local))
    mean_shape = shaped((rows, HD), F32)
    rank_shape = shaped((rows, rank))
    cross_shape = shaped((rows, rank), F32)
    probs_shape = shaped((blocks, heads, size, size))
    grads_shape = (sides, 2 * rank + 16, own)
    half_shape = shaped(grads_shape[1:])
    weights_shape = shaped((sections, sides, slice_rows(own), HD))
    forward_rows = 2 * rows + HD

    def call(kernel, operands, specs, outs, name, **more):
        return pl.pallas_call(
            kernel,
            grid=(1,),
            in_specs=specs,
            out_specs=vmem_specs(len(outs)),
            out_shape=outs,
            compiler_params=PARAMS,
            name=name,
            **more,
        )(*operands)

    def layer_of(index):
        return layer_spec(weights_shape.shape, index)

    x, cot, mask, mean, probs, mixed, pay, weights = call(
        functools.partial(first_kernel, length, groups, sections),
        (*received, *mine, *theirs),
        vmem_specs(groups + 2 * sections),
        [
            wide_shape,
            wide_shape,
            shaped((blocks, size, size)),
            mean_shape,
            probs_shape,
            wide_shape,
            shaped((forward_rows, HD)),
            weights_shape,
        ],
        "forward_first",
        scratch_shapes=[
            pltpu.VMEM((rows, HD), BF),
            pltpu.SemaphoreType.DMA((sections, sides)),
        ],
    )
    xs, means, reduceds, crosses = [x], [mean], [], [None]
    all_probs, all_mixed = [probs], [mixed]
    for layer in range(1, top):
        pays = exchange(pay)
        last = layer == top - 1
        operands = (*pays, xs[-1], means[-1], mask, weights, weights)
        specs = vmem_specs(len(pays) + 3) + [layer_of(layer - 1), layer_of(layer)]
        outs = [
            wide_shape,
            mean_shape,
            rank_shape,
            cross_shape,
            probs_shape,
            wide_shape,
            shaped((forward_rows + (rows if last else 0), HD)),
        ]
        if last:
            operands += (cot, weights)
            specs += vmem_specs(1) + [layer_of(layer + 1)]
        x, mean, reduced, cross, probs, mixed, pay = call(
            functools.partial(middle_kernel, len(pays), last, float(width)),
            operands,
            specs,
            outs,
            "forward_middle",
        )
        xs.append(x)
        means.append(mean)
        reduceds.append(reduced)
        crosses.append(cross)
        all_probs.append(probs)
        all_mixed.append(mixed)

    pays = exchange(pay)
    back_rows = rows + 16 * blocks
    x, mean, reduced, cross, turn_grads, carried, pay = call(
        functools.partial(turn_kernel, len(pays), float(width)),
        (*pays, xs[-1], means[-1], mask, weights, weights, cot),
        vmem_specs(len(pays) + 3) + [layer_of(top - 1), layer_of(top)] + vmem_specs(1),
        [
            wide_shape,
            mean_shape,
            rank_shape,
            cross_shape,
            shaped(grads_shape),
            wide_shape,
            shaped((back_rows + rows, HD)),
        ],
        "turn",
        scratch_shapes=[
            pltpu.VMEM(probs_shape.shape, BF),
            pltpu.VMEM(wide_shape.shape, BF),
        ],
    )
    xs.append(x)
    means.append(mean)
    reduceds.append(reduced)
    crosses.append(cross)

    kept, taken = [None] * sections, [None] * sections
    for layer in range(top - 1, -1, -1):
        pays = exchange(pay)
        after_turn = layer == top - 1
        to_first = layer == 0
        operands = (
            *pays, carried, xs[layer + 1], means[layer + 1], crosses[layer + 1],
            xs[layer], means[layer], mask, weights,
        )
        specs = vmem_specs(len(pays) + 7) + [layer_of(layer)]
        if not to_first:
            operands += (weights,)
            specs += [layer_of(layer - 1)]
        operands += (all_probs[layer], all_mixed[layer], reduceds[layer])
        specs += vmem_specs(3)
        outs = [half_shape] * 2
        if after_turn:
            operands += (cot, turn_grads)
            specs += vmem_specs(2)
            outs += [half_shape] * 2
        if not to_first:
            outs += [wide_shape, shaped((back_rows, HD))]
        result = call(
            functools.partial(back_kernel, len(pays), after_turn, to_first, float(width)),
            operands,
            specs,
            outs,
            "backward",
            scratch_shapes=[pltpu.VMEM(wide_shape.shape, BF), pltpu.VMEM(grads_shape, BF)],
        )
        kept[layer], taken[layer] = result[0], swapped(result[1])
        if after_turn:
            kept[top], taken[top] = result[2], swapped(result[3])
        if not to_first:
            carried, pay = result[-2:]

    parts = call(
        functools.partial(combine_kernel, sections),
        (*kept, *taken),
        vmem_specs(2 * sections),
        [half_shape] * sections,
        "combine",
        scratch_shapes=[pltpu.VMEM((sections,) + grads_shape[1:], BF)],
    )
    arrived = [parts[0]] + [across(parts[distance], distance) for distance in range(1, sections)]
    gain_grad, first_grad, second_grad = call(
        functools.partial(finish_kernel, sections),
        arrived,
        vmem_specs(sections),
        [
            shaped((1, own), F32),
            shaped((1, own, rank), F32),
            shaped((1, rank, own), F32),
        ],
        "finish",
    )
    return (gain_grad, first_grad, second_grad)


def solution(mesh):
    fine = Mesh(
        mesh.devices.reshape(mesh.shape["pipe"], mesh.shape["dp"] // 2, 2), ("pipe", "z", "core")
    )
    data = ("z", "core")
    in_specs = (
        P(None, data, None, None),
        P(None, data, None, None),
        P(None, data, None),
        P(None, data),
        P("pipe", data),
        P("pipe", data, None),
        P("pipe", None, data),
    )
    out_specs = (P("pipe", data), P("pipe", data, None), P("pipe", None, data))
    mapped = jax.shard_map(
        per_device, mesh=fine, in_specs=in_specs, out_specs=out_specs, check_vma=False
    )

    return mapped
```

```python
import functools

import jax
import jax.numpy as jnp
from jax import lax
from jax.experimental import pallas as pl
from jax.experimental.pallas import tpu as pltpu
from jax.sharding import Mesh, PartitionSpec as P

HD = 128
EPS = 1e-05
BF = jnp.bfloat16
F32 = jnp.float32
PARAMS = pltpu.CompilerParams(vmem_limit_bytes=48 * 1024 * 1024)
PACK_PARAMS = pltpu.CompilerParams(vmem_limit_bytes=60 * 1024 * 1024)


def dot(a, b):
    return jnp.dot(a, b, preferred_element_type=F32)


def dot_nt(a, b):
    return lax.dot_general(a, b, (((1,), (1,)), ((), ())), preferred_element_type=F32)


def dot_tn(a, b):
    return lax.dot_general(a, b, (((0,), (0,)), ((), ())), preferred_element_type=F32)


def two_parts(value):
    high = value.astype(BF)
    return high, (value - high.astype(F32)).astype(BF)


def vmem_specs(count):
    return [pl.BlockSpec(memory_space=pltpu.VMEM)] * count


def layer_spec(shape, layer):
    return pl.BlockSpec((1,) + shape[1:], lambda *_: (layer, 0, 0, 0))


def slice_rows(own):
    return 2 * own + 16


def pack_kernel(groups, micro_local, *refs):
    tokens, cotangents, starts, counts, gain, first, second = refs[:7]
    parts, weights = refs[7 : 7 + groups], refs[7 + groups]
    tok, cot, starts_in, counts_in, gain_in, second_in, sems = refs[8 + groups :]
    directions, micro_count, length, width = tokens.shape
    local = width // groups
    own = first.shape[1]
    section = lax.axis_index("pipe")
    group = lax.axis_index("z")
    picks = []
    copies = [
        pltpu.make_async_copy(second.at[0], second_in, sems.at[0]),
        pltpu.make_async_copy(gain, gain_in, sems.at[1]),
        pltpu.make_async_copy(first.at[0], weights.at[pl.ds(0, own)], sems.at[2]),
        pltpu.make_async_copy(starts, starts_in, sems.at[3]),
        pltpu.make_async_copy(counts, counts_in, sems.at[4]),
    ]
    for micro in range(micro_local):
        wanted = section * micro_local + micro
        slot = jnp.minimum(wanted, directions * micro_count - 1)
        direction, place = slot // micro_count, slot % micro_count
        picks.append((wanted < directions * micro_count, direction, place))
        rows = pl.ds(micro * length, length)
        copies.append(
            pltpu.make_async_copy(
                tokens.at[direction, place], tok.at[rows], sems.at[5 + 2 * micro]
            )
        )
        copies.append(
            pltpu.make_async_copy(
                cotangents.at[direction, place], cot.at[rows], sems.at[6 + 2 * micro]
            )
        )
    for copy in copies:
        copy.start()
    for copy in copies:
        copy.wait()
    weights[own : 2 * own, :] = second_in[...].astype(F32).T.astype(BF)
    gains = [gain_in[0:1, head * HD : (head + 1) * HD].astype(F32) for head in range(own // HD)]
    gains.append(jnp.zeros((16 - own // HD, HD), F32))
    weights[2 * own :, :] = jnp.concatenate(gains, axis=0).astype(BF)
    for micro, (keep, direction, place) in enumerate(picks):
        rows = slice(micro * length, (micro + 1) * length)
        widened = tok[rows, :].astype(F32)
        mean = jnp.mean(widened * widened, axis=1, keepdims=True)
        mean_high, mean_low = two_parts(mean)
        position = lax.broadcasted_iota(jnp.int32, (length, HD), 0)
        document = jnp.zeros((length, HD), jnp.int32)
        for entry in range(starts.shape[2]):
            begun = starts_in[direction, place, entry] <= position
            begun = begun & (entry < counts_in[direction, place])
            document = document + begun.astype(jnp.int32)
        lane = lax.broadcasted_iota(jnp.int32, (length, HD), 1)
        tail = jnp.where(
            lane == 0,
            document.astype(F32),
            jnp.where(lane == 1, mean_high.astype(F32), mean_low.astype(F32)),
        ).astype(BF)
        for shift in range(groups):
            start = pl.multiple_of(((group + shift) % groups) * local, local)
            parts[shift][rows, 0:local] = tok[rows, pl.ds(start, local)]
            cotangent = cot[rows, pl.ds(start, local)]
            parts[shift][rows, local : 2 * local] = jnp.where(
                keep, cotangent, jnp.zeros_like(cotangent)
            )
            parts[shift][rows, 2 * local :] = tail


def pack(tokens, cotangents, starts, counts, gain, first, second, groups, micro_local):
    length, width = tokens.shape[2:]
    own = first.shape[1]
    local = width // groups
    rows = micro_local * length
    shape = jax.ShapeDtypeStruct
    results = pl.pallas_call(
        functools.partial(pack_kernel, groups, micro_local),
        in_specs=[pl.BlockSpec(memory_space=pltpu.HBM)] * 7,
        out_specs=vmem_specs(groups + 1),
        out_shape=[shape((rows, 2 * local + HD), BF)] * groups
        + [shape((slice_rows(own), HD), BF)],
        scratch_shapes=[
            pltpu.VMEM((rows, width), BF),
            pltpu.VMEM((rows, width), BF),
            pltpu.SMEM(starts.shape, jnp.int32),
            pltpu.SMEM(counts.shape, jnp.int32),
            pltpu.VMEM(gain.shape, BF),
            pltpu.VMEM(second.shape[1:], BF),
            pltpu.SemaphoreType.DMA((5 + 2 * micro_local,)),
        ],
        compiler_params=PACK_PARAMS,
        name="pack",
    )(tokens, cotangents, starts, counts, gain, first, second)
    return results[:groups], results[groups]


def head_gain(weights, head):
    own = (weights.shape[2] - 16) // 2
    per_slice = own // HD
    row = 2 * own + head % per_slice
    return weights[0, head // per_slice, row : row + 1, :].astype(F32)


def block_size(rows):
    return HD if rows % HD == 0 else rows


def to_rank(value, weights, at):
    own = (weights.shape[2] - 16) // 2
    total = None
    for side in range(weights.shape[1]):
        term = dot(value[:, side * own : (side + 1) * own], weights[0, side, at : at + own, :])
        total = term if total is None else total + term
    return total


def from_rank(value, weights, at, side):
    own = (weights.shape[2] - 16) // 2
    return dot_nt(value, weights[0, side, at : at + own, :])


def gram(weights):
    own = (weights.shape[2] - 16) // 2
    total = None
    for side in range(weights.shape[1]):
        part = weights[0, side, own : 2 * own, :]
        term = dot_tn(part, part)
        total = term if total is None else total + term
    return total


def attend(x, mean, weights, mask, probs, mixed):
    rows, local = x.shape
    size = block_size(rows)
    factor = lax.rsqrt(mean + EPS)
    for block in range(rows // size):
        span = slice(block * size, (block + 1) * size)
        allowed = mask[block] > 0
        for head in range(local // HD):
            part = slice(head * HD, (head + 1) * HD)
            normed = (x[span, part].astype(F32) * factor[span] * head_gain(weights, head)).astype(BF)
            scores = dot_nt(normed, normed) * (1.0 / HD)
            raw = jnp.where(allowed, jnp.exp(scores), 0.0)
            prob = (raw / jnp.sum(raw, axis=1, keepdims=True)).astype(BF)
            probs[block, head] = prob
            mixed[span, part] = dot(prob, normed).astype(BF)


def send_forward(x, weights, mixed, pay):
    rows = x.shape[0]
    own = (weights.shape[2] - 16) // 2
    pay[0:rows, :] = to_rank(mixed[...], weights, 0).astype(BF)
    pay[rows : 2 * rows, :] = to_rank(x[...], weights, own).astype(BF)
    pay[2 * rows : 2 * rows + HD, :] = gram(weights).astype(BF)


def total_of(pays, start, stop):
    total = pays[0][start:stop, :].astype(F32)
    for pay in pays[1:]:
        total = total + pay[start:stop, :].astype(F32)
    return total


def receive_forward(pays, x_before, mean_before, weights_before, width, x, mean, reduced, cross):
    rows, local = x_before.shape
    own = (weights_before.shape[2] - 16) // 2
    low_rank = total_of(pays, 0, rows).astype(BF)
    before = total_of(pays, rows, 2 * rows)
    high, low = two_parts(total_of(pays, 2 * rows, 2 * rows + HD))
    through = dot(low_rank, high) + dot(low_rank, low)
    wide = low_rank.astype(F32)
    change = jnp.sum(wide * (2.0 * before + through), axis=1, keepdims=True) / width
    new_mean = jnp.maximum(mean_before[:, 0:1] + change, 0.0)
    mean[...] = jnp.broadcast_to(new_mean, mean.shape)
    reduced[...] = low_rank
    cross[...] = before + through
    for side in range(weights_before.shape[1]):
        part = slice(side * own, (side + 1) * own)
        x[:, part] = (
            x_before[:, part].astype(F32) + from_rank(low_rank, weights_before, own, side)
        ).astype(BF)


def first_kernel(length, groups, sections, *refs):
    received, refs = refs[:groups], refs[groups:]
    mine, theirs = refs[:sections], refs[sections : 2 * sections]
    x, cot, mask, mean, probs, mixed, pay, weights, tails, sems = refs[2 * sections :]
    section, core = lax.axis_index("pipe"), lax.axis_index("core")
    rows, local = x.shape
    size = block_size(rows)
    copies = []
    for distance in range(sections):
        layer = section ^ distance
        for parts, side in ((mine, core), (theirs, 1 - core)):
            copies.append(
                pltpu.make_async_copy(
                    parts[distance], weights.at[layer, side], sems.at[distance, side]
                )
            )
    for copy in copies:
        copy.start()
    place_rows(received, tails, slice(2 * local, None))
    place_rows(received, x, slice(0, local))
    place_rows(received, cot, slice(local, 2 * local))
    tail = tails[...].astype(F32)
    mean[...] = jnp.broadcast_to(tail[:, 1:2] + tail[:, 2:3], mean.shape)
    build_mask(tail[:, 0:1], mask, size, length)
    for copy in copies:
        copy.wait()
    attend(x, mean[:, 0:1], weights, mask, probs, mixed)
    send_forward(x, weights, mixed, pay)


def place_rows(received, target, columns):
    groups = len(received)
    rows = received[0].shape[0]
    for shift, part in enumerate(received):
        source = (lax.axis_index("z") + groups - shift) % groups
        target[pl.ds(pl.multiple_of(source * rows, rows), rows), :] = part[:, columns]


def build_mask(document, mask, size, length):
    query = lax.broadcasted_iota(jnp.int32, (size, size), 0)
    key = lax.broadcasted_iota(jnp.int32, (size, size), 1)
    for block in range(mask.shape[0]):
        by_query = jnp.broadcast_to(document[block * size : (block + 1) * size], (size, size))
        by_key = by_query.T
        allowed = (by_query == by_key) & (key <= query) & (query // length == key // length)
        mask[block] = allowed.astype(F32).astype(BF)


def middle_kernel(count, last, width, *refs):
    pays, refs = refs[:count], refs[count:]
    x_before, mean_before, mask, weights_before, weights = refs[:5]
    refs = refs[5:]
    if last:
        cot, weights_after = refs[:2]
        refs = refs[2:]
    x, mean, reduced, cross, probs, mixed, pay = refs
    receive_forward(
        pays, x_before, mean_before, weights_before, width, x, mean, reduced, cross
    )
    attend(x, mean[:, 0:1], weights, mask, probs, mixed)
    send_forward(x, weights, mixed, pay)
    if last:
        rows = x.shape[0]
        own = (weights.shape[2] - 16) // 2
        pay[2 * rows + HD :, :] = to_rank(cot[...], weights_after, own).astype(BF)


def layer_backward(
    dout, dred, x, mean, mask, weights, weights_before, probs, mixed, reduced, grads, carried, pay
):
    rows, local = x.shape
    size = block_size(rows)
    own = (weights.shape[2] - 16) // 2
    per_slice = own // HD
    rank = dred.shape[1]
    factor = lax.rsqrt(mean + EPS)
    first = dot_tn(dred, mixed[...]).astype(BF)
    for side in range(weights.shape[1]):
        grads[side, 0:rank, :] = first[:, side * own : (side + 1) * own]
    if reduced is not None:
        second = dot_tn(reduced, dout[...]).astype(BF)
        for side in range(weights.shape[1]):
            grads[side, rank : 2 * rank, :] = second[:, side * own : (side + 1) * own]
    back_mixed = [
        from_rank(dred, weights, 0, side).astype(BF) for side in range(weights.shape[1])
    ]
    gain_sums = [None] * (local // HD)
    for block in range(rows // size):
        span = slice(block * size, (block + 1) * size)
        scale = factor[span]
        norm_dot = jnp.zeros((size, HD), F32)
        for head in range(local // HD):
            part = slice(head * HD, (head + 1) * HD)
            side, inner = head // per_slice, (head % per_slice) * HD
            wide = x[span, part].astype(F32)
            gain = head_gain(weights, head)
            unit = wide * scale
            normed = (unit * gain).astype(BF)
            prob = probs[block, head]
            upstream = back_mixed[side][span, inner : inner + HD]
            back_prob = dot_nt(upstream, normed)
            prob_wide = prob.astype(F32)
            inner_sum = jnp.sum(back_prob * prob_wide, axis=1, keepdims=True)
            back_score = prob_wide * (back_prob - inner_sum) * (1.0 / HD)
            both = (back_score + back_score.T).astype(BF)
            back_normed = (dot_tn(prob, upstream) + dot(both, normed)).astype(BF).astype(F32)
            term = jnp.sum(back_normed * unit, axis=0, keepdims=True)
            gain_sums[head] = term if gain_sums[head] is None else gain_sums[head] + term
            if carried is not None:
                scaled = back_normed * gain
                norm_dot = norm_dot + scaled * wide
                carried[span, part] = (dout[span, part].astype(F32) + scaled * scale).astype(BF)
        if carried is not None:
            column = jnp.broadcast_to(jnp.sum(norm_dot, axis=1, keepdims=True), (size, size))
            line = column.T[0:1, :]
            high, low = two_parts(line)
            base = rows + 16 * block
            pay[base : base + 16, :] = jnp.concatenate(
                (high.astype(F32), low.astype(F32), jnp.zeros((14, size), F32)), axis=0
            ).astype(BF)
    zeros = jnp.zeros((15, HD), F32)
    for head in range(local // HD):
        side, inner = head // per_slice, (head % per_slice) * HD
        grads[side, 2 * rank : 2 * rank + 16, inner : inner + HD] = jnp.concatenate(
            (gain_sums[head], zeros), axis=0
        ).astype(BF)
    if carried is not None:
        pay[0:rows, :] = to_rank(carried[...], weights_before, own).astype(BF)


def turn_kernel(count, width, *refs):
    pays, refs = refs[:count], refs[count:]
    (x_before, mean_before, mask, weights_before, weights, cot) = refs[:6]
    (x, mean, reduced, cross, grads, carried, pay) = refs[6:13]
    probs, mixed = refs[13:]
    rows = x.shape[0]
    receive_forward(
        pays, x_before, mean_before, weights_before, width, x, mean, reduced, cross
    )
    attend(x, mean[:, 0:1], weights, mask, probs, mixed)
    dred = total_of(pays, 2 * rows + HD, 3 * rows + HD).astype(BF)
    layer_backward(
        cot, dred, x, mean[:, 0:1], mask, weights, weights_before, probs, mixed, None, grads,
        carried, pay,
    )
    pay[pay.shape[0] - rows :, :] = to_rank(mixed[...], weights, 0).astype(BF)


def split_sides(grads, keep, send):
    core = lax.axis_index("core")
    keep[...] = grads[core]
    send[...] = grads[1 - core]


def back_kernel(count, after_turn, to_first, width, *refs):
    pays, refs = refs[:count], refs[count:]
    carried_after, x_after, mean_after, cross_after = refs[:4]
    x, mean, mask, weights = refs[4:8]
    refs = refs[8:]
    weights_before = carried = pay = None
    if not to_first:
        weights_before, refs = refs[0], refs[1:]
    probs, mixed, reduced = refs[:3]
    refs = refs[3:]
    if after_turn:
        cot, turn_grads = refs[:2]
        refs = refs[2:]
    keep, send = refs[:2]
    refs = refs[2:]
    if after_turn:
        last_keep, last_send = refs[:2]
        refs = refs[2:]
    if not to_first:
        carried, pay = refs[:2]
        refs = refs[2:]
    dout, grads = refs
    rows, local = x.shape
    size = block_size(rows)
    own = (weights.shape[2] - 16) // 2
    rank = reduced.shape[1]
    dred_parts = []
    for block in range(rows // size):
        span = slice(block * size, (block + 1) * size)
        base = rows + 16 * block
        lines = total_of(pays, base, base + 16)
        line = lines[0:1] + lines[1:2]
        column = jnp.broadcast_to(line, (size, size)).T
        factor = lax.rsqrt(mean_after[span, 0:1] + EPS)
        pull = column[:, 0:1] * (factor * factor * factor / width)
        dred_parts.append(
            (
                total_of(pays, block * size, (block + 1) * size) - cross_after[span, :] * pull
            ).astype(BF)
        )
        dout[span, :] = (
            carried_after[span, :].astype(F32) - x_after[span, :].astype(F32) * pull
        ).astype(BF)
    dred = dred_parts[0] if len(dred_parts) == 1 else jnp.concatenate(dred_parts, axis=0)
    if after_turn:
        last_reduced = total_of(pays, pays[0].shape[0] - rows, pays[0].shape[0]).astype(BF)
        second = dot_tn(last_reduced, cot[...]).astype(BF)
        for side in range(weights.shape[1]):
            grads[side, 0:rank, :] = turn_grads[side, 0:rank, :]
            grads[side, rank : 2 * rank, :] = second[:, side * own : (side + 1) * own]
            grads[side, 2 * rank :, :] = turn_grads[side, 2 * rank :, :]
        split_sides(grads, last_keep, last_send)
    layer_backward(
        dout, dred, x, mean[:, 0:1], mask, weights, weights_before, probs, mixed, reduced[...],
        grads, carried, pay,
    )
    split_sides(grads, keep, send)


def add_kernel(near, far, total):
    total[...] = (near[...].astype(F32) + far[...].astype(F32)).astype(BF)


def combine_kernel(sections, *refs):
    kept, swapped = refs[:sections], refs[sections : 2 * sections]
    outs, sums = refs[2 * sections : 3 * sections], refs[3 * sections]
    section = lax.axis_index("pipe")
    for layer in range(sections):
        sums[layer] = (kept[layer][...].astype(F32) + swapped[layer][...].astype(F32)).astype(BF)
    for distance in range(sections):
        outs[distance][...] = sums[section ^ distance]


def finish_kernel(sections, *refs):
    parts = refs[:sections]
    gain, first, second = refs[sections:]
    rank = second.shape[1]
    total = parts[0][...].astype(F32)
    for part in parts[1:]:
        total = total + part[...].astype(F32)
    first[0] = total[0:rank].T
    second[0] = total[rank : 2 * rank]
    gain[...] = total[2 * rank : 2 * rank + 1]


def per_device(tokens, cotangents, starts, counts, layer_gains, first_map, second_map):
    sections = lax.axis_size("pipe")
    groups = lax.axis_size("z")
    directions, micro_count, length, width = tokens.shape
    micro_local = -(-directions * micro_count // sections)
    rows = groups * micro_local * length
    local = width // groups
    own = first_map.shape[1]
    rank = first_map.shape[2]
    heads = local // HD
    size = block_size(rows)
    blocks = rows // size
    sides = lax.axis_size("core")
    top = sections - 1

    def shifted(value, shift):
        return lax.ppermute(value, "z", [(i, (i + shift) % groups) for i in range(groups)])

    def across(value, distance):
        return lax.ppermute(value, "pipe", [(i, i ^ distance) for i in range(sections)])

    def swapped(value):
        return lax.ppermute(value, "core", [(i, 1 - i) for i in range(sides)])

    def exchange(pay):
        distance = 1
        while True:
            far = lax.ppermute(pay, "z", [(i, i ^ distance) for i in range(groups)])
            distance *= 2
            if distance >= groups:
                return [pay, far]
            pay = call(add_kernel, (pay, far), vmem_specs(2), [shaped(pay.shape)], "add_pair")[0]

    token_parts, packed = pack(
        tokens, cotangents, starts, counts, layer_gains, first_map, second_map, groups, micro_local
    )
    received = [token_parts[0]]
    received += [shifted(token_parts[shift], shift) for shift in range(1, groups)]
    mine = [packed] + [across(packed, distance) for distance in range(1, sections)]
    received, mine = lax.optimization_barrier((received, mine))
    theirs = [swapped(part) for part in mine]

    def shaped(shape, kind=BF):
        return jax.ShapeDtypeStruct(shape, kind)

    wide_shape = shaped((rows, local))
    mean_shape = shaped((rows, HD), F32)
    rank_shape = shaped((rows, rank))
    cross_shape = shaped((rows, rank), F32)
    probs_shape = shaped((blocks, heads, size, size))
    grads_shape = (sides, 2 * rank + 16, own)
    half_shape = shaped(grads_shape[1:])
    weights_shape = shaped((sections, sides, slice_rows(own), HD))
    forward_rows = 2 * rows + HD

    def call(kernel, operands, specs, outs, name, **more):
        return pl.pallas_call(
            kernel,
            grid=(1,),
            in_specs=specs,
            out_specs=vmem_specs(len(outs)),
            out_shape=outs,
            compiler_params=PARAMS,
            name=name,
            **more,
        )(*operands)

    def layer_of(index):
        return layer_spec(weights_shape.shape, index)

    x, cot, mask, mean, probs, mixed, pay, weights = call(
        functools.partial(first_kernel, length, groups, sections),
        (*received, *mine, *theirs),
        vmem_specs(groups + 2 * sections),
        [
            wide_shape,
            wide_shape,
            shaped((blocks, size, size)),
            mean_shape,
            probs_shape,
            wide_shape,
            shaped((forward_rows, HD)),
            weights_shape,
        ],
        "forward_first",
        scratch_shapes=[
            pltpu.VMEM((rows, HD), BF),
            pltpu.SemaphoreType.DMA((sections, sides)),
        ],
    )
    xs, means, reduceds, crosses = [x], [mean], [], [None]
    all_probs, all_mixed = [probs], [mixed]
    for layer in range(1, top):
        pays = exchange(pay)
        last = layer == top - 1
        operands = (*pays, xs[-1], means[-1], mask, weights, weights)
        specs = vmem_specs(len(pays) + 3) + [layer_of(layer - 1), layer_of(layer)]
        outs = [
            wide_shape,
            mean_shape,
            rank_shape,
            cross_shape,
            probs_shape,
            wide_shape,
            shaped((forward_rows + (rows if last else 0), HD)),
        ]
        if last:
            operands += (cot, weights)
            specs += vmem_specs(1) + [layer_of(layer + 1)]
        x, mean, reduced, cross, probs, mixed, pay = call(
            functools.partial(middle_kernel, len(pays), last, float(width)),
            operands,
            specs,
            outs,
            "forward_middle",
        )
        xs.append(x)
        means.append(mean)
        reduceds.append(reduced)
        crosses.append(cross)
        all_probs.append(probs)
        all_mixed.append(mixed)

    pays = exchange(pay)
    back_rows = rows + 16 * blocks
    x, mean, reduced, cross, turn_grads, carried, pay = call(
        functools.partial(turn_kernel, len(pays), float(width)),
        (*pays, xs[-1], means[-1], mask, weights, weights, cot),
        vmem_specs(len(pays) + 3) + [layer_of(top - 1), layer_of(top)] + vmem_specs(1),
        [
            wide_shape,
            mean_shape,
            rank_shape,
            cross_shape,
            shaped(grads_shape),
            wide_shape,
            shaped((back_rows + rows, HD)),
        ],
        "turn",
        scratch_shapes=[
            pltpu.VMEM(probs_shape.shape, BF),
            pltpu.VMEM(wide_shape.shape, BF),
        ],
    )
    xs.append(x)
    means.append(mean)
    reduceds.append(reduced)
    crosses.append(cross)

    kept, taken = [None] * sections, [None] * sections
    for layer in range(top - 1, -1, -1):
        pays = exchange(pay)
        after_turn = layer == top - 1
        to_first = layer == 0
        operands = (
            *pays, carried, xs[layer + 1], means[layer + 1], crosses[layer + 1],
            xs[layer], means[layer], mask, weights,
        )
        specs = vmem_specs(len(pays) + 7) + [layer_of(layer)]
        if not to_first:
            operands += (weights,)
            specs += [layer_of(layer - 1)]
        operands += (all_probs[layer], all_mixed[layer], reduceds[layer])
        specs += vmem_specs(3)
        outs = [half_shape] * 2
        if after_turn:
            operands += (cot, turn_grads)
            specs += vmem_specs(2)
            outs += [half_shape] * 2
        if not to_first:
            outs += [wide_shape, shaped((back_rows, HD))]
        result = call(
            functools.partial(back_kernel, len(pays), after_turn, to_first, float(width)),
            operands,
            specs,
            outs,
            "backward",
            scratch_shapes=[pltpu.VMEM(wide_shape.shape, BF), pltpu.VMEM(grads_shape, BF)],
        )
        kept[layer], taken[layer] = result[0], swapped(result[1])
        if after_turn:
            kept[top], taken[top] = result[2], swapped(result[3])
        if not to_first:
            carried, pay = result[-2:]

    parts = call(
        functools.partial(combine_kernel, sections),
        (*kept, *taken),
        vmem_specs(2 * sections),
        [half_shape] * sections,
        "combine",
        scratch_shapes=[pltpu.VMEM((sections,) + grads_shape[1:], BF)],
    )
    arrived = [parts[0]] + [across(parts[distance], distance) for distance in range(1, sections)]
    gain_grad, first_grad, second_grad = call(
        functools.partial(finish_kernel, sections),
        arrived,
        vmem_specs(sections),
        [
            shaped((1, own), F32),
            shaped((1, own, rank), F32),
            shaped((1, rank, own), F32),
        ],
        "finish",
    )
    return (gain_grad, first_grad, second_grad)


def solution(mesh):
    fine = Mesh(
        mesh.devices.reshape(mesh.shape["pipe"], mesh.shape["dp"] // 2, 2), ("pipe", "z", "core")
    )
    data = ("z", "core")
    in_specs = (
        P(None, data, None, None),
        P(None, data, None, None),
        P(None, data, None),
        P(None, data),
        P("pipe", data),
        P("pipe", data, None),
        P("pipe", None, data),
    )
    out_specs = (P("pipe", data), P("pipe", data, None), P("pipe", None, data))
    mapped = jax.shard_map(
        per_device, mesh=fine, in_specs=in_specs, out_specs=out_specs, check_vma=False
    )

    return mapped
```

```python
import functools

import jax
import jax.numpy as jnp
from jax import lax
from jax.experimental import pallas as pl
from jax.experimental.pallas import tpu as pltpu
from jax.sharding import Mesh, PartitionSpec as P

HD = 128
EPS = 1e-05
BF = jnp.bfloat16
F32 = jnp.float32
PARAMS = pltpu.CompilerParams(vmem_limit_bytes=48 * 1024 * 1024)
PACK_PARAMS = pltpu.CompilerParams(vmem_limit_bytes=60 * 1024 * 1024)


def dot(a, b):
    return jnp.dot(a, b, preferred_element_type=F32)


def dot_nt(a, b):
    return lax.dot_general(a, b, (((1,), (1,)), ((), ())), preferred_element_type=F32)


def dot_tn(a, b):
    return lax.dot_general(a, b, (((0,), (0,)), ((), ())), preferred_element_type=F32)


def two_parts(value):
    high = value.astype(BF)
    return high, (value - high.astype(F32)).astype(BF)


def vmem_specs(count):
    return [pl.BlockSpec(memory_space=pltpu.VMEM)] * count


def layer_spec(shape, layer):
    return pl.BlockSpec((1,) + shape[1:], lambda *_: (layer, 0, 0, 0))


def slice_rows(own):
    return 2 * own + 16


def pack_kernel(groups, micro_local, *refs):
    tokens, cotangents, starts, counts, gain, first, second = refs[:7]
    parts, weights = refs[7 : 7 + groups], refs[7 + groups]
    tok, cot, starts_in, counts_in, gain_in, second_in, sems = refs[8 + groups :]
    directions, micro_count, length, width = tokens.shape
    local = width // groups
    own = first.shape[1]
    section = lax.axis_index("pipe")
    group = lax.axis_index("z")
    picks = []
    copies = [
        pltpu.make_async_copy(second.at[0], second_in, sems.at[0]),
        pltpu.make_async_copy(gain, gain_in, sems.at[1]),
        pltpu.make_async_copy(first.at[0], weights.at[pl.ds(0, own)], sems.at[2]),
        pltpu.make_async_copy(starts, starts_in, sems.at[3]),
        pltpu.make_async_copy(counts, counts_in, sems.at[4]),
    ]
    for micro in range(micro_local):
        wanted = section * micro_local + micro
        slot = jnp.minimum(wanted, directions * micro_count - 1)
        direction, place = slot // micro_count, slot % micro_count
        picks.append((wanted < directions * micro_count, direction, place))
        rows = pl.ds(micro * length, length)
        copies.append(
            pltpu.make_async_copy(
                tokens.at[direction, place], tok.at[rows], sems.at[5 + 2 * micro]
            )
        )
        copies.append(
            pltpu.make_async_copy(
                cotangents.at[direction, place], cot.at[rows], sems.at[6 + 2 * micro]
            )
        )
    for copy in copies:
        copy.start()
    for copy in copies:
        copy.wait()
    weights[own : 2 * own, :] = second_in[...].astype(F32).T.astype(BF)
    gains = [gain_in[0:1, head * HD : (head + 1) * HD].astype(F32) for head in range(own // HD)]
    gains.append(jnp.zeros((16 - own // HD, HD), F32))
    weights[2 * own :, :] = jnp.concatenate(gains, axis=0).astype(BF)
    for micro, (keep, direction, place) in enumerate(picks):
        rows = slice(micro * length, (micro + 1) * length)
        widened = tok[rows, :].astype(F32)
        mean = jnp.mean(widened * widened, axis=1, keepdims=True)
        mean_high, mean_low = two_parts(mean)
        position = lax.broadcasted_iota(jnp.int32, (length, HD), 0)
        document = jnp.zeros((length, HD), jnp.int32)
        for entry in range(starts.shape[2]):
            begun = starts_in[direction, place, entry] <= position
            begun = begun & (entry < counts_in[direction, place])
            document = document + begun.astype(jnp.int32)
        lane = lax.broadcasted_iota(jnp.int32, (length, HD), 1)
        tail = jnp.where(
            lane == 0,
            document.astype(F32),
            jnp.where(lane == 1, mean_high.astype(F32), mean_low.astype(F32)),
        ).astype(BF)
        for shift in range(groups):
            start = pl.multiple_of(((group + shift) % groups) * local, local)
            parts[shift][rows, 0:local] = tok[rows, pl.ds(start, local)]
            cotangent = cot[rows, pl.ds(start, local)]
            parts[shift][rows, local : 2 * local] = jnp.where(
                keep, cotangent, jnp.zeros_like(cotangent)
            )
            parts[shift][rows, 2 * local :] = tail


def pack(tokens, cotangents, starts, counts, gain, first, second, groups, micro_local):
    length, width = tokens.shape[2:]
    own = first.shape[1]
    local = width // groups
    rows = micro_local * length
    shape = jax.ShapeDtypeStruct
    results = pl.pallas_call(
        functools.partial(pack_kernel, groups, micro_local),
        in_specs=[pl.BlockSpec(memory_space=pltpu.HBM)] * 7,
        out_specs=vmem_specs(groups + 1),
        out_shape=[shape((rows, 2 * local + HD), BF)] * groups
        + [shape((slice_rows(own), HD), BF)],
        scratch_shapes=[
            pltpu.VMEM((rows, width), BF),
            pltpu.VMEM((rows, width), BF),
            pltpu.SMEM(starts.shape, jnp.int32),
            pltpu.SMEM(counts.shape, jnp.int32),
            pltpu.VMEM(gain.shape, BF),
            pltpu.VMEM(second.shape[1:], BF),
            pltpu.SemaphoreType.DMA((5 + 2 * micro_local,)),
        ],
        compiler_params=PACK_PARAMS,
        name="pack",
    )(tokens, cotangents, starts, counts, gain, first, second)
    return results[:groups], results[groups]


def head_gain(weights, head):
    own = (weights.shape[2] - 16) // 2
    per_slice = own // HD
    row = 2 * own + head % per_slice
    return weights[0, head // per_slice, row : row + 1, :].astype(F32)


def block_size(rows):
    return HD if rows % HD == 0 else rows


def to_rank(value, weights, at):
    own = (weights.shape[2] - 16) // 2
    total = None
    for side in range(weights.shape[1]):
        term = dot(value[:, side * own : (side + 1) * own], weights[0, side, at : at + own, :])
        total = term if total is None else total + term
    return total


def from_rank(value, weights, at, side):
    own = (weights.shape[2] - 16) // 2
    return dot_nt(value, weights[0, side, at : at + own, :])


def gram(weights):
    own = (weights.shape[2] - 16) // 2
    total = None
    for side in range(weights.shape[1]):
        part = weights[0, side, own : 2 * own, :]
        term = dot_tn(part, part)
        total = term if total is None else total + term
    return total


def attend(x, mean, weights, mask, probs, mixed):
    rows, local = x.shape
    size = block_size(rows)
    factor = lax.rsqrt(mean + EPS)
    for block in range(rows // size):
        span = slice(block * size, (block + 1) * size)
        allowed = mask[block] > 0
        for head in range(local // HD):
            part = slice(head * HD, (head + 1) * HD)
            normed = (x[span, part].astype(F32) * factor[span] * head_gain(weights, head)).astype(BF)
            scores = dot_nt(normed, normed) * (1.0 / HD)
            raw = jnp.where(allowed, jnp.exp(scores), 0.0)
            prob = (raw / jnp.sum(raw, axis=1, keepdims=True)).astype(BF)
            probs[block, head] = prob
            mixed[span, part] = dot(prob, normed).astype(BF)


def send_forward(x, weights, mixed, pay):
    rows = x.shape[0]
    own = (weights.shape[2] - 16) // 2
    pay[0:rows, :] = to_rank(mixed[...], weights, 0).astype(BF)
    pay[rows : 2 * rows, :] = to_rank(x[...], weights, own).astype(BF)


def total_of(pays, start, stop):
    total = pays[0][start:stop, :].astype(F32)
    for pay in pays[1:]:
        total = total + pay[start:stop, :].astype(F32)
    return total


def receive_forward(
    pays, gram_total, x_before, mean_before, weights_before, width, x, mean, reduced, cross
):
    rows, local = x_before.shape
    own = (weights_before.shape[2] - 16) // 2
    low_rank = total_of(pays, 0, rows).astype(BF)
    before = total_of(pays, rows, 2 * rows)
    high, low = two_parts(gram_total)
    through = dot(low_rank, high) + dot(low_rank, low)
    wide = low_rank.astype(F32)
    change = jnp.sum(wide * (2.0 * before + through), axis=1, keepdims=True) / width
    new_mean = jnp.maximum(mean_before[:, 0:1] + change, 0.0)
    mean[...] = jnp.broadcast_to(new_mean, mean.shape)
    reduced[...] = low_rank
    cross[...] = before + through
    for side in range(weights_before.shape[1]):
        part = slice(side * own, (side + 1) * own)
        x[:, part] = (
            x_before[:, part].astype(F32) + from_rank(low_rank, weights_before, own, side)
        ).astype(BF)


def arrange_kernel(length, groups, *refs):
    received, packed = refs[:groups], refs[groups]
    x, cot, mask, mean, packed_out, tails = refs[groups + 1 :]
    rows, local = x.shape
    place_rows(received, tails, slice(2 * local, None))
    place_rows(received, x, slice(0, local))
    place_rows(received, cot, slice(local, 2 * local))
    tail = tails[...].astype(F32)
    mean[...] = jnp.broadcast_to(tail[:, 1:2] + tail[:, 2:3], mean.shape)
    build_mask(tail[:, 0:1], mask, block_size(rows), length)
    packed_out[...] = packed[...]


def first_kernel(sections, *refs):
    mine, theirs = refs[:sections], refs[sections : 2 * sections]
    x, cot, mask, mean, probs, mixed, pay, side, weights, sems = refs[2 * sections :]
    section, core = lax.axis_index("pipe"), lax.axis_index("core")
    rows = x.shape[0]
    copies = []
    for distance in range(sections):
        layer = section ^ distance
        for parts, place in ((mine, core), (theirs, 1 - core)):
            copies.append(
                pltpu.make_async_copy(
                    parts[distance], weights.at[layer, place], sems.at[distance, place]
                )
            )
    for copy in copies:
        copy.start()
    for copy in copies:
        copy.wait()
    own = (weights.shape[2] - 16) // 2
    layers = [weights.at[pl.ds(layer, 1)] for layer in range(sections)]
    attend(x, mean[:, 0:1], layers[0], mask, probs, mixed)
    send_forward(x, layers[0], mixed, pay)
    pay[2 * rows :, :] = gram(layers[0]).astype(BF)
    side[0:rows, :] = to_rank(cot[...], layers[-1], own).astype(BF)
    for layer in range(1, sections - 1):
        base = rows + HD * (layer - 1)
        side[base : base + HD, :] = gram(layers[layer]).astype(BF)


def place_rows(received, target, columns):
    groups = len(received)
    rows = received[0].shape[0]
    for shift, part in enumerate(received):
        source = (lax.axis_index("z") + groups - shift) % groups
        target[pl.ds(pl.multiple_of(source * rows, rows), rows), :] = part[:, columns]


def build_mask(document, mask, size, length):
    query = lax.broadcasted_iota(jnp.int32, (size, size), 0)
    key = lax.broadcasted_iota(jnp.int32, (size, size), 1)
    for block in range(mask.shape[0]):
        by_query = jnp.broadcast_to(document[block * size : (block + 1) * size], (size, size))
        by_key = by_query.T
        allowed = (by_query == by_key) & (key <= query) & (query // length == key // length)
        mask[block] = allowed.astype(F32).astype(BF)


def gram_of(pays, sides, layer, rows):
    if layer == 0:
        return total_of(pays, 2 * rows, 2 * rows + HD)
    base = rows + HD * (layer - 1)
    return total_of(sides, base, base + HD)


def middle_kernel(count, layer, width, *refs):
    pays, sides, refs = refs[:count], refs[count : 2 * count], refs[2 * count :]
    if layer == 1:
        sides, refs = (), sides + refs
    x_before, mean_before, mask, weights_before, weights = refs[:5]
    x, mean, reduced, cross, probs, mixed, pay = refs[5:]
    receive_forward(
        pays, gram_of(pays, sides, layer - 1, x.shape[0]), x_before, mean_before, weights_before,
        width, x, mean, reduced, cross,
    )
    attend(x, mean[:, 0:1], weights, mask, probs, mixed)
    send_forward(x, weights, mixed, pay)


def layer_backward(
    dout, dred, x, mean, mask, weights, weights_before, probs, mixed, reduced, grads, carried, pay
):
    rows, local = x.shape
    size = block_size(rows)
    own = (weights.shape[2] - 16) // 2
    per_slice = own // HD
    rank = dred.shape[1]
    factor = lax.rsqrt(mean + EPS)
    first = dot_tn(dred, mixed[...]).astype(BF)
    for side in range(weights.shape[1]):
        grads[side, 0:rank, :] = first[:, side * own : (side + 1) * own]
    if reduced is not None:
        second = dot_tn(reduced, dout[...]).astype(BF)
        for side in range(weights.shape[1]):
            grads[side, rank : 2 * rank, :] = second[:, side * own : (side + 1) * own]
    back_mixed = [
        from_rank(dred, weights, 0, side).astype(BF) for side in range(weights.shape[1])
    ]
    gain_sums = [None] * (local // HD)
    for block in range(rows // size):
        span = slice(block * size, (block + 1) * size)
        scale = factor[span]
        norm_dot = jnp.zeros((size, HD), F32)
        for head in range(local // HD):
            part = slice(head * HD, (head + 1) * HD)
            side, inner = head // per_slice, (head % per_slice) * HD
            wide = x[span, part].astype(F32)
            gain = head_gain(weights, head)
            unit = wide * scale
            normed = (unit * gain).astype(BF)
            prob = probs[block, head]
            upstream = back_mixed[side][span, inner : inner + HD]
            back_prob = dot_nt(upstream, normed)
            prob_wide = prob.astype(F32)
            inner_sum = jnp.sum(back_prob * prob_wide, axis=1, keepdims=True)
            back_score = prob_wide * (back_prob - inner_sum) * (1.0 / HD)
            both = (back_score + back_score.T).astype(BF)
            back_normed = (dot_tn(prob, upstream) + dot(both, normed)).astype(BF).astype(F32)
            term = jnp.sum(back_normed * unit, axis=0, keepdims=True)
            gain_sums[head] = term if gain_sums[head] is None else gain_sums[head] + term
            if carried is not None:
                scaled = back_normed * gain
                norm_dot = norm_dot + scaled * wide
                carried[span, part] = (dout[span, part].astype(F32) + scaled * scale).astype(BF)
        if carried is not None:
            column = jnp.broadcast_to(jnp.sum(norm_dot, axis=1, keepdims=True), (size, size))
            line = column.T[0:1, :]
            high, low = two_parts(line)
            base = rows + 16 * block
            pay[base : base + 16, :] = jnp.concatenate(
                (high.astype(F32), low.astype(F32), jnp.zeros((14, size), F32)), axis=0
            ).astype(BF)
    zeros = jnp.zeros((15, HD), F32)
    for head in range(local // HD):
        side, inner = head // per_slice, (head % per_slice) * HD
        grads[side, 2 * rank : 2 * rank + 16, inner : inner + HD] = jnp.concatenate(
            (gain_sums[head], zeros), axis=0
        ).astype(BF)
    if carried is not None:
        pay[0:rows, :] = to_rank(carried[...], weights_before, own).astype(BF)


def turn_kernel(count, layer, width, *refs):
    pays, sides, refs = refs[:count], refs[count : 2 * count], refs[2 * count :]
    (x_before, mean_before, mask, weights_before, weights, cot) = refs[:6]
    (x, mean, reduced, cross, grads, carried, pay, last_part) = refs[6:14]
    probs, mixed = refs[14:]
    rows = x.shape[0]
    receive_forward(
        pays, gram_of(pays, sides, layer - 1, rows), x_before, mean_before, weights_before,
        width, x, mean, reduced, cross,
    )
    attend(x, mean[:, 0:1], weights, mask, probs, mixed)
    last_part[...] = to_rank(mixed[...], weights, 0).astype(BF)
    dred = total_of(sides, 0, rows).astype(BF)
    layer_backward(
        cot, dred, x, mean[:, 0:1], mask, weights, weights_before, probs, mixed, None, grads,
        carried, pay,
    )


def split_sides(grads, keep, send):
    core = lax.axis_index("core")
    keep[...] = grads[core]
    send[...] = grads[1 - core]


def back_kernel(count, with_last, to_first, width, *refs):
    pays, refs = refs[:count], refs[count:]
    carried_after, x_after, mean_after, cross_after = refs[:4]
    x, mean, mask, weights = refs[4:8]
    refs = refs[8:]
    weights_before = carried = pay = None
    if not to_first:
        weights_before, refs = refs[0], refs[1:]
    probs, mixed, reduced = refs[:3]
    refs = refs[3:]
    if with_last:
        last_parts, cot, turn_grads = refs[:count], refs[count], refs[count + 1]
        refs = refs[count + 2 :]
    keep, send = refs[:2]
    refs = refs[2:]
    if with_last:
        last_keep, last_send = refs[:2]
        refs = refs[2:]
    if not to_first:
        carried, pay = refs[:2]
        refs = refs[2:]
    dout, grads = refs
    rows, local = x.shape
    size = block_size(rows)
    own = (weights.shape[2] - 16) // 2
    rank = reduced.shape[1]
    dred_parts = []
    for block in range(rows // size):
        span = slice(block * size, (block + 1) * size)
        base = rows + 16 * block
        lines = total_of(pays, base, base + 16)
        line = lines[0:1] + lines[1:2]
        column = jnp.broadcast_to(line, (size, size)).T
        factor = lax.rsqrt(mean_after[span, 0:1] + EPS)
        pull = column[:, 0:1] * (factor * factor * factor / width)
        dred_parts.append(
            (
                total_of(pays, block * size, (block + 1) * size) - cross_after[span, :] * pull
            ).astype(BF)
        )
        dout[span, :] = (
            carried_after[span, :].astype(F32) - x_after[span, :].astype(F32) * pull
        ).astype(BF)
    dred = dred_parts[0] if len(dred_parts) == 1 else jnp.concatenate(dred_parts, axis=0)
    if with_last:
        last_reduced = total_of(last_parts, 0, rows).astype(BF)
        second = dot_tn(last_reduced, cot[...]).astype(BF)
        for side in range(weights.shape[1]):
            grads[side, 0:rank, :] = turn_grads[side, 0:rank, :]
            grads[side, rank : 2 * rank, :] = second[:, side * own : (side + 1) * own]
            grads[side, 2 * rank :, :] = turn_grads[side, 2 * rank :, :]
        split_sides(grads, last_keep, last_send)
    layer_backward(
        dout, dred, x, mean[:, 0:1], mask, weights, weights_before, probs, mixed, reduced[...],
        grads, carried, pay,
    )
    split_sides(grads, keep, send)


def combine_kernel(sections, *refs):
    kept, swapped = refs[:sections], refs[sections : 2 * sections]
    outs, sums = refs[2 * sections : 3 * sections], refs[3 * sections]
    section = lax.axis_index("pipe")
    for layer in range(sections):
        sums[layer] = (kept[layer][...].astype(F32) + swapped[layer][...].astype(F32)).astype(BF)
    for distance in range(sections):
        outs[distance][...] = sums[section ^ distance]


def finish_kernel(sections, *refs):
    parts = refs[:sections]
    gain, first, second = refs[sections:]
    rank = second.shape[1]
    total = parts[0][...].astype(F32)
    for part in parts[1:]:
        total = total + part[...].astype(F32)
    first[0] = total[0:rank].T
    second[0] = total[rank : 2 * rank]
    gain[...] = total[2 * rank : 2 * rank + 1]


def per_device(tokens, cotangents, starts, counts, layer_gains, first_map, second_map):
    sections = lax.axis_size("pipe")
    groups = lax.axis_size("z")
    directions, micro_count, length, width = tokens.shape
    micro_local = -(-directions * micro_count // sections)
    rows = groups * micro_local * length
    local = width // groups
    own = first_map.shape[1]
    rank = first_map.shape[2]
    heads = local // HD
    size = block_size(rows)
    blocks = rows // size
    sides = lax.axis_size("core")
    top = sections - 1

    def shifted(value, shift):
        return lax.ppermute(value, "z", [(i, (i + shift) % groups) for i in range(groups)])

    def across(value, distance):
        return lax.ppermute(value, "pipe", [(i, i ^ distance) for i in range(sections)])

    def swapped(value):
        return lax.ppermute(value, "core", [(i, 1 - i) for i in range(sides)])

    def exchange(pay):
        return [pay] + [shifted(pay, shift) for shift in range(1, groups)]

    token_parts, packed = pack(
        tokens, cotangents, starts, counts, layer_gains, first_map, second_map, groups, micro_local
    )
    received = [token_parts[0]]
    received += [shifted(token_parts[shift], shift) for shift in range(1, groups)]
    mine = [packed] + [across(packed, distance) for distance in range(1, sections)]
    received, mine = lax.optimization_barrier((received, mine))
    theirs = [swapped(part) for part in mine]

    def shaped(shape, kind=BF):
        return jax.ShapeDtypeStruct(shape, kind)

    wide_shape = shaped((rows, local))
    mean_shape = shaped((rows, HD), F32)
    rank_shape = shaped((rows, rank))
    cross_shape = shaped((rows, rank), F32)
    probs_shape = shaped((blocks, heads, size, size))
    grads_shape = (sides, 2 * rank + 16, own)
    half_shape = shaped(grads_shape[1:])
    weights_shape = shaped((sections, sides, slice_rows(own), HD))

    def call(kernel, operands, specs, outs, name, **more):
        return pl.pallas_call(
            kernel,
            grid=(1,),
            in_specs=specs,
            out_specs=vmem_specs(len(outs)),
            out_shape=outs,
            compiler_params=PARAMS,
            name=name,
            **more,
        )(*operands)

    def layer_of(index):
        return layer_spec(weights_shape.shape, index)

    x, cot, mask, mean, mine[0] = call(
        functools.partial(arrange_kernel, length, groups),
        (*received, mine[0]),
        vmem_specs(groups + 1),
        [
            wide_shape,
            wide_shape,
            shaped((blocks, size, size)),
            mean_shape,
            shaped(packed.shape),
        ],
        "arrange",
        scratch_shapes=[pltpu.VMEM((rows, HD), BF)],
    )
    probs, mixed, pay, side, weights = call(
        functools.partial(first_kernel, sections),
        (*mine, *theirs, x, cot, mask, mean),
        vmem_specs(2 * sections + 4),
        [
            probs_shape,
            wide_shape,
            shaped((2 * rows + HD, HD)),
            shaped((rows + HD * (top - 1), HD)),
            weights_shape,
        ],
        "forward_first",
        scratch_shapes=[pltpu.SemaphoreType.DMA((sections, sides))],
    )
    xs, means, reduceds, crosses = [x], [mean], [], [None]
    all_probs, all_mixed = [probs], [mixed]
    pays = exchange(pay)
    arrived = exchange(side)
    for layer in range(1, top):
        operands = (*pays, *(arrived if layer > 1 else ()))
        specs = vmem_specs(len(operands) + 3) + [layer_of(layer - 1), layer_of(layer)]
        x, mean, reduced, cross, probs, mixed, pay = call(
            functools.partial(middle_kernel, groups, layer, float(width)),
            (*operands, xs[-1], means[-1], mask, weights, weights),
            specs,
            [
                wide_shape,
                mean_shape,
                rank_shape,
                cross_shape,
                probs_shape,
                wide_shape,
                shaped((2 * rows, HD)),
            ],
            "forward_middle",
        )
        xs.append(x)
        means.append(mean)
        reduceds.append(reduced)
        crosses.append(cross)
        all_probs.append(probs)
        all_mixed.append(mixed)
        pays = exchange(pay)

    back_rows = rows + 16 * blocks
    x, mean, reduced, cross, turn_grads, carried, pay, last_part = call(
        functools.partial(turn_kernel, groups, top, float(width)),
        (*pays, *arrived, xs[-1], means[-1], mask, weights, weights, cot),
        vmem_specs(2 * groups + 3) + [layer_of(top - 1), layer_of(top)] + vmem_specs(1),
        [
            wide_shape,
            mean_shape,
            rank_shape,
            cross_shape,
            shaped(grads_shape),
            wide_shape,
            shaped((back_rows, HD)),
            rank_shape,
        ],
        "turn",
        scratch_shapes=[
            pltpu.VMEM(probs_shape.shape, BF),
            pltpu.VMEM(wide_shape.shape, BF),
        ],
    )
    xs.append(x)
    means.append(mean)
    reduceds.append(reduced)
    crosses.append(cross)

    kept, taken = [None] * sections, [None] * sections
    for layer in range(top - 1, -1, -1):
        pays = exchange(pay)
        if layer == top - 1:
            last_parts = exchange(last_part)
        with_last = layer == top - 2
        to_first = layer == 0
        operands = (
            *pays, carried, xs[layer + 1], means[layer + 1], crosses[layer + 1],
            xs[layer], means[layer], mask, weights,
        )
        specs = vmem_specs(len(pays) + 7) + [layer_of(layer)]
        if not to_first:
            operands += (weights,)
            specs += [layer_of(layer - 1)]
        operands += (all_probs[layer], all_mixed[layer], reduceds[layer])
        specs += vmem_specs(3)
        outs = [half_shape] * 2
        if with_last:
            operands += (*last_parts, cot, turn_grads)
            specs += vmem_specs(groups + 2)
            outs += [half_shape] * 2
        if not to_first:
            outs += [wide_shape, shaped((back_rows, HD))]
        result = call(
            functools.partial(back_kernel, groups, with_last, to_first, float(width)),
            operands,
            specs,
            outs,
            "backward",
            scratch_shapes=[pltpu.VMEM(wide_shape.shape, BF), pltpu.VMEM(grads_shape, BF)],
        )
        kept[layer], taken[layer] = result[0], swapped(result[1])
        if with_last:
            kept[top], taken[top] = result[2], swapped(result[3])
        if not to_first:
            carried, pay = result[-2:]

    parts = call(
        functools.partial(combine_kernel, sections),
        (*kept, *taken),
        vmem_specs(2 * sections),
        [half_shape] * sections,
        "combine",
        scratch_shapes=[pltpu.VMEM((sections,) + grads_shape[1:], BF)],
    )
    arrived = [parts[0]] + [across(parts[distance], distance) for distance in range(1, sections)]
    gain_grad, first_grad, second_grad = call(
        functools.partial(finish_kernel, sections),
        arrived,
        vmem_specs(sections),
        [
            shaped((1, own), F32),
            shaped((1, own, rank), F32),
            shaped((1, rank, own), F32),
        ],
        "finish",
    )
    return (gain_grad, first_grad, second_grad)


def solution(mesh):
    fine = Mesh(
        mesh.devices.reshape(mesh.shape["pipe"], mesh.shape["dp"] // 2, 2), ("pipe", "z", "core")
    )
    data = ("z", "core")
    in_specs = (
        P(None, data, None, None),
        P(None, data, None, None),
        P(None, data, None),
        P(None, data),
        P("pipe", data),
        P("pipe", data, None),
        P("pipe", None, data),
    )
    out_specs = (P("pipe", data), P("pipe", data, None), P("pipe", None, data))
    mapped = jax.shard_map(
        per_device, mesh=fine, in_specs=in_specs, out_specs=out_specs, check_vma=False
    )

    return mapped
```

```python
import functools

import jax
import jax.numpy as jnp
from jax import lax
from jax.experimental import pallas as pl
from jax.experimental.pallas import tpu as pltpu
from jax.sharding import Mesh, PartitionSpec as P

HD = 128
EPS = 1e-05
BF = jnp.bfloat16
F32 = jnp.float32
PARAMS = pltpu.CompilerParams(vmem_limit_bytes=48 * 1024 * 1024)
PACK_PARAMS = pltpu.CompilerParams(vmem_limit_bytes=60 * 1024 * 1024)


def dot(a, b):
    return jnp.dot(a, b, preferred_element_type=F32)


def dot_nt(a, b):
    return lax.dot_general(a, b, (((1,), (1,)), ((), ())), preferred_element_type=F32)


def dot_tn(a, b):
    return lax.dot_general(a, b, (((0,), (0,)), ((), ())), preferred_element_type=F32)


def two_parts(value):
    high = value.astype(BF)
    return high, (value - high.astype(F32)).astype(BF)


def member():
    return lax.axis_index("zl") * lax.axis_size("core") + lax.axis_index("core")


def vmem_specs(count):
    return [pl.BlockSpec(memory_space=pltpu.VMEM)] * count


def layer_spec(shape, layer):
    return pl.BlockSpec((1,) + shape[1:], lambda *_: (layer, 0, 0, 0))


def slice_rows(own):
    return 2 * own + 16


def pack_kernel(groups, micro_local, *refs):
    tokens, cotangents, starts, counts, gain, first, second = refs[:7]
    parts, weights = refs[7 : 7 + groups], refs[7 + groups]
    tok, cot, starts_in, counts_in, gain_in, second_in, sems = refs[8 + groups :]
    directions, micro_count, length, width = tokens.shape
    own = first.shape[1]
    local = width // groups
    section = lax.axis_index("pipe")
    picks = []
    copies = [
        pltpu.make_async_copy(second.at[0], second_in, sems.at[0]),
        pltpu.make_async_copy(gain, gain_in, sems.at[1]),
        pltpu.make_async_copy(first.at[0], weights.at[pl.ds(0, own)], sems.at[2]),
        pltpu.make_async_copy(starts, starts_in, sems.at[3]),
        pltpu.make_async_copy(counts, counts_in, sems.at[4]),
    ]
    for micro in range(micro_local):
        wanted = section * micro_local + micro
        slot = jnp.minimum(wanted, directions * micro_count - 1)
        direction, place = slot // micro_count, slot % micro_count
        picks.append((wanted < directions * micro_count, direction, place))
        rows = pl.ds(micro * length, length)
        copies.append(
            pltpu.make_async_copy(
                tokens.at[direction, place], tok.at[rows], sems.at[5 + 2 * micro]
            )
        )
        copies.append(
            pltpu.make_async_copy(
                cotangents.at[direction, place], cot.at[rows], sems.at[6 + 2 * micro]
            )
        )
    for copy in copies:
        copy.start()
    for copy in copies:
        copy.wait()
    weights[own : 2 * own, :] = second_in[...].astype(F32).T.astype(BF)
    gains = [gain_in[0:1, head * HD : (head + 1) * HD].astype(F32) for head in range(own // HD)]
    gains.append(jnp.zeros((16 - own // HD, HD), F32))
    weights[2 * own :, :] = jnp.concatenate(gains, axis=0).astype(BF)
    for micro, (keep, direction, place) in enumerate(picks):
        rows = slice(micro * length, (micro + 1) * length)
        widened = tok[rows, :].astype(F32)
        mean = jnp.mean(widened * widened, axis=1, keepdims=True)
        mean_high, mean_low = two_parts(mean)
        position = lax.broadcasted_iota(jnp.int32, (length, HD), 0)
        document = jnp.zeros((length, HD), jnp.int32)
        for entry in range(starts.shape[2]):
            begun = starts_in[direction, place, entry] <= position
            begun = begun & (entry < counts_in[direction, place])
            document = document + begun.astype(jnp.int32)
        lane = lax.broadcasted_iota(jnp.int32, (length, HD), 1)
        tail = jnp.where(
            lane == 0,
            document.astype(F32),
            jnp.where(lane == 1, mean_high.astype(F32), mean_low.astype(F32)),
        ).astype(BF)
        for distance in range(groups):
            for side in range(local // own):
                start = pl.multiple_of((side * groups + (member() ^ distance)) * own, own)
                at = side * own
                parts[distance][rows, at : at + own] = tok[rows, pl.ds(start, own)]
                cotangent = cot[rows, pl.ds(start, own)]
                parts[distance][rows, local + at : local + at + own] = jnp.where(
                    keep, cotangent, jnp.zeros_like(cotangent)
                )
            parts[distance][rows, 2 * local :] = tail


def pack(tokens, cotangents, starts, counts, gain, first, second, groups, micro_local):
    length, width = tokens.shape[2:]
    own = first.shape[1]
    local = width // groups
    rows = micro_local * length
    shape = jax.ShapeDtypeStruct
    results = pl.pallas_call(
        functools.partial(pack_kernel, groups, micro_local),
        in_specs=[pl.BlockSpec(memory_space=pltpu.HBM)] * 7,
        out_specs=vmem_specs(groups + 1),
        out_shape=[shape((rows, 2 * local + HD), BF)] * groups
        + [shape((slice_rows(own), HD), BF)],
        scratch_shapes=[
            pltpu.VMEM((rows, width), BF),
            pltpu.VMEM((rows, width), BF),
            pltpu.SMEM(starts.shape, jnp.int32),
            pltpu.SMEM(counts.shape, jnp.int32),
            pltpu.VMEM(gain.shape, BF),
            pltpu.VMEM(second.shape[1:], BF),
            pltpu.SemaphoreType.DMA((5 + 2 * micro_local,)),
        ],
        compiler_params=PACK_PARAMS,
        name="pack",
    )(tokens, cotangents, starts, counts, gain, first, second)
    return results[:groups], results[groups]


def head_gain(weights, head):
    own = (weights.shape[2] - 16) // 2
    per_slice = own // HD
    row = 2 * own + head % per_slice
    return weights[0, head // per_slice, row : row + 1, :].astype(F32)


def block_size(rows):
    return HD if rows % HD == 0 else rows


def to_rank(value, weights, at):
    own = (weights.shape[2] - 16) // 2
    total = None
    for side in range(weights.shape[1]):
        term = dot(value[:, side * own : (side + 1) * own], weights[0, side, at : at + own, :])
        total = term if total is None else total + term
    return total


def from_rank(value, weights, at, side):
    own = (weights.shape[2] - 16) // 2
    return dot_nt(value, weights[0, side, at : at + own, :])


def gram(weights):
    own = (weights.shape[2] - 16) // 2
    total = None
    for side in range(weights.shape[1]):
        part = weights[0, side, own : 2 * own, :]
        term = dot_tn(part, part)
        total = term if total is None else total + term
    return total


def attend(x, mean, weights, mask, probs, mixed):
    rows, local = x.shape
    size = block_size(rows)
    factor = lax.rsqrt(mean + EPS)
    for block in range(rows // size):
        span = slice(block * size, (block + 1) * size)
        allowed = mask[block] > 0
        for head in range(local // HD):
            part = slice(head * HD, (head + 1) * HD)
            normed = (x[span, part].astype(F32) * factor[span] * head_gain(weights, head)).astype(BF)
            scores = dot_nt(normed, normed) * (1.0 / HD)
            raw = jnp.where(allowed, jnp.exp(scores), 0.0)
            prob = (raw / jnp.sum(raw, axis=1, keepdims=True)).astype(BF)
            probs[block, head] = prob
            mixed[span, part] = dot(prob, normed).astype(BF)


def send_forward(x, weights, mixed, pay):
    rows = x.shape[0]
    own = (weights.shape[2] - 16) // 2
    pay[0:rows, :] = to_rank(mixed[...], weights, 0).astype(BF)
    pay[rows : 2 * rows, :] = to_rank(x[...], weights, own).astype(BF)


def total_of(pays, start, stop):
    total = pays[0][start:stop, :].astype(F32)
    for pay in pays[1:]:
        total = total + pay[start:stop, :].astype(F32)
    return total


def receive_forward(
    pays, gram_total, x_before, mean_before, weights_before, width, x, mean, reduced, cross
):
    rows, local = x_before.shape
    own = (weights_before.shape[2] - 16) // 2
    low_rank = total_of(pays, 0, rows).astype(BF)
    before = total_of(pays, rows, 2 * rows)
    high, low = two_parts(gram_total)
    through = dot(low_rank, high) + dot(low_rank, low)
    wide = low_rank.astype(F32)
    change = jnp.sum(wide * (2.0 * before + through), axis=1, keepdims=True) / width
    new_mean = jnp.maximum(mean_before[:, 0:1] + change, 0.0)
    mean[...] = jnp.broadcast_to(new_mean, mean.shape)
    reduced[...] = low_rank
    cross[...] = before + through
    for side in range(weights_before.shape[1]):
        part = slice(side * own, (side + 1) * own)
        x[:, part] = (
            x_before[:, part].astype(F32) + from_rank(low_rank, weights_before, own, side)
        ).astype(BF)


def arrange_kernel(length, groups, *refs):
    received, packed = refs[:groups], refs[groups]
    x, cot, mask, mean, packed_out, tails = refs[groups + 1 :]
    rows, local = x.shape
    place_rows(received, tails, slice(2 * local, None))
    place_rows(received, x, slice(0, local))
    place_rows(received, cot, slice(local, 2 * local))
    tail = tails[...].astype(F32)
    mean[...] = jnp.broadcast_to(tail[:, 1:2] + tail[:, 2:3], mean.shape)
    build_mask(tail[:, 0:1], mask, block_size(rows), length)
    packed_out[...] = packed[...]


def first_kernel(sections, sides, *refs):
    parts, refs = refs[: sections * sides], refs[sections * sides :]
    x, cot, mask, mean, probs, mixed, pay, side, weights, sems = refs
    section, half = lax.axis_index("pipe"), lax.axis_index("zh")
    rows = x.shape[0]
    copies = []
    for far in range(sides):
        for distance in range(sections):
            copies.append(
                pltpu.make_async_copy(
                    parts[far * sections + distance],
                    weights.at[section ^ distance, half ^ far],
                    sems.at[distance, far],
                )
            )
    for copy in copies:
        copy.start()
    for copy in copies:
        copy.wait()
    own = (weights.shape[2] - 16) // 2
    layers = [weights.at[pl.ds(layer, 1)] for layer in range(sections)]
    attend(x, mean[:, 0:1], layers[0], mask, probs, mixed)
    send_forward(x, layers[0], mixed, pay)
    pay[2 * rows :, :] = gram(layers[0]).astype(BF)
    side[0:rows, :] = to_rank(cot[...], layers[-1], own).astype(BF)
    for layer in range(1, sections - 1):
        base = rows + HD * (layer - 1)
        side[base : base + HD, :] = gram(layers[layer]).astype(BF)


def place_rows(received, target, columns):
    rows = received[0].shape[0]
    for distance, part in enumerate(received):
        source = member() ^ distance
        target[pl.ds(pl.multiple_of(source * rows, rows), rows), :] = part[:, columns]


def build_mask(document, mask, size, length):
    query = lax.broadcasted_iota(jnp.int32, (size, size), 0)
    key = lax.broadcasted_iota(jnp.int32, (size, size), 1)
    for block in range(mask.shape[0]):
        by_query = jnp.broadcast_to(document[block * size : (block + 1) * size], (size, size))
        by_key = by_query.T
        allowed = (by_query == by_key) & (key <= query) & (query // length == key // length)
        mask[block] = allowed.astype(F32).astype(BF)


def gram_of(pays, sides, layer, rows):
    if layer == 0:
        return total_of(pays, 2 * rows, 2 * rows + HD)
    base = rows + HD * (layer - 1)
    return total_of(sides, base, base + HD)


def middle_kernel(count, layer, width, *refs):
    pays, sides, refs = refs[:count], refs[count : 2 * count], refs[2 * count :]
    if layer == 1:
        sides, refs = (), sides + refs
    x_before, mean_before, mask, weights_before, weights = refs[:5]
    x, mean, reduced, cross, probs, mixed, pay = refs[5:]
    receive_forward(
        pays, gram_of(pays, sides, layer - 1, x.shape[0]), x_before, mean_before, weights_before,
        width, x, mean, reduced, cross,
    )
    attend(x, mean[:, 0:1], weights, mask, probs, mixed)
    send_forward(x, weights, mixed, pay)


def layer_backward(
    dout, dred, x, mean, mask, weights, weights_before, probs, mixed, reduced, grads, carried, pay
):
    rows, local = x.shape
    size = block_size(rows)
    own = (weights.shape[2] - 16) // 2
    per_slice = own // HD
    rank = dred.shape[1]
    factor = lax.rsqrt(mean + EPS)
    first = dot_tn(dred, mixed[...]).astype(BF)
    for side in range(weights.shape[1]):
        grads[side, 0:rank, :] = first[:, side * own : (side + 1) * own]
    if reduced is not None:
        second = dot_tn(reduced, dout[...]).astype(BF)
        for side in range(weights.shape[1]):
            grads[side, rank : 2 * rank, :] = second[:, side * own : (side + 1) * own]
    back_mixed = [
        from_rank(dred, weights, 0, side).astype(BF) for side in range(weights.shape[1])
    ]
    gain_sums = [None] * (local // HD)
    for block in range(rows // size):
        span = slice(block * size, (block + 1) * size)
        scale = factor[span]
        norm_dot = jnp.zeros((size, HD), F32)
        for head in range(local // HD):
            part = slice(head * HD, (head + 1) * HD)
            side, inner = head // per_slice, (head % per_slice) * HD
            wide = x[span, part].astype(F32)
            gain = head_gain(weights, head)
            unit = wide * scale
            normed = (unit * gain).astype(BF)
            prob = probs[block, head]
            upstream = back_mixed[side][span, inner : inner + HD]
            back_prob = dot_nt(upstream, normed)
            prob_wide = prob.astype(F32)
            inner_sum = jnp.sum(back_prob * prob_wide, axis=1, keepdims=True)
            back_score = prob_wide * (back_prob - inner_sum) * (1.0 / HD)
            both = (back_score + back_score.T).astype(BF)
            back_normed = (dot_tn(prob, upstream) + dot(both, normed)).astype(BF).astype(F32)
            term = jnp.sum(back_normed * unit, axis=0, keepdims=True)
            gain_sums[head] = term if gain_sums[head] is None else gain_sums[head] + term
            if carried is not None:
                scaled = back_normed * gain
                norm_dot = norm_dot + scaled * wide
                carried[span, part] = (dout[span, part].astype(F32) + scaled * scale).astype(BF)
        if carried is not None:
            column = jnp.broadcast_to(jnp.sum(norm_dot, axis=1, keepdims=True), (size, size))
            line = column.T[0:1, :]
            high, low = two_parts(line)
            base = rows + 16 * block
            pay[base : base + 16, :] = jnp.concatenate(
                (high.astype(F32), low.astype(F32), jnp.zeros((14, size), F32)), axis=0
            ).astype(BF)
    zeros = jnp.zeros((15, HD), F32)
    for head in range(local // HD):
        side, inner = head // per_slice, (head % per_slice) * HD
        grads[side, 2 * rank : 2 * rank + 16, inner : inner + HD] = jnp.concatenate(
            (gain_sums[head], zeros), axis=0
        ).astype(BF)
    if carried is not None:
        pay[0:rows, :] = to_rank(carried[...], weights_before, own).astype(BF)


def turn_kernel(count, layer, width, *refs):
    pays, sides, refs = refs[:count], refs[count : 2 * count], refs[2 * count :]
    (x_before, mean_before, mask, weights_before, weights, cot) = refs[:6]
    (x, mean, reduced, cross, grads, carried, pay, last_part) = refs[6:14]
    probs, mixed = refs[14:]
    rows = x.shape[0]
    receive_forward(
        pays, gram_of(pays, sides, layer - 1, rows), x_before, mean_before, weights_before,
        width, x, mean, reduced, cross,
    )
    attend(x, mean[:, 0:1], weights, mask, probs, mixed)
    last_part[...] = to_rank(mixed[...], weights, 0).astype(BF)
    dred = total_of(sides, 0, rows).astype(BF)
    layer_backward(
        cot, dred, x, mean[:, 0:1], mask, weights, weights_before, probs, mixed, None, grads,
        carried, pay,
    )


def split_sides(grads, outs):
    for far, out in enumerate(outs):
        out[...] = grads[lax.axis_index("zh") ^ far]


def back_kernel(count, with_last, to_first, width, *refs):
    pays, refs = refs[:count], refs[count:]
    carried_after, x_after, mean_after, cross_after = refs[:4]
    x, mean, mask, weights = refs[4:8]
    refs = refs[8:]
    weights_before = carried = pay = None
    if not to_first:
        weights_before, refs = refs[0], refs[1:]
    probs, mixed, reduced = refs[:3]
    refs = refs[3:]
    if with_last:
        last_parts, cot, turn_grads = refs[:count], refs[count], refs[count + 1]
        refs = refs[count + 2 :]
    sides = weights.shape[1]
    outs, refs = refs[:sides], refs[sides:]
    if with_last:
        last_outs, refs = refs[:sides], refs[sides:]
    if not to_first:
        carried, pay = refs[:2]
        refs = refs[2:]
    dout, grads = refs
    rows, local = x.shape
    size = block_size(rows)
    own = (weights.shape[2] - 16) // 2
    rank = reduced.shape[1]
    dred_parts = []
    for block in range(rows // size):
        span = slice(block * size, (block + 1) * size)
        base = rows + 16 * block
        lines = total_of(pays, base, base + 16)
        line = lines[0:1] + lines[1:2]
        column = jnp.broadcast_to(line, (size, size)).T
        factor = lax.rsqrt(mean_after[span, 0:1] + EPS)
        pull = column[:, 0:1] * (factor * factor * factor / width)
        dred_parts.append(
            (
                total_of(pays, block * size, (block + 1) * size) - cross_after[span, :] * pull
            ).astype(BF)
        )
        dout[span, :] = (
            carried_after[span, :].astype(F32) - x_after[span, :].astype(F32) * pull
        ).astype(BF)
    dred = dred_parts[0] if len(dred_parts) == 1 else jnp.concatenate(dred_parts, axis=0)
    if with_last:
        last_reduced = total_of(last_parts, 0, rows).astype(BF)
        second = dot_tn(last_reduced, cot[...]).astype(BF)
        for side in range(weights.shape[1]):
            grads[side, 0:rank, :] = turn_grads[side, 0:rank, :]
            grads[side, rank : 2 * rank, :] = second[:, side * own : (side + 1) * own]
            grads[side, 2 * rank :, :] = turn_grads[side, 2 * rank :, :]
        split_sides(grads, last_outs)
    layer_backward(
        dout, dred, x, mean[:, 0:1], mask, weights, weights_before, probs, mixed, reduced[...],
        grads, carried, pay,
    )
    split_sides(grads, outs)


def combine_kernel(sections, sides, *refs):
    parts, refs = refs[: sections * sides], refs[sections * sides :]
    outs, sums = refs[:sections], refs[sections]
    section = lax.axis_index("pipe")
    for layer in range(sections):
        total = parts[layer * sides][...].astype(F32)
        for part in parts[layer * sides + 1 : (layer + 1) * sides]:
            total = total + part[...].astype(F32)
        sums[layer] = total.astype(BF)
    for distance in range(sections):
        outs[distance][...] = sums[section ^ distance]


def finish_kernel(sections, *refs):
    parts = refs[:sections]
    gain, first, second = refs[sections:]
    rank = second.shape[1]
    total = parts[0][...].astype(F32)
    for part in parts[1:]:
        total = total + part[...].astype(F32)
    first[0] = total[0:rank].T
    second[0] = total[rank : 2 * rank]
    gain[...] = total[2 * rank : 2 * rank + 1]


def per_device(tokens, cotangents, starts, counts, layer_gains, first_map, second_map):
    sections = lax.axis_size("pipe")
    groups = lax.axis_size("zl") * lax.axis_size("core")
    directions, micro_count, length, width = tokens.shape
    micro_local = -(-directions * micro_count // sections)
    rows = groups * micro_local * length
    local = width // groups
    own = first_map.shape[1]
    rank = first_map.shape[2]
    heads = local // HD
    size = block_size(rows)
    blocks = rows // size
    sides = lax.axis_size("zh")
    top = sections - 1

    def moved(value, axes, distance):
        size = lax.axis_size(axes)
        return lax.ppermute(value, axes, [(i, i ^ distance) for i in range(size)])

    def each(values, axes):
        return [values[0]] + [
            moved(value, axes, distance) for distance, value in enumerate(values) if distance
        ]

    def exchange(pay):
        return each([pay] * groups, ("zl", "core"))

    token_parts, packed = pack(
        tokens, cotangents, starts, counts, layer_gains, first_map, second_map, groups, micro_local
    )
    packed_far = each([packed] * sides, "zh")
    mine = each([packed] * sections, "pipe")
    received = each(token_parts, ("zl", "core"))
    received, mine, packed_far = lax.optimization_barrier((received, mine, packed_far))
    for part in packed_far[1:]:
        mine = mine + each([part] * sections, "pipe")

    def shaped(shape, kind=BF):
        return jax.ShapeDtypeStruct(shape, kind)

    wide_shape = shaped((rows, local))
    mean_shape = shaped((rows, HD), F32)
    rank_shape = shaped((rows, rank))
    cross_shape = shaped((rows, rank), F32)
    probs_shape = shaped((blocks, heads, size, size))
    grads_shape = (sides, 2 * rank + 16, own)
    half_shape = shaped(grads_shape[1:])
    weights_shape = shaped((sections, sides, slice_rows(own), HD))

    def call(kernel, operands, specs, outs, name, **more):
        return pl.pallas_call(
            kernel,
            grid=(1,),
            in_specs=specs,
            out_specs=vmem_specs(len(outs)),
            out_shape=outs,
            compiler_params=PARAMS,
            name=name,
            **more,
        )(*operands)

    def layer_of(index):
        return layer_spec(weights_shape.shape, index)

    x, cot, mask, mean, mine[0] = call(
        functools.partial(arrange_kernel, length, groups),
        (*received, mine[0]),
        vmem_specs(groups + 1),
        [
            wide_shape,
            wide_shape,
            shaped((blocks, size, size)),
            mean_shape,
            shaped(packed.shape),
        ],
        "arrange",
        scratch_shapes=[pltpu.VMEM((rows, HD), BF)],
    )
    probs, mixed, pay, side, weights = call(
        functools.partial(first_kernel, sections, sides),
        (*mine, x, cot, mask, mean),
        vmem_specs(sides * sections + 4),
        [
            probs_shape,
            wide_shape,
            shaped((2 * rows + HD, HD)),
            shaped((rows + HD * (top - 1), HD)),
            weights_shape,
        ],
        "forward_first",
        scratch_shapes=[pltpu.SemaphoreType.DMA((sections, sides))],
    )
    xs, means, reduceds, crosses = [x], [mean], [], [None]
    all_probs, all_mixed = [probs], [mixed]
    pays = exchange(pay)
    arrived = exchange(side)
    for layer in range(1, top):
        operands = (*pays, *(arrived if layer > 1 else ()))
        specs = vmem_specs(len(operands) + 3) + [layer_of(layer - 1), layer_of(layer)]
        x, mean, reduced, cross, probs, mixed, pay = call(
            functools.partial(middle_kernel, groups, layer, float(width)),
            (*operands, xs[-1], means[-1], mask, weights, weights),
            specs,
            [
                wide_shape,
                mean_shape,
                rank_shape,
                cross_shape,
                probs_shape,
                wide_shape,
                shaped((2 * rows, HD)),
            ],
            "forward_middle",
        )
        xs.append(x)
        means.append(mean)
        reduceds.append(reduced)
        crosses.append(cross)
        all_probs.append(probs)
        all_mixed.append(mixed)
        pays = exchange(pay)

    back_rows = rows + 16 * blocks
    x, mean, reduced, cross, turn_grads, carried, pay, last_part = call(
        functools.partial(turn_kernel, groups, top, float(width)),
        (*pays, *arrived, xs[-1], means[-1], mask, weights, weights, cot),
        vmem_specs(2 * groups + 3) + [layer_of(top - 1), layer_of(top)] + vmem_specs(1),
        [
            wide_shape,
            mean_shape,
            rank_shape,
            cross_shape,
            shaped(grads_shape),
            wide_shape,
            shaped((back_rows, HD)),
            rank_shape,
        ],
        "turn",
        scratch_shapes=[
            pltpu.VMEM(probs_shape.shape, BF),
            pltpu.VMEM(wide_shape.shape, BF),
        ],
    )
    xs.append(x)
    means.append(mean)
    reduceds.append(reduced)
    crosses.append(cross)

    halves = [None] * sections
    for layer in range(top - 1, -1, -1):
        pays = exchange(pay)
        if layer == top - 1:
            last_parts = exchange(last_part)
        with_last = layer == top - 2
        to_first = layer == 0
        operands = (
            *pays, carried, xs[layer + 1], means[layer + 1], crosses[layer + 1],
            xs[layer], means[layer], mask, weights,
        )
        specs = vmem_specs(len(pays) + 7) + [layer_of(layer)]
        if not to_first:
            operands += (weights,)
            specs += [layer_of(layer - 1)]
        operands += (all_probs[layer], all_mixed[layer], reduceds[layer])
        specs += vmem_specs(3)
        outs = [half_shape] * sides
        if with_last:
            operands += (*last_parts, cot, turn_grads)
            specs += vmem_specs(groups + 2)
            outs += [half_shape] * sides
        if not to_first:
            outs += [wide_shape, shaped((back_rows, HD))]
        result = call(
            functools.partial(back_kernel, groups, with_last, to_first, float(width)),
            operands,
            specs,
            outs,
            "backward",
            scratch_shapes=[pltpu.VMEM(wide_shape.shape, BF), pltpu.VMEM(grads_shape, BF)],
        )
        halves[layer] = each(result[:sides], "zh")
        if with_last:
            halves[top] = each(result[sides : 2 * sides], "zh")
        if not to_first:
            carried, pay = result[-2:]

    parts = call(
        functools.partial(combine_kernel, sections, sides),
        sum(halves, []),
        vmem_specs(sections * sides),
        [half_shape] * sections,
        "combine",
        scratch_shapes=[pltpu.VMEM((sections,) + grads_shape[1:], BF)],
    )
    arrived = each(parts, "pipe")
    gain_grad, first_grad, second_grad = call(
        functools.partial(finish_kernel, sections),
        arrived,
        vmem_specs(sections),
        [
            shaped((1, own), F32),
            shaped((1, own, rank), F32),
            shaped((1, rank, own), F32),
        ],
        "finish",
    )
    return (gain_grad, first_grad, second_grad)


def solution(mesh):
    fine = Mesh(
        mesh.devices.reshape(mesh.shape["pipe"], mesh.shape["dp"] // 4, 2, 2),
        ("pipe", "zh", "zl", "core"),
    )
    data = ("zh", "zl", "core")
    in_specs = (
        P(None, data, None, None),
        P(None, data, None, None),
        P(None, data, None),
        P(None, data),
        P("pipe", data),
        P("pipe", data, None),
        P("pipe", None, data),
    )
    out_specs = (P("pipe", data), P("pipe", data, None), P("pipe", None, data))
    mapped = jax.shard_map(
        per_device, mesh=fine, in_specs=in_specs, out_specs=out_specs, check_vma=False
    )

    return mapped
```

```python
import functools

import jax
import jax.numpy as jnp
from jax import lax
from jax.experimental import pallas as pl
from jax.experimental.pallas import tpu as pltpu
from jax.sharding import Mesh, PartitionSpec as P

HD = 128
EPS = 1e-05
FOLDED = HD + 16
BF = jnp.bfloat16
F32 = jnp.float32
PARAMS = pltpu.CompilerParams(vmem_limit_bytes=48 * 1024 * 1024)
PACK_PARAMS = pltpu.CompilerParams(vmem_limit_bytes=60 * 1024 * 1024)


def dot(a, b):
    return jnp.dot(a, b, preferred_element_type=F32)


def dot_nt(a, b):
    return lax.dot_general(a, b, (((1,), (1,)), ((), ())), preferred_element_type=F32)


def dot_tn(a, b):
    return lax.dot_general(a, b, (((0,), (0,)), ((), ())), preferred_element_type=F32)


def two_parts(value):
    high = value.astype(BF)
    return high, (value - high.astype(F32)).astype(BF)


def vmem_specs(count):
    return [pl.BlockSpec(memory_space=pltpu.VMEM)] * count


def layer_spec(shape, layer):
    return pl.BlockSpec((1,) + shape[1:], lambda *_: (layer, 0, 0, 0))


def slice_rows(own):
    return 2 * own + 16


def pack_weights_kernel(gain, first, second, weights, gain_in, second_in, sems):
    own = first.shape[1]
    copies = [
        pltpu.make_async_copy(second.at[0], second_in, sems.at[0]),
        pltpu.make_async_copy(gain, gain_in, sems.at[1]),
        pltpu.make_async_copy(first.at[0], weights.at[pl.ds(0, own)], sems.at[2]),
    ]
    for copy in copies:
        copy.start()
    for copy in copies:
        copy.wait()
    weights[own : 2 * own, :] = second_in[...].astype(F32).T.astype(BF)
    gains = [gain_in[0:1, head * HD : (head + 1) * HD].astype(F32) for head in range(own // HD)]
    gains.append(jnp.zeros((16 - own // HD, HD), F32))
    weights[2 * own :, :] = jnp.concatenate(gains, axis=0).astype(BF)


def pack_weights(gain, first, second):
    own = first.shape[1]
    return pl.pallas_call(
        pack_weights_kernel,
        in_specs=[pl.BlockSpec(memory_space=pltpu.HBM)] * 3,
        out_specs=pl.BlockSpec(memory_space=pltpu.VMEM),
        out_shape=jax.ShapeDtypeStruct((slice_rows(own), HD), BF),
        scratch_shapes=[
            pltpu.VMEM(gain.shape, BF),
            pltpu.VMEM(second.shape[1:], BF),
            pltpu.SemaphoreType.DMA((3,)),
        ],
        compiler_params=PACK_PARAMS,
        name="pack_weights",
    )(gain, first, second)


def pack_tokens_kernel(groups, micro_local, *refs):
    tokens, cotangents, starts, counts = refs[:4]
    parts = refs[4 : 4 + groups]
    tok, cot, starts_in, counts_in, sems = refs[4 + groups :]
    directions, micro_count, length, width = tokens.shape
    local = width // groups
    section = lax.axis_index("pipe")
    group = lax.axis_index("z")
    picks = []
    copies = [
        pltpu.make_async_copy(starts, starts_in, sems.at[0]),
        pltpu.make_async_copy(counts, counts_in, sems.at[1]),
    ]
    for micro in range(micro_local):
        wanted = section * micro_local + micro
        slot = jnp.minimum(wanted, directions * micro_count - 1)
        direction, place = slot // micro_count, slot % micro_count
        picks.append((wanted < directions * micro_count, direction, place))
        rows = pl.ds(micro * length, length)
        copies.append(
            pltpu.make_async_copy(
                tokens.at[direction, place], tok.at[rows], sems.at[2 + 2 * micro]
            )
        )
        copies.append(
            pltpu.make_async_copy(
                cotangents.at[direction, place], cot.at[rows], sems.at[3 + 2 * micro]
            )
        )
    for copy in copies:
        copy.start()
    for copy in copies:
        copy.wait()
    for micro, (keep, direction, place) in enumerate(picks):
        rows = slice(micro * length, (micro + 1) * length)
        widened = tok[rows, :].astype(F32)
        mean = jnp.mean(widened * widened, axis=1, keepdims=True)
        mean_high, mean_low = two_parts(mean)
        position = lax.broadcasted_iota(jnp.int32, (length, HD), 0)
        document = jnp.zeros((length, HD), jnp.int32)
        for entry in range(starts.shape[2]):
            begun = starts_in[direction, place, entry] <= position
            begun = begun & (entry < counts_in[direction, place])
            document = document + begun.astype(jnp.int32)
        lane = lax.broadcasted_iota(jnp.int32, (length, HD), 1)
        tail = jnp.where(
            lane == 0,
            document.astype(F32),
            jnp.where(lane == 1, mean_high.astype(F32), mean_low.astype(F32)),
        ).astype(BF)
        for shift in range(groups):
            start = pl.multiple_of(((group + shift) % groups) * local, local)
            parts[shift][rows, 0:local] = tok[rows, pl.ds(start, local)]
            cotangent = cot[rows, pl.ds(start, local)]
            parts[shift][rows, local : 2 * local] = jnp.where(
                keep, cotangent, jnp.zeros_like(cotangent)
            )
            parts[shift][rows, 2 * local :] = tail


def pack_tokens(tokens, cotangents, starts, counts, groups, micro_local):
    length, width = tokens.shape[2:]
    local = width // groups
    rows = micro_local * length
    return pl.pallas_call(
        functools.partial(pack_tokens_kernel, groups, micro_local),
        in_specs=[pl.BlockSpec(memory_space=pltpu.HBM)] * 4,
        out_specs=vmem_specs(groups),
        out_shape=[jax.ShapeDtypeStruct((rows, 2 * local + HD), BF)] * groups,
        scratch_shapes=[
            pltpu.VMEM((rows, width), BF),
            pltpu.VMEM((rows, width), BF),
            pltpu.SMEM(starts.shape, jnp.int32),
            pltpu.SMEM(counts.shape, jnp.int32),
            pltpu.SemaphoreType.DMA((2 + 2 * micro_local,)),
        ],
        compiler_params=PACK_PARAMS,
        name="pack_tokens",
    )(tokens, cotangents, starts, counts)


def head_gain(weights, head):
    own = (weights.shape[2] - 16) // 2
    per_slice = own // HD
    row = 2 * own + head % per_slice
    return weights[0, head // per_slice, row : row + 1, :].astype(F32)


def block_size(rows):
    return HD if rows % HD == 0 else rows


def to_rank(value, weights, at):
    own = (weights.shape[2] - 16) // 2
    total = None
    for side in range(weights.shape[1]):
        term = dot(value[:, side * own : (side + 1) * own], weights[0, side, at : at + own, :])
        total = term if total is None else total + term
    return total


def from_rank(value, weights, at, side):
    own = (weights.shape[2] - 16) // 2
    return dot_nt(value, weights[0, side, at : at + own, :])


def gram(weights):
    own = (weights.shape[2] - 16) // 2
    total = None
    for side in range(weights.shape[1]):
        part = weights[0, side, own : 2 * own, :]
        term = dot_tn(part, part)
        total = term if total is None else total + term
    return total


def attend(x, mean, weights, mask, probs, mixed):
    rows, local = x.shape
    size = block_size(rows)
    factor = lax.rsqrt(mean + EPS)
    for block in range(rows // size):
        span = slice(block * size, (block + 1) * size)
        allowed = mask[block] > 0
        for head in range(local // HD):
            part = slice(head * HD, (head + 1) * HD)
            normed = (x[span, part].astype(F32) * factor[span] * head_gain(weights, head)).astype(BF)
            scores = dot_nt(normed, normed) * (1.0 / HD)
            raw = jnp.where(allowed, jnp.exp(scores), 0.0)
            prob = (raw / jnp.sum(raw, axis=1, keepdims=True)).astype(BF)
            probs[block, head] = prob
            mixed[span, part] = dot(prob, normed).astype(BF)


def send_forward(x, weights, mixed, pay):
    rows = x.shape[0]
    own = (weights.shape[2] - 16) // 2
    pay[0:rows, :] = to_rank(mixed[...], weights, 0).astype(BF)
    pay[rows : 2 * rows, :] = to_rank(x[...], weights, own).astype(BF)


def total_of(pays, start, stop):
    total = pays[0][start:stop, :].astype(F32)
    for pay in pays[1:]:
        total = total + pay[start:stop, :].astype(F32)
    return total


def receive_forward(
    pays, gram_total, x_before, mean_before, weights_before, width, x, mean, reduced, cross
):
    rows, local = x_before.shape
    own = (weights_before.shape[2] - 16) // 2
    low_rank = total_of(pays, 0, rows).astype(BF)
    before = total_of(pays, rows, 2 * rows)
    high, low = two_parts(gram_total)
    through = dot(low_rank, high) + dot(low_rank, low)
    wide = low_rank.astype(F32)
    change = jnp.sum(wide * (2.0 * before + through), axis=1, keepdims=True) / width
    new_mean = jnp.maximum(mean_before[:, 0:1] + change, 0.0)
    mean[...] = jnp.broadcast_to(new_mean, mean.shape)
    reduced[...] = low_rank
    cross[...] = before + through
    for side in range(weights_before.shape[1]):
        part = slice(side * own, (side + 1) * own)
        x[:, part] = (
            x_before[:, part].astype(F32) + from_rank(low_rank, weights_before, own, side)
        ).astype(BF)


def arrange_kernel(length, groups, *refs):
    received, packed = refs[:groups], refs[groups]
    x, cot, mask, mean, packed_out, tails = refs[groups + 1 :]
    rows, local = x.shape
    place_rows(received, tails, slice(2 * local, None))
    place_rows(received, x, slice(0, local))
    place_rows(received, cot, slice(local, 2 * local))
    tail = tails[...].astype(F32)
    mean[...] = jnp.broadcast_to(tail[:, 1:2] + tail[:, 2:3], mean.shape)
    build_mask(tail[:, 0:1], mask, block_size(rows), length)
    packed_out[...] = packed[...]


def first_kernel(sections, *refs):
    mine, theirs = refs[:sections], refs[sections : 2 * sections]
    x, cot, mask, mean, probs, mixed, pay, side, weights, sems = refs[2 * sections :]
    section, core = lax.axis_index("pipe"), lax.axis_index("core")
    rows = x.shape[0]
    copies = []
    for distance in range(sections):
        layer = section ^ distance
        for parts, place in ((mine, core), (theirs, 1 - core)):
            copies.append(
                pltpu.make_async_copy(
                    parts[distance], weights.at[layer, place], sems.at[layer, place]
                )
            )
    for copy in copies:
        copy.start()

    def arrived(layer):
        for place in range(weights.shape[1]):
            pltpu.make_async_copy(mine[0], weights.at[layer, place], sems.at[layer, place]).wait()

    arrived(0)
    own = (weights.shape[2] - 16) // 2
    layers = [weights.at[pl.ds(layer, 1)] for layer in range(sections)]
    attend(x, mean[:, 0:1], layers[0], mask, probs, mixed)
    send_forward(x, layers[0], mixed, pay)
    arrived(1)
    pay[2 * rows :, :] = fold_grams(layers[0], layers[1])
    for layer in range(2, sections):
        arrived(layer)
    side[0:rows, :] = to_rank(cot[...], layers[-1], own).astype(BF)
    for layer in range(2, sections - 1, 2):
        base, height, folded = gram_place(layer, sections - 1, rows)
        both = fold_grams(layers[layer], layers[layer + 1]) if folded else gram(layers[layer])
        side[base : base + height, :] = both.astype(BF)


def place_rows(received, target, columns):
    groups = len(received)
    rows = received[0].shape[0]
    for shift, part in enumerate(received):
        source = (lax.axis_index("z") + groups - shift) % groups
        target[pl.ds(pl.multiple_of(source * rows, rows), rows), :] = part[:, columns]


def build_mask(document, mask, size, length):
    query = lax.broadcasted_iota(jnp.int32, (size, size), 0)
    key = lax.broadcasted_iota(jnp.int32, (size, size), 1)
    for block in range(mask.shape[0]):
        by_query = jnp.broadcast_to(document[block * size : (block + 1) * size], (size, size))
        by_key = by_query.T
        allowed = (by_query == by_key) & (key <= query) & (query // length == key // length)
        mask[block] = allowed.astype(F32).astype(BF)


def fold_grams(weights, other):
    row, lane = square_places()
    upper, lower = gram(weights), gram(other)
    diagonal = jnp.sum(jnp.where(row == lane, lower, 0.0), axis=0, keepdims=True)
    folded = jnp.where(row <= lane, upper, lower)
    return jnp.concatenate((folded, diagonal, jnp.zeros((15, HD), F32)), axis=0).astype(BF)


def square_places():
    return (
        lax.broadcasted_iota(jnp.int32, (HD, HD), 0),
        lax.broadcasted_iota(jnp.int32, (HD, HD), 1),
    )


def gram_place(layer, top, rows):
    pair = layer // 2
    folded = 2 * pair + 1 < top
    base = 2 * rows if pair == 0 else rows + FOLDED * (pair - 1)
    return base, FOLDED if folded else HD, folded


def gram_of(sources, layer, top, rows):
    base, height, folded = gram_place(layer, top, rows)
    total = total_of(sources, base, base + height)
    if not folded:
        return total
    row, lane = square_places()
    square = total[0:HD]
    if layer % 2 == 0:
        return jnp.where(row <= lane, square, square.T)
    lower = jnp.where(row > lane, square, square.T)
    return jnp.where(row == lane, total[HD : HD + 1], lower)


def middle_kernel(count, layer, top, width, *refs):
    pays, sources, refs = refs[:count], refs[count : 2 * count], refs[2 * count :]
    if layer == 1:
        sources, refs = pays, sources + refs
    x_before, mean_before, mask, weights_before, weights = refs[:5]
    x, mean, reduced, cross, probs, mixed, pay = refs[5:]
    receive_forward(
        pays, gram_of(sources, layer - 1, top, x.shape[0]), x_before, mean_before, weights_before,
        width, x, mean, reduced, cross,
    )
    attend(x, mean[:, 0:1], weights, mask, probs, mixed)
    send_forward(x, weights, mixed, pay)


def layer_backward(
    dout, dred, x, mean, mask, weights, weights_before, probs, mixed, reduced, grads, carried, pay
):
    rows, local = x.shape
    size = block_size(rows)
    own = (weights.shape[2] - 16) // 2
    per_slice = own // HD
    rank = dred.shape[1]
    factor = lax.rsqrt(mean + EPS)
    first = dot_tn(dred, mixed[...]).astype(BF)
    for side in range(weights.shape[1]):
        grads[side, 0:rank, :] = first[:, side * own : (side + 1) * own]
    if reduced is not None:
        second = dot_tn(reduced, dout[...]).astype(BF)
        for side in range(weights.shape[1]):
            grads[side, rank : 2 * rank, :] = second[:, side * own : (side + 1) * own]
    back_mixed = [
        from_rank(dred, weights, 0, side).astype(BF) for side in range(weights.shape[1])
    ]
    gain_sums = [None] * (local // HD)
    for block in range(rows // size):
        span = slice(block * size, (block + 1) * size)
        scale = factor[span]
        norm_dot = jnp.zeros((size, HD), F32)
        for head in range(local // HD):
            part = slice(head * HD, (head + 1) * HD)
            side, inner = head // per_slice, (head % per_slice) * HD
            wide = x[span, part].astype(F32)
            gain = head_gain(weights, head)
            unit = wide * scale
            normed = (unit * gain).astype(BF)
            prob = probs[block, head]
            upstream = back_mixed[side][span, inner : inner + HD]
            back_prob = dot_nt(upstream, normed)
            prob_wide = prob.astype(F32)
            inner_sum = jnp.sum(back_prob * prob_wide, axis=1, keepdims=True)
            back_score = prob_wide * (back_prob - inner_sum) * (1.0 / HD)
            both = (back_score + back_score.T).astype(BF)
            back_normed = (dot_tn(prob, upstream) + dot(both, normed)).astype(BF).astype(F32)
            term = jnp.sum(back_normed * unit, axis=0, keepdims=True)
            gain_sums[head] = term if gain_sums[head] is None else gain_sums[head] + term
            if carried is not None:
                scaled = back_normed * gain
                norm_dot = norm_dot + scaled * wide
                carried[span, part] = (dout[span, part].astype(F32) + scaled * scale).astype(BF)
        if carried is not None:
            column = jnp.broadcast_to(jnp.sum(norm_dot, axis=1, keepdims=True), (size, size))
            line = column.T[0:1, :]
            high, low = two_parts(line)
            base = rows + 16 * block
            pay[base : base + 16, :] = jnp.concatenate(
                (high.astype(F32), low.astype(F32), jnp.zeros((14, size), F32)), axis=0
            ).astype(BF)
    zeros = jnp.zeros((15, HD), F32)
    for head in range(local // HD):
        side, inner = head // per_slice, (head % per_slice) * HD
        grads[side, 2 * rank : 2 * rank + 16, inner : inner + HD] = jnp.concatenate(
            (gain_sums[head], zeros), axis=0
        ).astype(BF)
    if carried is not None:
        pay[0:rows, :] = to_rank(carried[...], weights_before, own).astype(BF)


def turn_kernel(count, layer, width, *refs):
    pays, sides, refs = refs[:count], refs[count : 2 * count], refs[2 * count :]
    (x_before, mean_before, mask, weights_before, weights, cot) = refs[:6]
    (x, mean, reduced, cross, grads, carried, pay) = refs[6:13]
    probs, mixed = refs[13:]
    rows = x.shape[0]
    receive_forward(
        pays, gram_of(sides, layer - 1, layer, rows), x_before, mean_before, weights_before,
        width, x, mean, reduced, cross,
    )
    attend(x, mean[:, 0:1], weights, mask, probs, mixed)
    pay[pay.shape[0] - rows :, :] = to_rank(mixed[...], weights, 0).astype(BF)
    dred = total_of(sides, 0, rows).astype(BF)
    layer_backward(
        cot, dred, x, mean[:, 0:1], mask, weights, weights_before, probs, mixed, None, grads,
        carried, pay,
    )


def split_sides(grads, keep, send):
    core = lax.axis_index("core")
    keep[...] = grads[core]
    send[...] = grads[1 - core]


def back_kernel(count, with_last, to_first, width, *refs):
    pays, refs = refs[:count], refs[count:]
    carried_after, x_after, mean_after, cross_after = refs[:4]
    x, mean, mask, weights = refs[4:8]
    refs = refs[8:]
    weights_before = carried = pay = None
    if not to_first:
        weights_before, refs = refs[0], refs[1:]
    probs, mixed, reduced = refs[:3]
    refs = refs[3:]
    if with_last:
        cot, turn_grads = refs[:2]
        refs = refs[2:]
    keep, send = refs[:2]
    refs = refs[2:]
    if with_last:
        last_keep, last_send = refs[:2]
        refs = refs[2:]
    if not to_first:
        carried, pay = refs[:2]
        refs = refs[2:]
    dout, grads = refs
    rows, local = x.shape
    size = block_size(rows)
    own = (weights.shape[2] - 16) // 2
    rank = reduced.shape[1]
    dred_parts = []
    for block in range(rows // size):
        span = slice(block * size, (block + 1) * size)
        base = rows + 16 * block
        lines = total_of(pays, base, base + 16)
        line = lines[0:1] + lines[1:2]
        column = jnp.broadcast_to(line, (size, size)).T
        factor = lax.rsqrt(mean_after[span, 0:1] + EPS)
        pull = column[:, 0:1] * (factor * factor * factor / width)
        dred_parts.append(
            (
                total_of(pays, block * size, (block + 1) * size) - cross_after[span, :] * pull
            ).astype(BF)
        )
        dout[span, :] = (
            carried_after[span, :].astype(F32) - x_after[span, :].astype(F32) * pull
        ).astype(BF)
    dred = dred_parts[0] if len(dred_parts) == 1 else jnp.concatenate(dred_parts, axis=0)
    if with_last:
        last_reduced = total_of(pays, pays[0].shape[0] - rows, pays[0].shape[0]).astype(BF)
        second = dot_tn(last_reduced, cot[...]).astype(BF)
        for side in range(weights.shape[1]):
            grads[side, 0:rank, :] = turn_grads[side, 0:rank, :]
            grads[side, rank : 2 * rank, :] = second[:, side * own : (side + 1) * own]
            grads[side, 2 * rank :, :] = turn_grads[side, 2 * rank :, :]
        split_sides(grads, last_keep, last_send)
    layer_backward(
        dout, dred, x, mean[:, 0:1], mask, weights, weights_before, probs, mixed, reduced[...],
        grads, carried, pay,
    )
    split_sides(grads, keep, send)


def combine_kernel(sections, *refs):
    kept, swapped = refs[:sections], refs[sections : 2 * sections]
    outs, sums = refs[2 * sections : 3 * sections], refs[3 * sections]
    section = lax.axis_index("pipe")
    for layer in range(sections):
        sums[layer] = (kept[layer][...].astype(F32) + swapped[layer][...].astype(F32)).astype(BF)
    for distance in range(sections):
        outs[distance][...] = sums[section ^ distance]


def finish_kernel(sections, *refs):
    parts = refs[:sections]
    gain, first, second = refs[sections:]
    rank = second.shape[1]
    total = parts[0][...].astype(F32)
    for part in parts[1:]:
        total = total + part[...].astype(F32)
    first[0] = total[0:rank].T
    second[0] = total[rank : 2 * rank]
    gain[...] = total[2 * rank : 2 * rank + 1]


def per_device(tokens, cotangents, starts, counts, layer_gains, first_map, second_map):
    sections = lax.axis_size("pipe")
    groups = lax.axis_size("z")
    directions, micro_count, length, width = tokens.shape
    micro_local = -(-directions * micro_count // sections)
    rows = groups * micro_local * length
    local = width // groups
    own = first_map.shape[1]
    rank = first_map.shape[2]
    heads = local // HD
    size = block_size(rows)
    blocks = rows // size
    sides = lax.axis_size("core")
    top = sections - 1

    def shifted(value, shift):
        return lax.ppermute(value, "z", [(i, (i + shift) % groups) for i in range(groups)])

    def across(value, distance):
        return lax.ppermute(value, "pipe", [(i, i ^ distance) for i in range(sections)])

    def swapped(value):
        return lax.ppermute(value, "core", [(i, 1 - i) for i in range(sides)])

    def exchange(pay):
        return [pay] + [shifted(pay, shift) for shift in range(1, groups)]

    packed = pack_weights(layer_gains, first_map, second_map)
    mine = [packed] + [across(packed, distance) for distance in range(1, sections)]
    tokens, packed = lax.optimization_barrier((tokens, packed))
    token_parts = pack_tokens(tokens, cotangents, starts, counts, groups, micro_local)
    received = [token_parts[0]]
    received += [shifted(token_parts[shift], shift) for shift in range(1, groups)]
    received, mine = lax.optimization_barrier((received, mine))
    theirs = [swapped(part) for part in mine]

    def shaped(shape, kind=BF):
        return jax.ShapeDtypeStruct(shape, kind)

    wide_shape = shaped((rows, local))
    mean_shape = shaped((rows, HD), F32)
    rank_shape = shaped((rows, rank))
    cross_shape = shaped((rows, rank), F32)
    probs_shape = shaped((blocks, heads, size, size))
    grads_shape = (sides, 2 * rank + 16, own)
    half_shape = shaped(grads_shape[1:])
    weights_shape = shaped((sections, sides, slice_rows(own), HD))

    def call(kernel, operands, specs, outs, name, **more):
        return pl.pallas_call(
            kernel,
            grid=(1,),
            in_specs=specs,
            out_specs=vmem_specs(len(outs)),
            out_shape=outs,
            compiler_params=PARAMS,
            name=name,
            **more,
        )(*operands)

    def layer_of(index):
        return layer_spec(weights_shape.shape, index)

    x, cot, mask, mean, mine[0] = call(
        functools.partial(arrange_kernel, length, groups),
        (*received, mine[0]),
        vmem_specs(groups + 1),
        [
            wide_shape,
            wide_shape,
            shaped((blocks, size, size)),
            mean_shape,
            shaped(packed.shape),
        ],
        "arrange",
        scratch_shapes=[pltpu.VMEM((rows, HD), BF)],
    )
    last_gram = gram_place(top - 1, top, rows)
    side_rows = last_gram[0] + last_gram[1]
    probs, mixed, pay, side, weights = call(
        functools.partial(first_kernel, sections),
        (*mine, *theirs, x, cot, mask, mean),
        vmem_specs(2 * sections + 4),
        [
            probs_shape,
            wide_shape,
            shaped((2 * rows + FOLDED, HD)),
            shaped((side_rows, HD)),
            weights_shape,
        ],
        "forward_first",
        scratch_shapes=[pltpu.SemaphoreType.DMA((sections, sides))],
    )
    xs, means, reduceds, crosses = [x], [mean], [], [None]
    all_probs, all_mixed = [probs], [mixed]
    first_pays = pays = exchange(pay)
    arrived = exchange(side)
    for layer in range(1, top):
        operands = (*pays, *((), first_pays, arrived)[min(layer, 3) - 1])
        specs = vmem_specs(len(operands) + 3) + [layer_of(layer - 1), layer_of(layer)]
        x, mean, reduced, cross, probs, mixed, pay = call(
            functools.partial(middle_kernel, groups, layer, top, float(width)),
            (*operands, xs[-1], means[-1], mask, weights, weights),
            specs,
            [
                wide_shape,
                mean_shape,
                rank_shape,
                cross_shape,
                probs_shape,
                wide_shape,
                shaped((2 * rows, HD)),
            ],
            "forward_middle",
        )
        xs.append(x)
        means.append(mean)
        reduceds.append(reduced)
        crosses.append(cross)
        all_probs.append(probs)
        all_mixed.append(mixed)
        pays = exchange(pay)

    back_rows = rows + 16 * blocks
    x, mean, reduced, cross, turn_grads, carried, pay = call(
        functools.partial(turn_kernel, groups, top, float(width)),
        (*pays, *arrived, xs[-1], means[-1], mask, weights, weights, cot),
        vmem_specs(2 * groups + 3) + [layer_of(top - 1), layer_of(top)] + vmem_specs(1),
        [
            wide_shape,
            mean_shape,
            rank_shape,
            cross_shape,
            shaped(grads_shape),
            wide_shape,
            shaped((back_rows + rows, HD)),
        ],
        "turn",
        scratch_shapes=[
            pltpu.VMEM(probs_shape.shape, BF),
            pltpu.VMEM(wide_shape.shape, BF),
        ],
    )
    xs.append(x)
    means.append(mean)
    reduceds.append(reduced)
    crosses.append(cross)

    kept, taken = [None] * sections, [None] * sections
    for layer in range(top - 1, -1, -1):
        pays = exchange(pay)
        with_last = layer == top - 1
        to_first = layer == 0
        operands = (
            *pays, carried, xs[layer + 1], means[layer + 1], crosses[layer + 1],
            xs[layer], means[layer], mask, weights,
        )
        specs = vmem_specs(len(pays) + 7) + [layer_of(layer)]
        if not to_first:
            operands += (weights,)
            specs += [layer_of(layer - 1)]
        operands += (all_probs[layer], all_mixed[layer], reduceds[layer])
        specs += vmem_specs(3)
        outs = [half_shape] * 2
        if with_last:
            operands += (cot, turn_grads)
            specs += vmem_specs(2)
            outs += [half_shape] * 2
        if not to_first:
            outs += [wide_shape, shaped((back_rows, HD))]
        result = call(
            functools.partial(back_kernel, groups, with_last, to_first, float(width)),
            operands,
            specs,
            outs,
            "backward",
            scratch_shapes=[pltpu.VMEM(wide_shape.shape, BF), pltpu.VMEM(grads_shape, BF)],
        )
        kept[layer], taken[layer] = result[0], swapped(result[1])
        if with_last:
            kept[top], taken[top] = result[2], swapped(result[3])
        if not to_first:
            carried, pay = result[-2:]

    parts = call(
        functools.partial(combine_kernel, sections),
        (*kept, *taken),
        vmem_specs(2 * sections),
        [half_shape] * sections,
        "combine",
        scratch_shapes=[pltpu.VMEM((sections,) + grads_shape[1:], BF)],
    )
    arrived = [parts[0]] + [across(parts[distance], distance) for distance in range(1, sections)]
    gain_grad, first_grad, second_grad = call(
        functools.partial(finish_kernel, sections),
        arrived,
        vmem_specs(sections),
        [
            shaped((1, own), F32),
            shaped((1, own, rank), F32),
            shaped((1, rank, own), F32),
        ],
        "finish",
    )
    return (gain_grad, first_grad, second_grad)


def solution(mesh):
    fine = Mesh(
        mesh.devices.reshape(mesh.shape["pipe"], mesh.shape["dp"] // 2, 2), ("pipe", "z", "core")
    )
    data = ("z", "core")
    in_specs = (
        P(None, data, None, None),
        P(None, data, None, None),
        P(None, data, None),
        P(None, data),
        P("pipe", data),
        P("pipe", data, None),
        P("pipe", None, data),
    )
    out_specs = (P("pipe", data), P("pipe", data, None), P("pipe", None, data))
    mapped = jax.shard_map(
        per_device, mesh=fine, in_specs=in_specs, out_specs=out_specs, check_vma=False
    )

    return mapped
```

```python
import functools

import jax
import jax.numpy as jnp
from jax import lax
from jax.experimental import pallas as pl
from jax.experimental.pallas import tpu as pltpu
from jax.sharding import Mesh, PartitionSpec as P

HD = 128
EPS = 1e-05
FOLDED = HD + 16
BF = jnp.bfloat16
F32 = jnp.float32
PARAMS = pltpu.CompilerParams(vmem_limit_bytes=48 * 1024 * 1024)
PACK_PARAMS = pltpu.CompilerParams(vmem_limit_bytes=60 * 1024 * 1024)


def dot(a, b):
    return jnp.dot(a, b, preferred_element_type=F32)


def dot_nt(a, b):
    return lax.dot_general(a, b, (((1,), (1,)), ((), ())), preferred_element_type=F32)


def dot_tn(a, b):
    return lax.dot_general(a, b, (((0,), (0,)), ((), ())), preferred_element_type=F32)


def two_parts(value):
    high = value.astype(BF)
    return high, (value - high.astype(F32)).astype(BF)


def vmem_specs(count):
    return [pl.BlockSpec(memory_space=pltpu.VMEM)] * count


def layer_spec(shape, layer):
    return pl.BlockSpec((1,) + shape[1:], lambda *_: (layer, 0, 0, 0))


def slice_rows(own):
    return 2 * own + 16


def pack_kernel(groups, micro_local, *refs):
    tokens, cotangents, starts, counts, gain, first, second = refs[:7]
    parts, weights = refs[7 : 7 + groups], refs[7 + groups]
    tok, cot, starts_in, counts_in, gain_in, second_in, sems = refs[8 + groups :]
    directions, micro_count, length, width = tokens.shape
    local = width // groups
    own = first.shape[1]
    section = lax.axis_index("pipe")
    group = lax.axis_index("z")
    picks = []
    copies = [
        pltpu.make_async_copy(second.at[0], second_in, sems.at[0]),
        pltpu.make_async_copy(gain, gain_in, sems.at[1]),
        pltpu.make_async_copy(first.at[0], weights.at[pl.ds(0, own)], sems.at[2]),
        pltpu.make_async_copy(starts, starts_in, sems.at[3]),
        pltpu.make_async_copy(counts, counts_in, sems.at[4]),
    ]
    for micro in range(micro_local):
        wanted = section * micro_local + micro
        slot = jnp.minimum(wanted, directions * micro_count - 1)
        direction, place = slot // micro_count, slot % micro_count
        picks.append((wanted < directions * micro_count, direction, place))
        rows = pl.ds(micro * length, length)
        copies.append(
            pltpu.make_async_copy(
                tokens.at[direction, place], tok.at[rows], sems.at[5 + 2 * micro]
            )
        )
        copies.append(
            pltpu.make_async_copy(
                cotangents.at[direction, place], cot.at[rows], sems.at[6 + 2 * micro]
            )
        )
    for copy in copies:
        copy.start()
    for copy in copies:
        copy.wait()
    weights[own : 2 * own, :] = second_in[...].astype(F32).T.astype(BF)
    gains = [gain_in[0:1, head * HD : (head + 1) * HD].astype(F32) for head in range(own // HD)]
    gains.append(jnp.zeros((16 - own // HD, HD), F32))
    weights[2 * own :, :] = jnp.concatenate(gains, axis=0).astype(BF)
    for micro, (keep, direction, place) in enumerate(picks):
        rows = slice(micro * length, (micro + 1) * length)
        widened = tok[rows, :].astype(F32)
        mean = jnp.mean(widened * widened, axis=1, keepdims=True)
        mean_high, mean_low = two_parts(mean)
        position = lax.broadcasted_iota(jnp.int32, (length, HD), 0)
        document = jnp.zeros((length, HD), jnp.int32)
        for entry in range(starts.shape[2]):
            begun = starts_in[direction, place, entry] <= position
            begun = begun & (entry < counts_in[direction, place])
            document = document + begun.astype(jnp.int32)
        lane = lax.broadcasted_iota(jnp.int32, (length, HD), 1)
        tail = jnp.where(
            lane == 0,
            document.astype(F32),
            jnp.where(lane == 1, mean_high.astype(F32), mean_low.astype(F32)),
        ).astype(BF)
        for shift in range(groups):
            start = pl.multiple_of((group ^ shift) * local, local)
            parts[shift][rows, 0:local] = tok[rows, pl.ds(start, local)]
            cotangent = cot[rows, pl.ds(start, local)]
            parts[shift][rows, local : 2 * local] = jnp.where(
                keep, cotangent, jnp.zeros_like(cotangent)
            )
            parts[shift][rows, 2 * local :] = tail


def pack(tokens, cotangents, starts, counts, gain, first, second, groups, micro_local):
    length, width = tokens.shape[2:]
    own = first.shape[1]
    local = width // groups
    rows = micro_local * length
    shape = jax.ShapeDtypeStruct
    results = pl.pallas_call(
        functools.partial(pack_kernel, groups, micro_local),
        in_specs=[pl.BlockSpec(memory_space=pltpu.HBM)] * 7,
        out_specs=vmem_specs(groups + 1),
        out_shape=[shape((rows, 2 * local + HD), BF)] * groups
        + [shape((slice_rows(own), HD), BF)],
        scratch_shapes=[
            pltpu.VMEM((rows, width), BF),
            pltpu.VMEM((rows, width), BF),
            pltpu.SMEM(starts.shape, jnp.int32),
            pltpu.SMEM(counts.shape, jnp.int32),
            pltpu.VMEM(gain.shape, BF),
            pltpu.VMEM(second.shape[1:], BF),
            pltpu.SemaphoreType.DMA((5 + 2 * micro_local,)),
        ],
        compiler_params=PACK_PARAMS,
        name="pack",
    )(tokens, cotangents, starts, counts, gain, first, second)
    return results[:groups], results[groups]


def head_gain(weights, head):
    own = (weights.shape[2] - 16) // 2
    per_slice = own // HD
    row = 2 * own + head % per_slice
    return weights[0, head // per_slice, row : row + 1, :].astype(F32)


def block_size(rows):
    return HD if rows % HD == 0 else rows


def to_rank(value, weights, at):
    own = (weights.shape[2] - 16) // 2
    total = None
    for side in range(weights.shape[1]):
        term = dot(value[:, side * own : (side + 1) * own], weights[0, side, at : at + own, :])
        total = term if total is None else total + term
    return total


def from_rank(value, weights, at, side):
    own = (weights.shape[2] - 16) // 2
    return dot_nt(value, weights[0, side, at : at + own, :])


def gram(weights):
    own = (weights.shape[2] - 16) // 2
    total = None
    for side in range(weights.shape[1]):
        part = weights[0, side, own : 2 * own, :]
        term = dot_tn(part, part)
        total = term if total is None else total + term
    return total


def attend(x, mean, weights, mask, probs, mixed):
    rows, local = x.shape
    size = block_size(rows)
    factor = lax.rsqrt(mean + EPS)
    for block in range(rows // size):
        span = slice(block * size, (block + 1) * size)
        allowed = mask[block] > 0
        for head in range(local // HD):
            part = slice(head * HD, (head + 1) * HD)
            normed = (x[span, part].astype(F32) * factor[span] * head_gain(weights, head)).astype(BF)
            scores = dot_nt(normed, normed) * (1.0 / HD)
            raw = jnp.where(allowed, jnp.exp(scores), 0.0)
            prob = (raw / jnp.sum(raw, axis=1, keepdims=True)).astype(BF)
            probs[block, head] = prob
            mixed[span, part] = dot(prob, normed).astype(BF)


def send_forward(x, weights, mixed, pay):
    rows = x.shape[0]
    own = (weights.shape[2] - 16) // 2
    pay[0:rows, :] = to_rank(mixed[...], weights, 0).astype(BF)
    pay[rows : 2 * rows, :] = to_rank(x[...], weights, own).astype(BF)


def total_of(pays, start, stop):
    total = pays[0][start:stop, :].astype(F32)
    for pay in pays[1:]:
        total = total + pay[start:stop, :].astype(F32)
    return total


def receive_forward(
    pays, gram_total, x_before, mean_before, weights_before, width, x, mean, reduced, cross
):
    rows, local = x_before.shape
    own = (weights_before.shape[2] - 16) // 2
    low_rank = total_of(pays, 0, rows).astype(BF)
    before = total_of(pays, rows, 2 * rows)
    high, low = two_parts(gram_total)
    through = dot(low_rank, high) + dot(low_rank, low)
    wide = low_rank.astype(F32)
    change = jnp.sum(wide * (2.0 * before + through), axis=1, keepdims=True) / width
    new_mean = jnp.maximum(mean_before[:, 0:1] + change, 0.0)
    mean[...] = jnp.broadcast_to(new_mean, mean.shape)
    reduced[...] = low_rank
    cross[...] = before + through
    for side in range(weights_before.shape[1]):
        part = slice(side * own, (side + 1) * own)
        x[:, part] = (
            x_before[:, part].astype(F32) + from_rank(low_rank, weights_before, own, side)
        ).astype(BF)


def arrange_kernel(length, groups, *refs):
    received, packed = refs[:groups], refs[groups]
    x, cot, mask, mean, packed_out, tails = refs[groups + 1 :]
    rows, local = x.shape
    place_rows(received, tails, slice(2 * local, None))
    place_rows(received, x, slice(0, local))
    place_rows(received, cot, slice(local, 2 * local))
    tail = tails[...].astype(F32)
    mean[...] = jnp.broadcast_to(tail[:, 1:2] + tail[:, 2:3], mean.shape)
    build_mask(tail[:, 0:1], mask, block_size(rows), length)
    packed_out[...] = packed[...]


def first_kernel(sections, *refs):
    mine, theirs = refs[:sections], refs[sections : 2 * sections]
    x, cot, mask, mean, probs, mixed, pay, side, weights, sems = refs[2 * sections :]
    section, core = lax.axis_index("pipe"), lax.axis_index("core")
    rows = x.shape[0]
    copies = []
    for distance in range(sections):
        layer = section ^ distance
        for parts, place in ((mine, core), (theirs, 1 - core)):
            copies.append(
                pltpu.make_async_copy(
                    parts[distance], weights.at[layer, place], sems.at[layer, place]
                )
            )
    for copy in copies:
        copy.start()

    def arrived(layer):
        for place in range(weights.shape[1]):
            pltpu.make_async_copy(mine[0], weights.at[layer, place], sems.at[layer, place]).wait()

    arrived(0)
    own = (weights.shape[2] - 16) // 2
    layers = [weights.at[pl.ds(layer, 1)] for layer in range(sections)]
    attend(x, mean[:, 0:1], layers[0], mask, probs, mixed)
    send_forward(x, layers[0], mixed, pay)
    arrived(1)
    pay[2 * rows :, :] = fold_grams(layers[0], layers[1])
    for layer in range(2, sections):
        arrived(layer)
    side[0:rows, :] = to_rank(cot[...], layers[-1], own).astype(BF)
    for layer in range(2, sections - 1, 2):
        base, height, folded = gram_place(layer, sections - 1, rows)
        both = fold_grams(layers[layer], layers[layer + 1]) if folded else gram(layers[layer])
        side[base : base + height, :] = both.astype(BF)


def place_rows(received, target, columns):
    rows = received[0].shape[0]
    for shift, part in enumerate(received):
        source = lax.axis_index("z") ^ shift
        target[pl.ds(pl.multiple_of(source * rows, rows), rows), :] = part[:, columns]


def build_mask(document, mask, size, length):
    query = lax.broadcasted_iota(jnp.int32, (size, size), 0)
    key = lax.broadcasted_iota(jnp.int32, (size, size), 1)
    for block in range(mask.shape[0]):
        by_query = jnp.broadcast_to(document[block * size : (block + 1) * size], (size, size))
        by_key = by_query.T
        allowed = (by_query == by_key) & (key <= query) & (query // length == key // length)
        mask[block] = allowed.astype(F32).astype(BF)


def fold_grams(weights, other):
    row, lane = square_places()
    upper, lower = gram(weights), gram(other)
    diagonal = jnp.sum(jnp.where(row == lane, lower, 0.0), axis=0, keepdims=True)
    folded = jnp.where(row <= lane, upper, lower)
    return jnp.concatenate((folded, diagonal, jnp.zeros((15, HD), F32)), axis=0).astype(BF)


def square_places():
    return (
        lax.broadcasted_iota(jnp.int32, (HD, HD), 0),
        lax.broadcasted_iota(jnp.int32, (HD, HD), 1),
    )


def gram_place(layer, top, rows):
    pair = layer // 2
    folded = 2 * pair + 1 < top
    base = 2 * rows if pair == 0 else rows + FOLDED * (pair - 1)
    return base, FOLDED if folded else HD, folded


def gram_of(sources, layer, top, rows):
    base, height, folded = gram_place(layer, top, rows)
    total = total_of(sources, base, base + height)
    if not folded:
        return total
    row, lane = square_places()
    square = total[0:HD]
    if layer % 2 == 0:
        return jnp.where(row <= lane, square, square.T)
    lower = jnp.where(row > lane, square, square.T)
    return jnp.where(row == lane, total[HD : HD + 1], lower)


def middle_kernel(count, layer, top, width, *refs):
    pays, sources, refs = refs[:count], refs[count : 2 * count], refs[2 * count :]
    if layer == 1:
        sources, refs = pays, sources + refs
    x_before, mean_before, mask, weights_before, weights = refs[:5]
    x, mean, reduced, cross, probs, mixed, pay = refs[5:]
    receive_forward(
        pays, gram_of(sources, layer - 1, top, x.shape[0]), x_before, mean_before, weights_before,
        width, x, mean, reduced, cross,
    )
    attend(x, mean[:, 0:1], weights, mask, probs, mixed)
    send_forward(x, weights, mixed, pay)


def layer_backward(
    dout, dred, x, mean, mask, weights, weights_before, probs, mixed, reduced, grads, carried, pay
):
    rows, local = x.shape
    size = block_size(rows)
    own = (weights.shape[2] - 16) // 2
    per_slice = own // HD
    rank = dred.shape[1]
    factor = lax.rsqrt(mean + EPS)
    first = dot_tn(dred, mixed[...]).astype(BF)
    for side in range(weights.shape[1]):
        grads[side, 0:rank, :] = first[:, side * own : (side + 1) * own]
    if reduced is not None:
        second = dot_tn(reduced, dout[...]).astype(BF)
        for side in range(weights.shape[1]):
            grads[side, rank : 2 * rank, :] = second[:, side * own : (side + 1) * own]
    back_mixed = [
        from_rank(dred, weights, 0, side).astype(BF) for side in range(weights.shape[1])
    ]
    gain_sums = [None] * (local // HD)
    for block in range(rows // size):
        span = slice(block * size, (block + 1) * size)
        scale = factor[span]
        norm_dot = jnp.zeros((size, HD), F32)
        for head in range(local // HD):
            part = slice(head * HD, (head + 1) * HD)
            side, inner = head // per_slice, (head % per_slice) * HD
            wide = x[span, part].astype(F32)
            gain = head_gain(weights, head)
            unit = wide * scale
            normed = (unit * gain).astype(BF)
            prob = probs[block, head]
            upstream = back_mixed[side][span, inner : inner + HD]
            back_prob = dot_nt(upstream, normed)
            prob_wide = prob.astype(F32)
            inner_sum = jnp.sum(back_prob * prob_wide, axis=1, keepdims=True)
            back_score = prob_wide * (back_prob - inner_sum) * (1.0 / HD)
            both = (back_score + back_score.T).astype(BF)
            back_normed = (dot_tn(prob, upstream) + dot(both, normed)).astype(BF).astype(F32)
            term = jnp.sum(back_normed * unit, axis=0, keepdims=True)
            gain_sums[head] = term if gain_sums[head] is None else gain_sums[head] + term
            if carried is not None:
                scaled = back_normed * gain
                norm_dot = norm_dot + scaled * wide
                carried[span, part] = (dout[span, part].astype(F32) + scaled * scale).astype(BF)
        if carried is not None:
            column = jnp.broadcast_to(jnp.sum(norm_dot, axis=1, keepdims=True), (size, size))
            line = column.T[0:1, :]
            high, low = two_parts(line)
            base = rows + 16 * block
            pay[base : base + 16, :] = jnp.concatenate(
                (high.astype(F32), low.astype(F32), jnp.zeros((14, size), F32)), axis=0
            ).astype(BF)
    zeros = jnp.zeros((15, HD), F32)
    for head in range(local // HD):
        side, inner = head // per_slice, (head % per_slice) * HD
        grads[side, 2 * rank : 2 * rank + 16, inner : inner + HD] = jnp.concatenate(
            (gain_sums[head], zeros), axis=0
        ).astype(BF)
    if carried is not None:
        pay[0:rows, :] = to_rank(carried[...], weights_before, own).astype(BF)


def turn_kernel(count, layer, width, *refs):
    pays, sides, refs = refs[:count], refs[count : 2 * count], refs[2 * count :]
    (x_before, mean_before, mask, weights_before, weights, cot) = refs[:6]
    (x, mean, reduced, cross, grads, carried, pay) = refs[6:13]
    probs, mixed = refs[13:]
    rows = x.shape[0]
    receive_forward(
        pays, gram_of(sides, layer - 1, layer, rows), x_before, mean_before, weights_before,
        width, x, mean, reduced, cross,
    )
    attend(x, mean[:, 0:1], weights, mask, probs, mixed)
    pay[pay.shape[0] - rows :, :] = to_rank(mixed[...], weights, 0).astype(BF)
    dred = total_of(sides, 0, rows).astype(BF)
    layer_backward(
        cot, dred, x, mean[:, 0:1], mask, weights, weights_before, probs, mixed, None, grads,
        carried, pay,
    )


def split_sides(grads, keep, send):
    core = lax.axis_index("core")
    keep[...] = grads[core]
    send[...] = grads[1 - core]


def back_kernel(count, with_last, to_first, width, *refs):
    pays, refs = refs[:count], refs[count:]
    carried_after, x_after, mean_after, cross_after = refs[:4]
    x, mean, mask, weights = refs[4:8]
    refs = refs[8:]
    weights_before = carried = pay = None
    if not to_first:
        weights_before, refs = refs[0], refs[1:]
    probs, mixed, reduced = refs[:3]
    refs = refs[3:]
    if with_last:
        cot, turn_grads = refs[:2]
        refs = refs[2:]
    keep, send = refs[:2]
    refs = refs[2:]
    if with_last:
        last_keep, last_send = refs[:2]
        refs = refs[2:]
    if not to_first:
        carried, pay = refs[:2]
        refs = refs[2:]
    dout, grads = refs
    rows, local = x.shape
    size = block_size(rows)
    own = (weights.shape[2] - 16) // 2
    rank = reduced.shape[1]
    dred_parts = []
    for block in range(rows // size):
        span = slice(block * size, (block + 1) * size)
        base = rows + 16 * block
        lines = total_of(pays, base, base + 16)
        line = lines[0:1] + lines[1:2]
        column = jnp.broadcast_to(line, (size, size)).T
        factor = lax.rsqrt(mean_after[span, 0:1] + EPS)
        pull = column[:, 0:1] * (factor * factor * factor / width)
        dred_parts.append(
            (
                total_of(pays, block * size, (block + 1) * size) - cross_after[span, :] * pull
            ).astype(BF)
        )
        dout[span, :] = (
            carried_after[span, :].astype(F32) - x_after[span, :].astype(F32) * pull
        ).astype(BF)
    dred = dred_parts[0] if len(dred_parts) == 1 else jnp.concatenate(dred_parts, axis=0)
    if with_last:
        last_reduced = total_of(pays, pays[0].shape[0] - rows, pays[0].shape[0]).astype(BF)
        second = dot_tn(last_reduced, cot[...]).astype(BF)
        for side in range(weights.shape[1]):
            grads[side, 0:rank, :] = turn_grads[side, 0:rank, :]
            grads[side, rank : 2 * rank, :] = second[:, side * own : (side + 1) * own]
            grads[side, 2 * rank :, :] = turn_grads[side, 2 * rank :, :]
        split_sides(grads, last_keep, last_send)
    layer_backward(
        dout, dred, x, mean[:, 0:1], mask, weights, weights_before, probs, mixed, reduced[...],
        grads, carried, pay,
    )
    split_sides(grads, keep, send)


def combine_kernel(sections, *refs):
    kept, swapped = refs[:sections], refs[sections : 2 * sections]
    outs, sums = refs[2 * sections : 3 * sections], refs[3 * sections]
    section = lax.axis_index("pipe")
    for layer in range(sections):
        sums[layer] = (kept[layer][...].astype(F32) + swapped[layer][...].astype(F32)).astype(BF)
    for distance in range(sections):
        outs[distance][...] = sums[section ^ distance]


def finish_kernel(sections, *refs):
    parts = refs[:sections]
    gain, first, second = refs[sections:]
    rank = second.shape[1]
    total = parts[0][...].astype(F32)
    for part in parts[1:]:
        total = total + part[...].astype(F32)
    first[0] = total[0:rank].T
    second[0] = total[rank : 2 * rank]
    gain[...] = total[2 * rank : 2 * rank + 1]


def per_device(tokens, cotangents, starts, counts, layer_gains, first_map, second_map):
    sections = lax.axis_size("pipe")
    groups = lax.axis_size("z")
    directions, micro_count, length, width = tokens.shape
    micro_local = -(-directions * micro_count // sections)
    rows = groups * micro_local * length
    local = width // groups
    own = first_map.shape[1]
    rank = first_map.shape[2]
    heads = local // HD
    size = block_size(rows)
    blocks = rows // size
    sides = lax.axis_size("core")
    top = sections - 1

    def shifted(value, shift):
        return lax.ppermute(value, "z", [(i, i ^ shift) for i in range(groups)])

    def across(value, distance):
        return lax.ppermute(value, "pipe", [(i, i ^ distance) for i in range(sections)])

    def swapped(value):
        return lax.ppermute(value, "core", [(i, 1 - i) for i in range(sides)])

    def exchange(pay):
        return [pay] + [shifted(pay, shift) for shift in range(1, groups)]

    token_parts, packed = pack(
        tokens, cotangents, starts, counts, layer_gains, first_map, second_map, groups, micro_local
    )
    mine = [packed] + [across(packed, distance) for distance in range(1, sections)]
    received = [token_parts[0]]
    received += [shifted(token_parts[shift], shift) for shift in range(1, groups)]
    received, mine = lax.optimization_barrier((received, mine))
    theirs = [swapped(part) for part in mine]

    def shaped(shape, kind=BF):
        return jax.ShapeDtypeStruct(shape, kind)

    wide_shape = shaped((rows, local))
    mean_shape = shaped((rows, HD), F32)
    rank_shape = shaped((rows, rank))
    cross_shape = shaped((rows, rank), F32)
    probs_shape = shaped((blocks, heads, size, size))
    grads_shape = (sides, 2 * rank + 16, own)
    half_shape = shaped(grads_shape[1:])
    weights_shape = shaped((sections, sides, slice_rows(own), HD))

    def call(kernel, operands, specs, outs, name, **more):
        return pl.pallas_call(
            kernel,
            grid=(1,),
            in_specs=specs,
            out_specs=vmem_specs(len(outs)),
            out_shape=outs,
            compiler_params=PARAMS,
            name=name,
            **more,
        )(*operands)

    def layer_of(index):
        return layer_spec(weights_shape.shape, index)

    x, cot, mask, mean, mine[0] = call(
        functools.partial(arrange_kernel, length, groups),
        (*received, mine[0]),
        vmem_specs(groups + 1),
        [
            wide_shape,
            wide_shape,
            shaped((blocks, size, size)),
            mean_shape,
            shaped(packed.shape),
        ],
        "arrange",
        scratch_shapes=[pltpu.VMEM((rows, HD), BF)],
    )
    last_gram = gram_place(top - 1, top, rows)
    side_rows = last_gram[0] + last_gram[1]
    probs, mixed, pay, side, weights = call(
        functools.partial(first_kernel, sections),
        (*mine, *theirs, x, cot, mask, mean),
        vmem_specs(2 * sections + 4),
        [
            probs_shape,
            wide_shape,
            shaped((2 * rows + FOLDED, HD)),
            shaped((side_rows, HD)),
            weights_shape,
        ],
        "forward_first",
        scratch_shapes=[pltpu.SemaphoreType.DMA((sections, sides))],
    )
    xs, means, reduceds, crosses = [x], [mean], [], [None]
    all_probs, all_mixed = [probs], [mixed]
    first_pays = pays = exchange(pay)
    arrived = exchange(side)
    for layer in range(1, top):
        operands = (*pays, *((), first_pays, arrived)[min(layer, 3) - 1])
        specs = vmem_specs(len(operands) + 3) + [layer_of(layer - 1), layer_of(layer)]
        x, mean, reduced, cross, probs, mixed, pay = call(
            functools.partial(middle_kernel, groups, layer, top, float(width)),
            (*operands, xs[-1], means[-1], mask, weights, weights),
            specs,
            [
                wide_shape,
                mean_shape,
                rank_shape,
                cross_shape,
                probs_shape,
                wide_shape,
                shaped((2 * rows, HD)),
            ],
            "forward_middle",
        )
        xs.append(x)
        means.append(mean)
        reduceds.append(reduced)
        crosses.append(cross)
        all_probs.append(probs)
        all_mixed.append(mixed)
        pays = exchange(pay)

    back_rows = rows + 16 * blocks
    x, mean, reduced, cross, turn_grads, carried, pay = call(
        functools.partial(turn_kernel, groups, top, float(width)),
        (*pays, *arrived, xs[-1], means[-1], mask, weights, weights, cot),
        vmem_specs(2 * groups + 3) + [layer_of(top - 1), layer_of(top)] + vmem_specs(1),
        [
            wide_shape,
            mean_shape,
            rank_shape,
            cross_shape,
            shaped(grads_shape),
            wide_shape,
            shaped((back_rows + rows, HD)),
        ],
        "turn",
        scratch_shapes=[
            pltpu.VMEM(probs_shape.shape, BF),
            pltpu.VMEM(wide_shape.shape, BF),
        ],
    )
    xs.append(x)
    means.append(mean)
    reduceds.append(reduced)
    crosses.append(cross)

    kept, taken = [None] * sections, [None] * sections
    for layer in range(top - 1, -1, -1):
        pays = exchange(pay)
        with_last = layer == top - 1
        to_first = layer == 0
        operands = (
            *pays, carried, xs[layer + 1], means[layer + 1], crosses[layer + 1],
            xs[layer], means[layer], mask, weights,
        )
        specs = vmem_specs(len(pays) + 7) + [layer_of(layer)]
        if not to_first:
            operands += (weights,)
            specs += [layer_of(layer - 1)]
        operands += (all_probs[layer], all_mixed[layer], reduceds[layer])
        specs += vmem_specs(3)
        outs = [half_shape] * 2
        if with_last:
            operands += (cot, turn_grads)
            specs += vmem_specs(2)
            outs += [half_shape] * 2
        if not to_first:
            outs += [wide_shape, shaped((back_rows, HD))]
        result = call(
            functools.partial(back_kernel, groups, with_last, to_first, float(width)),
            operands,
            specs,
            outs,
            "backward",
            scratch_shapes=[pltpu.VMEM(wide_shape.shape, BF), pltpu.VMEM(grads_shape, BF)],
        )
        kept[layer], taken[layer] = result[0], swapped(result[1])
        if with_last:
            kept[top], taken[top] = result[2], swapped(result[3])
        if not to_first:
            carried, pay = result[-2:]

    parts = call(
        functools.partial(combine_kernel, sections),
        (*kept, *taken),
        vmem_specs(2 * sections),
        [half_shape] * sections,
        "combine",
        scratch_shapes=[pltpu.VMEM((sections,) + grads_shape[1:], BF)],
    )
    arrived = [parts[0]] + [across(parts[distance], distance) for distance in range(1, sections)]
    gain_grad, first_grad, second_grad = call(
        functools.partial(finish_kernel, sections),
        arrived,
        vmem_specs(sections),
        [
            shaped((1, own), F32),
            shaped((1, own, rank), F32),
            shaped((1, rank, own), F32),
        ],
        "finish",
    )
    return (gain_grad, first_grad, second_grad)


def solution(mesh):
    fine = Mesh(
        mesh.devices.reshape(mesh.shape["pipe"], mesh.shape["dp"] // 2, 2), ("pipe", "z", "core")
    )
    data = ("z", "core")
    in_specs = (
        P(None, data, None, None),
        P(None, data, None, None),
        P(None, data, None),
        P(None, data),
        P("pipe", data),
        P("pipe", data, None),
        P("pipe", None, data),
    )
    out_specs = (P("pipe", data), P("pipe", data, None), P("pipe", None, data))
    mapped = jax.shard_map(
        per_device, mesh=fine, in_specs=in_specs, out_specs=out_specs, check_vma=False
    )

    return mapped
```

```python
import functools

import jax
import jax.numpy as jnp
from jax import lax
from jax.experimental import pallas as pl
from jax.experimental.pallas import tpu as pltpu
from jax.sharding import Mesh, PartitionSpec as P

HD = 128
EPS = 1e-05
FOLDED = HD + 16
BF = jnp.bfloat16
F32 = jnp.float32
PARAMS = pltpu.CompilerParams(vmem_limit_bytes=48 * 1024 * 1024)
PACK_PARAMS = pltpu.CompilerParams(vmem_limit_bytes=60 * 1024 * 1024)


def dot(a, b):
    return jnp.dot(a, b, preferred_element_type=F32)


def dot_nt(a, b):
    return lax.dot_general(a, b, (((1,), (1,)), ((), ())), preferred_element_type=F32)


def dot_tn(a, b):
    return lax.dot_general(a, b, (((0,), (0,)), ((), ())), preferred_element_type=F32)


def two_parts(value):
    high = value.astype(BF)
    return high, (value - high.astype(F32)).astype(BF)


def vmem_specs(count):
    return [pl.BlockSpec(memory_space=pltpu.VMEM)] * count


def layer_of(weights, layer):
    return weights.at[pl.ds(layer, 1)]


def slice_rows(own):
    return 2 * own + 16


def pack_kernel(groups, micro_local, *refs):
    tokens, cotangents, starts, counts, gain, first, second = refs[:7]
    parts, weights = refs[7 : 7 + groups], refs[7 + groups]
    tok, cot, starts_in, counts_in, gain_in, second_in, sems = refs[8 + groups :]
    directions, micro_count, length, width = tokens.shape
    local = width // groups
    own = first.shape[1]
    section = lax.axis_index("pipe")
    group = lax.axis_index("z")
    picks = []
    copies = [
        pltpu.make_async_copy(second.at[0], second_in, sems.at[0]),
        pltpu.make_async_copy(gain, gain_in, sems.at[1]),
        pltpu.make_async_copy(first.at[0], weights.at[pl.ds(0, own)], sems.at[2]),
        pltpu.make_async_copy(starts, starts_in, sems.at[3]),
        pltpu.make_async_copy(counts, counts_in, sems.at[4]),
    ]
    for micro in range(micro_local):
        wanted = section * micro_local + micro
        slot = jnp.minimum(wanted, directions * micro_count - 1)
        direction, place = slot // micro_count, slot % micro_count
        picks.append((wanted < directions * micro_count, direction, place))
        rows = pl.ds(micro * length, length)
        copies.append(
            pltpu.make_async_copy(
                tokens.at[direction, place], tok.at[rows], sems.at[5 + 2 * micro]
            )
        )
        copies.append(
            pltpu.make_async_copy(
                cotangents.at[direction, place], cot.at[rows], sems.at[6 + 2 * micro]
            )
        )
    for copy in copies:
        copy.start()
    for copy in copies[:5]:
        copy.wait()
    weights[own : 2 * own, :] = second_in[...].astype(F32).T.astype(BF)
    gains = [gain_in[0:1, head * HD : (head + 1) * HD].astype(F32) for head in range(own // HD)]
    gains.append(jnp.zeros((16 - own // HD, HD), F32))
    weights[2 * own :, :] = jnp.concatenate(gains, axis=0).astype(BF)
    for copy in copies[5:]:
        copy.wait()
    for micro, (keep, direction, place) in enumerate(picks):
        rows = slice(micro * length, (micro + 1) * length)
        widened = tok[rows, :].astype(F32)
        mean = jnp.mean(widened * widened, axis=1, keepdims=True)
        mean_high, mean_low = two_parts(mean)
        position = lax.broadcasted_iota(jnp.int32, (length, HD), 0)
        document = jnp.zeros((length, HD), jnp.int32)
        for entry in range(starts.shape[2]):
            begun = starts_in[direction, place, entry] <= position
            begun = begun & (entry < counts_in[direction, place])
            document = document + begun.astype(jnp.int32)
        lane = lax.broadcasted_iota(jnp.int32, (length, HD), 1)
        tail = jnp.where(
            lane == 0,
            document.astype(F32),
            jnp.where(lane == 1, mean_high.astype(F32), mean_low.astype(F32)),
        ).astype(BF)
        for shift in range(groups):
            start = pl.multiple_of((group ^ shift) * local, local)
            parts[shift][rows, 0:local] = tok[rows, pl.ds(start, local)]
            cotangent = cot[rows, pl.ds(start, local)]
            parts[shift][rows, local : 2 * local] = jnp.where(
                keep, cotangent, jnp.zeros_like(cotangent)
            )
            parts[shift][rows, 2 * local :] = tail


def pack(tokens, cotangents, starts, counts, gain, first, second, groups, micro_local):
    length, width = tokens.shape[2:]
    own = first.shape[1]
    local = width // groups
    rows = micro_local * length
    shape = jax.ShapeDtypeStruct
    results = pl.pallas_call(
        functools.partial(pack_kernel, groups, micro_local),
        in_specs=[pl.BlockSpec(memory_space=pltpu.HBM)] * 7,
        out_specs=vmem_specs(groups + 1),
        out_shape=[shape((rows, 2 * local + HD), BF)] * groups
        + [shape((slice_rows(own), HD), BF)],
        scratch_shapes=[
            pltpu.VMEM((rows, width), BF),
            pltpu.VMEM((rows, width), BF),
            pltpu.SMEM(starts.shape, jnp.int32),
            pltpu.SMEM(counts.shape, jnp.int32),
            pltpu.VMEM(gain.shape, BF),
            pltpu.VMEM(second.shape[1:], BF),
            pltpu.SemaphoreType.DMA((5 + 2 * micro_local,)),
        ],
        compiler_params=PACK_PARAMS,
        name="pack",
    )(tokens, cotangents, starts, counts, gain, first, second)
    return results[:groups], results[groups]


def head_gain(weights, head):
    own = (weights.shape[2] - 16) // 2
    per_slice = own // HD
    row = 2 * own + head % per_slice
    return weights[0, head // per_slice, row : row + 1, :].astype(F32)


def block_size(rows):
    return HD if rows % HD == 0 else rows


def to_rank(value, weights, at):
    own = (weights.shape[2] - 16) // 2
    total = None
    for side in range(weights.shape[1]):
        term = dot(value[:, side * own : (side + 1) * own], weights[0, side, at : at + own, :])
        total = term if total is None else total + term
    return total


def from_rank(value, weights, at, side):
    own = (weights.shape[2] - 16) // 2
    return dot_nt(value, weights[0, side, at : at + own, :])


def gram(weights):
    own = (weights.shape[2] - 16) // 2
    total = None
    for side in range(weights.shape[1]):
        part = weights[0, side, own : 2 * own, :]
        term = dot_tn(part, part)
        total = term if total is None else total + term
    return total


def attend(x, mean, weights, mask, probs, mixed):
    rows, local = x.shape
    size = block_size(rows)
    factor = lax.rsqrt(mean + EPS)
    for block in range(rows // size):
        span = slice(block * size, (block + 1) * size)
        allowed = mask[block] > 0
        for head in range(local // HD):
            part = slice(head * HD, (head + 1) * HD)
            normed = (x[span, part].astype(F32) * factor[span] * head_gain(weights, head)).astype(BF)
            scores = dot_nt(normed, normed) * (1.0 / HD)
            raw = jnp.where(allowed, jnp.exp(scores), 0.0)
            prob = (raw * (1.0 / jnp.sum(raw, axis=1, keepdims=True))).astype(BF)
            probs[block, head] = prob
            mixed[span, part] = dot(prob, normed).astype(BF)


def send_forward(x, weights, mixed, pay):
    rows = x.shape[0]
    own = (weights.shape[2] - 16) // 2
    pay[0:rows, :] = to_rank(mixed[...], weights, 0).astype(BF)
    pay[rows : 2 * rows, :] = to_rank(x[...], weights, own).astype(BF)


def total_of(pays, start, stop):
    total = pays[0][start:stop, :].astype(F32)
    for pay in pays[1:]:
        total = total + pay[start:stop, :].astype(F32)
    return total


def receive_forward(
    pays, gram_total, x_before, mean_before, weights_before, width, x, mean, reduced, cross
):
    rows, local = x_before.shape
    own = (weights_before.shape[2] - 16) // 2
    low_rank = total_of(pays, 0, rows).astype(BF)
    before = total_of(pays, rows, 2 * rows)
    high, low = two_parts(gram_total)
    through = dot(low_rank, high) + dot(low_rank, low)
    wide = low_rank.astype(F32)
    change = jnp.sum(wide * (2.0 * before + through), axis=1, keepdims=True) / width
    new_mean = jnp.maximum(mean_before[:, 0:1] + change, 0.0)
    mean[...] = jnp.broadcast_to(new_mean, mean.shape)
    reduced[...] = low_rank
    cross[...] = before + through
    for side in range(weights_before.shape[1]):
        part = slice(side * own, (side + 1) * own)
        x[:, part] = (
            x_before[:, part].astype(F32) + from_rank(low_rank, weights_before, own, side)
        ).astype(BF)


def arrange_kernel(length, groups, *refs):
    received, packed = refs[:groups], refs[groups]
    x, cot, mask, mean, packed_out, tails = refs[groups + 1 :]
    rows, local = x.shape
    place_rows(received, tails, slice(2 * local, None))
    place_rows(received, x, slice(0, local))
    place_rows(received, cot, slice(local, 2 * local))
    tail = tails[...].astype(F32)
    mean[...] = jnp.broadcast_to(tail[:, 1:2] + tail[:, 2:3], mean.shape)
    build_mask(tail[:, 0:1], mask, block_size(rows), length)
    packed_out[...] = packed[...]


def first_kernel(sections, *refs):
    mine, theirs = refs[:sections], refs[sections : 2 * sections]
    x, cot, mask, mean, probs, mixed, pay, side, weights, sems = refs[2 * sections :]
    section, core = lax.axis_index("pipe"), lax.axis_index("core")
    rows = x.shape[0]
    copies = []
    for distance in range(sections):
        layer = section ^ distance
        for parts, place in ((mine, core), (theirs, 1 - core)):
            copies.append(
                pltpu.make_async_copy(
                    parts[distance], weights.at[layer, place], sems.at[layer, place]
                )
            )
    for wanted_now in (True, False):
        for distance in range(sections):

            @pl.when((section == distance) == wanted_now)
            def _(distance=distance):
                copies[2 * distance].start()
                copies[2 * distance + 1].start()

    def arrived(layer):
        for place in range(weights.shape[1]):
            pltpu.make_async_copy(mine[0], weights.at[layer, place], sems.at[layer, place]).wait()

    arrived(0)
    own = (weights.shape[2] - 16) // 2
    layers = [layer_of(weights, layer) for layer in range(sections)]
    attend(x, mean[:, 0:1], layers[0], mask, probs, mixed)
    send_forward(x, layers[0], mixed, pay)
    arrived(1)
    pay[2 * rows :, :] = fold_grams(layers[0], layers[1])
    for layer in range(2, sections):
        arrived(layer)
    side[0:rows, :] = to_rank(cot[...], layers[-1], own).astype(BF)
    for layer in range(2, sections - 1, 2):
        base, height, folded = gram_place(layer, sections - 1, rows)
        both = fold_grams(layers[layer], layers[layer + 1]) if folded else gram(layers[layer])
        side[base : base + height, :] = both.astype(BF)


def place_rows(received, target, columns):
    rows = received[0].shape[0]
    for shift, part in enumerate(received):
        source = lax.axis_index("z") ^ shift
        target[pl.ds(pl.multiple_of(source * rows, rows), rows), :] = part[:, columns]


def build_mask(document, mask, size, length):
    query = lax.broadcasted_iota(jnp.int32, (size, size), 0)
    key = lax.broadcasted_iota(jnp.int32, (size, size), 1)
    for block in range(mask.shape[0]):
        by_query = jnp.broadcast_to(document[block * size : (block + 1) * size], (size, size))
        by_key = by_query.T
        allowed = (by_query == by_key) & (key <= query) & (query // length == key // length)
        mask[block] = allowed.astype(F32).astype(BF)


def fold_grams(weights, other):
    row, lane = square_places()
    upper, lower = gram(weights), gram(other)
    diagonal = jnp.sum(jnp.where(row == lane, lower, 0.0), axis=0, keepdims=True)
    folded = jnp.where(row <= lane, upper, lower)
    return jnp.concatenate((folded, diagonal, jnp.zeros((15, HD), F32)), axis=0).astype(BF)


def square_places():
    return (
        lax.broadcasted_iota(jnp.int32, (HD, HD), 0),
        lax.broadcasted_iota(jnp.int32, (HD, HD), 1),
    )


def gram_place(layer, top, rows):
    pair = layer // 2
    folded = 2 * pair + 1 < top
    base = 2 * rows if pair == 0 else rows + FOLDED * (pair - 1)
    return base, FOLDED if folded else HD, folded


def gram_of(sources, layer, top, rows):
    base, height, folded = gram_place(layer, top, rows)
    total = total_of(sources, base, base + height)
    if not folded:
        return total
    row, lane = square_places()
    square = total[0:HD]
    if layer % 2 == 0:
        return jnp.where(row <= lane, square, square.T)
    lower = jnp.where(row > lane, square, square.T)
    return jnp.where(row == lane, total[HD : HD + 1], lower)


def middle_kernel(count, layer, top, width, *refs):
    pays, sources, refs = refs[:count], refs[count : 2 * count], refs[2 * count :]
    if layer == 1:
        sources, refs = pays, sources + refs
    x_before, mean_before, mask, weights = refs[:4]
    x, mean, reduced, cross, probs, mixed, pay = refs[4:]
    weights_before, weights = layer_of(weights, layer - 1), layer_of(weights, layer)
    receive_forward(
        pays, gram_of(sources, layer - 1, top, x.shape[0]), x_before, mean_before, weights_before,
        width, x, mean, reduced, cross,
    )
    attend(x, mean[:, 0:1], weights, mask, probs, mixed)
    send_forward(x, weights, mixed, pay)


def layer_backward(
    dout, dred, x, mean, mask, weights, weights_before, probs, mixed, reduced, grads, carried, pay
):
    rows, local = x.shape
    size = block_size(rows)
    own = (weights.shape[2] - 16) // 2
    per_slice = own // HD
    rank = dred.shape[1]
    factor = lax.rsqrt(mean + EPS)
    first = dot_tn(dred, mixed[...]).astype(BF)
    for side in range(weights.shape[1]):
        grads[side, 0:rank, :] = first[:, side * own : (side + 1) * own]
    if reduced is not None:
        second = dot_tn(reduced, dout[...]).astype(BF)
        for side in range(weights.shape[1]):
            grads[side, rank : 2 * rank, :] = second[:, side * own : (side + 1) * own]
    back_mixed = [
        from_rank(dred, weights, 0, side).astype(BF) for side in range(weights.shape[1])
    ]
    gain_sums = [None] * (local // HD)
    for block in range(rows // size):
        span = slice(block * size, (block + 1) * size)
        scale = factor[span]
        norm_dot = jnp.zeros((size, HD), F32)
        for head in range(local // HD):
            part = slice(head * HD, (head + 1) * HD)
            side, inner = head // per_slice, (head % per_slice) * HD
            wide = x[span, part].astype(F32)
            gain = head_gain(weights, head)
            unit = wide * scale
            normed = (unit * gain).astype(BF)
            prob = probs[block, head]
            upstream = back_mixed[side][span, inner : inner + HD]
            back_prob = dot_nt(upstream, normed)
            prob_wide = prob.astype(F32)
            inner_sum = jnp.sum(back_prob * prob_wide, axis=1, keepdims=True)
            back_score = prob_wide * (back_prob - inner_sum) * (1.0 / HD)
            both = (back_score + back_score.T).astype(BF)
            back_normed = (dot_tn(prob, upstream) + dot(both, normed)).astype(BF).astype(F32)
            term = jnp.sum(back_normed * unit, axis=0, keepdims=True)
            gain_sums[head] = term if gain_sums[head] is None else gain_sums[head] + term
            if carried is not None:
                scaled = back_normed * gain
                norm_dot = norm_dot + scaled * wide
                carried[span, part] = (dout[span, part].astype(F32) + scaled * scale).astype(BF)
        if carried is not None:
            column = jnp.broadcast_to(jnp.sum(norm_dot, axis=1, keepdims=True), (size, size))
            line = column.T[0:1, :]
            high, low = two_parts(line)
            base = rows + 16 * block
            pay[base : base + 16, :] = jnp.concatenate(
                (high.astype(F32), low.astype(F32), jnp.zeros((14, size), F32)), axis=0
            ).astype(BF)
    zeros = jnp.zeros((15, HD), F32)
    for head in range(local // HD):
        side, inner = head // per_slice, (head % per_slice) * HD
        grads[side, 2 * rank : 2 * rank + 16, inner : inner + HD] = jnp.concatenate(
            (gain_sums[head], zeros), axis=0
        ).astype(BF)
    if carried is not None:
        pay[0:rows, :] = to_rank(carried[...], weights_before, own).astype(BF)


def turn_kernel(count, layer, width, *refs):
    pays, sides, refs = refs[:count], refs[count : 2 * count], refs[2 * count :]
    x_before, mean_before, mask, weights, cot = refs[:5]
    x, mean, reduced, cross, grads, carried, pay = refs[5:12]
    probs, mixed = refs[12:]
    rows = x.shape[0]
    weights_before, weights = layer_of(weights, layer - 1), layer_of(weights, layer)
    receive_forward(
        pays, gram_of(sides, layer - 1, layer, rows), x_before, mean_before, weights_before,
        width, x, mean, reduced, cross,
    )
    attend(x, mean[:, 0:1], weights, mask, probs, mixed)
    pay[pay.shape[0] - rows :, :] = to_rank(mixed[...], weights, 0).astype(BF)
    dred = total_of(sides, 0, rows).astype(BF)
    layer_backward(
        cot, dred, x, mean[:, 0:1], mask, weights, weights_before, probs, mixed, None, grads,
        carried, pay,
    )


def split_sides(grads, keep, send):
    core = lax.axis_index("core")
    keep[...] = grads[core]
    send[...] = grads[1 - core]


def back_kernel(count, with_last, layer, width, *refs):
    pays, refs = refs[:count], refs[count:]
    carried_after, x_after, mean_after, cross_after = refs[:4]
    x, mean, mask, weights = refs[4:8]
    refs = refs[8:]
    weights_before = carried = pay = None
    if layer:
        weights_before = layer_of(weights, layer - 1)
    weights = layer_of(weights, layer)
    probs, mixed, reduced = refs[:3]
    refs = refs[3:]
    if with_last:
        cot, turn_grads = refs[:2]
        refs = refs[2:]
    keep, send = refs[:2]
    refs = refs[2:]
    if with_last:
        last_keep, last_send = refs[:2]
        refs = refs[2:]
    if layer:
        carried, pay = refs[:2]
        refs = refs[2:]
    dout, grads = refs
    rows, local = x.shape
    size = block_size(rows)
    own = (weights.shape[2] - 16) // 2
    rank = reduced.shape[1]
    dred_parts = []
    for block in range(rows // size):
        span = slice(block * size, (block + 1) * size)
        base = rows + 16 * block
        lines = total_of(pays, base, base + 16)
        line = lines[0:1] + lines[1:2]
        column = jnp.broadcast_to(line, (size, size)).T
        factor = lax.rsqrt(mean_after[span, 0:1] + EPS)
        pull = column[:, 0:1] * (factor * factor * factor / width)
        dred_parts.append(
            (
                total_of(pays, block * size, (block + 1) * size) - cross_after[span, :] * pull
            ).astype(BF)
        )
        dout[span, :] = (
            carried_after[span, :].astype(F32) - x_after[span, :].astype(F32) * pull
        ).astype(BF)
    dred = dred_parts[0] if len(dred_parts) == 1 else jnp.concatenate(dred_parts, axis=0)
    if with_last:
        last_reduced = total_of(pays, pays[0].shape[0] - rows, pays[0].shape[0]).astype(BF)
        second = dot_tn(last_reduced, cot[...]).astype(BF)
        for side in range(weights.shape[1]):
            grads[side, 0:rank, :] = turn_grads[side, 0:rank, :]
            grads[side, rank : 2 * rank, :] = second[:, side * own : (side + 1) * own]
            grads[side, 2 * rank :, :] = turn_grads[side, 2 * rank :, :]
        split_sides(grads, last_keep, last_send)
    layer_backward(
        dout, dred, x, mean[:, 0:1], mask, weights, weights_before, probs, mixed, reduced[...],
        grads, carried, pay,
    )
    split_sides(grads, keep, send)


def combine_kernel(sections, *refs):
    kept, swapped = refs[:sections], refs[sections : 2 * sections]
    outs, sums = refs[2 * sections : 3 * sections], refs[3 * sections]
    section = lax.axis_index("pipe")
    for layer in range(sections):
        sums[layer] = (kept[layer][...].astype(F32) + swapped[layer][...].astype(F32)).astype(BF)
    for distance in range(sections):
        outs[distance][...] = sums[section ^ distance]


def finish_kernel(sections, *refs):
    parts = refs[:sections]
    gain, first, second = refs[sections:]
    rank = second.shape[1]
    total = parts[0][...].astype(F32)
    for part in parts[1:]:
        total = total + part[...].astype(F32)
    first[0] = total[0:rank].T
    second[0] = total[rank : 2 * rank]
    gain[...] = total[2 * rank : 2 * rank + 1]


def per_device(tokens, cotangents, starts, counts, layer_gains, first_map, second_map):
    sections = lax.axis_size("pipe")
    groups = lax.axis_size("z")
    directions, micro_count, length, width = tokens.shape
    micro_local = -(-directions * micro_count // sections)
    rows = groups * micro_local * length
    local = width // groups
    own = first_map.shape[1]
    rank = first_map.shape[2]
    heads = local // HD
    size = block_size(rows)
    blocks = rows // size
    sides = lax.axis_size("core")
    top = sections - 1

    def shifted(value, shift):
        return lax.ppermute(value, "z", [(i, i ^ shift) for i in range(groups)])

    def across(value, distance):
        return lax.ppermute(value, "pipe", [(i, i ^ distance) for i in range(sections)])

    def swapped(value):
        return lax.ppermute(value, "core", [(i, 1 - i) for i in range(sides)])

    def exchange(pay):
        return [pay] + [shifted(pay, shift) for shift in range(1, groups)]

    token_parts, packed = pack(
        tokens, cotangents, starts, counts, layer_gains, first_map, second_map, groups, micro_local
    )
    mine = [packed] + [across(packed, distance) for distance in range(1, sections)]
    received = [token_parts[0]]
    received += [shifted(token_parts[shift], shift) for shift in range(1, groups)]
    received, mine = lax.optimization_barrier((received, mine))
    theirs = [swapped(part) for part in mine]

    def shaped(shape, kind=BF):
        return jax.ShapeDtypeStruct(shape, kind)

    wide_shape = shaped((rows, local))
    mean_shape = shaped((rows, HD), F32)
    rank_shape = shaped((rows, rank))
    cross_shape = shaped((rows, rank), F32)
    probs_shape = shaped((blocks, heads, size, size))
    grads_shape = (sides, 2 * rank + 16, own)
    half_shape = shaped(grads_shape[1:])
    weights_shape = shaped((sections, sides, slice_rows(own), HD))

    def call(kernel, operands, specs, outs, name, **more):
        return pl.pallas_call(
            kernel,
            in_specs=specs,
            out_specs=vmem_specs(len(outs)),
            out_shape=outs,
            compiler_params=PARAMS,
            name=name,
            **more,
        )(*operands)

    x, cot, mask, mean, mine[0] = call(
        functools.partial(arrange_kernel, length, groups),
        (*received, mine[0]),
        vmem_specs(groups + 1),
        [
            wide_shape,
            wide_shape,
            shaped((blocks, size, size)),
            mean_shape,
            shaped(packed.shape),
        ],
        "arrange",
        scratch_shapes=[pltpu.VMEM((rows, HD), BF)],
    )
    last_gram = gram_place(top - 1, top, rows)
    side_rows = last_gram[0] + last_gram[1]
    probs, mixed, pay, side, weights = call(
        functools.partial(first_kernel, sections),
        (*mine, *theirs, x, cot, mask, mean),
        vmem_specs(2 * sections + 4),
        [
            probs_shape,
            wide_shape,
            shaped((2 * rows + FOLDED, HD)),
            shaped((side_rows, HD)),
            weights_shape,
        ],
        "forward_first",
        scratch_shapes=[pltpu.SemaphoreType.DMA((sections, sides))],
    )
    xs, means, reduceds, crosses = [x], [mean], [], [None]
    all_probs, all_mixed = [probs], [mixed]
    first_pays = pays = exchange(pay)
    arrived = exchange(side)
    for layer in range(1, top):
        operands = (*pays, *((), first_pays, arrived)[min(layer, 3) - 1])
        specs = vmem_specs(len(operands) + 4)
        x, mean, reduced, cross, probs, mixed, pay = call(
            functools.partial(middle_kernel, groups, layer, top, float(width)),
            (*operands, xs[-1], means[-1], mask, weights),
            specs,
            [
                wide_shape,
                mean_shape,
                rank_shape,
                cross_shape,
                probs_shape,
                wide_shape,
                shaped((2 * rows, HD)),
            ],
            "forward_middle",
        )
        xs.append(x)
        means.append(mean)
        reduceds.append(reduced)
        crosses.append(cross)
        all_probs.append(probs)
        all_mixed.append(mixed)
        pays = exchange(pay)

    back_rows = rows + 16 * blocks
    x, mean, reduced, cross, turn_grads, carried, pay = call(
        functools.partial(turn_kernel, groups, top, float(width)),
        (*pays, *arrived, xs[-1], means[-1], mask, weights, cot),
        vmem_specs(2 * groups + 5),
        [
            wide_shape,
            mean_shape,
            rank_shape,
            cross_shape,
            shaped(grads_shape),
            wide_shape,
            shaped((back_rows + rows, HD)),
        ],
        "turn",
        scratch_shapes=[
            pltpu.VMEM(probs_shape.shape, BF),
            pltpu.VMEM(wide_shape.shape, BF),
        ],
    )
    xs.append(x)
    means.append(mean)
    reduceds.append(reduced)
    crosses.append(cross)

    kept, taken = [None] * sections, [None] * sections
    for layer in range(top - 1, -1, -1):
        pays = exchange(pay)
        with_last = layer == top - 1
        to_first = layer == 0
        operands = (
            *pays, carried, xs[layer + 1], means[layer + 1], crosses[layer + 1],
            xs[layer], means[layer], mask, weights,
        )
        operands += (all_probs[layer], all_mixed[layer], reduceds[layer])
        outs = [half_shape] * 2
        if with_last:
            operands += (cot, turn_grads)
            outs += [half_shape] * 2
        if not to_first:
            outs += [wide_shape, shaped((back_rows, HD))]
        result = call(
            functools.partial(back_kernel, groups, with_last, layer, float(width)),
            operands,
            vmem_specs(len(operands)),
            outs,
            "backward",
            scratch_shapes=[pltpu.VMEM(wide_shape.shape, BF), pltpu.VMEM(grads_shape, BF)],
        )
        kept[layer], taken[layer] = result[0], swapped(result[1])
        if with_last:
            kept[top], taken[top] = result[2], swapped(result[3])
        if not to_first:
            carried, pay = result[-2:]

    parts = call(
        functools.partial(combine_kernel, sections),
        (*kept, *taken),
        vmem_specs(2 * sections),
        [half_shape] * sections,
        "combine",
        scratch_shapes=[pltpu.VMEM((sections,) + grads_shape[1:], BF)],
    )
    arrived = [parts[0]] + [across(parts[distance], distance) for distance in range(1, sections)]
    gain_grad, first_grad, second_grad = call(
        functools.partial(finish_kernel, sections),
        arrived,
        vmem_specs(sections),
        [
            shaped((1, own), F32),
            shaped((1, own, rank), F32),
            shaped((1, rank, own), F32),
        ],
        "finish",
    )
    return (gain_grad, first_grad, second_grad)


def solution(mesh):
    fine = Mesh(
        mesh.devices.reshape(mesh.shape["pipe"], mesh.shape["dp"] // 2, 2), ("pipe", "z", "core")
    )
    data = ("z", "core")
    in_specs = (
        P(None, data, None, None),
        P(None, data, None, None),
        P(None, data, None),
        P(None, data),
        P("pipe", data),
        P("pipe", data, None),
        P("pipe", None, data),
    )
    out_specs = (P("pipe", data), P("pipe", data, None), P("pipe", None, data))
    mapped = jax.shard_map(
        per_device, mesh=fine, in_specs=in_specs, out_specs=out_specs, check_vma=False
    )

    return mapped
```

```python
import functools

import jax
import jax.numpy as jnp
from jax import lax
from jax.experimental import pallas as pl
from jax.experimental.pallas import tpu as pltpu
from jax.sharding import Mesh, PartitionSpec as P

HD = 128
EPS = 1e-05
FOLDED = HD + 16
BF = jnp.bfloat16
F32 = jnp.float32
PARAMS = pltpu.CompilerParams(vmem_limit_bytes=48 * 1024 * 1024)
PACK_PARAMS = pltpu.CompilerParams(vmem_limit_bytes=60 * 1024 * 1024)


def dot(a, b):
    return jnp.dot(a, b, preferred_element_type=F32)


def dot_nt(a, b):
    return lax.dot_general(a, b, (((1,), (1,)), ((), ())), preferred_element_type=F32)


def dot_tn(a, b):
    return lax.dot_general(a, b, (((0,), (0,)), ((), ())), preferred_element_type=F32)


def two_parts(value):
    high = value.astype(BF)
    return high, (value - high.astype(F32)).astype(BF)


def vmem_specs(count):
    return [pl.BlockSpec(memory_space=pltpu.VMEM)] * count


def layer_of(weights, layer):
    return weights.at[pl.ds(layer, 1)]


def slice_rows(own):
    return 2 * own + 16


def pack_kernel(groups, micro_local, *refs):
    tokens, cotangents, starts, counts, gain, first, second = refs[:7]
    parts, weights = refs[7 : 7 + groups], refs[7 + groups]
    tok, cot, starts_in, counts_in, gain_in, second_in, sems = refs[8 + groups :]
    directions, micro_count, length, width = tokens.shape
    local = width // groups
    own = first.shape[1]
    section = lax.axis_index("pipe")
    group = lax.axis_index("z")
    picks = []
    copies = [
        pltpu.make_async_copy(second.at[0], second_in, sems.at[0]),
        pltpu.make_async_copy(gain, gain_in, sems.at[1]),
        pltpu.make_async_copy(first.at[0], weights.at[pl.ds(0, own)], sems.at[2]),
        pltpu.make_async_copy(starts, starts_in, sems.at[3]),
        pltpu.make_async_copy(counts, counts_in, sems.at[4]),
    ]
    for micro in range(micro_local):
        wanted = section * micro_local + micro
        slot = jnp.minimum(wanted, directions * micro_count - 1)
        direction, place = slot // micro_count, slot % micro_count
        picks.append((wanted < directions * micro_count, direction, place))
        rows = pl.ds(micro * length, length)
        copies.append(
            pltpu.make_async_copy(
                tokens.at[direction, place], tok.at[rows], sems.at[5 + 2 * micro]
            )
        )
        copies.append(
            pltpu.make_async_copy(
                cotangents.at[direction, place], cot.at[rows], sems.at[6 + 2 * micro]
            )
        )
    for copy in copies:
        copy.start()
    for copy in copies[:5]:
        copy.wait()
    weights[own : 2 * own, :] = second_in[...].astype(F32).T.astype(BF)
    gains = [gain_in[0:1, head * HD : (head + 1) * HD].astype(F32) for head in range(own // HD)]
    gains.append(jnp.zeros((16 - own // HD, HD), F32))
    weights[2 * own :, :] = jnp.concatenate(gains, axis=0).astype(BF)
    for copy in copies[5:]:
        copy.wait()
    for micro, (keep, direction, place) in enumerate(picks):
        rows = slice(micro * length, (micro + 1) * length)
        widened = tok[rows, :].astype(F32)
        mean = jnp.mean(widened * widened, axis=1, keepdims=True)
        mean_high, mean_low = two_parts(mean)
        position = lax.broadcasted_iota(jnp.int32, (length, HD), 0)
        document = jnp.zeros((length, HD), jnp.int32)
        for entry in range(starts.shape[2]):
            begun = starts_in[direction, place, entry] <= position
            begun = begun & (entry < counts_in[direction, place])
            document = document + begun.astype(jnp.int32)
        lane = lax.broadcasted_iota(jnp.int32, (length, HD), 1)
        tail = jnp.where(
            lane == 0,
            document.astype(F32),
            jnp.where(lane == 1, mean_high.astype(F32), mean_low.astype(F32)),
        ).astype(BF)
        for shift in range(groups):
            start = pl.multiple_of((group ^ shift) * local, local)
            parts[shift][rows, 0:local] = tok[rows, pl.ds(start, local)]
            cotangent = cot[rows, pl.ds(start, local)]
            parts[shift][rows, local : 2 * local] = jnp.where(
                keep, cotangent, jnp.zeros_like(cotangent)
            )
            parts[shift][rows, 2 * local :] = tail


def pack(tokens, cotangents, starts, counts, gain, first, second, groups, micro_local):
    length, width = tokens.shape[2:]
    own = first.shape[1]
    local = width // groups
    rows = micro_local * length
    shape = jax.ShapeDtypeStruct
    results = pl.pallas_call(
        functools.partial(pack_kernel, groups, micro_local),
        in_specs=[pl.BlockSpec(memory_space=pltpu.HBM)] * 7,
        out_specs=vmem_specs(groups + 1),
        out_shape=[shape((rows, 2 * local + HD), BF)] * groups
        + [shape((slice_rows(own), HD), BF)],
        scratch_shapes=[
            pltpu.VMEM((rows, width), BF),
            pltpu.VMEM((rows, width), BF),
            pltpu.SMEM(starts.shape, jnp.int32),
            pltpu.SMEM(counts.shape, jnp.int32),
            pltpu.VMEM(gain.shape, BF),
            pltpu.VMEM(second.shape[1:], BF),
            pltpu.SemaphoreType.DMA((5 + 2 * micro_local,)),
        ],
        compiler_params=PACK_PARAMS,
        name="pack",
    )(tokens, cotangents, starts, counts, gain, first, second)
    return results[:groups], results[groups]


def head_gain(weights, head):
    own = (weights.shape[2] - 16) // 2
    per_slice = own // HD
    row = 2 * own + head % per_slice
    return weights[0, head // per_slice, row : row + 1, :].astype(F32)


def block_size(rows):
    return HD if rows % HD == 0 else rows


def to_rank(value, weights, at):
    own = (weights.shape[2] - 16) // 2
    total = None
    for side in range(weights.shape[1]):
        term = dot(value[:, side * own : (side + 1) * own], weights[0, side, at : at + own, :])
        total = term if total is None else total + term
    return total


def from_rank(value, weights, at, side):
    own = (weights.shape[2] - 16) // 2
    return dot_nt(value, weights[0, side, at : at + own, :])


def gram(weights):
    own = (weights.shape[2] - 16) // 2
    total = None
    for side in range(weights.shape[1]):
        part = weights[0, side, own : 2 * own, :]
        term = dot_tn(part, part)
        total = term if total is None else total + term
    return total


def attend(x, mean, weights, mask, probs, mixed):
    rows, local = x.shape
    size = block_size(rows)
    factor = lax.rsqrt(mean + EPS)
    heads = range(local // HD)
    gains = [head_gain(weights, head) for head in heads]
    for block in range(rows // size):
        span = slice(block * size, (block + 1) * size)
        allowed = mask[block] > 0
        wide = x[span, :].astype(F32) * factor[span]
        normed = [(wide[:, head * HD : (head + 1) * HD] * gains[head]).astype(BF) for head in heads]
        scores = [dot_nt(value, value) for value in normed]
        raw = [jnp.where(allowed, jnp.exp(score * (1.0 / HD)), 0.0) for score in scores]
        shares = [1.0 / jnp.sum(value, axis=1, keepdims=True) for value in raw]
        prob = [(value * share).astype(BF) for value, share in zip(raw, shares)]
        result = [dot(left, right).astype(BF) for left, right in zip(prob, normed)]
        for head in heads:
            probs[block, head] = prob[head]
            mixed[span, head * HD : (head + 1) * HD] = result[head]


def send_forward(x, weights, mixed, pay):
    rows = x.shape[0]
    own = (weights.shape[2] - 16) // 2
    pay[0:rows, :] = to_rank(mixed[...], weights, 0).astype(BF)
    pay[rows : 2 * rows, :] = to_rank(x[...], weights, own).astype(BF)


def total_of(pays, start, stop):
    total = pays[0][start:stop, :].astype(F32)
    for pay in pays[1:]:
        total = total + pay[start:stop, :].astype(F32)
    return total


def receive_forward(
    pays, gram_total, x_before, mean_before, weights_before, width, x, mean, reduced, cross
):
    rows, local = x_before.shape
    own = (weights_before.shape[2] - 16) // 2
    low_rank = total_of(pays, 0, rows).astype(BF)
    before = total_of(pays, rows, 2 * rows)
    high, low = two_parts(gram_total)
    through = dot(low_rank, high) + dot(low_rank, low)
    wide = low_rank.astype(F32)
    change = jnp.sum(wide * (2.0 * before + through), axis=1, keepdims=True) / width
    new_mean = jnp.maximum(mean_before[:, 0:1] + change, 0.0)
    mean[...] = jnp.broadcast_to(new_mean, mean.shape)
    reduced[...] = low_rank
    cross[...] = before + through
    for side in range(weights_before.shape[1]):
        part = slice(side * own, (side + 1) * own)
        x[:, part] = (
            x_before[:, part].astype(F32) + from_rank(low_rank, weights_before, own, side)
        ).astype(BF)


def arrange_kernel(length, groups, *refs):
    received, packed = refs[:groups], refs[groups]
    x, cot, mask, mean, packed_out, tails = refs[groups + 1 :]
    rows, local = x.shape
    place_rows(received, tails, slice(2 * local, None))
    place_rows(received, x, slice(0, local))
    place_rows(received, cot, slice(local, 2 * local))
    tail = tails[...].astype(F32)
    mean[...] = jnp.broadcast_to(tail[:, 1:2] + tail[:, 2:3], mean.shape)
    build_mask(tail[:, 0:1], mask, block_size(rows), length)
    packed_out[...] = packed[...]


def first_kernel(sections, *refs):
    mine, theirs = refs[:sections], refs[sections : 2 * sections]
    x, cot, mask, mean, probs, mixed, pay, side, weights, sems = refs[2 * sections :]
    section, core = lax.axis_index("pipe"), lax.axis_index("core")
    rows = x.shape[0]
    copies = []
    for distance in range(sections):
        layer = section ^ distance
        for parts, place in ((mine, core), (theirs, 1 - core)):
            copies.append(
                pltpu.make_async_copy(
                    parts[distance], weights.at[layer, place], sems.at[layer, place]
                )
            )
    for wanted_now in (True, False):
        for distance in range(sections):

            @pl.when((section == distance) == wanted_now)
            def _(distance=distance):
                copies[2 * distance].start()
                copies[2 * distance + 1].start()

    def arrived(layer):
        for place in range(weights.shape[1]):
            pltpu.make_async_copy(mine[0], weights.at[layer, place], sems.at[layer, place]).wait()

    arrived(0)
    own = (weights.shape[2] - 16) // 2
    layers = [layer_of(weights, layer) for layer in range(sections)]
    attend(x, mean[:, 0:1], layers[0], mask, probs, mixed)
    send_forward(x, layers[0], mixed, pay)
    arrived(1)
    pay[2 * rows :, :] = fold_grams(layers[0], layers[1])
    for layer in range(2, sections):
        arrived(layer)
    side[0:rows, :] = to_rank(cot[...], layers[-1], own).astype(BF)
    for layer in range(2, sections - 1, 2):
        base, height, folded = gram_place(layer, sections - 1, rows)
        both = fold_grams(layers[layer], layers[layer + 1]) if folded else gram(layers[layer])
        side[base : base + height, :] = both.astype(BF)


def place_rows(received, target, columns):
    rows = received[0].shape[0]
    for shift, part in enumerate(received):
        source = lax.axis_index("z") ^ shift
        target[pl.ds(pl.multiple_of(source * rows, rows), rows), :] = part[:, columns]


def build_mask(document, mask, size, length):
    query = lax.broadcasted_iota(jnp.int32, (size, size), 0)
    key = lax.broadcasted_iota(jnp.int32, (size, size), 1)
    for block in range(mask.shape[0]):
        by_query = jnp.broadcast_to(document[block * size : (block + 1) * size], (size, size))
        by_key = by_query.T
        allowed = (by_query == by_key) & (key <= query) & (query // length == key // length)
        mask[block] = allowed.astype(F32).astype(BF)


def fold_grams(weights, other):
    row, lane = square_places()
    upper, lower = gram(weights), gram(other)
    diagonal = jnp.sum(jnp.where(row == lane, lower, 0.0), axis=0, keepdims=True)
    folded = jnp.where(row <= lane, upper, lower)
    return jnp.concatenate((folded, diagonal, jnp.zeros((15, HD), F32)), axis=0).astype(BF)


def square_places():
    return (
        lax.broadcasted_iota(jnp.int32, (HD, HD), 0),
        lax.broadcasted_iota(jnp.int32, (HD, HD), 1),
    )


def gram_place(layer, top, rows):
    pair = layer // 2
    folded = 2 * pair + 1 < top
    base = 2 * rows if pair == 0 else rows + FOLDED * (pair - 1)
    return base, FOLDED if folded else HD, folded


def gram_of(sources, layer, top, rows):
    base, height, folded = gram_place(layer, top, rows)
    total = total_of(sources, base, base + height)
    if not folded:
        return total
    row, lane = square_places()
    square = total[0:HD]
    if layer % 2 == 0:
        return jnp.where(row <= lane, square, square.T)
    lower = jnp.where(row > lane, square, square.T)
    return jnp.where(row == lane, total[HD : HD + 1], lower)


def middle_kernel(count, layer, top, width, *refs):
    pays, sources, refs = refs[:count], refs[count : 2 * count], refs[2 * count :]
    if layer == 1:
        sources, refs = pays, sources + refs
    x_before, mean_before, mask, weights = refs[:4]
    x, mean, reduced, cross, probs, mixed, pay = refs[4:]
    weights_before, weights = layer_of(weights, layer - 1), layer_of(weights, layer)
    receive_forward(
        pays, gram_of(sources, layer - 1, top, x.shape[0]), x_before, mean_before, weights_before,
        width, x, mean, reduced, cross,
    )
    attend(x, mean[:, 0:1], weights, mask, probs, mixed)
    send_forward(x, weights, mixed, pay)


def layer_backward(
    dout, dred, x, mean, mask, weights, weights_before, probs, mixed, reduced, grads, carried, pay
):
    rows, local = x.shape
    size = block_size(rows)
    own = (weights.shape[2] - 16) // 2
    per_slice = own // HD
    rank = dred.shape[1]
    factor = lax.rsqrt(mean + EPS)
    first = dot_tn(dred, mixed[...]).astype(BF)
    for side in range(weights.shape[1]):
        grads[side, 0:rank, :] = first[:, side * own : (side + 1) * own]
    if reduced is not None:
        second = dot_tn(reduced, dout[...]).astype(BF)
        for side in range(weights.shape[1]):
            grads[side, rank : 2 * rank, :] = second[:, side * own : (side + 1) * own]
    back_mixed = [
        from_rank(dred, weights, 0, side).astype(BF) for side in range(weights.shape[1])
    ]
    heads = range(local // HD)
    gains = [head_gain(weights, head) for head in heads]
    gain_sums = [None] * len(heads)
    for block in range(rows // size):
        span = slice(block * size, (block + 1) * size)
        scale = factor[span]
        parts = [slice(head * HD, (head + 1) * HD) for head in heads]
        wide = [x[span, part].astype(F32) for part in parts]
        prob = [probs[block, head] for head in heads]
        onward = [None if carried is None else dout[span, part].astype(F32) for part in parts]
        unit = [value * scale for value in wide]
        normed = [(value * gain).astype(BF) for value, gain in zip(unit, gains)]
        upstream = []
        for head in heads:
            inner = (head % per_slice) * HD
            upstream.append(back_mixed[head // per_slice][span, inner : inner + HD])
        back_prob = [dot_nt(left, right) for left, right in zip(upstream, normed)]
        through = [dot_tn(left, right) for left, right in zip(prob, upstream)]
        both = []
        for head in heads:
            prob_wide = prob[head].astype(F32)
            inner_sum = jnp.sum(back_prob[head] * prob_wide, axis=1, keepdims=True)
            back_score = prob_wide * (back_prob[head] - inner_sum) * (1.0 / HD)
            both.append((back_score + back_score.T).astype(BF))
        back_normed = [
            (through[head] + dot(both[head], normed[head])).astype(BF).astype(F32) for head in heads
        ]
        norm_dot = jnp.zeros((size, HD), F32)
        for head in heads:
            term = jnp.sum(back_normed[head] * unit[head], axis=0, keepdims=True)
            gain_sums[head] = term if gain_sums[head] is None else gain_sums[head] + term
            if carried is not None:
                scaled = back_normed[head] * gains[head]
                norm_dot = norm_dot + scaled * wide[head]
                carried[span, parts[head]] = (onward[head] + scaled * scale).astype(BF)
        if carried is not None:
            column = jnp.broadcast_to(jnp.sum(norm_dot, axis=1, keepdims=True), (size, size))
            line = column.T[0:1, :]
            high, low = two_parts(line)
            base = rows + 16 * block
            pay[base : base + 16, :] = jnp.concatenate(
                (high.astype(F32), low.astype(F32), jnp.zeros((14, size), F32)), axis=0
            ).astype(BF)
    zeros = jnp.zeros((15, HD), F32)
    for head in range(local // HD):
        side, inner = head // per_slice, (head % per_slice) * HD
        grads[side, 2 * rank : 2 * rank + 16, inner : inner + HD] = jnp.concatenate(
            (gain_sums[head], zeros), axis=0
        ).astype(BF)
    if carried is not None:
        pay[0:rows, :] = to_rank(carried[...], weights_before, own).astype(BF)


def turn_kernel(count, layer, width, *refs):
    pays, sides, refs = refs[:count], refs[count : 2 * count], refs[2 * count :]
    x_before, mean_before, mask, weights, cot = refs[:5]
    x, mean, reduced, cross, grads, carried, pay = refs[5:12]
    probs, mixed = refs[12:]
    rows = x.shape[0]
    weights_before, weights = layer_of(weights, layer - 1), layer_of(weights, layer)
    receive_forward(
        pays, gram_of(sides, layer - 1, layer, rows), x_before, mean_before, weights_before,
        width, x, mean, reduced, cross,
    )
    attend(x, mean[:, 0:1], weights, mask, probs, mixed)
    pay[pay.shape[0] - rows :, :] = to_rank(mixed[...], weights, 0).astype(BF)
    dred = total_of(sides, 0, rows).astype(BF)
    layer_backward(
        cot, dred, x, mean[:, 0:1], mask, weights, weights_before, probs, mixed, None, grads,
        carried, pay,
    )


def split_sides(grads, keep, send):
    core = lax.axis_index("core")
    keep[...] = grads[core]
    send[...] = grads[1 - core]


def back_kernel(count, with_last, layer, width, *refs):
    pays, refs = refs[:count], refs[count:]
    carried_after, x_after, mean_after, cross_after = refs[:4]
    x, mean, mask, weights = refs[4:8]
    refs = refs[8:]
    weights_before = carried = pay = None
    if layer:
        weights_before = layer_of(weights, layer - 1)
    weights = layer_of(weights, layer)
    probs, mixed, reduced = refs[:3]
    refs = refs[3:]
    if with_last:
        cot, turn_grads = refs[:2]
        refs = refs[2:]
    keep, send = refs[:2]
    refs = refs[2:]
    if with_last:
        last_keep, last_send = refs[:2]
        refs = refs[2:]
    if layer:
        carried, pay = refs[:2]
        refs = refs[2:]
    dout, grads = refs
    rows, local = x.shape
    size = block_size(rows)
    own = (weights.shape[2] - 16) // 2
    rank = reduced.shape[1]
    dred_parts = []
    for block in range(rows // size):
        span = slice(block * size, (block + 1) * size)
        base = rows + 16 * block
        lines = total_of(pays, base, base + 16)
        line = lines[0:1] + lines[1:2]
        column = jnp.broadcast_to(line, (size, size)).T
        factor = lax.rsqrt(mean_after[span, 0:1] + EPS)
        pull = column[:, 0:1] * (factor * factor * factor / width)
        dred_parts.append(
            (
                total_of(pays, block * size, (block + 1) * size) - cross_after[span, :] * pull
            ).astype(BF)
        )
        dout[span, :] = (
            carried_after[span, :].astype(F32) - x_after[span, :].astype(F32) * pull
        ).astype(BF)
    dred = dred_parts[0] if len(dred_parts) == 1 else jnp.concatenate(dred_parts, axis=0)
    if with_last:
        last_reduced = total_of(pays, pays[0].shape[0] - rows, pays[0].shape[0]).astype(BF)
        second = dot_tn(last_reduced, cot[...]).astype(BF)
        for side in range(weights.shape[1]):
            grads[side, 0:rank, :] = turn_grads[side, 0:rank, :]
            grads[side, rank : 2 * rank, :] = second[:, side * own : (side + 1) * own]
            grads[side, 2 * rank :, :] = turn_grads[side, 2 * rank :, :]
        split_sides(grads, last_keep, last_send)
    layer_backward(
        dout, dred, x, mean[:, 0:1], mask, weights, weights_before, probs, mixed, reduced[...],
        grads, carried, pay,
    )
    split_sides(grads, keep, send)


def combine_kernel(sections, *refs):
    kept, swapped = refs[:sections], refs[sections : 2 * sections]
    outs, sums = refs[2 * sections : 3 * sections], refs[3 * sections]
    section = lax.axis_index("pipe")
    for layer in range(sections):
        sums[layer] = (kept[layer][...].astype(F32) + swapped[layer][...].astype(F32)).astype(BF)
    for distance in range(sections):
        outs[distance][...] = sums[section ^ distance]


def finish_kernel(sections, *refs):
    parts = refs[:sections]
    gain, first, second = refs[sections:]
    rank = second.shape[1]
    total = parts[0][...].astype(F32)
    for part in parts[1:]:
        total = total + part[...].astype(F32)
    first[0] = total[0:rank].T
    second[0] = total[rank : 2 * rank]
    gain[...] = total[2 * rank : 2 * rank + 1]


def per_device(tokens, cotangents, starts, counts, layer_gains, first_map, second_map):
    sections = lax.axis_size("pipe")
    groups = lax.axis_size("z")
    directions, micro_count, length, width = tokens.shape
    micro_local = -(-directions * micro_count // sections)
    rows = groups * micro_local * length
    local = width // groups
    own = first_map.shape[1]
    rank = first_map.shape[2]
    heads = local // HD
    size = block_size(rows)
    blocks = rows // size
    sides = lax.axis_size("core")
    top = sections - 1

    def shifted(value, shift):
        return lax.ppermute(value, "z", [(i, i ^ shift) for i in range(groups)])

    def across(value, distance):
        return lax.ppermute(value, "pipe", [(i, i ^ distance) for i in range(sections)])

    def swapped(value):
        return lax.ppermute(value, "core", [(i, 1 - i) for i in range(sides)])

    def exchange(pay):
        return [pay] + [shifted(pay, shift) for shift in range(1, groups)]

    token_parts, packed = pack(
        tokens, cotangents, starts, counts, layer_gains, first_map, second_map, groups, micro_local
    )
    mine = [packed] + [across(packed, distance) for distance in range(1, sections)]
    received = [token_parts[0]]
    received += [shifted(token_parts[shift], shift) for shift in range(1, groups)]
    received, mine = lax.optimization_barrier((received, mine))
    theirs = [swapped(part) for part in mine]

    def shaped(shape, kind=BF):
        return jax.ShapeDtypeStruct(shape, kind)

    wide_shape = shaped((rows, local))
    mean_shape = shaped((rows, HD), F32)
    rank_shape = shaped((rows, rank))
    cross_shape = shaped((rows, rank), F32)
    probs_shape = shaped((blocks, heads, size, size))
    grads_shape = (sides, 2 * rank + 16, own)
    half_shape = shaped(grads_shape[1:])
    weights_shape = shaped((sections, sides, slice_rows(own), HD))

    def call(kernel, operands, specs, outs, name, **more):
        return pl.pallas_call(
            kernel,
            in_specs=specs,
            out_specs=vmem_specs(len(outs)),
            out_shape=outs,
            compiler_params=PARAMS,
            name=name,
            **more,
        )(*operands)

    x, cot, mask, mean, mine[0] = call(
        functools.partial(arrange_kernel, length, groups),
        (*received, mine[0]),
        vmem_specs(groups + 1),
        [
            wide_shape,
            wide_shape,
            shaped((blocks, size, size)),
            mean_shape,
            shaped(packed.shape),
        ],
        "arrange",
        scratch_shapes=[pltpu.VMEM((rows, HD), BF)],
    )
    last_gram = gram_place(top - 1, top, rows)
    side_rows = last_gram[0] + last_gram[1]
    probs, mixed, pay, side, weights = call(
        functools.partial(first_kernel, sections),
        (*mine, *theirs, x, cot, mask, mean),
        vmem_specs(2 * sections + 4),
        [
            probs_shape,
            wide_shape,
            shaped((2 * rows + FOLDED, HD)),
            shaped((side_rows, HD)),
            weights_shape,
        ],
        "forward_first",
        scratch_shapes=[pltpu.SemaphoreType.DMA((sections, sides))],
    )
    xs, means, reduceds, crosses = [x], [mean], [], [None]
    all_probs, all_mixed = [probs], [mixed]
    first_pays = pays = exchange(pay)
    arrived = exchange(side)
    for layer in range(1, top):
        operands = (*pays, *((), first_pays, arrived)[min(layer, 3) - 1])
        specs = vmem_specs(len(operands) + 4)
        x, mean, reduced, cross, probs, mixed, pay = call(
            functools.partial(middle_kernel, groups, layer, top, float(width)),
            (*operands, xs[-1], means[-1], mask, weights),
            specs,
            [
                wide_shape,
                mean_shape,
                rank_shape,
                cross_shape,
                probs_shape,
                wide_shape,
                shaped((2 * rows, HD)),
            ],
            "forward_middle",
        )
        xs.append(x)
        means.append(mean)
        reduceds.append(reduced)
        crosses.append(cross)
        all_probs.append(probs)
        all_mixed.append(mixed)
        pays = exchange(pay)

    back_rows = rows + 16 * blocks
    x, mean, reduced, cross, turn_grads, carried, pay = call(
        functools.partial(turn_kernel, groups, top, float(width)),
        (*pays, *arrived, xs[-1], means[-1], mask, weights, cot),
        vmem_specs(2 * groups + 5),
        [
            wide_shape,
            mean_shape,
            rank_shape,
            cross_shape,
            shaped(grads_shape),
            wide_shape,
            shaped((back_rows + rows, HD)),
        ],
        "turn",
        scratch_shapes=[
            pltpu.VMEM(probs_shape.shape, BF),
            pltpu.VMEM(wide_shape.shape, BF),
        ],
    )
    xs.append(x)
    means.append(mean)
    reduceds.append(reduced)
    crosses.append(cross)

    kept, taken = [None] * sections, [None] * sections
    for layer in range(top - 1, -1, -1):
        pays = exchange(pay)
        with_last = layer == top - 1
        to_first = layer == 0
        operands = (
            *pays, carried, xs[layer + 1], means[layer + 1], crosses[layer + 1],
            xs[layer], means[layer], mask, weights,
        )
        operands += (all_probs[layer], all_mixed[layer], reduceds[layer])
        outs = [half_shape] * 2
        if with_last:
            operands += (cot, turn_grads)
            outs += [half_shape] * 2
        if not to_first:
            outs += [wide_shape, shaped((back_rows, HD))]
        result = call(
            functools.partial(back_kernel, groups, with_last, layer, float(width)),
            operands,
            vmem_specs(len(operands)),
            outs,
            "backward",
            scratch_shapes=[pltpu.VMEM(wide_shape.shape, BF), pltpu.VMEM(grads_shape, BF)],
        )
        kept[layer], taken[layer] = result[0], swapped(result[1])
        if with_last:
            kept[top], taken[top] = result[2], swapped(result[3])
        if not to_first:
            carried, pay = result[-2:]

    parts = call(
        functools.partial(combine_kernel, sections),
        (*kept, *taken),
        vmem_specs(2 * sections),
        [half_shape] * sections,
        "combine",
        scratch_shapes=[pltpu.VMEM((sections,) + grads_shape[1:], BF)],
    )
    arrived = [parts[0]] + [across(parts[distance], distance) for distance in range(1, sections)]
    gain_grad, first_grad, second_grad = call(
        functools.partial(finish_kernel, sections),
        arrived,
        vmem_specs(sections),
        [
            shaped((1, own), F32),
            shaped((1, own, rank), F32),
            shaped((1, rank, own), F32),
        ],
        "finish",
    )
    return (gain_grad, first_grad, second_grad)


def solution(mesh):
    fine = Mesh(
        mesh.devices.reshape(mesh.shape["pipe"], mesh.shape["dp"] // 2, 2), ("pipe", "z", "core")
    )
    data = ("z", "core")
    in_specs = (
        P(None, data, None, None),
        P(None, data, None, None),
        P(None, data, None),
        P(None, data),
        P("pipe", data),
        P("pipe", data, None),
        P("pipe", None, data),
    )
    out_specs = (P("pipe", data), P("pipe", data, None), P("pipe", None, data))
    mapped = jax.shard_map(
        per_device, mesh=fine, in_specs=in_specs, out_specs=out_specs, check_vma=False
    )

    return mapped
```

```python
import functools

import jax
import jax.numpy as jnp
from jax import lax
from jax.experimental import pallas as pl
from jax.experimental.pallas import tpu as pltpu
from jax.sharding import Mesh, PartitionSpec as P

HD = 128
EPS = 1e-05
FOLDED = HD + 16
BF = jnp.bfloat16
F32 = jnp.float32
PARAMS = pltpu.CompilerParams(vmem_limit_bytes=48 * 1024 * 1024)
PACK_PARAMS = pltpu.CompilerParams(vmem_limit_bytes=60 * 1024 * 1024)


def dot(a, b):
    return jnp.dot(a, b, preferred_element_type=F32)


def dot_nt(a, b):
    return lax.dot_general(a, b, (((1,), (1,)), ((), ())), preferred_element_type=F32)


def dot_tn(a, b):
    return lax.dot_general(a, b, (((0,), (0,)), ((), ())), preferred_element_type=F32)


def two_parts(value):
    high = value.astype(BF)
    return high, (value - high.astype(F32)).astype(BF)


def vmem_specs(count):
    return [pl.BlockSpec(memory_space=pltpu.VMEM)] * count


def layer_of(weights, layer):
    return weights.at[pl.ds(layer, 1)]


def slice_rows(own):
    return 2 * own + 16


def pack_kernel(groups, micro_local, *refs):
    tokens, cotangents, starts, counts, gain, first, second = refs[:7]
    parts, weights = refs[7 : 7 + groups], refs[7 + groups]
    tok, cot, starts_in, counts_in, gain_in, second_in, sems = refs[8 + groups :]
    directions, micro_count, length, width = tokens.shape
    local = width // groups
    own = first.shape[1]
    section = lax.axis_index("pipe")
    group = lax.axis_index("z")
    picks = []
    copies = [
        pltpu.make_async_copy(second.at[0], second_in, sems.at[0]),
        pltpu.make_async_copy(gain, gain_in, sems.at[1]),
        pltpu.make_async_copy(first.at[0], weights.at[pl.ds(0, own)], sems.at[2]),
        pltpu.make_async_copy(starts, starts_in, sems.at[3]),
        pltpu.make_async_copy(counts, counts_in, sems.at[4]),
    ]
    for micro in range(micro_local):
        wanted = section * micro_local + micro
        slot = jnp.minimum(wanted, directions * micro_count - 1)
        direction, place = slot // micro_count, slot % micro_count
        picks.append((wanted < directions * micro_count, direction, place))
        rows = pl.ds(micro * length, length)
        copies.append(
            pltpu.make_async_copy(
                tokens.at[direction, place], tok.at[rows], sems.at[5 + 2 * micro]
            )
        )
        copies.append(
            pltpu.make_async_copy(
                cotangents.at[direction, place], cot.at[rows], sems.at[6 + 2 * micro]
            )
        )
    for copy in copies:
        copy.start()
    for copy in copies[:5]:
        copy.wait()
    weights[own : 2 * own, :] = second_in[...].astype(F32).T.astype(BF)
    gains = [gain_in[0:1, head * HD : (head + 1) * HD].astype(F32) for head in range(own // HD)]
    gains.append(jnp.zeros((16 - own // HD, HD), F32))
    weights[2 * own :, :] = jnp.concatenate(gains, axis=0).astype(BF)
    for copy in copies[5:]:
        copy.wait()
    for micro, (keep, direction, place) in enumerate(picks):
        rows = slice(micro * length, (micro + 1) * length)
        widened = tok[rows, :].astype(F32)
        mean = jnp.mean(widened * widened, axis=1, keepdims=True)
        mean_high, mean_low = two_parts(mean)
        position = lax.broadcasted_iota(jnp.int32, (length, HD), 0)
        document = jnp.zeros((length, HD), jnp.int32)
        for entry in range(starts.shape[2]):
            begun = starts_in[direction, place, entry] <= position
            begun = begun & (entry < counts_in[direction, place])
            document = document + begun.astype(jnp.int32)
        lane = lax.broadcasted_iota(jnp.int32, (length, HD), 1)
        tail = jnp.where(
            lane == 0,
            document.astype(F32),
            jnp.where(lane == 1, mean_high.astype(F32), mean_low.astype(F32)),
        ).astype(BF)
        for shift in range(groups):
            start = pl.multiple_of((group ^ shift) * local, local)
            parts[shift][rows, 0:local] = tok[rows, pl.ds(start, local)]
            cotangent = cot[rows, pl.ds(start, local)]
            parts[shift][rows, local : 2 * local] = jnp.where(
                keep, cotangent, jnp.zeros_like(cotangent)
            )
            parts[shift][rows, 2 * local :] = tail


def pack(tokens, cotangents, starts, counts, gain, first, second, groups, micro_local):
    length, width = tokens.shape[2:]
    own = first.shape[1]
    local = width // groups
    rows = micro_local * length
    shape = jax.ShapeDtypeStruct
    results = pl.pallas_call(
        functools.partial(pack_kernel, groups, micro_local),
        in_specs=[pl.BlockSpec(memory_space=pltpu.HBM)] * 7,
        out_specs=vmem_specs(groups + 1),
        out_shape=[shape((rows, 2 * local + HD), BF)] * groups
        + [shape((slice_rows(own), HD), BF)],
        scratch_shapes=[
            pltpu.VMEM((rows, width), BF),
            pltpu.VMEM((rows, width), BF),
            pltpu.SMEM(starts.shape, jnp.int32),
            pltpu.SMEM(counts.shape, jnp.int32),
            pltpu.VMEM(gain.shape, BF),
            pltpu.VMEM(second.shape[1:], BF),
            pltpu.SemaphoreType.DMA((5 + 2 * micro_local,)),
        ],
        compiler_params=PACK_PARAMS,
        name="pack",
    )(tokens, cotangents, starts, counts, gain, first, second)
    return results[:groups], results[groups]


def head_gain(weights, head):
    own = (weights.shape[2] - 16) // 2
    per_slice = own // HD
    row = 2 * own + head % per_slice
    return weights[0, head // per_slice, row : row + 1, :].astype(F32)


def block_size(rows):
    return HD if rows % HD == 0 else rows


def to_rank(value, weights, at):
    own = (weights.shape[2] - 16) // 2
    total = None
    for side in range(weights.shape[1]):
        term = dot(value[:, side * own : (side + 1) * own], weights[0, side, at : at + own, :])
        total = term if total is None else total + term
    return total


def from_rank(value, weights, at, side):
    own = (weights.shape[2] - 16) // 2
    return dot_nt(value, weights[0, side, at : at + own, :])


def gram(weights):
    own = (weights.shape[2] - 16) // 2
    total = None
    for side in range(weights.shape[1]):
        part = weights[0, side, own : 2 * own, :]
        term = dot_tn(part, part)
        total = term if total is None else total + term
    return total


def attend(x, mean, weights, mask, probs, mixed):
    rows, local = x.shape
    size = block_size(rows)
    factor = lax.rsqrt(mean + EPS)
    heads = range(local // HD)
    gains = [head_gain(weights, head) for head in heads]
    for block in range(rows // size):
        span = slice(block * size, (block + 1) * size)
        allowed = mask[block] > 0
        wide = x[span, :].astype(F32) * factor[span]
        normed = [(wide[:, head * HD : (head + 1) * HD] * gains[head]).astype(BF) for head in heads]
        scores = [dot_nt(value, value) for value in normed]
        raw = [jnp.where(allowed, jnp.exp(score * (1.0 / HD)), 0.0) for score in scores]
        shares = [1.0 / jnp.sum(value, axis=1, keepdims=True) for value in raw]
        prob = [(value * share).astype(BF) for value, share in zip(raw, shares)]
        result = [dot(left, right).astype(BF) for left, right in zip(prob, normed)]
        for head in heads:
            probs[block, head] = prob[head]
            mixed[span, head * HD : (head + 1) * HD] = result[head]


def send_forward(x, weights, mixed, pay):
    rows = x.shape[0]
    own = (weights.shape[2] - 16) // 2
    pay[0:rows, :] = to_rank(mixed[...], weights, 0).astype(BF)
    pay[rows : 2 * rows, :] = to_rank(x[...], weights, own).astype(BF)


def total_of(pays, start, stop):
    total = pays[0][start:stop, :].astype(F32)
    for pay in pays[1:]:
        total = total + pay[start:stop, :].astype(F32)
    return total


def receive_forward(
    pays, gram_total, x_before, mean_before, weights_before, width, x, mean, reduced, cross
):
    rows, local = x_before.shape
    own = (weights_before.shape[2] - 16) // 2
    low_rank = total_of(pays, 0, rows).astype(BF)
    before = total_of(pays, rows, 2 * rows)
    high, low = two_parts(gram_total)
    through = dot(low_rank, high) + dot(low_rank, low)
    wide = low_rank.astype(F32)
    change = jnp.sum(wide * (2.0 * before + through), axis=1, keepdims=True) / width
    new_mean = jnp.maximum(mean_before[:, 0:1] + change, 0.0)
    mean[...] = jnp.broadcast_to(new_mean, mean.shape)
    reduced[...] = low_rank
    cross[...] = before + through
    for side in range(weights_before.shape[1]):
        part = slice(side * own, (side + 1) * own)
        x[:, part] = (
            x_before[:, part].astype(F32) + from_rank(low_rank, weights_before, own, side)
        ).astype(BF)


def arrange_kernel(length, order, *refs):
    groups = len(order)
    received, packed = [refs[order.index(place)] for place in range(groups)], refs[groups]
    x, cot, mask, mean, packed_out, tails = refs[groups + 1 :]
    rows, local = x.shape
    place_rows(received, tails, slice(2 * local, None))
    place_rows(received, x, slice(0, local))
    place_rows(received, cot, slice(local, 2 * local))
    tail = tails[...].astype(F32)
    mean[...] = jnp.broadcast_to(tail[:, 1:2] + tail[:, 2:3], mean.shape)
    build_mask(tail[:, 0:1], mask, block_size(rows), length)
    packed_out[...] = packed[...]


def first_kernel(sections, *refs):
    mine, theirs = refs[:sections], refs[sections : 2 * sections]
    x, mask, mean, probs, mixed, pay, weights, sems = refs[2 * sections :]
    section, core = lax.axis_index("pipe"), lax.axis_index("core")
    rows = x.shape[0]
    copies = []
    for distance in range(sections):
        layer = section ^ distance
        for parts, place in ((mine, core), (theirs, 1 - core)):
            copies.append(
                pltpu.make_async_copy(
                    parts[distance], weights.at[layer, place], sems.at[layer, place]
                )
            )
    for wanted_now in (True, False):
        for distance in range(sections):

            @pl.when((section == distance) == wanted_now)
            def _(distance=distance):
                copies[2 * distance].start()
                copies[2 * distance + 1].start()

    def arrived(layer):
        for place in range(weights.shape[1]):
            pltpu.make_async_copy(mine[0], weights.at[layer, place], sems.at[layer, place]).wait()

    arrived(0)
    own = (weights.shape[2] - 16) // 2
    layers = [layer_of(weights, layer) for layer in range(sections)]
    attend(x, mean[:, 0:1], layers[0], mask, probs, mixed)
    send_forward(x, layers[0], mixed, pay)
    arrived(1)
    pay[2 * rows :, :] = fold_grams(layers[0], layers[1])
    for layer in range(2, sections):
        arrived(layer)


def side_kernel(weights, cot, side):
    rows = cot.shape[0]
    sections = weights.shape[0]
    own = (weights.shape[2] - 16) // 2
    layers = [layer_of(weights, layer) for layer in range(sections)]
    side[0:rows, :] = to_rank(cot[...], layers[-1], own).astype(BF)
    for layer in range(2, sections - 1, 2):
        base, height, folded = gram_place(layer, sections - 1, rows)
        both = fold_grams(layers[layer], layers[layer + 1]) if folded else gram(layers[layer])
        side[base : base + height, :] = both.astype(BF)


def place_rows(received, target, columns):
    rows = received[0].shape[0]
    for shift, part in enumerate(received):
        source = lax.axis_index("z") ^ shift
        target[pl.ds(pl.multiple_of(source * rows, rows), rows), :] = part[:, columns]


def build_mask(document, mask, size, length):
    query = lax.broadcasted_iota(jnp.int32, (size, size), 0)
    key = lax.broadcasted_iota(jnp.int32, (size, size), 1)
    for block in range(mask.shape[0]):
        by_query = jnp.broadcast_to(document[block * size : (block + 1) * size], (size, size))
        by_key = by_query.T
        allowed = (by_query == by_key) & (key <= query) & (query // length == key // length)
        mask[block] = allowed.astype(F32).astype(BF)


def fold_grams(weights, other):
    row, lane = square_places()
    upper, lower = gram(weights), gram(other)
    diagonal = jnp.sum(jnp.where(row == lane, lower, 0.0), axis=0, keepdims=True)
    folded = jnp.where(row <= lane, upper, lower)
    return jnp.concatenate((folded, diagonal, jnp.zeros((15, HD), F32)), axis=0).astype(BF)


def square_places():
    return (
        lax.broadcasted_iota(jnp.int32, (HD, HD), 0),
        lax.broadcasted_iota(jnp.int32, (HD, HD), 1),
    )


def gram_place(layer, top, rows):
    pair = layer // 2
    folded = 2 * pair + 1 < top
    base = 2 * rows if pair == 0 else rows + FOLDED * (pair - 1)
    return base, FOLDED if folded else HD, folded


def gram_of(sources, layer, top, rows):
    base, height, folded = gram_place(layer, top, rows)
    total = total_of(sources, base, base + height)
    if not folded:
        return total
    row, lane = square_places()
    square = total[0:HD]
    if layer % 2 == 0:
        return jnp.where(row <= lane, square, square.T)
    lower = jnp.where(row > lane, square, square.T)
    return jnp.where(row == lane, total[HD : HD + 1], lower)


def middle_kernel(count, layer, top, width, *refs):
    pays, sources, refs = refs[:count], refs[count : 2 * count], refs[2 * count :]
    if layer == 1:
        sources, refs = pays, sources + refs
    x_before, mean_before, mask, weights = refs[:4]
    x, mean, reduced, cross, probs, mixed, pay = refs[4:]
    weights_before, weights = layer_of(weights, layer - 1), layer_of(weights, layer)
    receive_forward(
        pays, gram_of(sources, layer - 1, top, x.shape[0]), x_before, mean_before, weights_before,
        width, x, mean, reduced, cross,
    )
    attend(x, mean[:, 0:1], weights, mask, probs, mixed)
    send_forward(x, weights, mixed, pay)


def layer_backward(dout, dred, x, mean, weights, weights_before, probs, gain_row, carried, pay):
    rows, local = x.shape
    size = block_size(rows)
    own = (weights.shape[2] - 16) // 2
    per_slice = own // HD
    factor = lax.rsqrt(mean + EPS)
    back_mixed = [
        from_rank(dred, weights, 0, side).astype(BF) for side in range(weights.shape[1])
    ]
    heads = range(local // HD)
    gains = [head_gain(weights, head) for head in heads]
    gain_sums = [None] * len(heads)
    for block in range(rows // size):
        span = slice(block * size, (block + 1) * size)
        scale = factor[span]
        parts = [slice(head * HD, (head + 1) * HD) for head in heads]
        wide = [x[span, part].astype(F32) for part in parts]
        prob = [probs[block, head] for head in heads]
        onward = [None if carried is None else dout[span, part].astype(F32) for part in parts]
        unit = [value * scale for value in wide]
        normed = [(value * gain).astype(BF) for value, gain in zip(unit, gains)]
        upstream = []
        for head in heads:
            inner = (head % per_slice) * HD
            upstream.append(back_mixed[head // per_slice][span, inner : inner + HD])
        back_prob = [dot_nt(left, right) for left, right in zip(upstream, normed)]
        through = [dot_tn(left, right) for left, right in zip(prob, upstream)]
        both = []
        for head in heads:
            prob_wide = prob[head].astype(F32)
            inner_sum = jnp.sum(back_prob[head] * prob_wide, axis=1, keepdims=True)
            back_score = prob_wide * (back_prob[head] - inner_sum) * (1.0 / HD)
            both.append((back_score + back_score.T).astype(BF))
        back_normed = [
            (through[head] + dot(both[head], normed[head])).astype(BF).astype(F32) for head in heads
        ]
        norm_dot = jnp.zeros((size, HD), F32)
        for head in heads:
            term = jnp.sum(back_normed[head] * unit[head], axis=0, keepdims=True)
            gain_sums[head] = term if gain_sums[head] is None else gain_sums[head] + term
            if carried is not None:
                scaled = back_normed[head] * gains[head]
                norm_dot = norm_dot + scaled * wide[head]
                carried[span, parts[head]] = (onward[head] + scaled * scale).astype(BF)
        if carried is not None:
            column = jnp.broadcast_to(jnp.sum(norm_dot, axis=1, keepdims=True), (size, size))
            line = column.T[0:1, :]
            high, low = two_parts(line)
            base = rows + 16 * block
            pay[base : base + 16, :] = jnp.concatenate(
                (high.astype(F32), low.astype(F32), jnp.zeros((14, size), F32)), axis=0
            ).astype(BF)
    zeros = jnp.zeros((15, HD), F32)
    for head in heads:
        gain_row[:, head * HD : (head + 1) * HD] = jnp.concatenate(
            (gain_sums[head], zeros), axis=0
        ).astype(BF)
    if carried is not None:
        pay[0:rows, :] = to_rank(carried[...], weights_before, own).astype(BF)


def turn_kernel(count, layer, width, *refs):
    pays, sides, refs = refs[:count], refs[count : 2 * count], refs[2 * count :]
    x_before, mean_before, mask, weights, cot = refs[:5]
    x, mean, reduced, cross, mixed, dred_out, gain_row, carried, pay, probs = refs[5:]
    rows = x.shape[0]
    weights_before, weights = layer_of(weights, layer - 1), layer_of(weights, layer)
    receive_forward(
        pays, gram_of(sides, layer - 1, layer, rows), x_before, mean_before, weights_before,
        width, x, mean, reduced, cross,
    )
    attend(x, mean[:, 0:1], weights, mask, probs, mixed)
    dred = total_of(sides, 0, rows).astype(BF)
    dred_out[...] = dred
    layer_backward(
        cot[...], dred, x, mean[:, 0:1], weights, weights_before, probs, gain_row, carried, pay
    )
    pay[pay.shape[0] - rows :, :] = to_rank(mixed[...], weights, 0).astype(BF)


def receive_backward(pays, carried_after, x_after, mean_after, cross_after, width):
    rows = x_after.shape[0]
    size = block_size(rows)
    douts, dreds = [], []
    for block in range(rows // size):
        span = slice(block * size, (block + 1) * size)
        base = rows + 16 * block
        lines = total_of(pays, base, base + 16)
        column = jnp.broadcast_to(lines[0:1] + lines[1:2], (size, size)).T
        factor = lax.rsqrt(mean_after[span, 0:1] + EPS)
        pull = column[:, 0:1] * (factor * factor * factor / width)
        own_total = total_of(pays, block * size, (block + 1) * size)
        dreds.append((own_total - cross_after[span, :] * pull).astype(BF))
        douts.append(
            (carried_after[span, :].astype(F32) - x_after[span, :].astype(F32) * pull).astype(BF)
        )
    if len(douts) == 1:
        return douts[0], dreds[0]
    return jnp.concatenate(douts, axis=0), jnp.concatenate(dreds, axis=0)


def back_kernel(count, layer, width, *refs):
    pays, refs = refs[:count], refs[count:]
    carried_after, x_after, mean_after, cross_after, x, mean, weights, probs = refs[:8]
    carried, pay, dout_out, dred_out, gain_row = refs[8:]
    dout, dred = receive_backward(pays, carried_after, x_after, mean_after, cross_after, width)
    layer_backward(
        dout, dred, x, mean[:, 0:1], layer_of(weights, layer), layer_of(weights, layer - 1), probs,
        gain_row, carried, pay,
    )
    dout_out[...] = dout
    dred_out[...] = dred


def split_grads(first, second, gain_row, wide, keep, send):
    rank = first.shape[0]
    own = keep.shape[1]
    core = lax.axis_index("core")
    wide[0:rank, :] = first.astype(BF)
    wide[rank : 2 * rank, :] = second.astype(BF)
    if gain_row is not None:
        wide[2 * rank :, :] = gain_row[...]
    keep[...] = wide[:, pl.ds(pl.multiple_of(core * own, own), own)]
    send[...] = wide[:, pl.ds(pl.multiple_of((1 - core) * own, own), own)]


def grads_kernel(count, *refs):
    sources, refs = refs[:count], refs[count:]
    dout, dred, mixed, gain_row, keep, send, wide = refs
    rows = dout.shape[0]
    height = sources[0].shape[0]
    reduced = total_of(sources, height - rows, height).astype(BF)
    first, second = dot_tn(dred[...], mixed[...]), dot_tn(reduced, dout[...])
    split_grads(first, second, gain_row, wide, keep, send)


def back_first_kernel(count, width, *refs):
    pays, refs = refs[:count], refs[count:]
    carried_after, x_after, mean_after, cross_after, x, mean, weights, probs, mixed = refs[:9]
    reduced, keep, send, wide = refs[9:]
    rank = reduced.shape[1]
    dout, dred = receive_backward(pays, carried_after, x_after, mean_after, cross_after, width)
    first, second = dot_tn(dred, mixed[...]), dot_tn(reduced[...], dout)
    layer_backward(
        dout, dred, x, mean[:, 0:1], layer_of(weights, 0), None, probs, wide.at[pl.ds(2 * rank, 16)],
        None, None,
    )
    split_grads(first, second, None, wide, keep, send)


def combine_kernel(sections, *refs):
    kept, swapped = refs[:sections], refs[sections : 2 * sections]
    outs, sums = refs[2 * sections : 3 * sections], refs[3 * sections]
    section = lax.axis_index("pipe")
    for layer in range(sections):
        sums[layer] = (kept[layer][...].astype(F32) + swapped[layer][...].astype(F32)).astype(BF)
    for distance in range(sections):
        outs[distance][...] = sums[section ^ distance]


def finish_kernel(sections, *refs):
    parts = refs[:sections]
    gain, first, second = refs[sections:]
    rank = second.shape[1]
    total = parts[0][...].astype(F32)
    for part in parts[1:]:
        total = total + part[...].astype(F32)
    first[0] = total[0:rank].T
    second[0] = total[rank : 2 * rank]
    gain[...] = total[2 * rank : 2 * rank + 1]


def per_device(tokens, cotangents, starts, counts, layer_gains, first_map, second_map):
    sections = lax.axis_size("pipe")
    groups = lax.axis_size("z")
    directions, micro_count, length, width = tokens.shape
    micro_local = -(-directions * micro_count // sections)
    rows = groups * micro_local * length
    local = width // groups
    own = first_map.shape[1]
    rank = first_map.shape[2]
    heads = local // HD
    size = block_size(rows)
    blocks = rows // size
    sides = lax.axis_size("core")
    top = sections - 1

    def shifted(value, shift):
        return lax.ppermute(value, "z", [(i, i ^ shift) for i in range(groups)])

    def across(value, distance):
        return lax.ppermute(value, "pipe", [(i, i ^ distance) for i in range(sections)])

    def swapped(value):
        return lax.ppermute(value, "core", [(i, 1 - i) for i in range(sides)])

    def exchange(pay):
        return [pay] + [shifted(pay, shift) for shift in range(1, groups)]

    token_parts, packed = pack(
        tokens, cotangents, starts, counts, layer_gains, first_map, second_map, groups, micro_local
    )
    mine = [packed] + [across(packed, distance) for distance in range(1, sections)]
    order = [0] + list(range(groups - 1, 0, -1))
    received = [token_parts[0]] + [shifted(token_parts[place], place) for place in order[1:]]
    received, mine = lax.optimization_barrier((received, mine))
    theirs = [swapped(part) for part in mine]

    def shaped(shape, kind=BF):
        return jax.ShapeDtypeStruct(shape, kind)

    wide_shape = shaped((rows, local))
    mean_shape = shaped((rows, HD), F32)
    rank_shape = shaped((rows, rank))
    cross_shape = shaped((rows, rank), F32)
    probs_shape = shaped((blocks, heads, size, size))
    grads_shape = (sides, 2 * rank + 16, own)
    half_shape = shaped(grads_shape[1:])
    weights_shape = shaped((sections, sides, slice_rows(own), HD))

    def call(kernel, operands, specs, outs, name, **more):
        return pl.pallas_call(
            kernel,
            in_specs=specs,
            out_specs=vmem_specs(len(outs)),
            out_shape=outs,
            compiler_params=PARAMS,
            name=name,
            **more,
        )(*operands)

    x, cot, mask, mean, mine[0] = call(
        functools.partial(arrange_kernel, length, order),
        (*received, mine[0]),
        vmem_specs(groups + 1),
        [
            wide_shape,
            wide_shape,
            shaped((blocks, size, size)),
            mean_shape,
            shaped(packed.shape),
        ],
        "arrange",
        scratch_shapes=[pltpu.VMEM((rows, HD), BF)],
    )
    last_gram = gram_place(top - 1, top, rows)
    side_rows = last_gram[0] + last_gram[1]
    probs, mixed, pay, weights = call(
        functools.partial(first_kernel, sections),
        (*mine, *theirs, x, mask, mean),
        vmem_specs(2 * sections + 3),
        [probs_shape, wide_shape, shaped((2 * rows + FOLDED, HD)), weights_shape],
        "forward_first",
        scratch_shapes=[pltpu.SemaphoreType.DMA((sections, sides))],
    )
    xs, means, reduceds, crosses = [x], [mean], [], [None]
    all_probs, all_mixed = [probs], [mixed]
    first_pays = pays = exchange(pay)
    side = call(side_kernel, (weights, cot), vmem_specs(2), [shaped((side_rows, HD))], "side")[0]
    arrived = exchange(side)
    for layer in range(1, top):
        operands = (*pays, *((), first_pays, arrived)[min(layer, 3) - 1])
        specs = vmem_specs(len(operands) + 4)
        x, mean, reduced, cross, probs, mixed, pay = call(
            functools.partial(middle_kernel, groups, layer, top, float(width)),
            (*operands, xs[-1], means[-1], mask, weights),
            specs,
            [
                wide_shape,
                mean_shape,
                rank_shape,
                cross_shape,
                probs_shape,
                wide_shape,
                shaped((2 * rows, HD)),
            ],
            "forward_middle",
        )
        xs.append(x)
        means.append(mean)
        reduceds.append(reduced)
        crosses.append(cross)
        all_probs.append(probs)
        all_mixed.append(mixed)
        pays = exchange(pay)

    back_rows = rows + 16 * blocks
    gain_shape = shaped((16, local))
    wide_scratch = [pltpu.VMEM((2 * rank + 16, local), BF)]
    x, mean, reduced, cross, mixed, dred, gain_row, carried, pay = call(
        functools.partial(turn_kernel, groups, top, float(width)),
        (*pays, *arrived, xs[-1], means[-1], mask, weights, cot),
        vmem_specs(2 * groups + 5),
        [
            wide_shape,
            mean_shape,
            rank_shape,
            cross_shape,
            wide_shape,
            rank_shape,
            gain_shape,
            wide_shape,
            shaped((back_rows + rows, HD)),
        ],
        "turn",
        scratch_shapes=[pltpu.VMEM(probs_shape.shape, BF)],
    )
    xs.append(x)
    means.append(mean)
    reduceds.append(reduced)
    crosses.append(cross)
    all_mixed.append(mixed)

    def gradients(layer, sources, dout, dred, gain_row):
        operands = (*sources, dout, dred, all_mixed[layer], gain_row)
        keep, send = call(
            functools.partial(grads_kernel, len(sources)),
            operands,
            vmem_specs(len(operands)),
            [half_shape] * 2,
            "weight_grads",
            scratch_shapes=wide_scratch,
        )
        return keep, send

    pays = exchange(pay)
    halves = [None] * sections
    waiting = [(top, pays, cot, dred, gain_row)]
    for layer in range(top - 1, 0, -1):
        operands = (
            *pays, carried, xs[layer + 1], means[layer + 1], crosses[layer + 1],
            xs[layer], means[layer], weights, all_probs[layer],
        )
        carried, pay, dout, dred, gain_row = call(
            functools.partial(back_kernel, groups, layer, float(width)),
            operands,
            vmem_specs(len(operands)),
            [wide_shape, shaped((back_rows, HD)), wide_shape, rank_shape, gain_shape],
            "backward",
        )
        pays = exchange(pay)
        waiting.append((layer, [reduceds[layer]], dout, dred, gain_row))
        done = [gradients(*item) for item in waiting]
        pays, done = lax.optimization_barrier((pays, done))
        for item, (keep, send) in zip(waiting, done):
            halves[item[0]] = (keep, swapped(send))
        waiting = []
    operands = (
        *pays, carried, xs[1], means[1], crosses[1], xs[0], means[0], weights, all_probs[0],
        all_mixed[0], reduceds[0],
    )
    keep, send = call(
        functools.partial(back_first_kernel, groups, float(width)),
        operands,
        vmem_specs(len(operands)),
        [half_shape] * 2,
        "backward_first",
        scratch_shapes=wide_scratch,
    )
    halves[0] = (keep, swapped(send))

    parts = call(
        functools.partial(combine_kernel, sections),
        [pair[side] for side in range(2) for pair in halves],
        vmem_specs(2 * sections),
        [half_shape] * sections,
        "combine",
        scratch_shapes=[pltpu.VMEM((sections,) + grads_shape[1:], BF)],
    )
    arrived = [parts[0]] + [across(parts[distance], distance) for distance in range(1, sections)]
    gain_grad, first_grad, second_grad = call(
        functools.partial(finish_kernel, sections),
        arrived,
        vmem_specs(sections),
        [
            shaped((1, own), F32),
            shaped((1, own, rank), F32),
            shaped((1, rank, own), F32),
        ],
        "finish",
    )
    return (gain_grad, first_grad, second_grad)


def solution(mesh):
    fine = Mesh(
        mesh.devices.reshape(mesh.shape["pipe"], mesh.shape["dp"] // 2, 2), ("pipe", "z", "core")
    )
    data = ("z", "core")
    in_specs = (
        P(None, data, None, None),
        P(None, data, None, None),
        P(None, data, None),
        P(None, data),
        P("pipe", data),
        P("pipe", data, None),
        P("pipe", None, data),
    )
    out_specs = (P("pipe", data), P("pipe", data, None), P("pipe", None, data))
    mapped = jax.shard_map(
        per_device, mesh=fine, in_specs=in_specs, out_specs=out_specs, check_vma=False
    )

    return mapped
```

```python
import functools

import jax
import jax.numpy as jnp
from jax import lax
from jax.experimental import pallas as pl
from jax.experimental.pallas import tpu as pltpu
from jax.sharding import Mesh, PartitionSpec as P

HD = 128
EPS = 1e-05
FOLDED = HD + 16
BF = jnp.bfloat16
F32 = jnp.float32
PARAMS = pltpu.CompilerParams(vmem_limit_bytes=48 * 1024 * 1024)
PACK_PARAMS = pltpu.CompilerParams(vmem_limit_bytes=60 * 1024 * 1024)


def dot(a, b):
    return jnp.dot(a, b, preferred_element_type=F32)


def dot_nt(a, b):
    return lax.dot_general(a, b, (((1,), (1,)), ((), ())), preferred_element_type=F32)


def dot_tn(a, b):
    return lax.dot_general(a, b, (((0,), (0,)), ((), ())), preferred_element_type=F32)


def two_parts(value):
    high = value.astype(BF)
    return high, (value - high.astype(F32)).astype(BF)


def vmem_specs(count):
    return [pl.BlockSpec(memory_space=pltpu.VMEM)] * count


def layer_of(weights, layer):
    return weights.at[pl.ds(layer, 1)]


def slice_rows(own):
    return 2 * own + 16


def pack_kernel(groups, micro_local, *refs):
    tokens, cotangents, starts, counts, gain, first, second = refs[:7]
    parts, weights = refs[7 : 7 + groups], refs[7 + groups]
    tok, cot, starts_in, counts_in, gain_in, second_in, sems = refs[8 + groups :]
    directions, micro_count, length, width = tokens.shape
    local = width // groups
    own = first.shape[1]
    section = lax.axis_index("pipe")
    group = lax.axis_index("z")
    picks = []
    copies = [
        pltpu.make_async_copy(second.at[0], second_in, sems.at[0]),
        pltpu.make_async_copy(gain, gain_in, sems.at[1]),
        pltpu.make_async_copy(first.at[0], weights.at[pl.ds(0, own)], sems.at[2]),
        pltpu.make_async_copy(starts, starts_in, sems.at[3]),
        pltpu.make_async_copy(counts, counts_in, sems.at[4]),
    ]
    for micro in range(micro_local):
        wanted = section * micro_local + micro
        slot = jnp.minimum(wanted, directions * micro_count - 1)
        direction, place = slot // micro_count, slot % micro_count
        picks.append((wanted < directions * micro_count, direction, place))
        rows = pl.ds(micro * length, length)
        copies.append(
            pltpu.make_async_copy(
                tokens.at[direction, place], tok.at[rows], sems.at[5 + 2 * micro]
            )
        )
        copies.append(
            pltpu.make_async_copy(
                cotangents.at[direction, place], cot.at[rows], sems.at[6 + 2 * micro]
            )
        )
    for copy in copies:
        copy.start()
    for copy in copies[:5]:
        copy.wait()
    weights[own : 2 * own, :] = second_in[...].astype(F32).T.astype(BF)
    gains = [gain_in[0:1, head * HD : (head + 1) * HD].astype(F32) for head in range(own // HD)]
    gains.append(jnp.zeros((16 - own // HD, HD), F32))
    weights[2 * own :, :] = jnp.concatenate(gains, axis=0).astype(BF)
    for copy in copies[5:]:
        copy.wait()
    for micro, (keep, direction, place) in enumerate(picks):
        rows = slice(micro * length, (micro + 1) * length)
        widened = tok[rows, :].astype(F32)
        mean = jnp.mean(widened * widened, axis=1, keepdims=True)
        mean_high, mean_low = two_parts(mean)
        position = lax.broadcasted_iota(jnp.int32, (length, HD), 0)
        document = jnp.zeros((length, HD), jnp.int32)
        for entry in range(starts.shape[2]):
            begun = starts_in[direction, place, entry] <= position
            begun = begun & (entry < counts_in[direction, place])
            document = document + begun.astype(jnp.int32)
        lane = lax.broadcasted_iota(jnp.int32, (length, HD), 1)
        tail = jnp.where(
            lane == 0,
            document.astype(F32),
            jnp.where(lane == 1, mean_high.astype(F32), mean_low.astype(F32)),
        ).astype(BF)
        for shift in range(groups):
            start = pl.multiple_of((group ^ shift) * local, local)
            parts[shift][rows, 0:local] = tok[rows, pl.ds(start, local)]
            cotangent = cot[rows, pl.ds(start, local)]
            parts[shift][rows, local : 2 * local] = jnp.where(
                keep, cotangent, jnp.zeros_like(cotangent)
            )
            parts[shift][rows, 2 * local :] = tail


def pack(tokens, cotangents, starts, counts, gain, first, second, groups, micro_local):
    length, width = tokens.shape[2:]
    own = first.shape[1]
    local = width // groups
    rows = micro_local * length
    shape = jax.ShapeDtypeStruct
    results = pl.pallas_call(
        functools.partial(pack_kernel, groups, micro_local),
        in_specs=[pl.BlockSpec(memory_space=pltpu.HBM)] * 7,
        out_specs=vmem_specs(groups + 1),
        out_shape=[shape((rows, 2 * local + HD), BF)] * groups
        + [shape((slice_rows(own), HD), BF)],
        scratch_shapes=[
            pltpu.VMEM((rows, width), BF),
            pltpu.VMEM((rows, width), BF),
            pltpu.SMEM(starts.shape, jnp.int32),
            pltpu.SMEM(counts.shape, jnp.int32),
            pltpu.VMEM(gain.shape, BF),
            pltpu.VMEM(second.shape[1:], BF),
            pltpu.SemaphoreType.DMA((5 + 2 * micro_local,)),
        ],
        compiler_params=PACK_PARAMS,
        name="pack",
    )(tokens, cotangents, starts, counts, gain, first, second)
    return results[:groups], results[groups]


def head_gain(weights, head):
    own = (weights.shape[2] - 16) // 2
    per_slice = own // HD
    row = 2 * own + head % per_slice
    return weights[0, head // per_slice, row : row + 1, :].astype(F32)


def block_size(rows):
    return HD if rows % HD == 0 else rows


def to_rank(value, weights, at):
    own = (weights.shape[2] - 16) // 2
    total = None
    for side in range(weights.shape[1]):
        term = dot(value[:, side * own : (side + 1) * own], weights[0, side, at : at + own, :])
        total = term if total is None else total + term
    return total


def from_rank(value, weights, at, side):
    own = (weights.shape[2] - 16) // 2
    return dot_nt(value, weights[0, side, at : at + own, :])


def gram(weights):
    own = (weights.shape[2] - 16) // 2
    total = None
    for side in range(weights.shape[1]):
        part = weights[0, side, own : 2 * own, :]
        term = dot_tn(part, part)
        total = term if total is None else total + term
    return total


def attend(x, mean, weights, mask, probs, mixed):
    rows, local = x.shape
    size = block_size(rows)
    factor = lax.rsqrt(mean + EPS)
    heads = range(local // HD)
    gains = [head_gain(weights, head) for head in heads]
    for block in range(rows // size):
        span = slice(block * size, (block + 1) * size)
        allowed = mask[block] > 0
        wide = x[span, :].astype(F32) * factor[span]
        normed = [(wide[:, head * HD : (head + 1) * HD] * gains[head]).astype(BF) for head in heads]
        scores = [dot_nt(value, value) for value in normed]
        raw = [jnp.where(allowed, jnp.exp(score * (1.0 / HD)), 0.0) for score in scores]
        shares = [1.0 / jnp.sum(value, axis=1, keepdims=True) for value in raw]
        prob = [(value * share).astype(BF) for value, share in zip(raw, shares)]
        result = [dot(left, right).astype(BF) for left, right in zip(prob, normed)]
        for head in heads:
            probs[block, head] = prob[head]
            mixed[span, head * HD : (head + 1) * HD] = result[head]


def send_forward(x, weights, mixed, pay):
    rows = x.shape[0]
    own = (weights.shape[2] - 16) // 2
    pay[0:rows, :] = to_rank(mixed[...], weights, 0).astype(BF)
    pay[rows : 2 * rows, :] = to_rank(x[...], weights, own).astype(BF)


def total_of(pays, start, stop):
    total = pays[0][start:stop, :].astype(F32)
    for pay in pays[1:]:
        total = total + pay[start:stop, :].astype(F32)
    return total


def receive_forward(
    pays, gram_total, x_before, mean_before, weights_before, width, x, mean, reduced, cross
):
    rows, local = x_before.shape
    own = (weights_before.shape[2] - 16) // 2
    low_rank = total_of(pays, 0, rows).astype(BF)
    before = total_of(pays, rows, 2 * rows)
    high, low = two_parts(gram_total)
    through = dot(low_rank, high) + dot(low_rank, low)
    wide = low_rank.astype(F32)
    change = jnp.sum(wide * (2.0 * before + through), axis=1, keepdims=True) / width
    new_mean = jnp.maximum(mean_before[:, 0:1] + change, 0.0)
    mean[...] = jnp.broadcast_to(new_mean, mean.shape)
    reduced[...] = low_rank
    cross[...] = before + through
    for side in range(weights_before.shape[1]):
        part = slice(side * own, (side + 1) * own)
        x[:, part] = (
            x_before[:, part].astype(F32) + from_rank(low_rank, weights_before, own, side)
        ).astype(BF)


def own_kernel(part, packed, part_out, packed_out):
    part_out[...] = part[...]
    packed_out[...] = packed[...]


def arrange_kernel(length, order, *refs):
    groups = len(order)
    received = [refs[order.index(place)] for place in range(groups)]
    x, cot, mask, mean, tails = refs[groups:]
    rows, local = x.shape
    place_rows(received, tails, slice(2 * local, None))
    place_rows(received, x, slice(0, local))
    place_rows(received, cot, slice(local, 2 * local))
    tail = tails[...].astype(F32)
    mean[...] = jnp.broadcast_to(tail[:, 1:2] + tail[:, 2:3], mean.shape)
    build_mask(tail[:, 0:1], mask, block_size(rows), length)


def first_kernel(sections, *refs):
    mine, theirs = refs[:sections], refs[sections : 2 * sections]
    x, mask, mean, probs, mixed, pay, weights, sems = refs[2 * sections :]
    section, core = lax.axis_index("pipe"), lax.axis_index("core")
    rows = x.shape[0]
    copies = []
    for distance in range(sections):
        layer = section ^ distance
        for parts, place in ((mine, core), (theirs, 1 - core)):
            copies.append(
                pltpu.make_async_copy(
                    parts[distance], weights.at[layer, place], sems.at[layer, place]
                )
            )
    for wanted_now in (True, False):
        for distance in range(sections):

            @pl.when((section == distance) == wanted_now)
            def _(distance=distance):
                copies[2 * distance].start()
                copies[2 * distance + 1].start()

    def arrived(layer):
        for place in range(weights.shape[1]):
            pltpu.make_async_copy(mine[0], weights.at[layer, place], sems.at[layer, place]).wait()

    arrived(0)
    own = (weights.shape[2] - 16) // 2
    layers = [layer_of(weights, layer) for layer in range(sections)]
    attend(x, mean[:, 0:1], layers[0], mask, probs, mixed)
    send_forward(x, layers[0], mixed, pay)
    arrived(1)
    pay[2 * rows :, :] = fold_grams(layers[0], layers[1])
    for layer in range(2, sections):
        arrived(layer)


def side_kernel(weights, cot, side):
    rows = cot.shape[0]
    sections = weights.shape[0]
    own = (weights.shape[2] - 16) // 2
    layers = [layer_of(weights, layer) for layer in range(sections)]
    side[0:rows, :] = to_rank(cot[...], layers[-1], own).astype(BF)
    for layer in range(2, sections - 1, 2):
        base, height, folded = gram_place(layer, sections - 1, rows)
        both = fold_grams(layers[layer], layers[layer + 1]) if folded else gram(layers[layer])
        side[base : base + height, :] = both.astype(BF)


def place_rows(received, target, columns):
    rows = received[0].shape[0]
    for shift, part in enumerate(received):
        source = lax.axis_index("z") ^ shift
        target[pl.ds(pl.multiple_of(source * rows, rows), rows), :] = part[:, columns]


def build_mask(document, mask, size, length):
    query = lax.broadcasted_iota(jnp.int32, (size, size), 0)
    key = lax.broadcasted_iota(jnp.int32, (size, size), 1)
    for block in range(mask.shape[0]):
        by_query = jnp.broadcast_to(document[block * size : (block + 1) * size], (size, size))
        by_key = by_query.T
        allowed = (by_query == by_key) & (key <= query) & (query // length == key // length)
        mask[block] = allowed.astype(F32).astype(BF)


def fold_grams(weights, other):
    row, lane = square_places()
    upper, lower = gram(weights), gram(other)
    diagonal = jnp.sum(jnp.where(row == lane, lower, 0.0), axis=0, keepdims=True)
    folded = jnp.where(row <= lane, upper, lower)
    return jnp.concatenate((folded, diagonal, jnp.zeros((15, HD), F32)), axis=0).astype(BF)


def square_places():
    return (
        lax.broadcasted_iota(jnp.int32, (HD, HD), 0),
        lax.broadcasted_iota(jnp.int32, (HD, HD), 1),
    )


def gram_place(layer, top, rows):
    pair = layer // 2
    folded = 2 * pair + 1 < top
    base = 2 * rows if pair == 0 else rows + FOLDED * (pair - 1)
    return base, FOLDED if folded else HD, folded


def gram_of(sources, layer, top, rows):
    base, height, folded = gram_place(layer, top, rows)
    total = total_of(sources, base, base + height)
    if not folded:
        return total
    row, lane = square_places()
    square = total[0:HD]
    if layer % 2 == 0:
        return jnp.where(row <= lane, square, square.T)
    lower = jnp.where(row > lane, square, square.T)
    return jnp.where(row == lane, total[HD : HD + 1], lower)


def middle_kernel(count, layer, top, width, *refs):
    pays, sources, refs = refs[:count], refs[count : 2 * count], refs[2 * count :]
    if layer == 1:
        sources, refs = pays, sources + refs
    x_before, mean_before, mask, weights = refs[:4]
    x, mean, reduced, cross, probs, mixed, pay = refs[4:]
    weights_before, weights = layer_of(weights, layer - 1), layer_of(weights, layer)
    receive_forward(
        pays, gram_of(sources, layer - 1, top, x.shape[0]), x_before, mean_before, weights_before,
        width, x, mean, reduced, cross,
    )
    attend(x, mean[:, 0:1], weights, mask, probs, mixed)
    send_forward(x, weights, mixed, pay)


def layer_backward(dout, dred, x, mean, weights, weights_before, probs, gain_row, carried, pay):
    rows, local = x.shape
    size = block_size(rows)
    own = (weights.shape[2] - 16) // 2
    per_slice = own // HD
    factor = lax.rsqrt(mean + EPS)
    back_mixed = [
        from_rank(dred, weights, 0, side).astype(BF) for side in range(weights.shape[1])
    ]
    heads = range(local // HD)
    gains = [head_gain(weights, head) for head in heads]
    gain_sums = [None] * len(heads)
    for block in range(rows // size):
        span = slice(block * size, (block + 1) * size)
        scale = factor[span]
        parts = [slice(head * HD, (head + 1) * HD) for head in heads]
        wide = [x[span, part].astype(F32) for part in parts]
        prob = [probs[block, head] for head in heads]
        onward = [None if carried is None else dout[span, part].astype(F32) for part in parts]
        unit = [value * scale for value in wide]
        normed = [(value * gain).astype(BF) for value, gain in zip(unit, gains)]
        upstream = []
        for head in heads:
            inner = (head % per_slice) * HD
            upstream.append(back_mixed[head // per_slice][span, inner : inner + HD])
        back_prob = [dot_nt(left, right) for left, right in zip(upstream, normed)]
        through = [dot_tn(left, right) for left, right in zip(prob, upstream)]
        both = []
        for head in heads:
            prob_wide = prob[head].astype(F32)
            inner_sum = jnp.sum(back_prob[head] * prob_wide, axis=1, keepdims=True)
            back_score = prob_wide * (back_prob[head] - inner_sum) * (1.0 / HD)
            both.append((back_score + back_score.T).astype(BF))
        back_normed = [
            (through[head] + dot(both[head], normed[head])).astype(BF).astype(F32) for head in heads
        ]
        norm_dot = jnp.zeros((size, HD), F32)
        for head in heads:
            term = jnp.sum(back_normed[head] * unit[head], axis=0, keepdims=True)
            gain_sums[head] = term if gain_sums[head] is None else gain_sums[head] + term
            if carried is not None:
                scaled = back_normed[head] * gains[head]
                norm_dot = norm_dot + scaled * wide[head]
                carried[span, parts[head]] = (onward[head] + scaled * scale).astype(BF)
        if carried is not None:
            column = jnp.broadcast_to(jnp.sum(norm_dot, axis=1, keepdims=True), (size, size))
            line = column.T[0:1, :]
            high, low = two_parts(line)
            base = rows + 16 * block
            pay[base : base + 16, :] = jnp.concatenate(
                (high.astype(F32), low.astype(F32), jnp.zeros((14, size), F32)), axis=0
            ).astype(BF)
    zeros = jnp.zeros((15, HD), F32)
    for head in heads:
        gain_row[:, head * HD : (head + 1) * HD] = jnp.concatenate(
            (gain_sums[head], zeros), axis=0
        ).astype(BF)
    if carried is not None:
        pay[0:rows, :] = to_rank(carried[...], weights_before, own).astype(BF)


def turn_kernel(count, layer, width, *refs):
    pays, sides, refs = refs[:count], refs[count : 2 * count], refs[2 * count :]
    x_before, mean_before, mask, weights, cot = refs[:5]
    x, mean, reduced, cross, mixed, dred_out, gain_row, carried, pay, probs = refs[5:]
    rows = x.shape[0]
    weights_before, weights = layer_of(weights, layer - 1), layer_of(weights, layer)
    receive_forward(
        pays, gram_of(sides, layer - 1, layer, rows), x_before, mean_before, weights_before,
        width, x, mean, reduced, cross,
    )
    attend(x, mean[:, 0:1], weights, mask, probs, mixed)
    dred = total_of(sides, 0, rows).astype(BF)
    dred_out[...] = dred
    layer_backward(
        cot[...], dred, x, mean[:, 0:1], weights, weights_before, probs, gain_row, carried, pay
    )
    pay[pay.shape[0] - rows :, :] = to_rank(mixed[...], weights, 0).astype(BF)


def receive_backward(pays, carried_after, x_after, mean_after, cross_after, width):
    rows = x_after.shape[0]
    size = block_size(rows)
    douts, dreds = [], []
    for block in range(rows // size):
        span = slice(block * size, (block + 1) * size)
        base = rows + 16 * block
        lines = total_of(pays, base, base + 16)
        column = jnp.broadcast_to(lines[0:1] + lines[1:2], (size, size)).T
        factor = lax.rsqrt(mean_after[span, 0:1] + EPS)
        pull = column[:, 0:1] * (factor * factor * factor / width)
        own_total = total_of(pays, block * size, (block + 1) * size)
        dreds.append((own_total - cross_after[span, :] * pull).astype(BF))
        douts.append(
            (carried_after[span, :].astype(F32) - x_after[span, :].astype(F32) * pull).astype(BF)
        )
    if len(douts) == 1:
        return douts[0], dreds[0]
    return jnp.concatenate(douts, axis=0), jnp.concatenate(dreds, axis=0)


def back_kernel(count, layer, width, *refs):
    pays, refs = refs[:count], refs[count:]
    carried_after, x_after, mean_after, cross_after, x, mean, weights, probs = refs[:8]
    carried, pay, dout_out, dred_out, gain_row = refs[8:]
    dout, dred = receive_backward(pays, carried_after, x_after, mean_after, cross_after, width)
    layer_backward(
        dout, dred, x, mean[:, 0:1], layer_of(weights, layer), layer_of(weights, layer - 1), probs,
        gain_row, carried, pay,
    )
    dout_out[...] = dout
    dred_out[...] = dred


def split_grads(first, second, gain_row, wide, keep, send):
    rank = first.shape[0]
    own = keep.shape[1]
    core = lax.axis_index("core")
    wide[0:rank, :] = first.astype(BF)
    wide[rank : 2 * rank, :] = second.astype(BF)
    if gain_row is not None:
        wide[2 * rank :, :] = gain_row[...]
    keep[...] = wide[:, pl.ds(pl.multiple_of(core * own, own), own)]
    send[...] = wide[:, pl.ds(pl.multiple_of((1 - core) * own, own), own)]


def grads_kernel(count, *refs):
    sources, refs = refs[:count], refs[count:]
    dout, dred, mixed, gain_row, keep, send, wide = refs
    rows = dout.shape[0]
    height = sources[0].shape[0]
    reduced = total_of(sources, height - rows, height).astype(BF)
    first, second = dot_tn(dred[...], mixed[...]), dot_tn(reduced, dout[...])
    split_grads(first, second, gain_row, wide, keep, send)


def back_first_kernel(count, width, *refs):
    pays, refs = refs[:count], refs[count:]
    carried_after, x_after, mean_after, cross_after, x, mean, weights, probs, mixed = refs[:9]
    reduced, keep, send, wide = refs[9:]
    rank = reduced.shape[1]
    dout, dred = receive_backward(pays, carried_after, x_after, mean_after, cross_after, width)
    first, second = dot_tn(dred, mixed[...]), dot_tn(reduced[...], dout)
    layer_backward(
        dout, dred, x, mean[:, 0:1], layer_of(weights, 0), None, probs, wide.at[pl.ds(2 * rank, 16)],
        None, None,
    )
    split_grads(first, second, None, wide, keep, send)


def combine_kernel(sections, *refs):
    kept, swapped = refs[:sections], refs[sections : 2 * sections]
    outs, sums = refs[2 * sections : 3 * sections], refs[3 * sections]
    section = lax.axis_index("pipe")
    for layer in range(sections):
        sums[layer] = (kept[layer][...].astype(F32) + swapped[layer][...].astype(F32)).astype(BF)
    for distance in range(sections):
        outs[distance][...] = sums[section ^ distance]


def finish_kernel(sections, *refs):
    parts = refs[:sections]
    gain, first, second = refs[sections:]
    rank = second.shape[1]
    total = parts[0][...].astype(F32)
    for part in parts[1:]:
        total = total + part[...].astype(F32)
    first[0] = total[0:rank].T
    second[0] = total[rank : 2 * rank]
    gain[...] = total[2 * rank : 2 * rank + 1]


def per_device(tokens, cotangents, starts, counts, layer_gains, first_map, second_map):
    sections = lax.axis_size("pipe")
    groups = lax.axis_size("z")
    directions, micro_count, length, width = tokens.shape
    micro_local = -(-directions * micro_count // sections)
    rows = groups * micro_local * length
    local = width // groups
    own = first_map.shape[1]
    rank = first_map.shape[2]
    heads = local // HD
    size = block_size(rows)
    blocks = rows // size
    sides = lax.axis_size("core")
    top = sections - 1

    def shifted(value, shift):
        return lax.ppermute(value, "z", [(i, i ^ shift) for i in range(groups)])

    def across(value, distance):
        return lax.ppermute(value, "pipe", [(i, i ^ distance) for i in range(sections)])

    def swapped(value):
        return lax.ppermute(value, "core", [(i, 1 - i) for i in range(sides)])

    exchange_order = sorted(range(1, groups), key=lambda place: (place != 3, place))

    def exchange(pay):
        return [pay] + [shifted(pay, place) for place in exchange_order]

    token_parts, packed = pack(
        tokens, cotangents, starts, counts, layer_gains, first_map, second_map, groups, micro_local
    )
    mine = [packed] + [across(packed, distance) for distance in range(1, sections)]
    order = [0] + list(range(groups - 1, 0, -1))
    received = [token_parts[0]] + [shifted(token_parts[place], place) for place in order[1:]]
    def shaped(shape, kind=BF):
        return jax.ShapeDtypeStruct(shape, kind)

    def call(kernel, operands, specs, outs, name, **more):
        return pl.pallas_call(
            kernel,
            in_specs=specs,
            out_specs=vmem_specs(len(outs)),
            out_shape=outs,
            compiler_params=PARAMS,
            name=name,
            **more,
        )(*operands)

    received[0], mine[0] = call(
        own_kernel,
        (received[0], packed),
        vmem_specs(2),
        [shaped(received[0].shape), shaped(packed.shape)],
        "own_parts",
    )
    received, mine = lax.optimization_barrier((received, mine))
    theirs = [swapped(part) for part in mine]

    wide_shape = shaped((rows, local))
    mean_shape = shaped((rows, HD), F32)
    rank_shape = shaped((rows, rank))
    cross_shape = shaped((rows, rank), F32)
    probs_shape = shaped((blocks, heads, size, size))
    grads_shape = (sides, 2 * rank + 16, own)
    half_shape = shaped(grads_shape[1:])
    weights_shape = shaped((sections, sides, slice_rows(own), HD))

    x, cot, mask, mean = call(
        functools.partial(arrange_kernel, length, order),
        received,
        vmem_specs(groups),
        [wide_shape, wide_shape, shaped((blocks, size, size)), mean_shape],
        "arrange",
        scratch_shapes=[pltpu.VMEM((rows, HD), BF)],
    )
    last_gram = gram_place(top - 1, top, rows)
    side_rows = last_gram[0] + last_gram[1]
    probs, mixed, pay, weights = call(
        functools.partial(first_kernel, sections),
        (*mine, *theirs, x, mask, mean),
        vmem_specs(2 * sections + 3),
        [probs_shape, wide_shape, shaped((2 * rows + FOLDED, HD)), weights_shape],
        "forward_first",
        scratch_shapes=[pltpu.SemaphoreType.DMA((sections, sides))],
    )
    xs, means, reduceds, crosses = [x], [mean], [], [None]
    all_probs, all_mixed = [probs], [mixed]
    first_pays = pays = exchange(pay)
    side = call(side_kernel, (weights, cot), vmem_specs(2), [shaped((side_rows, HD))], "side")[0]
    arrived = exchange(side)
    for layer in range(1, top):
        operands = (*pays, *((), first_pays, arrived)[min(layer, 3) - 1])
        specs = vmem_specs(len(operands) + 4)
        x, mean, reduced, cross, probs, mixed, pay = call(
            functools.partial(middle_kernel, groups, layer, top, float(width)),
            (*operands, xs[-1], means[-1], mask, weights),
            specs,
            [
                wide_shape,
                mean_shape,
                rank_shape,
                cross_shape,
                probs_shape,
                wide_shape,
                shaped((2 * rows, HD)),
            ],
            "forward_middle",
        )
        xs.append(x)
        means.append(mean)
        reduceds.append(reduced)
        crosses.append(cross)
        all_probs.append(probs)
        all_mixed.append(mixed)
        pays = exchange(pay)

    back_rows = rows + 16 * blocks
    gain_shape = shaped((16, local))
    wide_scratch = [pltpu.VMEM((2 * rank + 16, local), BF)]
    x, mean, reduced, cross, mixed, dred, gain_row, carried, pay = call(
        functools.partial(turn_kernel, groups, top, float(width)),
        (*pays, *arrived, xs[-1], means[-1], mask, weights, cot),
        vmem_specs(2 * groups + 5),
        [
            wide_shape,
            mean_shape,
            rank_shape,
            cross_shape,
            wide_shape,
            rank_shape,
            gain_shape,
            wide_shape,
            shaped((back_rows + rows, HD)),
        ],
        "turn",
        scratch_shapes=[pltpu.VMEM(probs_shape.shape, BF)],
    )
    xs.append(x)
    means.append(mean)
    reduceds.append(reduced)
    crosses.append(cross)
    all_mixed.append(mixed)

    def gradients(layer, sources, dout, dred, gain_row):
        operands = (*sources, dout, dred, all_mixed[layer], gain_row)
        keep, send = call(
            functools.partial(grads_kernel, len(sources)),
            operands,
            vmem_specs(len(operands)),
            [half_shape] * 2,
            "weight_grads",
            scratch_shapes=wide_scratch,
        )
        return keep, send

    pays = exchange(pay)
    halves = [None] * sections
    waiting = [(top, pays, cot, dred, gain_row)]
    for layer in range(top - 1, 0, -1):
        operands = (
            *pays, carried, xs[layer + 1], means[layer + 1], crosses[layer + 1],
            xs[layer], means[layer], weights, all_probs[layer],
        )
        carried, pay, dout, dred, gain_row = call(
            functools.partial(back_kernel, groups, layer, float(width)),
            operands,
            vmem_specs(len(operands)),
            [wide_shape, shaped((back_rows, HD)), wide_shape, rank_shape, gain_shape],
            "backward",
        )
        pays = exchange(pay)
        waiting.append((layer, [reduceds[layer]], dout, dred, gain_row))
        done = [gradients(*item) for item in waiting]
        pays, done = lax.optimization_barrier((pays, done))
        for item, (keep, send) in zip(waiting, done):
            halves[item[0]] = (keep, swapped(send))
        waiting = []
    operands = (
        *pays, carried, xs[1], means[1], crosses[1], xs[0], means[0], weights, all_probs[0],
        all_mixed[0], reduceds[0],
    )
    keep, send = call(
        functools.partial(back_first_kernel, groups, float(width)),
        operands,
        vmem_specs(len(operands)),
        [half_shape] * 2,
        "backward_first",
        scratch_shapes=wide_scratch,
    )
    halves[0] = (keep, swapped(send))

    parts = call(
        functools.partial(combine_kernel, sections),
        [pair[side] for side in range(2) for pair in halves],
        vmem_specs(2 * sections),
        [half_shape] * sections,
        "combine",
        scratch_shapes=[pltpu.VMEM((sections,) + grads_shape[1:], BF)],
    )
    arrived = [parts[0]] + [across(parts[distance], distance) for distance in range(1, sections)]
    gain_grad, first_grad, second_grad = call(
        functools.partial(finish_kernel, sections),
        arrived,
        vmem_specs(sections),
        [
            shaped((1, own), F32),
            shaped((1, own, rank), F32),
            shaped((1, rank, own), F32),
        ],
        "finish",
    )
    return (gain_grad, first_grad, second_grad)


def solution(mesh):
    fine = Mesh(
        mesh.devices.reshape(mesh.shape["pipe"], mesh.shape["dp"] // 2, 2), ("pipe", "z", "core")
    )
    data = ("z", "core")
    in_specs = (
        P(None, data, None, None),
        P(None, data, None, None),
        P(None, data, None),
        P(None, data),
        P("pipe", data),
        P("pipe", data, None),
        P("pipe", None, data),
    )
    out_specs = (P("pipe", data), P("pipe", data, None), P("pipe", None, data))
    mapped = jax.shard_map(
        per_device, mesh=fine, in_specs=in_specs, out_specs=out_specs, check_vma=False
    )

    return mapped
```

```python
import functools

import jax
import jax.numpy as jnp
from jax import lax
from jax.experimental import pallas as pl
from jax.experimental.pallas import tpu as pltpu
from jax.sharding import Mesh, PartitionSpec as P

HD = 128
EPS = 1e-05
FOLDED = HD + 16
BF = jnp.bfloat16
F32 = jnp.float32
PARAMS = pltpu.CompilerParams(vmem_limit_bytes=48 * 1024 * 1024)
PACK_PARAMS = pltpu.CompilerParams(vmem_limit_bytes=60 * 1024 * 1024)


def dot(a, b):
    return jnp.dot(a, b, preferred_element_type=F32)


def dot_nt(a, b):
    return lax.dot_general(a, b, (((1,), (1,)), ((), ())), preferred_element_type=F32)


def dot_tn(a, b):
    return lax.dot_general(a, b, (((0,), (0,)), ((), ())), preferred_element_type=F32)


def two_parts(value):
    high = value.astype(BF)
    return high, (value - high.astype(F32)).astype(BF)


def vmem_specs(count):
    return [pl.BlockSpec(memory_space=pltpu.VMEM)] * count


def layer_of(weights, layer):
    return weights.at[pl.ds(layer, 1)]


def slice_rows(own):
    return 2 * own + 16


def pack_kernel(groups, micro_local, *refs):
    tokens, cotangents, starts, counts, gain, first, second = refs[:7]
    parts, weights = refs[7 : 7 + groups], refs[7 + groups]
    tok, cot, starts_in, counts_in, gain_in, second_in, sems = refs[8 + groups :]
    directions, micro_count, length, width = tokens.shape
    local = width // groups
    own = first.shape[1]
    section = lax.axis_index("pipe")
    group = lax.axis_index("z")
    picks = []
    copies = [
        pltpu.make_async_copy(second.at[0], second_in, sems.at[0]),
        pltpu.make_async_copy(gain, gain_in, sems.at[1]),
        pltpu.make_async_copy(first.at[0], weights.at[pl.ds(0, own)], sems.at[2]),
        pltpu.make_async_copy(starts, starts_in, sems.at[3]),
        pltpu.make_async_copy(counts, counts_in, sems.at[4]),
    ]
    for micro in range(micro_local):
        wanted = section * micro_local + micro
        slot = jnp.minimum(wanted, directions * micro_count - 1)
        direction, place = slot // micro_count, slot % micro_count
        picks.append((wanted < directions * micro_count, direction, place))
        rows = pl.ds(micro * length, length)
        copies.append(
            pltpu.make_async_copy(
                tokens.at[direction, place], tok.at[rows], sems.at[5 + 2 * micro]
            )
        )
        copies.append(
            pltpu.make_async_copy(
                cotangents.at[direction, place], cot.at[rows], sems.at[6 + 2 * micro]
            )
        )
    for copy in copies:
        copy.start()
    for copy in copies[:5]:
        copy.wait()
    weights[own : 2 * own, :] = second_in[...].astype(F32).T.astype(BF)
    gains = [gain_in[0:1, head * HD : (head + 1) * HD].astype(F32) for head in range(own // HD)]
    gains.append(jnp.zeros((16 - own // HD, HD), F32))
    weights[2 * own :, :] = jnp.concatenate(gains, axis=0).astype(BF)
    for copy in copies[5:]:
        copy.wait()
    for micro, (keep, direction, place) in enumerate(picks):
        rows = slice(micro * length, (micro + 1) * length)
        widened = tok[rows, :].astype(F32)
        mean = jnp.mean(widened * widened, axis=1, keepdims=True)
        mean_high, mean_low = two_parts(mean)
        position = lax.broadcasted_iota(jnp.int32, (length, HD), 0)
        document = jnp.zeros((length, HD), jnp.int32)
        for entry in range(starts.shape[2]):
            begun = starts_in[direction, place, entry] <= position
            begun = begun & (entry < counts_in[direction, place])
            document = document + begun.astype(jnp.int32)
        lane = lax.broadcasted_iota(jnp.int32, (length, HD), 1)
        tail = jnp.where(
            lane == 0,
            document.astype(F32),
            jnp.where(lane == 1, mean_high.astype(F32), mean_low.astype(F32)),
        ).astype(BF)
        for shift in range(groups):
            start = pl.multiple_of((group ^ shift) * local, local)
            parts[shift][rows, 0:local] = tok[rows, pl.ds(start, local)]
            cotangent = cot[rows, pl.ds(start, local)]
            parts[shift][rows, local : 2 * local] = jnp.where(
                keep, cotangent, jnp.zeros_like(cotangent)
            )
            parts[shift][rows, 2 * local :] = tail


def pack(tokens, cotangents, starts, counts, gain, first, second, groups, micro_local):
    length, width = tokens.shape[2:]
    own = first.shape[1]
    local = width // groups
    rows = micro_local * length
    shape = jax.ShapeDtypeStruct
    results = pl.pallas_call(
        functools.partial(pack_kernel, groups, micro_local),
        in_specs=[pl.BlockSpec(memory_space=pltpu.HBM)] * 7,
        out_specs=vmem_specs(groups + 1),
        out_shape=[shape((rows, 2 * local + HD), BF)] * groups
        + [shape((slice_rows(own), HD), BF)],
        scratch_shapes=[
            pltpu.VMEM((rows, width), BF),
            pltpu.VMEM((rows, width), BF),
            pltpu.SMEM(starts.shape, jnp.int32),
            pltpu.SMEM(counts.shape, jnp.int32),
            pltpu.VMEM(gain.shape, BF),
            pltpu.VMEM(second.shape[1:], BF),
            pltpu.SemaphoreType.DMA((5 + 2 * micro_local,)),
        ],
        compiler_params=PACK_PARAMS,
        name="pack",
    )(tokens, cotangents, starts, counts, gain, first, second)
    return results[:groups], results[groups]


def head_gain(weights, head):
    own = (weights.shape[2] - 16) // 2
    per_slice = own // HD
    row = 2 * own + head % per_slice
    return weights[0, head // per_slice, row : row + 1, :].astype(F32)


def block_size(rows):
    return HD if rows % HD == 0 else rows


def to_rank(value, weights, at):
    own = (weights.shape[2] - 16) // 2
    total = None
    for side in range(weights.shape[1]):
        term = dot(value[:, side * own : (side + 1) * own], weights[0, side, at : at + own, :])
        total = term if total is None else total + term
    return total


def from_rank(value, weights, at, side):
    own = (weights.shape[2] - 16) // 2
    return dot_nt(value, weights[0, side, at : at + own, :])


def gram(weights):
    own = (weights.shape[2] - 16) // 2
    total = None
    for side in range(weights.shape[1]):
        part = weights[0, side, own : 2 * own, :]
        term = dot_tn(part, part)
        total = term if total is None else total + term
    return total


def attend(x, mean, weights, mask, probs, mixed):
    rows, local = x.shape
    size = block_size(rows)
    factor = lax.rsqrt(mean + EPS)
    heads = range(local // HD)
    gains = [head_gain(weights, head) for head in heads]
    for block in range(rows // size):
        span = slice(block * size, (block + 1) * size)
        allowed = mask[block] > 0
        wide = x[span, :].astype(F32) * factor[span]
        normed = [(wide[:, head * HD : (head + 1) * HD] * gains[head]).astype(BF) for head in heads]
        scores = [dot_nt(value, value) for value in normed]
        raw = [jnp.where(allowed, jnp.exp(score * (1.0 / HD)), 0.0) for score in scores]
        shares = [1.0 / jnp.sum(value, axis=1, keepdims=True) for value in raw]
        prob = [(value * share).astype(BF) for value, share in zip(raw, shares)]
        result = [dot(left, right).astype(BF) for left, right in zip(prob, normed)]
        for head in heads:
            probs[block, head] = prob[head]
            mixed[span, head * HD : (head + 1) * HD] = result[head]


def send_forward(x, weights, mixed, pay):
    rows = x.shape[0]
    own = (weights.shape[2] - 16) // 2
    pay[0:rows, :] = to_rank(mixed[...], weights, 0).astype(BF)
    pay[rows : 2 * rows, :] = to_rank(x[...], weights, own).astype(BF)


def total_of(pays, start, stop):
    total = pays[0][start:stop, :].astype(F32)
    for pay in pays[1:]:
        total = total + pay[start:stop, :].astype(F32)
    return total


def receive_forward(
    pays, gram_total, x_before, mean_before, weights_before, width, x, mean, reduced, cross
):
    rows, local = x_before.shape
    own = (weights_before.shape[2] - 16) // 2
    low_rank = total_of(pays, 0, rows).astype(BF)
    before = total_of(pays, rows, 2 * rows)
    high, low = two_parts(gram_total)
    through = dot(low_rank, high) + dot(low_rank, low)
    wide = low_rank.astype(F32)
    change = jnp.sum(wide * (2.0 * before + through), axis=1, keepdims=True) / width
    new_mean = jnp.maximum(mean_before[:, 0:1] + change, 0.0)
    mean[...] = jnp.broadcast_to(new_mean, mean.shape)
    reduced[...] = low_rank
    cross[...] = before + through
    for side in range(weights_before.shape[1]):
        part = slice(side * own, (side + 1) * own)
        x[:, part] = (
            x_before[:, part].astype(F32) + from_rank(low_rank, weights_before, own, side)
        ).astype(BF)


def own_kernel(part, packed, early, part_out, packed_out, early_out):
    part_out[...] = part[...]
    packed_out[...] = packed[...]
    early_out[...] = early[...]


def arrange_kernel(length, order, *refs):
    groups = len(order)
    received = [refs[order.index(place)] for place in range(groups)]
    x, cot, mask, mean, tails = refs[groups:]
    rows, local = x.shape
    place_rows(received, tails, slice(2 * local, None))
    place_rows(received, x, slice(0, local))
    place_rows(received, cot, slice(local, 2 * local))
    tail = tails[...].astype(F32)
    mean[...] = jnp.broadcast_to(tail[:, 1:2] + tail[:, 2:3], mean.shape)
    build_mask(tail[:, 0:1], mask, block_size(rows), length)


def first_kernel(sections, *refs):
    mine, theirs = refs[:sections], refs[sections : 2 * sections]
    x, mask, mean, probs, mixed, pay, weights, sems = refs[2 * sections :]
    section, core = lax.axis_index("pipe"), lax.axis_index("core")
    rows = x.shape[0]
    copies = []
    for distance in range(sections):
        layer = section ^ distance
        for parts, place in ((mine, core), (theirs, 1 - core)):
            copies.append(
                pltpu.make_async_copy(
                    parts[distance], weights.at[layer, place], sems.at[layer, place]
                )
            )
    for wanted_now in (True, False):
        for distance in range(sections):

            @pl.when((section == distance) == wanted_now)
            def _(distance=distance):
                copies[2 * distance].start()
                copies[2 * distance + 1].start()

    def arrived(layer):
        for place in range(weights.shape[1]):
            pltpu.make_async_copy(mine[0], weights.at[layer, place], sems.at[layer, place]).wait()

    arrived(0)
    own = (weights.shape[2] - 16) // 2
    layers = [layer_of(weights, layer) for layer in range(sections)]
    attend(x, mean[:, 0:1], layers[0], mask, probs, mixed)
    send_forward(x, layers[0], mixed, pay)
    arrived(1)
    pay[2 * rows :, :] = fold_grams(layers[0], layers[1])
    for layer in range(2, sections):
        arrived(layer)


def side_kernel(weights, cot, side):
    rows = cot.shape[0]
    sections = weights.shape[0]
    own = (weights.shape[2] - 16) // 2
    layers = [layer_of(weights, layer) for layer in range(sections)]
    side[0:rows, :] = to_rank(cot[...], layers[-1], own).astype(BF)
    for layer in range(2, sections - 1, 2):
        base, height, folded = gram_place(layer, sections - 1, rows)
        both = fold_grams(layers[layer], layers[layer + 1]) if folded else gram(layers[layer])
        side[base : base + height, :] = both.astype(BF)


def place_rows(received, target, columns):
    rows = received[0].shape[0]
    for shift, part in enumerate(received):
        source = lax.axis_index("z") ^ shift
        target[pl.ds(pl.multiple_of(source * rows, rows), rows), :] = part[:, columns]


def build_mask(document, mask, size, length):
    query = lax.broadcasted_iota(jnp.int32, (size, size), 0)
    key = lax.broadcasted_iota(jnp.int32, (size, size), 1)
    for block in range(mask.shape[0]):
        by_query = jnp.broadcast_to(document[block * size : (block + 1) * size], (size, size))
        by_key = by_query.T
        allowed = (by_query == by_key) & (key <= query) & (query // length == key // length)
        mask[block] = allowed.astype(F32).astype(BF)


def fold_grams(weights, other):
    row, lane = square_places()
    upper, lower = gram(weights), gram(other)
    diagonal = jnp.sum(jnp.where(row == lane, lower, 0.0), axis=0, keepdims=True)
    folded = jnp.where(row <= lane, upper, lower)
    return jnp.concatenate((folded, diagonal, jnp.zeros((15, HD), F32)), axis=0).astype(BF)


def square_places():
    return (
        lax.broadcasted_iota(jnp.int32, (HD, HD), 0),
        lax.broadcasted_iota(jnp.int32, (HD, HD), 1),
    )


def gram_place(layer, top, rows):
    pair = layer // 2
    folded = 2 * pair + 1 < top
    base = 2 * rows if pair == 0 else rows + FOLDED * (pair - 1)
    return base, FOLDED if folded else HD, folded


def gram_of(sources, layer, top, rows):
    base, height, folded = gram_place(layer, top, rows)
    total = total_of(sources, base, base + height)
    if not folded:
        return total
    row, lane = square_places()
    square = total[0:HD]
    if layer % 2 == 0:
        return jnp.where(row <= lane, square, square.T)
    lower = jnp.where(row > lane, square, square.T)
    return jnp.where(row == lane, total[HD : HD + 1], lower)


def middle_kernel(count, layer, top, width, *refs):
    pays, sources, refs = refs[:count], refs[count : 2 * count], refs[2 * count :]
    if layer == 1:
        sources, refs = pays, sources + refs
    x_before, mean_before, mask, weights = refs[:4]
    x, mean, reduced, cross, probs, mixed, pay = refs[4:]
    weights_before, weights = layer_of(weights, layer - 1), layer_of(weights, layer)
    receive_forward(
        pays, gram_of(sources, layer - 1, top, x.shape[0]), x_before, mean_before, weights_before,
        width, x, mean, reduced, cross,
    )
    attend(x, mean[:, 0:1], weights, mask, probs, mixed)
    send_forward(x, weights, mixed, pay)


def layer_backward(dout, dred, x, mean, weights, weights_before, probs, gain_row, carried, pay):
    rows, local = x.shape
    size = block_size(rows)
    own = (weights.shape[2] - 16) // 2
    per_slice = own // HD
    factor = lax.rsqrt(mean + EPS)
    back_mixed = [
        from_rank(dred, weights, 0, side).astype(BF) for side in range(weights.shape[1])
    ]
    heads = range(local // HD)
    gains = [head_gain(weights, head) for head in heads]
    gain_sums = [None] * len(heads)
    for block in range(rows // size):
        span = slice(block * size, (block + 1) * size)
        scale = factor[span]
        parts = [slice(head * HD, (head + 1) * HD) for head in heads]
        wide = [x[span, part].astype(F32) for part in parts]
        prob = [probs[block, head] for head in heads]
        onward = [None if carried is None else dout[span, part].astype(F32) for part in parts]
        unit = [value * scale for value in wide]
        normed = [(value * gain).astype(BF) for value, gain in zip(unit, gains)]
        upstream = []
        for head in heads:
            inner = (head % per_slice) * HD
            upstream.append(back_mixed[head // per_slice][span, inner : inner + HD])
        back_prob = [dot_nt(left, right) for left, right in zip(upstream, normed)]
        through = [dot_tn(left, right) for left, right in zip(prob, upstream)]
        both = []
        for head in heads:
            prob_wide = prob[head].astype(F32)
            inner_sum = jnp.sum(back_prob[head] * prob_wide, axis=1, keepdims=True)
            back_score = prob_wide * (back_prob[head] - inner_sum) * (1.0 / HD)
            both.append((back_score + back_score.T).astype(BF))
        back_normed = [
            (through[head] + dot(both[head], normed[head])).astype(BF).astype(F32) for head in heads
        ]
        norm_dot = jnp.zeros((size, HD), F32)
        for head in heads:
            term = jnp.sum(back_normed[head] * unit[head], axis=0, keepdims=True)
            gain_sums[head] = term if gain_sums[head] is None else gain_sums[head] + term
            if carried is not None:
                scaled = back_normed[head] * gains[head]
                norm_dot = norm_dot + scaled * wide[head]
                carried[span, parts[head]] = (onward[head] + scaled * scale).astype(BF)
        if carried is not None:
            column = jnp.broadcast_to(jnp.sum(norm_dot, axis=1, keepdims=True), (size, size))
            line = column.T[0:1, :]
            high, low = two_parts(line)
            base = rows + 16 * block
            pay[base : base + 16, :] = jnp.concatenate(
                (high.astype(F32), low.astype(F32), jnp.zeros((14, size), F32)), axis=0
            ).astype(BF)
    zeros = jnp.zeros((15, HD), F32)
    for head in heads:
        gain_row[:, head * HD : (head + 1) * HD] = jnp.concatenate(
            (gain_sums[head], zeros), axis=0
        ).astype(BF)
    if carried is not None:
        pay[0:rows, :] = to_rank(carried[...], weights_before, own).astype(BF)


def turn_kernel(count, layer, width, *refs):
    pays, sides, refs = refs[:count], refs[count : 2 * count], refs[2 * count :]
    x_before, mean_before, mask, weights, cot = refs[:5]
    x, mean, reduced, cross, mixed, dred_out, gain_row, carried, pay, probs = refs[5:]
    rows = x.shape[0]
    weights_before, weights = layer_of(weights, layer - 1), layer_of(weights, layer)
    receive_forward(
        pays, gram_of(sides, layer - 1, layer, rows), x_before, mean_before, weights_before,
        width, x, mean, reduced, cross,
    )
    attend(x, mean[:, 0:1], weights, mask, probs, mixed)
    dred = total_of(sides, 0, rows).astype(BF)
    dred_out[...] = dred
    layer_backward(
        cot[...], dred, x, mean[:, 0:1], weights, weights_before, probs, gain_row, carried, pay
    )
    pay[pay.shape[0] - rows :, :] = to_rank(mixed[...], weights, 0).astype(BF)


def receive_backward(pays, carried_after, x_after, mean_after, cross_after, width):
    rows = x_after.shape[0]
    size = block_size(rows)
    douts, dreds = [], []
    for block in range(rows // size):
        span = slice(block * size, (block + 1) * size)
        base = rows + 16 * block
        lines = total_of(pays, base, base + 16)
        column = jnp.broadcast_to(lines[0:1] + lines[1:2], (size, size)).T
        factor = lax.rsqrt(mean_after[span, 0:1] + EPS)
        pull = column[:, 0:1] * (factor * factor * factor / width)
        own_total = total_of(pays, block * size, (block + 1) * size)
        dreds.append((own_total - cross_after[span, :] * pull).astype(BF))
        douts.append(
            (carried_after[span, :].astype(F32) - x_after[span, :].astype(F32) * pull).astype(BF)
        )
    if len(douts) == 1:
        return douts[0], dreds[0]
    return jnp.concatenate(douts, axis=0), jnp.concatenate(dreds, axis=0)


def back_kernel(count, layer, width, *refs):
    pays, refs = refs[:count], refs[count:]
    carried_after, x_after, mean_after, cross_after, x, mean, weights, probs = refs[:8]
    carried, pay, dout_out, dred_out, gain_row = refs[8:]
    dout, dred = receive_backward(pays, carried_after, x_after, mean_after, cross_after, width)
    layer_backward(
        dout, dred, x, mean[:, 0:1], layer_of(weights, layer), layer_of(weights, layer - 1), probs,
        gain_row, carried, pay,
    )
    dout_out[...] = dout
    dred_out[...] = dred


def split_grads(dred, mixed, second, gain_row, wide, keep, send):
    rank = second.shape[0]
    own = keep.shape[1]
    core = lax.axis_index("core")
    for head in range(mixed.shape[1] // HD):
        part = slice(head * HD, (head + 1) * HD)
        wide[0:HD, head * rank : (head + 1) * rank] = dot_tn(mixed[:, part], dred).astype(BF)
    wide[rank : 2 * rank, :] = second.astype(BF)
    if gain_row is not None:
        wide[2 * rank :, :] = gain_row[...]
    keep[...] = wide[:, pl.ds(pl.multiple_of(core * own, own), own)]
    send[...] = wide[:, pl.ds(pl.multiple_of((1 - core) * own, own), own)]


def grads_kernel(count, *refs):
    sources, refs = refs[:count], refs[count:]
    dout, dred, mixed, gain_row, keep, send, wide = refs
    rows = dout.shape[0]
    height = sources[0].shape[0]
    reduced = total_of(sources, height - rows, height).astype(BF)
    second = dot_tn(reduced, dout[...])
    split_grads(dred[...], mixed, second, gain_row, wide, keep, send)


def back_first_kernel(count, width, *refs):
    pays, refs = refs[:count], refs[count:]
    carried_after, x_after, mean_after, cross_after, x, mean, weights, probs, mixed = refs[:9]
    reduced, keep, send, wide = refs[9:]
    rank = reduced.shape[1]
    dout, dred = receive_backward(pays, carried_after, x_after, mean_after, cross_after, width)
    second = dot_tn(reduced[...], dout)
    layer_backward(
        dout, dred, x, mean[:, 0:1], layer_of(weights, 0), None, probs, wide.at[pl.ds(2 * rank, 16)],
        None, None,
    )
    split_grads(dred, mixed, second, None, wide, keep, send)


def combine_kernel(sections, *refs):
    kept, swapped = refs[:sections], refs[sections : 2 * sections]
    outs, sums = refs[2 * sections : 3 * sections], refs[3 * sections]
    section = lax.axis_index("pipe")
    for layer in range(sections):
        sums[layer] = (kept[layer][...].astype(F32) + swapped[layer][...].astype(F32)).astype(BF)
    for distance in range(sections):
        outs[distance][...] = sums[section ^ distance]


def finish_kernel(sections, *refs):
    parts = refs[:sections]
    gain, first, second = refs[sections:]
    rank = second.shape[1]
    total = parts[0][...].astype(F32)
    for part in parts[1:]:
        total = total + part[...].astype(F32)
    for block in range(first.shape[1] // HD):
        first[0, block * HD : (block + 1) * HD, :] = total[0:HD, block * rank : (block + 1) * rank]
    second[0] = total[rank : 2 * rank]
    gain[...] = total[2 * rank : 2 * rank + 1]


def per_device(tokens, cotangents, starts, counts, layer_gains, first_map, second_map):
    sections = lax.axis_size("pipe")
    groups = lax.axis_size("z")
    directions, micro_count, length, width = tokens.shape
    micro_local = -(-directions * micro_count // sections)
    rows = groups * micro_local * length
    local = width // groups
    own = first_map.shape[1]
    rank = first_map.shape[2]
    heads = local // HD
    size = block_size(rows)
    blocks = rows // size
    sides = lax.axis_size("core")
    top = sections - 1

    def shifted(value, shift):
        return lax.ppermute(value, "z", [(i, i ^ shift) for i in range(groups)])

    def across(value, distance):
        return lax.ppermute(value, "pipe", [(i, i ^ distance) for i in range(sections)])

    def swapped(value):
        return lax.ppermute(value, "core", [(i, 1 - i) for i in range(sides)])

    def exchange(pay):
        return [pay] + [shifted(pay, place) for place in range(1, groups)]

    token_parts, packed = pack(
        tokens, cotangents, starts, counts, layer_gains, first_map, second_map, groups, micro_local
    )
    mine = [packed] + [across(packed, distance) for distance in range(1, sections)]
    order = [0] + list(range(groups - 1, 0, -1))
    received = [token_parts[0]] + [shifted(token_parts[place], place) for place in order[1:]]
    def shaped(shape, kind=BF):
        return jax.ShapeDtypeStruct(shape, kind)

    def call(kernel, operands, specs, outs, name, **more):
        return pl.pallas_call(
            kernel,
            in_specs=specs,
            out_specs=vmem_specs(len(outs)),
            out_shape=outs,
            compiler_params=PARAMS,
            name=name,
            **more,
        )(*operands)

    received[0], mine[0], mine[1] = call(
        own_kernel,
        (received[0], packed, mine[1]),
        vmem_specs(3),
        [shaped(received[0].shape), shaped(packed.shape), shaped(packed.shape)],
        "own_parts",
    )
    received, mine = lax.optimization_barrier((received, mine))
    theirs = [swapped(part) for part in mine]

    wide_shape = shaped((rows, local))
    mean_shape = shaped((rows, HD), F32)
    rank_shape = shaped((rows, rank))
    cross_shape = shaped((rows, rank), F32)
    probs_shape = shaped((blocks, heads, size, size))
    grads_shape = (sides, 2 * rank + 16, own)
    half_shape = shaped(grads_shape[1:])
    weights_shape = shaped((sections, sides, slice_rows(own), HD))

    x, cot, mask, mean = call(
        functools.partial(arrange_kernel, length, order),
        received,
        vmem_specs(groups),
        [wide_shape, wide_shape, shaped((blocks, size, size)), mean_shape],
        "arrange",
        scratch_shapes=[pltpu.VMEM((rows, HD), BF)],
    )
    last_gram = gram_place(top - 1, top, rows)
    side_rows = last_gram[0] + last_gram[1]
    probs, mixed, pay, weights = call(
        functools.partial(first_kernel, sections),
        (*mine, *theirs, x, mask, mean),
        vmem_specs(2 * sections + 3),
        [probs_shape, wide_shape, shaped((2 * rows + FOLDED, HD)), weights_shape],
        "forward_first",
        scratch_shapes=[pltpu.SemaphoreType.DMA((sections, sides))],
    )
    xs, means, reduceds, crosses = [x], [mean], [], [None]
    all_probs, all_mixed = [probs], [mixed]
    first_pays = pays = exchange(pay)
    side = call(side_kernel, (weights, cot), vmem_specs(2), [shaped((side_rows, HD))], "side")[0]
    arrived = exchange(side)
    for layer in range(1, top):
        operands = (*pays, *((), first_pays, arrived)[min(layer, 3) - 1])
        specs = vmem_specs(len(operands) + 4)
        x, mean, reduced, cross, probs, mixed, pay = call(
            functools.partial(middle_kernel, groups, layer, top, float(width)),
            (*operands, xs[-1], means[-1], mask, weights),
            specs,
            [
                wide_shape,
                mean_shape,
                rank_shape,
                cross_shape,
                probs_shape,
                wide_shape,
                shaped((2 * rows, HD)),
            ],
            "forward_middle",
        )
        xs.append(x)
        means.append(mean)
        reduceds.append(reduced)
        crosses.append(cross)
        all_probs.append(probs)
        all_mixed.append(mixed)
        pays = exchange(pay)

    back_rows = rows + 16 * blocks
    gain_shape = shaped((16, local))
    wide_scratch = [pltpu.VMEM((2 * rank + 16, local), BF)]
    x, mean, reduced, cross, mixed, dred, gain_row, carried, pay = call(
        functools.partial(turn_kernel, groups, top, float(width)),
        (*pays, *arrived, xs[-1], means[-1], mask, weights, cot),
        vmem_specs(2 * groups + 5),
        [
            wide_shape,
            mean_shape,
            rank_shape,
            cross_shape,
            wide_shape,
            rank_shape,
            gain_shape,
            wide_shape,
            shaped((back_rows + rows, HD)),
        ],
        "turn",
        scratch_shapes=[pltpu.VMEM(probs_shape.shape, BF)],
    )
    xs.append(x)
    means.append(mean)
    reduceds.append(reduced)
    crosses.append(cross)
    all_mixed.append(mixed)

    def gradients(layer, sources, dout, dred, gain_row):
        operands = (*sources, dout, dred, all_mixed[layer], gain_row)
        keep, send = call(
            functools.partial(grads_kernel, len(sources)),
            operands,
            vmem_specs(len(operands)),
            [half_shape] * 2,
            "weight_grads",
            scratch_shapes=wide_scratch,
        )
        return keep, send

    pays = exchange(pay)
    halves = [None] * sections
    waiting = [(top, pays, cot, dred, gain_row)]
    for layer in range(top - 1, 0, -1):
        operands = (
            *pays, carried, xs[layer + 1], means[layer + 1], crosses[layer + 1],
            xs[layer], means[layer], weights, all_probs[layer],
        )
        carried, pay, dout, dred, gain_row = call(
            functools.partial(back_kernel, groups, layer, float(width)),
            operands,
            vmem_specs(len(operands)),
            [wide_shape, shaped((back_rows, HD)), wide_shape, rank_shape, gain_shape],
            "backward",
        )
        pays = exchange(pay)
        waiting.append((layer, [reduceds[layer]], dout, dred, gain_row))
        done = [gradients(*item) for item in waiting]
        pays, done = lax.optimization_barrier((pays, done))
        for item, (keep, send) in zip(waiting, done):
            halves[item[0]] = (keep, swapped(send))
        waiting = []
    operands = (
        *pays, carried, xs[1], means[1], crosses[1], xs[0], means[0], weights, all_probs[0],
        all_mixed[0], reduceds[0],
    )
    keep, send = call(
        functools.partial(back_first_kernel, groups, float(width)),
        operands,
        vmem_specs(len(operands)),
        [half_shape] * 2,
        "backward_first",
        scratch_shapes=wide_scratch,
    )
    halves[0] = (keep, swapped(send))

    parts = call(
        functools.partial(combine_kernel, sections),
        [pair[side] for side in range(2) for pair in halves],
        vmem_specs(2 * sections),
        [half_shape] * sections,
        "combine",
        scratch_shapes=[pltpu.VMEM((sections,) + grads_shape[1:], BF)],
    )
    arrived = [parts[0]] + [across(parts[distance], distance) for distance in range(1, sections)]
    gain_grad, first_grad, second_grad = call(
        functools.partial(finish_kernel, sections),
        arrived,
        vmem_specs(sections),
        [
            shaped((1, own), F32),
            shaped((1, own, rank), F32),
            shaped((1, rank, own), F32),
        ],
        "finish",
    )
    return (gain_grad, first_grad, second_grad)


def solution(mesh):
    fine = Mesh(
        mesh.devices.reshape(mesh.shape["pipe"], mesh.shape["dp"] // 2, 2), ("pipe", "z", "core")
    )
    data = ("z", "core")
    in_specs = (
        P(None, data, None, None),
        P(None, data, None, None),
        P(None, data, None),
        P(None, data),
        P("pipe", data),
        P("pipe", data, None),
        P("pipe", None, data),
    )
    out_specs = (P("pipe", data), P("pipe", data, None), P("pipe", None, data))
    mapped = jax.shard_map(
        per_device, mesh=fine, in_specs=in_specs, out_specs=out_specs, check_vma=False
    )

    return mapped
```

```python
import functools

import jax
import jax.numpy as jnp
from jax import lax
from jax.experimental import pallas as pl
from jax.experimental.pallas import tpu as pltpu
from jax.sharding import Mesh, PartitionSpec as P

HD = 128
EPS = 1e-05
FOLDED = HD + 16
BF = jnp.bfloat16
F32 = jnp.float32
PARAMS = pltpu.CompilerParams(vmem_limit_bytes=48 * 1024 * 1024)
PACK_PARAMS = pltpu.CompilerParams(vmem_limit_bytes=60 * 1024 * 1024)


def dot(a, b):
    return jnp.dot(a, b, preferred_element_type=F32)


def dot_nt(a, b):
    return lax.dot_general(a, b, (((1,), (1,)), ((), ())), preferred_element_type=F32)


def dot_tn(a, b):
    return lax.dot_general(a, b, (((0,), (0,)), ((), ())), preferred_element_type=F32)


def two_parts(value):
    high = value.astype(BF)
    return high, (value - high.astype(F32)).astype(BF)


def vmem_specs(count):
    return [pl.BlockSpec(memory_space=pltpu.VMEM)] * count


def layer_of(weights, layer):
    return weights.at[pl.ds(layer, 1)]


def slice_rows(own):
    return 2 * own + 16


def pack_kernel(groups, micro_local, *refs):
    tokens, cotangents, starts, counts, gain, first, second = refs[:7]
    parts, weights = refs[7 : 7 + groups], refs[7 + groups]
    tok, cot, starts_in, counts_in, gain_in, second_in, sems = refs[8 + groups :]
    directions, micro_count, length, width = tokens.shape
    local = width // groups
    own = first.shape[1]
    section = lax.axis_index("pipe")
    group = lax.axis_index("z")
    picks = []
    copies = [
        pltpu.make_async_copy(second.at[0], second_in, sems.at[0]),
        pltpu.make_async_copy(gain, gain_in, sems.at[1]),
        pltpu.make_async_copy(first.at[0], weights.at[pl.ds(0, own)], sems.at[2]),
        pltpu.make_async_copy(starts, starts_in, sems.at[3]),
        pltpu.make_async_copy(counts, counts_in, sems.at[4]),
    ]
    for micro in range(micro_local):
        wanted = section * micro_local + micro
        slot = jnp.minimum(wanted, directions * micro_count - 1)
        direction, place = slot // micro_count, slot % micro_count
        picks.append((wanted < directions * micro_count, direction, place))
        rows = pl.ds(micro * length, length)
        copies.append(
            pltpu.make_async_copy(
                tokens.at[direction, place], tok.at[rows], sems.at[5 + 2 * micro]
            )
        )
        copies.append(
            pltpu.make_async_copy(
                cotangents.at[direction, place], cot.at[rows], sems.at[6 + 2 * micro]
            )
        )
    for copy in copies:
        copy.start()
    for copy in copies[:5]:
        copy.wait()
    weights[own : 2 * own, :] = second_in[...].astype(F32).T.astype(BF)
    gains = [gain_in[0:1, head * HD : (head + 1) * HD].astype(F32) for head in range(own // HD)]
    gains.append(jnp.zeros((16 - own // HD, HD), F32))
    weights[2 * own :, :] = jnp.concatenate(gains, axis=0).astype(BF)
    for copy in copies[5:]:
        copy.wait()
    for micro, (keep, direction, place) in enumerate(picks):
        rows = slice(micro * length, (micro + 1) * length)
        widened = tok[rows, :].astype(F32)
        mean = jnp.mean(widened * widened, axis=1, keepdims=True)
        mean_high, mean_low = two_parts(mean)
        position = lax.broadcasted_iota(jnp.int32, (length, HD), 0)
        document = jnp.zeros((length, HD), jnp.int32)
        for entry in range(starts.shape[2]):
            begun = starts_in[direction, place, entry] <= position
            begun = begun & (entry < counts_in[direction, place])
            document = document + begun.astype(jnp.int32)
        lane = lax.broadcasted_iota(jnp.int32, (length, HD), 1)
        tail = jnp.where(
            lane == 0,
            document.astype(F32),
            jnp.where(lane == 1, mean_high.astype(F32), mean_low.astype(F32)),
        ).astype(BF)
        for shift in range(groups):
            start = pl.multiple_of((group ^ shift) * local, local)
            parts[shift][rows, 0:local] = tok[rows, pl.ds(start, local)]
            cotangent = cot[rows, pl.ds(start, local)]
            parts[shift][rows, local : 2 * local] = jnp.where(
                keep, cotangent, jnp.zeros_like(cotangent)
            )
            parts[shift][rows, 2 * local :] = tail


def pack(tokens, cotangents, starts, counts, gain, first, second, groups, micro_local):
    length, width = tokens.shape[2:]
    own = first.shape[1]
    local = width // groups
    rows = micro_local * length
    shape = jax.ShapeDtypeStruct
    results = pl.pallas_call(
        functools.partial(pack_kernel, groups, micro_local),
        in_specs=[pl.BlockSpec(memory_space=pltpu.HBM)] * 7,
        out_specs=vmem_specs(groups + 1),
        out_shape=[shape((rows, 2 * local + HD), BF)] * groups
        + [shape((slice_rows(own), HD), BF)],
        scratch_shapes=[
            pltpu.VMEM((rows, width), BF),
            pltpu.VMEM((rows, width), BF),
            pltpu.SMEM(starts.shape, jnp.int32),
            pltpu.SMEM(counts.shape, jnp.int32),
            pltpu.VMEM(gain.shape, BF),
            pltpu.VMEM(second.shape[1:], BF),
            pltpu.SemaphoreType.DMA((5 + 2 * micro_local,)),
        ],
        compiler_params=PACK_PARAMS,
        name="pack",
    )(tokens, cotangents, starts, counts, gain, first, second)
    return results[:groups], results[groups]


def head_gain(weights, head):
    own = (weights.shape[2] - 16) // 2
    per_slice = own // HD
    row = 2 * own + head % per_slice
    return weights[0, head // per_slice, row : row + 1, :].astype(F32)


def block_size(rows):
    return HD if rows % HD == 0 else rows


def to_rank(value, weights, at):
    own = (weights.shape[2] - 16) // 2
    total = None
    for side in range(weights.shape[1]):
        term = dot(value[:, side * own : (side + 1) * own], weights[0, side, at : at + own, :])
        total = term if total is None else total + term
    return total


def from_rank(value, weights, at, side):
    own = (weights.shape[2] - 16) // 2
    return dot_nt(value, weights[0, side, at : at + own, :])


def gram(weights):
    own = (weights.shape[2] - 16) // 2
    total = None
    for side in range(weights.shape[1]):
        part = weights[0, side, own : 2 * own, :]
        term = dot_tn(part, part)
        total = term if total is None else total + term
    return total


def attend(x, mean, weights, mask, probs, mixed):
    rows, local = x.shape
    size = block_size(rows)
    factor = lax.rsqrt(mean + EPS)
    heads = range(local // HD)
    gains = [head_gain(weights, head) for head in heads]
    for block in range(rows // size):
        span = slice(block * size, (block + 1) * size)
        allowed = mask[block] > 0
        wide = x[span, :].astype(F32) * factor[span]
        normed = [(wide[:, head * HD : (head + 1) * HD] * gains[head]).astype(BF) for head in heads]
        scores = [dot_nt(value, value) for value in normed]
        raw = [jnp.where(allowed, jnp.exp(score * (1.0 / HD)), 0.0) for score in scores]
        shares = [1.0 / jnp.sum(value, axis=1, keepdims=True) for value in raw]
        prob = [(value * share).astype(BF) for value, share in zip(raw, shares)]
        result = [dot(left, right).astype(BF) for left, right in zip(prob, normed)]
        for head in heads:
            probs[block, head] = prob[head]
            mixed[span, head * HD : (head + 1) * HD] = result[head]


def send_forward(x, weights, mixed, pay):
    rows = x.shape[0]
    own = (weights.shape[2] - 16) // 2
    pay[0:rows, :] = to_rank(mixed[...], weights, 0).astype(BF)
    pay[rows : 2 * rows, :] = to_rank(x[...], weights, own).astype(BF)


def total_of(pays, start, stop):
    total = pays[0][start:stop, :].astype(F32)
    for pay in pays[1:]:
        total = total + pay[start:stop, :].astype(F32)
    return total


def receive_forward(
    pays, gram_total, x_before, mean_before, weights_before, width, x, mean, reduced, cross
):
    rows, local = x_before.shape
    own = (weights_before.shape[2] - 16) // 2
    low_rank = total_of(pays, 0, rows).astype(BF)
    before = total_of(pays, rows, 2 * rows)
    high, low = two_parts(gram_total)
    through = dot(low_rank, high) + dot(low_rank, low)
    wide = low_rank.astype(F32)
    change = jnp.sum(wide * (2.0 * before + through), axis=1, keepdims=True) / width
    new_mean = jnp.maximum(mean_before[:, 0:1] + change, 0.0)
    mean[...] = jnp.broadcast_to(new_mean, mean.shape)
    reduced[...] = low_rank
    cross[...] = before + through
    for side in range(weights_before.shape[1]):
        part = slice(side * own, (side + 1) * own)
        x[:, part] = (
            x_before[:, part].astype(F32) + from_rank(low_rank, weights_before, own, side)
        ).astype(BF)


def own_kernel(part, packed, early, part_out, packed_out, early_out):
    part_out[...] = part[...]
    packed_out[...] = packed[...]
    early_out[...] = early[...]


def arrange_kernel(length, order, *refs):
    groups = len(order)
    received = [refs[order.index(place)] for place in range(groups)]
    x, cot, mask, mean, tails = refs[groups:]
    rows, local = x.shape
    place_rows(received, tails, slice(2 * local, None))
    place_rows(received, x, slice(0, local))
    place_rows(received, cot, slice(local, 2 * local))
    tail = tails[...].astype(F32)
    mean[...] = jnp.broadcast_to(tail[:, 1:2] + tail[:, 2:3], mean.shape)
    build_mask(tail[:, 0:1], mask, block_size(rows), length)


def first_kernel(sections, *refs):
    mine, theirs = refs[:sections], refs[sections : 2 * sections]
    x, mask, mean, probs, mixed, pay, weights, sems = refs[2 * sections :]
    section, core = lax.axis_index("pipe"), lax.axis_index("core")
    rows = x.shape[0]
    copies = []
    for distance in range(sections):
        layer = section ^ distance
        for parts, place in ((mine, core), (theirs, 1 - core)):
            copies.append(
                pltpu.make_async_copy(
                    parts[distance], weights.at[layer, place], sems.at[layer, place]
                )
            )
    for wanted_now in (True, False):
        for distance in range(sections):

            @pl.when((section == distance) == wanted_now)
            def _(distance=distance):
                copies[2 * distance].start()
                copies[2 * distance + 1].start()

    def arrived(layer):
        for place in range(weights.shape[1]):
            pltpu.make_async_copy(mine[0], weights.at[layer, place], sems.at[layer, place]).wait()

    arrived(0)
    own = (weights.shape[2] - 16) // 2
    layers = [layer_of(weights, layer) for layer in range(sections)]
    attend(x, mean[:, 0:1], layers[0], mask, probs, mixed)
    send_forward(x, layers[0], mixed, pay)
    arrived(1)
    pay[2 * rows :, :] = fold_grams(layers[0], layers[1])
    for layer in range(2, sections):
        arrived(layer)


def side_kernel(weights, cot, side):
    rows = cot.shape[0]
    sections = weights.shape[0]
    own = (weights.shape[2] - 16) // 2
    layers = [layer_of(weights, layer) for layer in range(sections)]
    side[0:rows, :] = to_rank(cot[...], layers[-1], own).astype(BF)
    for layer in range(2, sections - 1, 2):
        base, height, folded = gram_place(layer, sections - 1, rows)
        both = fold_grams(layers[layer], layers[layer + 1]) if folded else gram(layers[layer])
        side[base : base + height, :] = both.astype(BF)


def place_rows(received, target, columns):
    rows = received[0].shape[0]
    for shift, part in enumerate(received):
        source = lax.axis_index("z") ^ shift
        target[pl.ds(pl.multiple_of(source * rows, rows), rows), :] = part[:, columns]


def build_mask(document, mask, size, length):
    query = lax.broadcasted_iota(jnp.int32, (size, size), 0)
    key = lax.broadcasted_iota(jnp.int32, (size, size), 1)
    for block in range(mask.shape[0]):
        by_query = jnp.broadcast_to(document[block * size : (block + 1) * size], (size, size))
        by_key = by_query.T
        allowed = (by_query == by_key) & (key <= query) & (query // length == key // length)
        mask[block] = allowed.astype(F32).astype(BF)


def fold_grams(weights, other):
    row, lane = square_places()
    upper, lower = gram(weights), gram(other)
    diagonal = jnp.sum(jnp.where(row == lane, lower, 0.0), axis=0, keepdims=True)
    folded = jnp.where(row <= lane, upper, lower)
    return jnp.concatenate((folded, diagonal, jnp.zeros((15, HD), F32)), axis=0).astype(BF)


def square_places():
    return (
        lax.broadcasted_iota(jnp.int32, (HD, HD), 0),
        lax.broadcasted_iota(jnp.int32, (HD, HD), 1),
    )


def gram_place(layer, top, rows):
    pair = layer // 2
    folded = 2 * pair + 1 < top
    base = 2 * rows if pair == 0 else rows + FOLDED * (pair - 1)
    return base, FOLDED if folded else HD, folded


def gram_of(sources, layer, top, rows):
    base, height, folded = gram_place(layer, top, rows)
    total = total_of(sources, base, base + height)
    if not folded:
        return total
    row, lane = square_places()
    square = total[0:HD]
    if layer % 2 == 0:
        return jnp.where(row <= lane, square, square.T)
    lower = jnp.where(row > lane, square, square.T)
    return jnp.where(row == lane, total[HD : HD + 1], lower)


def middle_kernel(count, layer, top, width, *refs):
    pays, sources, refs = refs[:count], refs[count : 2 * count], refs[2 * count :]
    if layer == 1:
        sources, refs = pays, sources + refs
    x_before, mean_before, mask, weights = refs[:4]
    x, mean, reduced, cross, probs, mixed, pay = refs[4:]
    weights_before, weights = layer_of(weights, layer - 1), layer_of(weights, layer)
    receive_forward(
        pays, gram_of(sources, layer - 1, top, x.shape[0]), x_before, mean_before, weights_before,
        width, x, mean, reduced, cross,
    )
    attend(x, mean[:, 0:1], weights, mask, probs, mixed)
    send_forward(x, weights, mixed, pay)


def layer_backward(dout, dred, x, mean, weights, weights_before, probs, gain_row, carried, pay):
    rows, local = x.shape
    size = block_size(rows)
    own = (weights.shape[2] - 16) // 2
    per_slice = own // HD
    factor = lax.rsqrt(mean + EPS)
    back_mixed = [
        from_rank(dred, weights, 0, side).astype(BF) for side in range(weights.shape[1])
    ]
    heads = range(local // HD)
    gains = [head_gain(weights, head) for head in heads]
    gain_sums = [None] * len(heads)
    for block in range(rows // size):
        span = slice(block * size, (block + 1) * size)
        scale = factor[span]
        parts = [slice(head * HD, (head + 1) * HD) for head in heads]
        wide = [x[span, part].astype(F32) for part in parts]
        prob = [probs[block, head] for head in heads]
        onward = [None if carried is None else dout[span, part].astype(F32) for part in parts]
        unit = [value * scale for value in wide]
        normed = [(value * gain).astype(BF) for value, gain in zip(unit, gains)]
        upstream = []
        for head in heads:
            inner = (head % per_slice) * HD
            upstream.append(back_mixed[head // per_slice][span, inner : inner + HD])
        back_prob = [dot_nt(left, right) for left, right in zip(upstream, normed)]
        through = [dot_tn(left, right) for left, right in zip(prob, upstream)]
        both = []
        for head in heads:
            prob_wide = prob[head].astype(F32)
            inner_sum = jnp.sum(back_prob[head] * prob_wide, axis=1, keepdims=True)
            back_score = prob_wide * (back_prob[head] - inner_sum) * (1.0 / HD)
            both.append((back_score + back_score.T).astype(BF))
        back_normed = [
            (through[head] + dot(both[head], normed[head])).astype(BF).astype(F32) for head in heads
        ]
        norm_dot = jnp.zeros((size, HD), F32)
        for head in heads:
            term = jnp.sum(back_normed[head] * unit[head], axis=0, keepdims=True)
            gain_sums[head] = term if gain_sums[head] is None else gain_sums[head] + term
            if carried is not None:
                scaled = back_normed[head] * gains[head]
                norm_dot = norm_dot + scaled * wide[head]
                carried[span, parts[head]] = (onward[head] + scaled * scale).astype(BF)
        if carried is not None:
            column = jnp.broadcast_to(jnp.sum(norm_dot, axis=1, keepdims=True), (size, size))
            line = column.T[0:1, :]
            high, low = two_parts(line)
            base = rows + 16 * block
            pay[base : base + 16, :] = jnp.concatenate(
                (high.astype(F32), low.astype(F32), jnp.zeros((14, size), F32)), axis=0
            ).astype(BF)
    zeros = jnp.zeros((15, HD), F32)
    for head in heads:
        gain_row[:, head * HD : (head + 1) * HD] = jnp.concatenate(
            (gain_sums[head], zeros), axis=0
        ).astype(BF)
    if carried is not None:
        pay[0:rows, :] = to_rank(carried[...], weights_before, own).astype(BF)


def turn_kernel(count, layer, width, *refs):
    pays, sides, refs = refs[:count], refs[count : 2 * count], refs[2 * count :]
    x_before, mean_before, mask, weights, cot = refs[:5]
    x, mean, reduced, cross, mixed, dred_out, gain_row, carried, pay, probs = refs[5:]
    rows = x.shape[0]
    weights_before, weights = layer_of(weights, layer - 1), layer_of(weights, layer)
    receive_forward(
        pays, gram_of(sides, layer - 1, layer, rows), x_before, mean_before, weights_before,
        width, x, mean, reduced, cross,
    )
    attend(x, mean[:, 0:1], weights, mask, probs, mixed)
    dred = total_of(sides, 0, rows).astype(BF)
    dred_out[...] = dred
    layer_backward(
        cot[...], dred, x, mean[:, 0:1], weights, weights_before, probs, gain_row, carried, pay
    )
    pay[pay.shape[0] - rows :, :] = to_rank(mixed[...], weights, 0).astype(BF)


def receive_backward(pays, carried_after, x_after, mean_after, cross_after, width):
    rows = x_after.shape[0]
    size = block_size(rows)
    douts, dreds = [], []
    for block in range(rows // size):
        span = slice(block * size, (block + 1) * size)
        base = rows + 16 * block
        lines = total_of(pays, base, base + 16)
        column = jnp.broadcast_to(lines[0:1] + lines[1:2], (size, size)).T
        factor = lax.rsqrt(mean_after[span, 0:1] + EPS)
        pull = column[:, 0:1] * (factor * factor * factor / width)
        own_total = total_of(pays, block * size, (block + 1) * size)
        dreds.append((own_total - cross_after[span, :] * pull).astype(BF))
        douts.append(
            (carried_after[span, :].astype(F32) - x_after[span, :].astype(F32) * pull).astype(BF)
        )
    if len(douts) == 1:
        return douts[0], dreds[0]
    return jnp.concatenate(douts, axis=0), jnp.concatenate(dreds, axis=0)


def back_kernel(count, layer, width, *refs):
    pays, refs = refs[:count], refs[count:]
    carried_after, x_after, mean_after, cross_after, x, mean, weights, probs = refs[:8]
    carried, pay, dout_out, dred_out, gain_row = refs[8:]
    dout, dred = receive_backward(pays, carried_after, x_after, mean_after, cross_after, width)
    layer_backward(
        dout, dred, x, mean[:, 0:1], layer_of(weights, layer), layer_of(weights, layer - 1), probs,
        gain_row, carried, pay,
    )
    dout_out[...] = dout
    dred_out[...] = dred


def split_grads(dred, mixed, reduced, dout, wide, keep, send):
    rank = reduced.shape[1]
    own = keep.shape[1]
    core = lax.axis_index("core")
    second = dot_tn(reduced, dout)
    for head in range(mixed.shape[1] // HD):
        part = slice(head * HD, (head + 1) * HD)
        wide[0:HD, head * rank : (head + 1) * rank] = dot_tn(mixed[:, part], dred).astype(BF)
    wide[rank:, :] = second.astype(BF)
    keep[...] = wide[:, pl.ds(pl.multiple_of(core * own, own), own)]
    send[...] = wide[:, pl.ds(pl.multiple_of((1 - core) * own, own), own)]


def grads_kernel(count, *refs):
    sources, refs = refs[:count], refs[count:]
    dout, dred, mixed, keep, send, wide = refs
    rows = dout.shape[0]
    height = sources[0].shape[0]
    reduced = total_of(sources, height - rows, height).astype(BF)
    split_grads(dred[...], mixed, reduced, dout[...], wide, keep, send)


def grads_first_kernel(count, width, *refs):
    pays, refs = refs[:count], refs[count:]
    carried_after, x_after, mean_after, cross_after, mixed, reduced = refs[:6]
    keep, send, dout_out, dred_out, wide = refs[6:]
    dout, dred = receive_backward(pays, carried_after, x_after, mean_after, cross_after, width)
    split_grads(dred, mixed, reduced[...], dout, wide, keep, send)
    dout_out[...] = dout
    dred_out[...] = dred


def back_first_kernel(dout, dred, x, mean, weights, probs, gain_row):
    layer_backward(
        dout[...], dred[...], x, mean[:, 0:1], layer_of(weights, 0), None, probs, gain_row, None, None
    )


def split_gains_kernel(sections, *refs):
    rows, keep, send = refs[:sections], refs[sections], refs[sections + 1]
    own = keep.shape[1]
    core = lax.axis_index("core")
    for layer, row in enumerate(rows):
        span = slice(layer * 16, (layer + 1) * 16)
        keep[span, :] = row[:, pl.ds(pl.multiple_of(core * own, own), own)]
        send[span, :] = row[:, pl.ds(pl.multiple_of((1 - core) * own, own), own)]


def combine_gains_kernel(keep, swapped, *outs):
    section = lax.axis_index("pipe")
    for distance, out in enumerate(outs):
        span = pl.ds(pl.multiple_of((section ^ distance) * 16, 16), 16)
        out[...] = (keep[span, :].astype(F32) + swapped[span, :].astype(F32)).astype(BF)


def combine_kernel(sections, *refs):
    kept, swapped = refs[:sections], refs[sections : 2 * sections]
    outs, sums = refs[2 * sections : 3 * sections], refs[3 * sections]
    section = lax.axis_index("pipe")
    for layer in range(sections):
        sums[layer] = (kept[layer][...].astype(F32) + swapped[layer][...].astype(F32)).astype(BF)
    for distance in range(sections):
        outs[distance][...] = sums[section ^ distance]


def finish_kernel(sections, *refs):
    parts, gain_parts = refs[:sections], refs[sections : 2 * sections]
    gain, first, second = refs[2 * sections :]
    rank = second.shape[1]
    total = parts[0][...].astype(F32)
    for part in parts[1:]:
        total = total + part[...].astype(F32)
    for block in range(first.shape[1] // HD):
        first[0, block * HD : (block + 1) * HD, :] = total[0:HD, block * rank : (block + 1) * rank]
    second[0] = total[rank : 2 * rank]
    gain[...] = total_of(gain_parts, 0, 16)[0:1]


def per_device(tokens, cotangents, starts, counts, layer_gains, first_map, second_map):
    sections = lax.axis_size("pipe")
    groups = lax.axis_size("z")
    directions, micro_count, length, width = tokens.shape
    micro_local = -(-directions * micro_count // sections)
    rows = groups * micro_local * length
    local = width // groups
    own = first_map.shape[1]
    rank = first_map.shape[2]
    heads = local // HD
    size = block_size(rows)
    blocks = rows // size
    sides = lax.axis_size("core")
    top = sections - 1

    def shifted(value, shift):
        return lax.ppermute(value, "z", [(i, i ^ shift) for i in range(groups)])

    def across(value, distance):
        return lax.ppermute(value, "pipe", [(i, i ^ distance) for i in range(sections)])

    def swapped(value):
        return lax.ppermute(value, "core", [(i, 1 - i) for i in range(sides)])

    def exchange(pay):
        return [pay] + [shifted(pay, place) for place in range(1, groups)]

    token_parts, packed = pack(
        tokens, cotangents, starts, counts, layer_gains, first_map, second_map, groups, micro_local
    )
    mine = [packed] + [across(packed, distance) for distance in range(1, sections)]
    order = [0] + list(range(groups - 1, 0, -1))
    received = [token_parts[0]] + [shifted(token_parts[place], place) for place in order[1:]]
    def shaped(shape, kind=BF):
        return jax.ShapeDtypeStruct(shape, kind)

    def call(kernel, operands, specs, outs, name, **more):
        return pl.pallas_call(
            kernel,
            in_specs=specs,
            out_specs=vmem_specs(len(outs)),
            out_shape=outs,
            compiler_params=PARAMS,
            name=name,
            **more,
        )(*operands)

    received[0], mine[0], mine[1] = call(
        own_kernel,
        (received[0], packed, mine[1]),
        vmem_specs(3),
        [shaped(received[0].shape), shaped(packed.shape), shaped(packed.shape)],
        "own_parts",
    )
    received, mine = lax.optimization_barrier((received, mine))
    theirs = [swapped(part) for part in mine]

    wide_shape = shaped((rows, local))
    mean_shape = shaped((rows, HD), F32)
    rank_shape = shaped((rows, rank))
    cross_shape = shaped((rows, rank), F32)
    probs_shape = shaped((blocks, heads, size, size))
    half_shape = shaped((2 * rank, own))
    gain_half = shaped((sections * 16, own))
    weights_shape = shaped((sections, sides, slice_rows(own), HD))

    x, cot, mask, mean = call(
        functools.partial(arrange_kernel, length, order),
        received,
        vmem_specs(groups),
        [wide_shape, wide_shape, shaped((blocks, size, size)), mean_shape],
        "arrange",
        scratch_shapes=[pltpu.VMEM((rows, HD), BF)],
    )
    last_gram = gram_place(top - 1, top, rows)
    side_rows = last_gram[0] + last_gram[1]
    probs, mixed, pay, weights = call(
        functools.partial(first_kernel, sections),
        (*mine, *theirs, x, mask, mean),
        vmem_specs(2 * sections + 3),
        [probs_shape, wide_shape, shaped((2 * rows + FOLDED, HD)), weights_shape],
        "forward_first",
        scratch_shapes=[pltpu.SemaphoreType.DMA((sections, sides))],
    )
    xs, means, reduceds, crosses = [x], [mean], [], [None]
    all_probs, all_mixed = [probs], [mixed]
    first_pays = pays = exchange(pay)
    side = call(side_kernel, (weights, cot), vmem_specs(2), [shaped((side_rows, HD))], "side")[0]
    arrived = exchange(side)
    for layer in range(1, top):
        operands = (*pays, *((), first_pays, arrived)[min(layer, 3) - 1])
        specs = vmem_specs(len(operands) + 4)
        x, mean, reduced, cross, probs, mixed, pay = call(
            functools.partial(middle_kernel, groups, layer, top, float(width)),
            (*operands, xs[-1], means[-1], mask, weights),
            specs,
            [
                wide_shape,
                mean_shape,
                rank_shape,
                cross_shape,
                probs_shape,
                wide_shape,
                shaped((2 * rows, HD)),
            ],
            "forward_middle",
        )
        xs.append(x)
        means.append(mean)
        reduceds.append(reduced)
        crosses.append(cross)
        all_probs.append(probs)
        all_mixed.append(mixed)
        pays = exchange(pay)

    back_rows = rows + 16 * blocks
    gain_shape = shaped((16, local))
    wide_scratch = [pltpu.VMEM((2 * rank, local), BF)]
    x, mean, reduced, cross, mixed, dred, gain_row, carried, pay = call(
        functools.partial(turn_kernel, groups, top, float(width)),
        (*pays, *arrived, xs[-1], means[-1], mask, weights, cot),
        vmem_specs(2 * groups + 5),
        [
            wide_shape,
            mean_shape,
            rank_shape,
            cross_shape,
            wide_shape,
            rank_shape,
            gain_shape,
            wide_shape,
            shaped((back_rows + rows, HD)),
        ],
        "turn",
        scratch_shapes=[pltpu.VMEM(probs_shape.shape, BF)],
    )
    xs.append(x)
    means.append(mean)
    reduceds.append(reduced)
    crosses.append(cross)
    all_mixed.append(mixed)

    def gradients(layer, sources, dout, dred):
        operands = (*sources, dout, dred, all_mixed[layer])
        keep, send = call(
            functools.partial(grads_kernel, len(sources)),
            operands,
            vmem_specs(len(operands)),
            [half_shape] * 2,
            "weight_grads",
            scratch_shapes=wide_scratch,
        )
        return keep, send

    pays = exchange(pay)
    halves = [None] * sections
    waiting = [(top, pays, cot, dred)]
    gain_rows = [gain_row]
    for layer in range(top - 1, 0, -1):
        operands = (
            *pays, carried, xs[layer + 1], means[layer + 1], crosses[layer + 1],
            xs[layer], means[layer], weights, all_probs[layer],
        )
        carried, pay, dout, dred, gain_row = call(
            functools.partial(back_kernel, groups, layer, float(width)),
            operands,
            vmem_specs(len(operands)),
            [wide_shape, shaped((back_rows, HD)), wide_shape, rank_shape, gain_shape],
            "backward",
        )
        pays = exchange(pay)
        waiting.append((layer, [reduceds[layer]], dout, dred))
        gain_rows.insert(0, gain_row)
        done = [gradients(*item) for item in waiting]
        pays, done = lax.optimization_barrier((pays, done))
        for item, (keep, send) in zip(waiting, done):
            halves[item[0]] = (keep, swapped(send))
        waiting = []
    operands = (*pays, carried, xs[1], means[1], crosses[1], all_mixed[0], reduceds[0])
    keep, send, dout, dred = call(
        functools.partial(grads_first_kernel, groups, float(width)),
        operands,
        vmem_specs(len(operands)),
        [half_shape, half_shape, wide_shape, rank_shape],
        "weight_grads_first",
        scratch_shapes=wide_scratch,
    )
    halves[0] = (keep, swapped(send))
    gain_row = call(
        back_first_kernel,
        (dout, dred, xs[0], means[0], weights, all_probs[0]),
        vmem_specs(6),
        [gain_shape],
        "backward_first",
    )[0]
    gain_keep, gain_send = call(
        functools.partial(split_gains_kernel, sections),
        (gain_row, *gain_rows),
        vmem_specs(sections),
        [gain_half] * 2,
        "split_gains",
    )
    gain_parts = call(
        combine_gains_kernel,
        (gain_keep, swapped(gain_send)),
        vmem_specs(2),
        [shaped((16, own))] * sections,
        "combine_gains",
    )

    parts = call(
        functools.partial(combine_kernel, sections),
        [pair[side] for side in range(2) for pair in halves],
        vmem_specs(2 * sections),
        [half_shape] * sections,
        "combine",
        scratch_shapes=[pltpu.VMEM((sections,) + half_shape.shape, BF)],
    )
    arrived = [parts[0]] + [across(parts[distance], distance) for distance in range(1, sections)]
    arrived += [gain_parts[0]]
    arrived += [across(gain_parts[distance], distance) for distance in range(1, sections)]
    gain_grad, first_grad, second_grad = call(
        functools.partial(finish_kernel, sections),
        arrived,
        vmem_specs(2 * sections),
        [
            shaped((1, own), F32),
            shaped((1, own, rank), F32),
            shaped((1, rank, own), F32),
        ],
        "finish",
    )
    return (gain_grad, first_grad, second_grad)


def solution(mesh):
    fine = Mesh(
        mesh.devices.reshape(mesh.shape["pipe"], mesh.shape["dp"] // 2, 2), ("pipe", "z", "core")
    )
    data = ("z", "core")
    in_specs = (
        P(None, data, None, None),
        P(None, data, None, None),
        P(None, data, None),
        P(None, data),
        P("pipe", data),
        P("pipe", data, None),
        P("pipe", None, data),
    )
    out_specs = (P("pipe", data), P("pipe", data, None), P("pipe", None, data))
    mapped = jax.shard_map(
        per_device, mesh=fine, in_specs=in_specs, out_specs=out_specs, check_vma=False
    )

    return mapped
```

```python
import functools

import jax
import jax.numpy as jnp
from jax import lax
from jax.experimental import pallas as pl
from jax.experimental.pallas import tpu as pltpu
from jax.sharding import Mesh, PartitionSpec as P

HD = 128
EPS = 1e-05
FOLDED = HD + 16
BF = jnp.bfloat16
F32 = jnp.float32
PARAMS = pltpu.CompilerParams(vmem_limit_bytes=48 * 1024 * 1024)
PACK_PARAMS = pltpu.CompilerParams(vmem_limit_bytes=60 * 1024 * 1024)


def dot(a, b):
    return jnp.dot(a, b, preferred_element_type=F32)


def dot_nt(a, b):
    return lax.dot_general(a, b, (((1,), (1,)), ((), ())), preferred_element_type=F32)


def dot_tn(a, b):
    return lax.dot_general(a, b, (((0,), (0,)), ((), ())), preferred_element_type=F32)


def two_parts(value):
    high = value.astype(BF)
    return high, (value - high.astype(F32)).astype(BF)


def vmem_specs(count):
    return [pl.BlockSpec(memory_space=pltpu.VMEM)] * count


def layer_of(weights, layer):
    return weights.at[pl.ds(layer, 1)]


def slice_rows(own):
    return 2 * own + 16


def pack_kernel(groups, micro_local, *refs):
    tokens, cotangents, starts, counts, gain, first, second = refs[:7]
    parts, weights = refs[7 : 7 + groups], refs[7 + groups]
    tok, cot, starts_in, counts_in, gain_in, second_in, sems = refs[8 + groups :]
    directions, micro_count, length, width = tokens.shape
    local = width // groups
    own = first.shape[1]
    section = lax.axis_index("pipe")
    group = lax.axis_index("z")
    picks = []
    copies = [
        pltpu.make_async_copy(second.at[0], second_in, sems.at[0]),
        pltpu.make_async_copy(gain, gain_in, sems.at[1]),
        pltpu.make_async_copy(first.at[0], weights.at[pl.ds(0, own)], sems.at[2]),
        pltpu.make_async_copy(starts, starts_in, sems.at[3]),
        pltpu.make_async_copy(counts, counts_in, sems.at[4]),
    ]
    for micro in range(micro_local):
        wanted = section * micro_local + micro
        slot = jnp.minimum(wanted, directions * micro_count - 1)
        direction, place = slot // micro_count, slot % micro_count
        picks.append((wanted < directions * micro_count, direction, place))
        rows = pl.ds(micro * length, length)
        copies.append(
            pltpu.make_async_copy(
                tokens.at[direction, place], tok.at[rows], sems.at[5 + 2 * micro]
            )
        )
        copies.append(
            pltpu.make_async_copy(
                cotangents.at[direction, place], cot.at[rows], sems.at[6 + 2 * micro]
            )
        )
    for copy in copies:
        copy.start()
    for copy in copies[:5]:
        copy.wait()
    weights[own : 2 * own, :] = second_in[...].astype(F32).T.astype(BF)
    gains = [gain_in[0:1, head * HD : (head + 1) * HD].astype(F32) for head in range(own // HD)]
    gains.append(jnp.zeros((16 - own // HD, HD), F32))
    weights[2 * own :, :] = jnp.concatenate(gains, axis=0).astype(BF)
    for copy in copies[5:]:
        copy.wait()
    for micro, (keep, direction, place) in enumerate(picks):
        rows = slice(micro * length, (micro + 1) * length)
        widened = tok[rows, :].astype(F32)
        mean = jnp.mean(widened * widened, axis=1, keepdims=True)
        mean_high, mean_low = two_parts(mean)
        position = lax.broadcasted_iota(jnp.int32, (length, HD), 0)
        document = jnp.zeros((length, HD), jnp.int32)
        for entry in range(starts.shape[2]):
            begun = starts_in[direction, place, entry] <= position
            begun = begun & (entry < counts_in[direction, place])
            document = document + begun.astype(jnp.int32)
        lane = lax.broadcasted_iota(jnp.int32, (length, HD), 1)
        tail = jnp.where(
            lane == 0,
            document.astype(F32),
            jnp.where(lane == 1, mean_high.astype(F32), mean_low.astype(F32)),
        ).astype(BF)
        for shift in range(groups):
            start = pl.multiple_of((group ^ shift) * local, local)
            parts[shift][rows, 0:local] = tok[rows, pl.ds(start, local)]
            cotangent = cot[rows, pl.ds(start, local)]
            parts[shift][rows, local : 2 * local] = jnp.where(
                keep, cotangent, jnp.zeros_like(cotangent)
            )
            parts[shift][rows, 2 * local :] = tail


def pack(tokens, cotangents, starts, counts, gain, first, second, groups, micro_local):
    length, width = tokens.shape[2:]
    own = first.shape[1]
    local = width // groups
    rows = micro_local * length
    shape = jax.ShapeDtypeStruct
    results = pl.pallas_call(
        functools.partial(pack_kernel, groups, micro_local),
        in_specs=[pl.BlockSpec(memory_space=pltpu.HBM)] * 7,
        out_specs=vmem_specs(groups + 1),
        out_shape=[shape((rows, 2 * local + HD), BF)] * groups
        + [shape((slice_rows(own), HD), BF)],
        scratch_shapes=[
            pltpu.VMEM((rows, width), BF),
            pltpu.VMEM((rows, width), BF),
            pltpu.SMEM(starts.shape, jnp.int32),
            pltpu.SMEM(counts.shape, jnp.int32),
            pltpu.VMEM(gain.shape, BF),
            pltpu.VMEM(second.shape[1:], BF),
            pltpu.SemaphoreType.DMA((5 + 2 * micro_local,)),
        ],
        compiler_params=PACK_PARAMS,
        name="pack",
    )(tokens, cotangents, starts, counts, gain, first, second)
    return results[:groups], results[groups]


def head_gain(weights, head):
    own = (weights.shape[2] - 16) // 2
    per_slice = own // HD
    row = 2 * own + head % per_slice
    return weights[0, head // per_slice, row : row + 1, :].astype(F32)


def block_size(rows):
    return HD if rows % HD == 0 else rows


def to_rank(value, weights, at):
    own = (weights.shape[2] - 16) // 2
    total = None
    for side in range(weights.shape[1]):
        term = dot(value[:, side * own : (side + 1) * own], weights[0, side, at : at + own, :])
        total = term if total is None else total + term
    return total


def from_rank(value, weights, at, side):
    own = (weights.shape[2] - 16) // 2
    return dot_nt(value, weights[0, side, at : at + own, :])


def gram(weights):
    own = (weights.shape[2] - 16) // 2
    total = None
    for side in range(weights.shape[1]):
        part = weights[0, side, own : 2 * own, :]
        term = dot_tn(part, part)
        total = term if total is None else total + term
    return total


def attend(x, mean, weights, mask, probs, mixed):
    rows, local = x.shape
    size = block_size(rows)
    factor = lax.rsqrt(mean + EPS)
    heads = range(local // HD)
    gains = [head_gain(weights, head) for head in heads]
    for block in range(rows // size):
        span = slice(block * size, (block + 1) * size)
        allowed = mask[block] > 0
        wide = x[span, :].astype(F32) * factor[span]
        normed = [(wide[:, head * HD : (head + 1) * HD] * gains[head]).astype(BF) for head in heads]
        scores = [dot_nt(value, value) for value in normed]
        raw = [jnp.where(allowed, jnp.exp(score * (1.0 / HD)), 0.0) for score in scores]
        shares = [1.0 / jnp.sum(value, axis=1, keepdims=True) for value in raw]
        prob = [(value * share).astype(BF) for value, share in zip(raw, shares)]
        result = [dot(left, right).astype(BF) for left, right in zip(prob, normed)]
        for head in heads:
            probs[block, head] = prob[head]
            mixed[span, head * HD : (head + 1) * HD] = result[head]


def send_forward(x, weights, mixed, pay):
    rows = x.shape[0]
    own = (weights.shape[2] - 16) // 2
    pay[0:rows, :] = to_rank(mixed[...], weights, 0).astype(BF)
    pay[rows : 2 * rows, :] = to_rank(x[...], weights, own).astype(BF)


def total_of(pays, start, stop):
    total = pays[0][start:stop, :].astype(F32)
    for pay in pays[1:]:
        total = total + pay[start:stop, :].astype(F32)
    return total


def receive_forward(
    pays, gram_total, x_before, mean_before, weights_before, width, x, mean, reduced, cross
):
    rows, local = x_before.shape
    own = (weights_before.shape[2] - 16) // 2
    low_rank = total_of(pays, 0, rows).astype(BF)
    before = total_of(pays, rows, 2 * rows)
    high, low = two_parts(gram_total)
    through = dot(low_rank, high) + dot(low_rank, low)
    wide = low_rank.astype(F32)
    change = jnp.sum(wide * (2.0 * before + through), axis=1, keepdims=True) / width
    new_mean = jnp.maximum(mean_before[:, 0:1] + change, 0.0)
    mean[...] = jnp.broadcast_to(new_mean, mean.shape)
    reduced[...] = low_rank
    cross[...] = before + through
    for side in range(weights_before.shape[1]):
        part = slice(side * own, (side + 1) * own)
        x[:, part] = (
            x_before[:, part].astype(F32) + from_rank(low_rank, weights_before, own, side)
        ).astype(BF)


def own_kernel(part, packed, early, part_out, packed_out, early_out):
    part_out[...] = part[...]
    packed_out[...] = packed[...]
    early_out[...] = early[...]


def arrange_kernel(length, order, *refs):
    groups = len(order)
    received = [refs[order.index(place)] for place in range(groups)]
    x, cot, mask, mean, tails = refs[groups:]
    rows, local = x.shape
    place_rows(received, tails, slice(2 * local, None))
    place_rows(received, x, slice(0, local))
    place_rows(received, cot, slice(local, 2 * local))
    tail = tails[...].astype(F32)
    mean[...] = jnp.broadcast_to(tail[:, 1:2] + tail[:, 2:3], mean.shape)
    build_mask(tail[:, 0:1], mask, block_size(rows), length)


def first_kernel(sections, *refs):
    mine, theirs = refs[:sections], refs[sections : 2 * sections]
    x, mask, mean, probs, mixed, pay, weights, sems = refs[2 * sections :]
    section, core = lax.axis_index("pipe"), lax.axis_index("core")
    rows = x.shape[0]
    copies = []
    for distance in range(sections):
        layer = section ^ distance
        for parts, place in ((mine, core), (theirs, 1 - core)):
            copies.append(
                pltpu.make_async_copy(
                    parts[distance], weights.at[layer, place], sems.at[layer, place]
                )
            )
    for wanted_now in (True, False):
        for distance in range(sections):

            @pl.when((section == distance) == wanted_now)
            def _(distance=distance):
                copies[2 * distance].start()
                copies[2 * distance + 1].start()

    def arrived(layer):
        for place in range(weights.shape[1]):
            pltpu.make_async_copy(mine[0], weights.at[layer, place], sems.at[layer, place]).wait()

    arrived(0)
    own = (weights.shape[2] - 16) // 2
    layers = [layer_of(weights, layer) for layer in range(sections)]
    attend(x, mean[:, 0:1], layers[0], mask, probs, mixed)
    send_forward(x, layers[0], mixed, pay)
    arrived(1)
    pay[2 * rows :, :] = fold_grams(layers[0], layers[1])
    for layer in range(2, sections):
        arrived(layer)


def side_kernel(weights, cot, side):
    rows = cot.shape[0]
    sections = weights.shape[0]
    own = (weights.shape[2] - 16) // 2
    layers = [layer_of(weights, layer) for layer in range(sections)]
    side[0:rows, :] = to_rank(cot[...], layers[-1], own).astype(BF)
    for layer in range(2, sections - 1, 2):
        base, height, folded = gram_place(layer, sections - 1, rows)
        both = fold_grams(layers[layer], layers[layer + 1]) if folded else gram(layers[layer])
        side[base : base + height, :] = both.astype(BF)


def place_rows(received, target, columns):
    rows = received[0].shape[0]
    for shift, part in enumerate(received):
        source = lax.axis_index("z") ^ shift
        target[pl.ds(pl.multiple_of(source * rows, rows), rows), :] = part[:, columns]


def build_mask(document, mask, size, length):
    query = lax.broadcasted_iota(jnp.int32, (size, size), 0)
    key = lax.broadcasted_iota(jnp.int32, (size, size), 1)
    for block in range(mask.shape[0]):
        by_query = jnp.broadcast_to(document[block * size : (block + 1) * size], (size, size))
        by_key = by_query.T
        allowed = (by_query == by_key) & (key <= query) & (query // length == key // length)
        mask[block] = allowed.astype(F32).astype(BF)


def fold_grams(weights, other):
    row, lane = square_places()
    upper, lower = gram(weights), gram(other)
    diagonal = jnp.sum(jnp.where(row == lane, lower, 0.0), axis=0, keepdims=True)
    folded = jnp.where(row <= lane, upper, lower)
    return jnp.concatenate((folded, diagonal, jnp.zeros((15, HD), F32)), axis=0).astype(BF)


def square_places():
    return (
        lax.broadcasted_iota(jnp.int32, (HD, HD), 0),
        lax.broadcasted_iota(jnp.int32, (HD, HD), 1),
    )


def gram_place(layer, top, rows):
    pair = layer // 2
    folded = 2 * pair + 1 < top
    base = 2 * rows if pair == 0 else rows + FOLDED * (pair - 1)
    return base, FOLDED if folded else HD, folded


def gram_of(sources, layer, top, rows):
    base, height, folded = gram_place(layer, top, rows)
    total = total_of(sources, base, base + height)
    if not folded:
        return total
    row, lane = square_places()
    square = total[0:HD]
    if layer % 2 == 0:
        return jnp.where(row <= lane, square, square.T)
    lower = jnp.where(row > lane, square, square.T)
    return jnp.where(row == lane, total[HD : HD + 1], lower)


def middle_kernel(count, layer, top, width, *refs):
    pays, sources, refs = refs[:count], refs[count : 2 * count], refs[2 * count :]
    if layer == 1:
        sources, refs = pays, sources + refs
    x_before, mean_before, mask, weights = refs[:4]
    x, mean, reduced, cross, probs, mixed, pay = refs[4:]
    weights_before, weights = layer_of(weights, layer - 1), layer_of(weights, layer)
    receive_forward(
        pays, gram_of(sources, layer - 1, top, x.shape[0]), x_before, mean_before, weights_before,
        width, x, mean, reduced, cross,
    )
    attend(x, mean[:, 0:1], weights, mask, probs, mixed)
    send_forward(x, weights, mixed, pay)


def layer_backward(dout, dred, x, mean, weights, weights_before, probs, gain_row, carried, pay):
    rows, local = x.shape
    size = block_size(rows)
    own = (weights.shape[2] - 16) // 2
    per_slice = own // HD
    factor = lax.rsqrt(mean + EPS)
    back_mixed = [
        from_rank(dred, weights, 0, side).astype(BF) for side in range(weights.shape[1])
    ]
    heads = range(local // HD)
    gains = [head_gain(weights, head) for head in heads]
    gain_sums = [None] * len(heads)
    for block in range(rows // size):
        span = slice(block * size, (block + 1) * size)
        scale = factor[span]
        parts = [slice(head * HD, (head + 1) * HD) for head in heads]
        wide = [x[span, part].astype(F32) for part in parts]
        prob = [probs[block, head] for head in heads]
        onward = [None if carried is None else dout[span, part].astype(F32) for part in parts]
        unit = [value * scale for value in wide]
        normed = [(value * gain).astype(BF) for value, gain in zip(unit, gains)]
        upstream = []
        for head in heads:
            inner = (head % per_slice) * HD
            upstream.append(back_mixed[head // per_slice][span, inner : inner + HD])
        back_prob = [dot_nt(left, right) for left, right in zip(upstream, normed)]
        through = [dot_tn(left, right) for left, right in zip(prob, upstream)]
        both = []
        for head in heads:
            prob_wide = prob[head].astype(F32)
            inner_sum = jnp.sum(back_prob[head] * prob_wide, axis=1, keepdims=True)
            back_score = prob_wide * (back_prob[head] - inner_sum) * (1.0 / HD)
            both.append((back_score + back_score.T).astype(BF))
        back_normed = [
            (through[head] + dot(both[head], normed[head])).astype(BF).astype(F32) for head in heads
        ]
        norm_dot = jnp.zeros((size, HD), F32)
        for head in heads:
            term = jnp.sum(back_normed[head] * unit[head], axis=0, keepdims=True)
            gain_sums[head] = term if gain_sums[head] is None else gain_sums[head] + term
            if carried is not None:
                scaled = back_normed[head] * gains[head]
                norm_dot = norm_dot + scaled * wide[head]
                carried[span, parts[head]] = (onward[head] + scaled * scale).astype(BF)
        if carried is not None:
            column = jnp.broadcast_to(jnp.sum(norm_dot, axis=1, keepdims=True), (size, size))
            line = column.T[0:1, :]
            high, low = two_parts(line)
            base = rows + 16 * block
            pay[base : base + 16, :] = jnp.concatenate(
                (high.astype(F32), low.astype(F32), jnp.zeros((14, size), F32)), axis=0
            ).astype(BF)
    zeros = jnp.zeros((15, HD), F32)
    for head in heads:
        gain_row[:, head * HD : (head + 1) * HD] = jnp.concatenate(
            (gain_sums[head], zeros), axis=0
        ).astype(BF)
    if carried is not None:
        pay[0:rows, :] = to_rank(carried[...], weights_before, own).astype(BF)


def turn_kernel(count, layer, width, *refs):
    pays, sides, refs = refs[:count], refs[count : 2 * count], refs[2 * count :]
    x_before, mean_before, mask, weights, cot = refs[:5]
    x, mean, reduced, cross, mixed, dred_out, gain_row, carried, pay, probs = refs[5:]
    rows = x.shape[0]
    weights_before, weights = layer_of(weights, layer - 1), layer_of(weights, layer)
    receive_forward(
        pays, gram_of(sides, layer - 1, layer, rows), x_before, mean_before, weights_before,
        width, x, mean, reduced, cross,
    )
    attend(x, mean[:, 0:1], weights, mask, probs, mixed)
    dred = total_of(sides, 0, rows).astype(BF)
    dred_out[...] = dred
    layer_backward(
        cot[...], dred, x, mean[:, 0:1], weights, weights_before, probs, gain_row, carried, pay
    )
    pay[pay.shape[0] - rows :, :] = to_rank(mixed[...], weights, 0).astype(BF)


def receive_backward(pays, carried_after, x_after, mean_after, cross_after, width):
    rows = x_after.shape[0]
    size = block_size(rows)
    douts, dreds = [], []
    for block in range(rows // size):
        span = slice(block * size, (block + 1) * size)
        base = rows + 16 * block
        lines = total_of(pays, base, base + 16)
        column = jnp.broadcast_to(lines[0:1] + lines[1:2], (size, size)).T
        factor = lax.rsqrt(mean_after[span, 0:1] + EPS)
        pull = column[:, 0:1] * (factor * factor * factor / width)
        own_total = total_of(pays, block * size, (block + 1) * size)
        dreds.append((own_total - cross_after[span, :] * pull).astype(BF))
        douts.append(
            (carried_after[span, :].astype(F32) - x_after[span, :].astype(F32) * pull).astype(BF)
        )
    if len(douts) == 1:
        return douts[0], dreds[0]
    return jnp.concatenate(douts, axis=0), jnp.concatenate(dreds, axis=0)


def back_kernel(count, layer, width, *refs):
    pays, refs = refs[:count], refs[count:]
    carried_after, x_after, mean_after, cross_after, x, mean, weights, probs = refs[:8]
    carried, pay, dout_out, dred_out, gain_row = refs[8:]
    dout, dred = receive_backward(pays, carried_after, x_after, mean_after, cross_after, width)
    layer_backward(
        dout, dred, x, mean[:, 0:1], layer_of(weights, layer), layer_of(weights, layer - 1), probs,
        gain_row, carried, pay,
    )
    dout_out[...] = dout
    dred_out[...] = dred


def split_grads(dred, mixed, second, gain_row, wide, keep, send):
    rank = second.shape[0]
    own = keep.shape[1]
    core = lax.axis_index("core")
    for head in range(mixed.shape[1] // HD):
        part = slice(head * HD, (head + 1) * HD)
        wide[0:HD, head * rank : (head + 1) * rank] = dot_tn(mixed[:, part], dred).astype(BF)
    wide[rank : 2 * rank, :] = second.astype(BF)
    if gain_row is not None:
        wide[2 * rank :, :] = gain_row[...]
    keep[...] = wide[:, pl.ds(pl.multiple_of(core * own, own), own)]
    send[...] = wide[:, pl.ds(pl.multiple_of((1 - core) * own, own), own)]


def grads_kernel(count, *refs):
    sources, refs = refs[:count], refs[count:]
    dout, dred, mixed, gain_row, keep, send, wide = refs
    rows = dout.shape[0]
    height = sources[0].shape[0]
    reduced = total_of(sources, height - rows, height).astype(BF)
    second = dot_tn(reduced, dout[...])
    split_grads(dred[...], mixed, second, gain_row, wide, keep, send)


def back_first_kernel(count, width, *refs):
    pays, refs = refs[:count], refs[count:]
    carried_after, x_after, mean_after, cross_after, x, mean, weights, probs, mixed = refs[:9]
    reduced, keep, send, wide = refs[9:]
    rank = reduced.shape[1]
    dout, dred = receive_backward(pays, carried_after, x_after, mean_after, cross_after, width)
    second = dot_tn(reduced[...], dout)
    layer_backward(
        dout, dred, x, mean[:, 0:1], layer_of(weights, 0), None, probs, wide.at[pl.ds(2 * rank, 16)],
        None, None,
    )
    split_grads(dred, mixed, second, None, wide, keep, send)


def combine_kernel(sections, *refs):
    kept, swapped = refs[:sections], refs[sections : 2 * sections]
    outs = refs[2 * sections :]
    section = lax.axis_index("pipe")
    for distance in range(sections):
        for layer in range(sections):

            @pl.when(section == layer ^ distance)
            def _(distance=distance, layer=layer):
                total = kept[layer][...].astype(F32) + swapped[layer][...].astype(F32)
                outs[distance][...] = total.astype(BF)


def finish_kernel(sections, *refs):
    parts = refs[:sections]
    gain, first, second = refs[sections:]
    rank = second.shape[1]
    total = parts[0][...].astype(F32)
    for part in parts[1:]:
        total = total + part[...].astype(F32)
    for block in range(first.shape[1] // HD):
        first[0, block * HD : (block + 1) * HD, :] = total[0:HD, block * rank : (block + 1) * rank]
    second[0] = total[rank : 2 * rank]
    gain[...] = total[2 * rank : 2 * rank + 1]


def per_device(tokens, cotangents, starts, counts, layer_gains, first_map, second_map):
    sections = lax.axis_size("pipe")
    groups = lax.axis_size("z")
    directions, micro_count, length, width = tokens.shape
    micro_local = -(-directions * micro_count // sections)
    rows = groups * micro_local * length
    local = width // groups
    own = first_map.shape[1]
    rank = first_map.shape[2]
    heads = local // HD
    size = block_size(rows)
    blocks = rows // size
    sides = lax.axis_size("core")
    top = sections - 1

    def shifted(value, shift):
        return lax.ppermute(value, "z", [(i, i ^ shift) for i in range(groups)])

    def across(value, distance):
        return lax.ppermute(value, "pipe", [(i, i ^ distance) for i in range(sections)])

    def swapped(value):
        return lax.ppermute(value, "core", [(i, 1 - i) for i in range(sides)])

    def exchange(pay):
        return [pay] + [shifted(pay, place) for place in range(1, groups)]

    token_parts, packed = pack(
        tokens, cotangents, starts, counts, layer_gains, first_map, second_map, groups, micro_local
    )
    mine = [packed] + [across(packed, distance) for distance in range(1, sections)]
    order = [0] + list(range(groups - 1, 0, -1))
    received = [token_parts[0]] + [shifted(token_parts[place], place) for place in order[1:]]
    def shaped(shape, kind=BF):
        return jax.ShapeDtypeStruct(shape, kind)

    def call(kernel, operands, specs, outs, name, **more):
        return pl.pallas_call(
            kernel,
            in_specs=specs,
            out_specs=vmem_specs(len(outs)),
            out_shape=outs,
            compiler_params=PARAMS,
            name=name,
            **more,
        )(*operands)

    received[0], mine[0], mine[1] = call(
        own_kernel,
        (received[0], packed, mine[1]),
        vmem_specs(3),
        [shaped(received[0].shape), shaped(packed.shape), shaped(packed.shape)],
        "own_parts",
    )
    received, mine = lax.optimization_barrier((received, mine))
    theirs = [swapped(part) for part in mine]

    wide_shape = shaped((rows, local))
    mean_shape = shaped((rows, HD), F32)
    rank_shape = shaped((rows, rank))
    cross_shape = shaped((rows, rank), F32)
    probs_shape = shaped((blocks, heads, size, size))
    grads_shape = (sides, 2 * rank + 16, own)
    half_shape = shaped(grads_shape[1:])
    weights_shape = shaped((sections, sides, slice_rows(own), HD))

    x, cot, mask, mean = call(
        functools.partial(arrange_kernel, length, order),
        received,
        vmem_specs(groups),
        [wide_shape, wide_shape, shaped((blocks, size, size)), mean_shape],
        "arrange",
        scratch_shapes=[pltpu.VMEM((rows, HD), BF)],
    )
    last_gram = gram_place(top - 1, top, rows)
    side_rows = last_gram[0] + last_gram[1]
    probs, mixed, pay, weights = call(
        functools.partial(first_kernel, sections),
        (*mine, *theirs, x, mask, mean),
        vmem_specs(2 * sections + 3),
        [probs_shape, wide_shape, shaped((2 * rows + FOLDED, HD)), weights_shape],
        "forward_first",
        scratch_shapes=[pltpu.SemaphoreType.DMA((sections, sides))],
    )
    xs, means, reduceds, crosses = [x], [mean], [], [None]
    all_probs, all_mixed = [probs], [mixed]
    first_pays = pays = exchange(pay)
    side = call(side_kernel, (weights, cot), vmem_specs(2), [shaped((side_rows, HD))], "side")[0]
    arrived = exchange(side)
    for layer in range(1, top):
        operands = (*pays, *((), first_pays, arrived)[min(layer, 3) - 1])
        specs = vmem_specs(len(operands) + 4)
        x, mean, reduced, cross, probs, mixed, pay = call(
            functools.partial(middle_kernel, groups, layer, top, float(width)),
            (*operands, xs[-1], means[-1], mask, weights),
            specs,
            [
                wide_shape,
                mean_shape,
                rank_shape,
                cross_shape,
                probs_shape,
                wide_shape,
                shaped((2 * rows, HD)),
            ],
            "forward_middle",
        )
        xs.append(x)
        means.append(mean)
        reduceds.append(reduced)
        crosses.append(cross)
        all_probs.append(probs)
        all_mixed.append(mixed)
        pays = exchange(pay)

    back_rows = rows + 16 * blocks
    gain_shape = shaped((16, local))
    wide_scratch = [pltpu.VMEM((2 * rank + 16, local), BF)]
    x, mean, reduced, cross, mixed, dred, gain_row, carried, pay = call(
        functools.partial(turn_kernel, groups, top, float(width)),
        (*pays, *arrived, xs[-1], means[-1], mask, weights, cot),
        vmem_specs(2 * groups + 5),
        [
            wide_shape,
            mean_shape,
            rank_shape,
            cross_shape,
            wide_shape,
            rank_shape,
            gain_shape,
            wide_shape,
            shaped((back_rows + rows, HD)),
        ],
        "turn",
        scratch_shapes=[pltpu.VMEM(probs_shape.shape, BF)],
    )
    xs.append(x)
    means.append(mean)
    reduceds.append(reduced)
    crosses.append(cross)
    all_mixed.append(mixed)

    def gradients(layer, sources, dout, dred, gain_row):
        operands = (*sources, dout, dred, all_mixed[layer], gain_row)
        keep, send = call(
            functools.partial(grads_kernel, len(sources)),
            operands,
            vmem_specs(len(operands)),
            [half_shape] * 2,
            "weight_grads",
            scratch_shapes=wide_scratch,
        )
        return keep, send

    pays = exchange(pay)
    halves = [None] * sections
    waiting = [(top, pays, cot, dred, gain_row)]
    for layer in range(top - 1, 0, -1):
        operands = (
            *pays, carried, xs[layer + 1], means[layer + 1], crosses[layer + 1],
            xs[layer], means[layer], weights, all_probs[layer],
        )
        carried, pay, dout, dred, gain_row = call(
            functools.partial(back_kernel, groups, layer, float(width)),
            operands,
            vmem_specs(len(operands)),
            [wide_shape, shaped((back_rows, HD)), wide_shape, rank_shape, gain_shape],
            "backward",
        )
        pays = exchange(pay)
        waiting.append((layer, [reduceds[layer]], dout, dred, gain_row))
        done = [gradients(*item) for item in waiting]
        if layer > 1:
            pays, done = lax.optimization_barrier((pays, done))
        for item, (keep, send) in zip(waiting, done):
            halves[item[0]] = (keep, swapped(send))
        waiting = []
    operands = (
        *pays, carried, xs[1], means[1], crosses[1], xs[0], means[0], weights, all_probs[0],
        all_mixed[0], reduceds[0],
    )
    keep, send = call(
        functools.partial(back_first_kernel, groups, float(width)),
        operands,
        vmem_specs(len(operands)),
        [half_shape] * 2,
        "backward_first",
        scratch_shapes=wide_scratch,
    )
    halves[0] = (keep, swapped(send))

    parts = call(
        functools.partial(combine_kernel, sections),
        [pair[side] for side in range(2) for pair in halves],
        vmem_specs(2 * sections),
        [half_shape] * sections,
        "combine",
    )
    arrived = [parts[0]] + [across(parts[distance], distance) for distance in range(1, sections)]
    gain_grad, first_grad, second_grad = call(
        functools.partial(finish_kernel, sections),
        arrived,
        vmem_specs(sections),
        [
            shaped((1, own), F32),
            shaped((1, own, rank), F32),
            shaped((1, rank, own), F32),
        ],
        "finish",
    )
    return (gain_grad, first_grad, second_grad)


def solution(mesh):
    fine = Mesh(
        mesh.devices.reshape(mesh.shape["pipe"], mesh.shape["dp"] // 2, 2), ("pipe", "z", "core")
    )
    data = ("z", "core")
    in_specs = (
        P(None, data, None, None),
        P(None, data, None, None),
        P(None, data, None),
        P(None, data),
        P("pipe", data),
        P("pipe", data, None),
        P("pipe", None, data),
    )
    out_specs = (P("pipe", data), P("pipe", data, None), P("pipe", None, data))
    mapped = jax.shard_map(
        per_device, mesh=fine, in_specs=in_specs, out_specs=out_specs, check_vma=False
    )

    return mapped
```

```python
import functools

import jax
import jax.numpy as jnp
from jax import lax
from jax.experimental import pallas as pl
from jax.experimental.pallas import tpu as pltpu
from jax.sharding import Mesh, PartitionSpec as P

HD = 128
EPS = 1e-05
FOLDED = HD + 16
BF = jnp.bfloat16
F32 = jnp.float32
PARAMS = pltpu.CompilerParams(vmem_limit_bytes=48 * 1024 * 1024)
PACK_PARAMS = pltpu.CompilerParams(vmem_limit_bytes=60 * 1024 * 1024)


def dot(a, b):
    return jnp.dot(a, b, preferred_element_type=F32)


def dot_nt(a, b):
    return lax.dot_general(a, b, (((1,), (1,)), ((), ())), preferred_element_type=F32)


def dot_tn(a, b):
    return lax.dot_general(a, b, (((0,), (0,)), ((), ())), preferred_element_type=F32)


def two_parts(value):
    high = value.astype(BF)
    return high, (value - high.astype(F32)).astype(BF)


def vmem_specs(count):
    return [pl.BlockSpec(memory_space=pltpu.VMEM)] * count


def layer_of(weights, layer):
    return weights.at[pl.ds(layer, 1)]


def slice_rows(own):
    return 2 * own + 16


def pack_kernel(groups, micro_local, *refs):
    tokens, cotangents, starts, counts, gain, first, second = refs[:7]
    parts, weights = refs[7 : 7 + groups], refs[7 + groups]
    tok, cot, starts_in, counts_in, gain_in, second_in, sems = refs[8 + groups :]
    directions, micro_count, length, width = tokens.shape
    local = width // groups
    own = first.shape[1]
    section = lax.axis_index("pipe")
    group = lax.axis_index("z")
    picks = []
    copies = [
        pltpu.make_async_copy(second.at[0], second_in, sems.at[0]),
        pltpu.make_async_copy(gain, gain_in, sems.at[1]),
        pltpu.make_async_copy(first.at[0], weights.at[pl.ds(0, own)], sems.at[2]),
        pltpu.make_async_copy(starts, starts_in, sems.at[3]),
        pltpu.make_async_copy(counts, counts_in, sems.at[4]),
    ]
    for micro in range(micro_local):
        wanted = section * micro_local + micro
        slot = jnp.minimum(wanted, directions * micro_count - 1)
        direction, place = slot // micro_count, slot % micro_count
        picks.append((wanted < directions * micro_count, direction, place))
        rows = pl.ds(micro * length, length)
        copies.append(
            pltpu.make_async_copy(
                tokens.at[direction, place], tok.at[rows], sems.at[5 + 2 * micro]
            )
        )
        copies.append(
            pltpu.make_async_copy(
                cotangents.at[direction, place], cot.at[rows], sems.at[6 + 2 * micro]
            )
        )
    for copy in copies:
        copy.start()
    for copy in copies[:5]:
        copy.wait()
    weights[own : 2 * own, :] = second_in[...].astype(F32).T.astype(BF)
    gains = [gain_in[0:1, head * HD : (head + 1) * HD].astype(F32) for head in range(own // HD)]
    gains.append(jnp.zeros((16 - own // HD, HD), F32))
    weights[2 * own :, :] = jnp.concatenate(gains, axis=0).astype(BF)
    for copy in copies[5:]:
        copy.wait()
    for micro, (keep, direction, place) in enumerate(picks):
        rows = slice(micro * length, (micro + 1) * length)
        widened = tok[rows, :].astype(F32)
        mean = jnp.mean(widened * widened, axis=1, keepdims=True)
        mean_high, mean_low = two_parts(mean)
        position = lax.broadcasted_iota(jnp.int32, (length, HD), 0)
        document = jnp.zeros((length, HD), jnp.int32)
        for entry in range(starts.shape[2]):
            begun = starts_in[direction, place, entry] <= position
            begun = begun & (entry < counts_in[direction, place])
            document = document + begun.astype(jnp.int32)
        lane = lax.broadcasted_iota(jnp.int32, (length, HD), 1)
        tail = jnp.where(
            lane == 0,
            document.astype(F32),
            jnp.where(lane == 1, mean_high.astype(F32), mean_low.astype(F32)),
        ).astype(BF)
        for shift in range(groups):
            start = pl.multiple_of((group ^ shift) * local, local)
            parts[shift][rows, 0:local] = tok[rows, pl.ds(start, local)]
            cotangent = cot[rows, pl.ds(start, local)]
            parts[shift][rows, local : 2 * local] = jnp.where(
                keep, cotangent, jnp.zeros_like(cotangent)
            )
            parts[shift][rows, 2 * local :] = tail


def pack(tokens, cotangents, starts, counts, gain, first, second, groups, micro_local):
    length, width = tokens.shape[2:]
    own = first.shape[1]
    local = width // groups
    rows = micro_local * length
    shape = jax.ShapeDtypeStruct
    results = pl.pallas_call(
        functools.partial(pack_kernel, groups, micro_local),
        in_specs=[pl.BlockSpec(memory_space=pltpu.HBM)] * 7,
        out_specs=vmem_specs(groups + 1),
        out_shape=[shape((rows, 2 * local + HD), BF)] * groups
        + [shape((slice_rows(own), HD), BF)],
        scratch_shapes=[
            pltpu.VMEM((rows, width), BF),
            pltpu.VMEM((rows, width), BF),
            pltpu.SMEM(starts.shape, jnp.int32),
            pltpu.SMEM(counts.shape, jnp.int32),
            pltpu.VMEM(gain.shape, BF),
            pltpu.VMEM(second.shape[1:], BF),
            pltpu.SemaphoreType.DMA((5 + 2 * micro_local,)),
        ],
        compiler_params=PACK_PARAMS,
        name="pack",
    )(tokens, cotangents, starts, counts, gain, first, second)
    return results[:groups], results[groups]


def head_gain(weights, head):
    own = (weights.shape[2] - 16) // 2
    per_slice = own // HD
    row = 2 * own + head % per_slice
    return weights[0, head // per_slice, row : row + 1, :].astype(F32)


def block_size(rows):
    return HD if rows % HD == 0 else rows


def to_rank(value, weights, at):
    own = (weights.shape[2] - 16) // 2
    total = None
    for side in range(weights.shape[1]):
        term = dot(value[:, side * own : (side + 1) * own], weights[0, side, at : at + own, :])
        total = term if total is None else total + term
    return total


def from_rank(value, weights, at, side):
    own = (weights.shape[2] - 16) // 2
    return dot_nt(value, weights[0, side, at : at + own, :])


def gram(weights):
    own = (weights.shape[2] - 16) // 2
    total = None
    for side in range(weights.shape[1]):
        part = weights[0, side, own : 2 * own, :]
        term = dot_tn(part, part)
        total = term if total is None else total + term
    return total


def attend(x, mean, weights, mask, probs, mixed):
    rows, local = x.shape
    size = block_size(rows)
    factor = lax.rsqrt(mean + EPS)
    heads = range(local // HD)
    gains = [head_gain(weights, head) for head in heads]
    for block in range(rows // size):
        span = slice(block * size, (block + 1) * size)
        allowed = mask[block] > 0
        wide = x[span, :].astype(F32) * factor[span]
        normed = [(wide[:, head * HD : (head + 1) * HD] * gains[head]).astype(BF) for head in heads]
        scores = [dot_nt(value, value) for value in normed]
        raw = [jnp.where(allowed, jnp.exp(score * (1.0 / HD)), 0.0) for score in scores]
        shares = [1.0 / jnp.sum(value, axis=1, keepdims=True) for value in raw]
        prob = [(value * share).astype(BF) for value, share in zip(raw, shares)]
        result = [dot(left, right).astype(BF) for left, right in zip(prob, normed)]
        for head in heads:
            probs[block, head] = prob[head]
            mixed[span, head * HD : (head + 1) * HD] = result[head]


def send_forward(x, weights, mixed, pay):
    rows = x.shape[0]
    own = (weights.shape[2] - 16) // 2
    pay[0:rows, :] = to_rank(mixed[...], weights, 0).astype(BF)
    pay[rows : 2 * rows, :] = to_rank(x[...], weights, own).astype(BF)


def total_of(pays, start, stop):
    total = pays[0][start:stop, :].astype(F32)
    for pay in pays[1:]:
        total = total + pay[start:stop, :].astype(F32)
    return total


def receive_forward(
    pays, gram_total, x_before, mean_before, weights_before, width, x, mean, reduced, cross
):
    rows, local = x_before.shape
    own = (weights_before.shape[2] - 16) // 2
    low_rank = total_of(pays, 0, rows).astype(BF)
    before = total_of(pays, rows, 2 * rows)
    high, low = two_parts(gram_total)
    through = dot(low_rank, high) + dot(low_rank, low)
    wide = low_rank.astype(F32)
    change = jnp.sum(wide * (2.0 * before + through), axis=1, keepdims=True) / width
    new_mean = jnp.maximum(mean_before[:, 0:1] + change, 0.0)
    mean[...] = jnp.broadcast_to(new_mean, mean.shape)
    reduced[...] = low_rank
    cross[...] = before + through
    for side in range(weights_before.shape[1]):
        part = slice(side * own, (side + 1) * own)
        x[:, part] = (
            x_before[:, part].astype(F32) + from_rank(low_rank, weights_before, own, side)
        ).astype(BF)


def own_kernel(part, packed, early, part_out, packed_out, early_out):
    part_out[...] = part[...]
    packed_out[...] = packed[...]
    early_out[...] = early[...]


def arrange_kernel(length, order, *refs):
    groups = len(order)
    received = [refs[order.index(place)] for place in range(groups)]
    x, cot, mask, mean, tails = refs[groups:]
    rows, local = x.shape
    place_rows(received, tails, slice(2 * local, None))
    place_rows(received, x, slice(0, local))
    place_rows(received, cot, slice(local, 2 * local))
    tail = tails[...].astype(F32)
    mean[...] = jnp.broadcast_to(tail[:, 1:2] + tail[:, 2:3], mean.shape)
    build_mask(tail[:, 0:1], mask, block_size(rows), length)


def first_kernel(sections, *refs):
    mine, theirs = refs[:sections], refs[sections : 2 * sections]
    x, mask, mean, probs, mixed, pay, weights, sems = refs[2 * sections :]
    section, core = lax.axis_index("pipe"), lax.axis_index("core")
    rows = x.shape[0]
    copies = []
    for distance in range(sections):
        layer = section ^ distance
        for parts, place in ((mine, core), (theirs, 1 - core)):
            copies.append(
                pltpu.make_async_copy(
                    parts[distance], weights.at[layer, place], sems.at[layer, place]
                )
            )
    for wanted_now in (True, False):
        for distance in range(sections):

            @pl.when((section == distance) == wanted_now)
            def _(distance=distance):
                copies[2 * distance].start()
                copies[2 * distance + 1].start()

    def arrived(layer):
        for place in range(weights.shape[1]):
            pltpu.make_async_copy(mine[0], weights.at[layer, place], sems.at[layer, place]).wait()

    arrived(0)
    own = (weights.shape[2] - 16) // 2
    layers = [layer_of(weights, layer) for layer in range(sections)]
    attend(x, mean[:, 0:1], layers[0], mask, probs, mixed)
    send_forward(x, layers[0], mixed, pay)
    arrived(1)
    pay[2 * rows :, :] = fold_grams(layers[0], layers[1])
    for layer in range(2, sections):
        arrived(layer)


def side_kernel(weights, cot, side):
    rows = cot.shape[0]
    sections = weights.shape[0]
    own = (weights.shape[2] - 16) // 2
    layers = [layer_of(weights, layer) for layer in range(sections)]
    side[0:rows, :] = to_rank(cot[...], layers[-1], own).astype(BF)
    for layer in range(2, sections - 1, 2):
        base, height, folded = gram_place(layer, sections - 1, rows)
        both = fold_grams(layers[layer], layers[layer + 1]) if folded else gram(layers[layer])
        side[base : base + height, :] = both.astype(BF)


def place_rows(received, target, columns):
    rows = received[0].shape[0]
    for shift, part in enumerate(received):
        source = lax.axis_index("z") ^ shift
        target[pl.ds(pl.multiple_of(source * rows, rows), rows), :] = part[:, columns]


def build_mask(document, mask, size, length):
    query = lax.broadcasted_iota(jnp.int32, (size, size), 0)
    key = lax.broadcasted_iota(jnp.int32, (size, size), 1)
    for block in range(mask.shape[0]):
        by_query = jnp.broadcast_to(document[block * size : (block + 1) * size], (size, size))
        by_key = by_query.T
        allowed = (by_query == by_key) & (key <= query) & (query // length == key // length)
        mask[block] = allowed.astype(F32).astype(BF)


def fold_grams(weights, other):
    row, lane = square_places()
    upper, lower = gram(weights), gram(other)
    diagonal = jnp.sum(jnp.where(row == lane, lower, 0.0), axis=0, keepdims=True)
    folded = jnp.where(row <= lane, upper, lower)
    return jnp.concatenate((folded, diagonal, jnp.zeros((15, HD), F32)), axis=0).astype(BF)


def square_places():
    return (
        lax.broadcasted_iota(jnp.int32, (HD, HD), 0),
        lax.broadcasted_iota(jnp.int32, (HD, HD), 1),
    )


def gram_place(layer, top, rows):
    pair = layer // 2
    folded = 2 * pair + 1 < top
    base = 2 * rows if pair == 0 else rows + FOLDED * (pair - 1)
    return base, FOLDED if folded else HD, folded


def gram_of(sources, layer, top, rows):
    base, height, folded = gram_place(layer, top, rows)
    total = total_of(sources, base, base + height)
    if not folded:
        return total
    row, lane = square_places()
    square = total[0:HD]
    if layer % 2 == 0:
        return jnp.where(row <= lane, square, square.T)
    lower = jnp.where(row > lane, square, square.T)
    return jnp.where(row == lane, total[HD : HD + 1], lower)


def middle_kernel(count, layer, top, width, *refs):
    pays, sources, refs = refs[:count], refs[count : 2 * count], refs[2 * count :]
    if layer == 1:
        sources, refs = pays, sources + refs
    x_before, mean_before, mask, weights = refs[:4]
    x, mean, reduced, cross, probs, mixed, pay = refs[4:]
    weights_before, weights = layer_of(weights, layer - 1), layer_of(weights, layer)
    receive_forward(
        pays, gram_of(sources, layer - 1, top, x.shape[0]), x_before, mean_before, weights_before,
        width, x, mean, reduced, cross,
    )
    attend(x, mean[:, 0:1], weights, mask, probs, mixed)
    send_forward(x, weights, mixed, pay)


def layer_backward(dout, dred, x, mean, weights, weights_before, probs, gain_row, carried, pay):
    rows, local = x.shape
    size = block_size(rows)
    own = (weights.shape[2] - 16) // 2
    per_slice = own // HD
    factor = lax.rsqrt(mean + EPS)
    back_mixed = [
        from_rank(dred, weights, 0, side).astype(BF) for side in range(weights.shape[1])
    ]
    heads = range(local // HD)
    gains = [head_gain(weights, head) for head in heads]
    gain_sums = [None] * len(heads)
    for block in range(rows // size):
        span = slice(block * size, (block + 1) * size)
        scale = factor[span]
        parts = [slice(head * HD, (head + 1) * HD) for head in heads]
        wide = [x[span, part].astype(F32) for part in parts]
        prob = [probs[block, head] for head in heads]
        onward = [None if carried is None else dout[span, part].astype(F32) for part in parts]
        unit = [value * scale for value in wide]
        normed = [(value * gain).astype(BF) for value, gain in zip(unit, gains)]
        upstream = []
        for head in heads:
            inner = (head % per_slice) * HD
            upstream.append(back_mixed[head // per_slice][span, inner : inner + HD])
        back_prob = [dot_nt(left, right) for left, right in zip(upstream, normed)]
        through = [dot_tn(left, right) for left, right in zip(prob, upstream)]
        both = []
        for head in heads:
            prob_wide = prob[head].astype(F32)
            inner_sum = jnp.sum(back_prob[head] * prob_wide, axis=1, keepdims=True)
            back_score = prob_wide * (back_prob[head] - inner_sum) * (1.0 / HD)
            both.append((back_score + back_score.T).astype(BF))
        back_normed = [
            (through[head] + dot(both[head], normed[head])).astype(BF).astype(F32) for head in heads
        ]
        norm_dot = jnp.zeros((size, HD), F32)
        for head in heads:
            term = jnp.sum(back_normed[head] * unit[head], axis=0, keepdims=True)
            gain_sums[head] = term if gain_sums[head] is None else gain_sums[head] + term
            if carried is not None:
                scaled = back_normed[head] * gains[head]
                norm_dot = norm_dot + scaled * wide[head]
                carried[span, parts[head]] = (onward[head] + scaled * scale).astype(BF)
        if carried is not None:
            column = jnp.broadcast_to(jnp.sum(norm_dot, axis=1, keepdims=True), (size, size))
            line = column.T[0:1, :]
            high, low = two_parts(line)
            base = rows + 16 * block
            pay[base : base + 16, :] = jnp.concatenate(
                (high.astype(F32), low.astype(F32), jnp.zeros((14, size), F32)), axis=0
            ).astype(BF)
    zeros = jnp.zeros((15, HD), F32)
    for head in heads:
        gain_row[:, head * HD : (head + 1) * HD] = jnp.concatenate(
            (gain_sums[head], zeros), axis=0
        ).astype(BF)
    if carried is not None:
        pay[0:rows, :] = to_rank(carried[...], weights_before, own).astype(BF)


def turn_kernel(count, layer, width, *refs):
    pays, sides, refs = refs[:count], refs[count : 2 * count], refs[2 * count :]
    x_before, mean_before, mask, weights, cot = refs[:5]
    x, mean, reduced, cross, mixed, dred_out, gain_row, carried, pay, probs = refs[5:]
    rows = x.shape[0]
    weights_before, weights = layer_of(weights, layer - 1), layer_of(weights, layer)
    receive_forward(
        pays, gram_of(sides, layer - 1, layer, rows), x_before, mean_before, weights_before,
        width, x, mean, reduced, cross,
    )
    attend(x, mean[:, 0:1], weights, mask, probs, mixed)
    dred = total_of(sides, 0, rows).astype(BF)
    dred_out[...] = dred
    layer_backward(
        cot[...], dred, x, mean[:, 0:1], weights, weights_before, probs, gain_row, carried, pay
    )
    pay[pay.shape[0] - rows :, :] = to_rank(mixed[...], weights, 0).astype(BF)


def receive_backward(pays, carried_after, x_after, mean_after, cross_after, width):
    rows = x_after.shape[0]
    size = block_size(rows)
    douts, dreds = [], []
    for block in range(rows // size):
        span = slice(block * size, (block + 1) * size)
        base = rows + 16 * block
        lines = total_of(pays, base, base + 16)
        column = jnp.broadcast_to(lines[0:1] + lines[1:2], (size, size)).T
        factor = lax.rsqrt(mean_after[span, 0:1] + EPS)
        pull = column[:, 0:1] * (factor * factor * factor / width)
        own_total = total_of(pays, block * size, (block + 1) * size)
        dreds.append((own_total - cross_after[span, :] * pull).astype(BF))
        douts.append(
            (carried_after[span, :].astype(F32) - x_after[span, :].astype(F32) * pull).astype(BF)
        )
    if len(douts) == 1:
        return douts[0], dreds[0]
    return jnp.concatenate(douts, axis=0), jnp.concatenate(dreds, axis=0)


def back_kernel(count, layer, width, *refs):
    pays, refs = refs[:count], refs[count:]
    carried_after, x_after, mean_after, cross_after, x, mean, weights, probs = refs[:8]
    carried, pay, dout_out, dred_out, gain_row = refs[8:]
    dout, dred = receive_backward(pays, carried_after, x_after, mean_after, cross_after, width)
    layer_backward(
        dout, dred, x, mean[:, 0:1], layer_of(weights, layer), layer_of(weights, layer - 1), probs,
        gain_row, carried, pay,
    )
    dout_out[...] = dout
    dred_out[...] = dred


def split_grads(dred, mixed, second, gain_row, wide, keep, send):
    rank = second.shape[0]
    own = keep.shape[1]
    core = lax.axis_index("core")
    for head in range(mixed.shape[1] // HD):
        part = slice(head * HD, (head + 1) * HD)
        wide[0:HD, head * rank : (head + 1) * rank] = dot_tn(mixed[:, part], dred).astype(BF)
    wide[rank : 2 * rank, :] = second.astype(BF)
    if gain_row is not None:
        wide[2 * rank :, :] = gain_row[...]
    keep[...] = wide[:, pl.ds(pl.multiple_of(core * own, own), own)]
    send[...] = wide[:, pl.ds(pl.multiple_of((1 - core) * own, own), own)]


def grads_kernel(count, *refs):
    sources, refs = refs[:count], refs[count:]
    dout, dred, mixed, gain_row, keep, send, wide = refs
    rows = dout.shape[0]
    height = sources[0].shape[0]
    reduced = total_of(sources, height - rows, height).astype(BF)
    second = dot_tn(reduced, dout[...])
    split_grads(dred[...], mixed, second, gain_row, wide, keep, send)


def back_first_kernel(count, width, *refs):
    pays, refs = refs[:count], refs[count:]
    carried_after, x_after, mean_after, cross_after, x, mean, weights, probs, mixed = refs[:9]
    reduced, keep, send, wide = refs[9:]
    rank = reduced.shape[1]
    dout, dred = receive_backward(pays, carried_after, x_after, mean_after, cross_after, width)
    second = dot_tn(reduced[...], dout)
    layer_backward(
        dout, dred, x, mean[:, 0:1], layer_of(weights, 0), None, probs, wide.at[pl.ds(2 * rank, 16)],
        None, None,
    )
    split_grads(dred, mixed, second, None, wide, keep, send)


def combine_kernel(sections, *refs):
    kept, swapped = refs[:sections], refs[sections : 2 * sections]
    outs = refs[2 * sections :]
    section = lax.axis_index("pipe")
    for distance in range(sections):
        for layer in range(sections):

            @pl.when(section == layer ^ distance)
            def _(distance=distance, layer=layer):
                total = kept[layer][...].astype(F32) + swapped[layer][...].astype(F32)
                outs[distance][...] = total.astype(BF)


def combine_halves_kernel(*refs):
    kept, swapped = refs[:4], refs[4:8]
    mine, by_x, by_y, later_x, later_y = refs[8:]
    rows = mine.shape[0]
    half = mine.shape[1] // 2
    section = lax.axis_index("pipe")
    for distance in range(4):
        for layer in range(4):

            @pl.when(section == layer ^ distance)
            def _(distance=distance, layer=layer):
                total = kept[layer][...].astype(F32) + swapped[layer][...].astype(F32)
                total = total.astype(BF)
                left, right = total[:, :half], total[:, half:]
                if distance == 0:
                    mine[...] = total
                elif distance == 1:
                    by_x[0:rows, :] = right
                    later_x[...] = left
                elif distance == 2:
                    by_y[0:rows, :] = left
                    later_y[...] = right
                else:
                    by_x[rows:, :] = right
                    by_y[rows:, :] = left


def relay_kernel(later_x, later_y, from_x, from_y, to_x, to_y):
    rows = later_x.shape[0]
    to_x[...] = (later_x[...].astype(F32) + from_y[rows:, :].astype(F32)).astype(BF)
    to_y[...] = (later_y[...].astype(F32) + from_x[rows:, :].astype(F32)).astype(BF)


def finish_halves_kernel(mine, from_x, from_y, last_x, last_y, gain, first, second):
    rank = second.shape[1]
    rows = mine.shape[0]
    half = mine.shape[1] // 2
    for side, (direct, relayed) in enumerate(((from_y, last_x), (from_x, last_y))):
        span = slice(side * half, (side + 1) * half)
        total = mine[:, span].astype(F32) + direct[0:rows, :].astype(F32)
        total = total + relayed[...].astype(F32)
        for block in range(half // rank):
            base = side * half + block * HD
            first[0, base : base + HD, :] = total[0:HD, block * rank : (block + 1) * rank]
        second[0, :, span] = total[rank : 2 * rank]
        gain[:, span] = total[2 * rank : 2 * rank + 1]


def finish_kernel(sections, *refs):
    parts = refs[:sections]
    gain, first, second = refs[sections:]
    rank = second.shape[1]
    total = parts[0][...].astype(F32)
    for part in parts[1:]:
        total = total + part[...].astype(F32)
    for block in range(first.shape[1] // HD):
        first[0, block * HD : (block + 1) * HD, :] = total[0:HD, block * rank : (block + 1) * rank]
    second[0] = total[rank : 2 * rank]
    gain[...] = total[2 * rank : 2 * rank + 1]


def per_device(tokens, cotangents, starts, counts, layer_gains, first_map, second_map):
    sections = lax.axis_size("pipe")
    groups = lax.axis_size("z")
    directions, micro_count, length, width = tokens.shape
    micro_local = -(-directions * micro_count // sections)
    rows = groups * micro_local * length
    local = width // groups
    own = first_map.shape[1]
    rank = first_map.shape[2]
    heads = local // HD
    size = block_size(rows)
    blocks = rows // size
    sides = lax.axis_size("core")
    top = sections - 1

    def shifted(value, shift):
        return lax.ppermute(value, "z", [(i, i ^ shift) for i in range(groups)])

    def across(value, distance):
        return lax.ppermute(value, "pipe", [(i, i ^ distance) for i in range(sections)])

    def swapped(value):
        return lax.ppermute(value, "core", [(i, 1 - i) for i in range(sides)])

    def exchange(pay):
        return [pay] + [shifted(pay, place) for place in range(1, groups)]

    token_parts, packed = pack(
        tokens, cotangents, starts, counts, layer_gains, first_map, second_map, groups, micro_local
    )
    mine = [packed] + [across(packed, distance) for distance in range(1, sections)]
    order = [0] + list(range(groups - 1, 0, -1))
    received = [token_parts[0]] + [shifted(token_parts[place], place) for place in order[1:]]
    def shaped(shape, kind=BF):
        return jax.ShapeDtypeStruct(shape, kind)

    def call(kernel, operands, specs, outs, name, **more):
        return pl.pallas_call(
            kernel,
            in_specs=specs,
            out_specs=vmem_specs(len(outs)),
            out_shape=outs,
            compiler_params=PARAMS,
            name=name,
            **more,
        )(*operands)

    received[0], mine[0], mine[1] = call(
        own_kernel,
        (received[0], packed, mine[1]),
        vmem_specs(3),
        [shaped(received[0].shape), shaped(packed.shape), shaped(packed.shape)],
        "own_parts",
    )
    received, mine = lax.optimization_barrier((received, mine))
    theirs = [swapped(part) for part in mine]

    wide_shape = shaped((rows, local))
    mean_shape = shaped((rows, HD), F32)
    rank_shape = shaped((rows, rank))
    cross_shape = shaped((rows, rank), F32)
    probs_shape = shaped((blocks, heads, size, size))
    grads_shape = (sides, 2 * rank + 16, own)
    half_shape = shaped(grads_shape[1:])
    weights_shape = shaped((sections, sides, slice_rows(own), HD))

    x, cot, mask, mean = call(
        functools.partial(arrange_kernel, length, order),
        received,
        vmem_specs(groups),
        [wide_shape, wide_shape, shaped((blocks, size, size)), mean_shape],
        "arrange",
        scratch_shapes=[pltpu.VMEM((rows, HD), BF)],
    )
    last_gram = gram_place(top - 1, top, rows)
    side_rows = last_gram[0] + last_gram[1]
    probs, mixed, pay, weights = call(
        functools.partial(first_kernel, sections),
        (*mine, *theirs, x, mask, mean),
        vmem_specs(2 * sections + 3),
        [probs_shape, wide_shape, shaped((2 * rows + FOLDED, HD)), weights_shape],
        "forward_first",
        scratch_shapes=[pltpu.SemaphoreType.DMA((sections, sides))],
    )
    xs, means, reduceds, crosses = [x], [mean], [], [None]
    all_probs, all_mixed = [probs], [mixed]
    first_pays = pays = exchange(pay)
    side = call(side_kernel, (weights, cot), vmem_specs(2), [shaped((side_rows, HD))], "side")[0]
    arrived = exchange(side)
    for layer in range(1, top):
        operands = (*pays, *((), first_pays, arrived)[min(layer, 3) - 1])
        specs = vmem_specs(len(operands) + 4)
        x, mean, reduced, cross, probs, mixed, pay = call(
            functools.partial(middle_kernel, groups, layer, top, float(width)),
            (*operands, xs[-1], means[-1], mask, weights),
            specs,
            [
                wide_shape,
                mean_shape,
                rank_shape,
                cross_shape,
                probs_shape,
                wide_shape,
                shaped((2 * rows, HD)),
            ],
            "forward_middle",
        )
        xs.append(x)
        means.append(mean)
        reduceds.append(reduced)
        crosses.append(cross)
        all_probs.append(probs)
        all_mixed.append(mixed)
        pays = exchange(pay)

    back_rows = rows + 16 * blocks
    gain_shape = shaped((16, local))
    wide_scratch = [pltpu.VMEM((2 * rank + 16, local), BF)]
    x, mean, reduced, cross, mixed, dred, gain_row, carried, pay = call(
        functools.partial(turn_kernel, groups, top, float(width)),
        (*pays, *arrived, xs[-1], means[-1], mask, weights, cot),
        vmem_specs(2 * groups + 5),
        [
            wide_shape,
            mean_shape,
            rank_shape,
            cross_shape,
            wide_shape,
            rank_shape,
            gain_shape,
            wide_shape,
            shaped((back_rows + rows, HD)),
        ],
        "turn",
        scratch_shapes=[pltpu.VMEM(probs_shape.shape, BF)],
    )
    xs.append(x)
    means.append(mean)
    reduceds.append(reduced)
    crosses.append(cross)
    all_mixed.append(mixed)

    def gradients(layer, sources, dout, dred, gain_row):
        operands = (*sources, dout, dred, all_mixed[layer], gain_row)
        keep, send = call(
            functools.partial(grads_kernel, len(sources)),
            operands,
            vmem_specs(len(operands)),
            [half_shape] * 2,
            "weight_grads",
            scratch_shapes=wide_scratch,
        )
        return keep, send

    pays = exchange(pay)
    halves = [None] * sections
    waiting = [(top, pays, cot, dred, gain_row)]
    for layer in range(top - 1, 0, -1):
        operands = (
            *pays, carried, xs[layer + 1], means[layer + 1], crosses[layer + 1],
            xs[layer], means[layer], weights, all_probs[layer],
        )
        carried, pay, dout, dred, gain_row = call(
            functools.partial(back_kernel, groups, layer, float(width)),
            operands,
            vmem_specs(len(operands)),
            [wide_shape, shaped((back_rows, HD)), wide_shape, rank_shape, gain_shape],
            "backward",
        )
        pays = exchange(pay)
        waiting.append((layer, [reduceds[layer]], dout, dred, gain_row))
        done = [gradients(*item) for item in waiting]
        if layer > 1:
            pays, done = lax.optimization_barrier((pays, done))
        for item, (keep, send) in zip(waiting, done):
            halves[item[0]] = (keep, swapped(send))
        waiting = []
    operands = (
        *pays, carried, xs[1], means[1], crosses[1], xs[0], means[0], weights, all_probs[0],
        all_mixed[0], reduceds[0],
    )
    keep, send = call(
        functools.partial(back_first_kernel, groups, float(width)),
        operands,
        vmem_specs(len(operands)),
        [half_shape] * 2,
        "backward_first",
        scratch_shapes=wide_scratch,
    )
    halves[0] = (keep, swapped(send))

    gradients_of = [
        shaped((1, own), F32),
        shaped((1, own, rank), F32),
        shaped((1, rank, own), F32),
    ]
    pieces = [pair[side] for side in range(2) for pair in halves]
    if sections == 4 and own % (2 * HD) == 0:
        height = half_shape.shape[0]
        double = shaped((2 * height, own // 2))
        single = shaped((height, own // 2))
        whole, by_x, by_y, later_x, later_y = call(
            combine_halves_kernel,
            pieces,
            vmem_specs(8),
            [half_shape, double, double, single, single],
            "combine",
        )
        from_x, from_y = across(by_x, 1), across(by_y, 2)
        to_x, to_y = call(
            relay_kernel,
            (later_x, later_y, from_x, from_y),
            vmem_specs(4),
            [single, single],
            "relay",
        )
        return tuple(
            call(
                finish_halves_kernel,
                (whole, from_x, from_y, across(to_x, 1), across(to_y, 2)),
                vmem_specs(5),
                gradients_of,
                "finish",
            )
        )
    parts = call(
        functools.partial(combine_kernel, sections),
        pieces,
        vmem_specs(2 * sections),
        [half_shape] * sections,
        "combine",
    )
    arrived = [parts[0]] + [across(parts[distance], distance) for distance in range(1, sections)]
    gain_grad, first_grad, second_grad = call(
        functools.partial(finish_kernel, sections),
        arrived,
        vmem_specs(sections),
        gradients_of,
        "finish",
    )
    return (gain_grad, first_grad, second_grad)


def solution(mesh):
    fine = Mesh(
        mesh.devices.reshape(mesh.shape["pipe"], mesh.shape["dp"] // 2, 2), ("pipe", "z", "core")
    )
    data = ("z", "core")
    in_specs = (
        P(None, data, None, None),
        P(None, data, None, None),
        P(None, data, None),
        P(None, data),
        P("pipe", data),
        P("pipe", data, None),
        P("pipe", None, data),
    )
    out_specs = (P("pipe", data), P("pipe", data, None), P("pipe", None, data))
    mapped = jax.shard_map(
        per_device, mesh=fine, in_specs=in_specs, out_specs=out_specs, check_vma=False
    )

    return mapped
```

```python
import functools

import jax
import jax.numpy as jnp
from jax import lax
from jax.experimental import pallas as pl
from jax.experimental.pallas import tpu as pltpu
from jax.sharding import Mesh, PartitionSpec as P

HD = 128
EPS = 1e-05
FOLDED = HD + 16
BF = jnp.bfloat16
F32 = jnp.float32
PARAMS = pltpu.CompilerParams(vmem_limit_bytes=48 * 1024 * 1024)
PACK_PARAMS = pltpu.CompilerParams(vmem_limit_bytes=60 * 1024 * 1024)


def dot(a, b):
    return jnp.dot(a, b, preferred_element_type=F32)


def dot_nt(a, b):
    return lax.dot_general(a, b, (((1,), (1,)), ((), ())), preferred_element_type=F32)


def dot_tn(a, b):
    return lax.dot_general(a, b, (((0,), (0,)), ((), ())), preferred_element_type=F32)


def two_parts(value):
    high = value.astype(BF)
    return high, (value - high.astype(F32)).astype(BF)


def vmem_specs(count):
    return [pl.BlockSpec(memory_space=pltpu.VMEM)] * count


def layer_of(weights, layer):
    return weights.at[pl.ds(layer, 1)]


def slice_rows(own):
    return 2 * own + 16


def pack_kernel(groups, micro_local, *refs):
    tokens, cotangents, starts, counts, gain, first, second = refs[:7]
    parts, weights = refs[7 : 7 + groups], refs[7 + groups]
    tok, cot, starts_in, counts_in, gain_in, second_in, sems = refs[8 + groups :]
    directions, micro_count, length, width = tokens.shape
    local = width // groups
    own = first.shape[1]
    section = lax.axis_index("pipe")
    group = lax.axis_index("z")
    picks = []
    copies = [
        pltpu.make_async_copy(second.at[0], second_in, sems.at[0]),
        pltpu.make_async_copy(gain, gain_in, sems.at[1]),
        pltpu.make_async_copy(first.at[0], weights.at[pl.ds(0, own)], sems.at[2]),
        pltpu.make_async_copy(starts, starts_in, sems.at[3]),
        pltpu.make_async_copy(counts, counts_in, sems.at[4]),
    ]
    for micro in range(micro_local):
        wanted = section * micro_local + micro
        slot = jnp.minimum(wanted, directions * micro_count - 1)
        direction, place = slot // micro_count, slot % micro_count
        picks.append((wanted < directions * micro_count, direction, place))
        rows = pl.ds(micro * length, length)
        copies.append(
            pltpu.make_async_copy(
                tokens.at[direction, place], tok.at[rows], sems.at[5 + 2 * micro]
            )
        )
        copies.append(
            pltpu.make_async_copy(
                cotangents.at[direction, place], cot.at[rows], sems.at[6 + 2 * micro]
            )
        )
    for copy in copies:
        copy.start()
    for copy in copies[:5]:
        copy.wait()
    weights[own : 2 * own, :] = second_in[...].astype(F32).T.astype(BF)
    gains = [gain_in[0:1, head * HD : (head + 1) * HD].astype(F32) for head in range(own // HD)]
    gains.append(jnp.zeros((16 - own // HD, HD), F32))
    weights[2 * own :, :] = jnp.concatenate(gains, axis=0).astype(BF)
    for copy in copies[5:]:
        copy.wait()
    for micro, (keep, direction, place) in enumerate(picks):
        rows = slice(micro * length, (micro + 1) * length)
        widened = tok[rows, :].astype(F32)
        mean = jnp.mean(widened * widened, axis=1, keepdims=True)
        mean_high, mean_low = two_parts(mean)
        position = lax.broadcasted_iota(jnp.int32, (length, HD), 0)
        document = jnp.zeros((length, HD), jnp.int32)
        for entry in range(starts.shape[2]):
            begun = starts_in[direction, place, entry] <= position
            begun = begun & (entry < counts_in[direction, place])
            document = document + begun.astype(jnp.int32)
        lane = lax.broadcasted_iota(jnp.int32, (length, HD), 1)
        tail = jnp.where(
            lane == 0,
            document.astype(F32),
            jnp.where(lane == 1, mean_high.astype(F32), mean_low.astype(F32)),
        ).astype(BF)
        for shift in range(groups):
            start = pl.multiple_of((group ^ shift) * local, local)
            parts[shift][rows, 0:local] = tok[rows, pl.ds(start, local)]
            cotangent = cot[rows, pl.ds(start, local)]
            parts[shift][rows, local : 2 * local] = jnp.where(
                keep, cotangent, jnp.zeros_like(cotangent)
            )
            parts[shift][rows, 2 * local :] = tail


def pack(tokens, cotangents, starts, counts, gain, first, second, groups, micro_local):
    length, width = tokens.shape[2:]
    own = first.shape[1]
    local = width // groups
    rows = micro_local * length
    shape = jax.ShapeDtypeStruct
    results = pl.pallas_call(
        functools.partial(pack_kernel, groups, micro_local),
        in_specs=[pl.BlockSpec(memory_space=pltpu.HBM)] * 7,
        out_specs=vmem_specs(groups + 1),
        out_shape=[shape((rows, 2 * local + HD), BF)] * groups
        + [shape((slice_rows(own), HD), BF)],
        scratch_shapes=[
            pltpu.VMEM((rows, width), BF),
            pltpu.VMEM((rows, width), BF),
            pltpu.SMEM(starts.shape, jnp.int32),
            pltpu.SMEM(counts.shape, jnp.int32),
            pltpu.VMEM(gain.shape, BF),
            pltpu.VMEM(second.shape[1:], BF),
            pltpu.SemaphoreType.DMA((5 + 2 * micro_local,)),
        ],
        compiler_params=PACK_PARAMS,
        name="pack",
    )(tokens, cotangents, starts, counts, gain, first, second)
    return results[:groups], results[groups]


def head_gain(weights, head):
    own = (weights.shape[2] - 16) // 2
    per_slice = own // HD
    row = 2 * own + head % per_slice
    return weights[0, head // per_slice, row : row + 1, :].astype(F32)


def block_size(rows):
    return HD if rows % HD == 0 else rows


def to_rank(value, weights, at):
    own = (weights.shape[2] - 16) // 2
    total = None
    for side in range(weights.shape[1]):
        term = dot(value[:, side * own : (side + 1) * own], weights[0, side, at : at + own, :])
        total = term if total is None else total + term
    return total


def from_rank(value, weights, at, side):
    own = (weights.shape[2] - 16) // 2
    return dot_nt(value, weights[0, side, at : at + own, :])


def gram(weights):
    own = (weights.shape[2] - 16) // 2
    total = None
    for side in range(weights.shape[1]):
        part = weights[0, side, own : 2 * own, :]
        term = dot_tn(part, part)
        total = term if total is None else total + term
    return total


def attend(x, mean, weights, mask, probs, mixed):
    rows, local = x.shape
    size = block_size(rows)
    factor = lax.rsqrt(mean + EPS)
    heads = range(local // HD)
    gains = [head_gain(weights, head) for head in heads]
    for block in range(rows // size):
        span = slice(block * size, (block + 1) * size)
        allowed = mask[block] > 0
        wide = x[span, :].astype(F32) * factor[span]
        normed = [(wide[:, head * HD : (head + 1) * HD] * gains[head]).astype(BF) for head in heads]
        scores = [dot_nt(value, value) for value in normed]
        raw = [jnp.where(allowed, jnp.exp(score * (1.0 / HD)), 0.0) for score in scores]
        shares = [1.0 / jnp.sum(value, axis=1, keepdims=True) for value in raw]
        prob = [(value * share).astype(BF) for value, share in zip(raw, shares)]
        result = [dot(left, right).astype(BF) for left, right in zip(prob, normed)]
        for head in heads:
            probs[block, head] = prob[head]
            mixed[span, head * HD : (head + 1) * HD] = result[head]


def send_forward(x, weights, mixed, pay):
    rows = x.shape[0]
    own = (weights.shape[2] - 16) // 2
    pay[0:rows, :] = to_rank(mixed[...], weights, 0).astype(BF)
    pay[rows : 2 * rows, :] = to_rank(x[...], weights, own).astype(BF)


def total_of(pays, start, stop):
    total = pays[0][start:stop, :].astype(F32)
    for pay in pays[1:]:
        total = total + pay[start:stop, :].astype(F32)
    return total


def receive_forward(
    pays, gram_total, x_before, mean_before, weights_before, width, x, mean, reduced, cross
):
    rows, local = x_before.shape
    own = (weights_before.shape[2] - 16) // 2
    low_rank = total_of(pays, 0, rows).astype(BF)
    before = total_of(pays, rows, 2 * rows)
    high, low = two_parts(gram_total)
    through = dot(low_rank, high) + dot(low_rank, low)
    wide = low_rank.astype(F32)
    change = jnp.sum(wide * (2.0 * before + through), axis=1, keepdims=True) / width
    new_mean = jnp.maximum(mean_before[:, 0:1] + change, 0.0)
    mean[...] = jnp.broadcast_to(new_mean, mean.shape)
    reduced[...] = low_rank
    cross[...] = before + through
    for side in range(weights_before.shape[1]):
        part = slice(side * own, (side + 1) * own)
        x[:, part] = (
            x_before[:, part].astype(F32) + from_rank(low_rank, weights_before, own, side)
        ).astype(BF)


def own_kernel(part, packed, early, part_out, packed_out, early_out):
    part_out[...] = part[...]
    packed_out[...] = packed[...]
    early_out[...] = early[...]


def arrange_kernel(length, order, *refs):
    groups = len(order)
    received = [refs[order.index(place)] for place in range(groups)]
    x, cot, mask, mean, tails = refs[groups:]
    rows, local = x.shape
    place_rows(received, tails, slice(2 * local, None))
    place_rows(received, x, slice(0, local))
    place_rows(received, cot, slice(local, 2 * local))
    tail = tails[...].astype(F32)
    mean[...] = jnp.broadcast_to(tail[:, 1:2] + tail[:, 2:3], mean.shape)
    build_mask(tail[:, 0:1], mask, block_size(rows), length)


def first_kernel(sections, *refs):
    mine, theirs = refs[:sections], refs[sections : 2 * sections]
    x, mask, mean, probs, mixed, pay, weights, sems = refs[2 * sections :]
    section, core = lax.axis_index("pipe"), lax.axis_index("core")
    rows = x.shape[0]
    copies = []
    for distance in range(sections):
        layer = section ^ distance
        for parts, place in ((mine, core), (theirs, 1 - core)):
            copies.append(
                pltpu.make_async_copy(
                    parts[distance], weights.at[layer, place], sems.at[layer, place]
                )
            )
    for wanted_now in (True, False):
        for distance in range(sections):

            @pl.when((section == distance) == wanted_now)
            def _(distance=distance):
                copies[2 * distance].start()
                copies[2 * distance + 1].start()

    def arrived(layer):
        for place in range(weights.shape[1]):
            pltpu.make_async_copy(mine[0], weights.at[layer, place], sems.at[layer, place]).wait()

    arrived(0)
    own = (weights.shape[2] - 16) // 2
    layers = [layer_of(weights, layer) for layer in range(sections)]
    attend(x, mean[:, 0:1], layers[0], mask, probs, mixed)
    send_forward(x, layers[0], mixed, pay)
    arrived(1)
    pay[2 * rows :, :] = fold_grams(layers[0], layers[1])
    for layer in range(2, sections):
        arrived(layer)


def side_kernel(weights, cot, side):
    rows = cot.shape[0]
    sections = weights.shape[0]
    own = (weights.shape[2] - 16) // 2
    layers = [layer_of(weights, layer) for layer in range(sections)]
    side[0:rows, :] = to_rank(cot[...], layers[-1], own).astype(BF)
    for layer in range(2, sections - 1, 2):
        base, height, folded = gram_place(layer, sections - 1, rows)
        both = fold_grams(layers[layer], layers[layer + 1]) if folded else gram(layers[layer])
        side[base : base + height, :] = both.astype(BF)


def place_rows(received, target, columns):
    rows = received[0].shape[0]
    for shift, part in enumerate(received):
        source = lax.axis_index("z") ^ shift
        target[pl.ds(pl.multiple_of(source * rows, rows), rows), :] = part[:, columns]


def build_mask(document, mask, size, length):
    query = lax.broadcasted_iota(jnp.int32, (size, size), 0)
    key = lax.broadcasted_iota(jnp.int32, (size, size), 1)
    for block in range(mask.shape[0]):
        by_query = jnp.broadcast_to(document[block * size : (block + 1) * size], (size, size))
        by_key = by_query.T
        allowed = (by_query == by_key) & (key <= query) & (query // length == key // length)
        mask[block] = allowed.astype(F32).astype(BF)


def fold_grams(weights, other):
    row, lane = square_places()
    upper, lower = gram(weights), gram(other)
    diagonal = jnp.sum(jnp.where(row == lane, lower, 0.0), axis=0, keepdims=True)
    folded = jnp.where(row <= lane, upper, lower)
    return jnp.concatenate((folded, diagonal, jnp.zeros((15, HD), F32)), axis=0).astype(BF)


def square_places():
    return (
        lax.broadcasted_iota(jnp.int32, (HD, HD), 0),
        lax.broadcasted_iota(jnp.int32, (HD, HD), 1),
    )


def gram_place(layer, top, rows):
    pair = layer // 2
    folded = 2 * pair + 1 < top
    base = 2 * rows if pair == 0 else rows + FOLDED * (pair - 1)
    return base, FOLDED if folded else HD, folded


def gram_of(sources, layer, top, rows):
    base, height, folded = gram_place(layer, top, rows)
    total = total_of(sources, base, base + height)
    if not folded:
        return total
    row, lane = square_places()
    square = total[0:HD]
    if layer % 2 == 0:
        return jnp.where(row <= lane, square, square.T)
    lower = jnp.where(row > lane, square, square.T)
    return jnp.where(row == lane, total[HD : HD + 1], lower)


def middle_kernel(count, layer, top, width, *refs):
    pays, sources, refs = refs[:count], refs[count : 2 * count], refs[2 * count :]
    if layer == 1:
        sources, refs = pays, sources + refs
    x_before, mean_before, mask, weights = refs[:4]
    x, mean, reduced, cross, probs, mixed, pay = refs[4:]
    weights_before, weights = layer_of(weights, layer - 1), layer_of(weights, layer)
    receive_forward(
        pays, gram_of(sources, layer - 1, top, x.shape[0]), x_before, mean_before, weights_before,
        width, x, mean, reduced, cross,
    )
    attend(x, mean[:, 0:1], weights, mask, probs, mixed)
    send_forward(x, weights, mixed, pay)


def layer_backward(dout, dred, x, mean, weights, weights_before, probs, gain_row, carried, pay):
    rows, local = x.shape
    size = block_size(rows)
    own = (weights.shape[2] - 16) // 2
    per_slice = own // HD
    factor = lax.rsqrt(mean + EPS)
    back_mixed = [
        from_rank(dred, weights, 0, side).astype(BF) for side in range(weights.shape[1])
    ]
    heads = range(local // HD)
    gains = [head_gain(weights, head) for head in heads]
    gain_sums = [None] * len(heads)
    for block in range(rows // size):
        span = slice(block * size, (block + 1) * size)
        scale = factor[span]
        parts = [slice(head * HD, (head + 1) * HD) for head in heads]
        wide = [x[span, part].astype(F32) for part in parts]
        prob = [probs[block, head] for head in heads]
        onward = [None if carried is None else dout[span, part].astype(F32) for part in parts]
        unit = [value * scale for value in wide]
        normed = [(value * gain).astype(BF) for value, gain in zip(unit, gains)]
        upstream = []
        for head in heads:
            inner = (head % per_slice) * HD
            upstream.append(back_mixed[head // per_slice][span, inner : inner + HD])
        back_prob = [dot_nt(left, right) for left, right in zip(upstream, normed)]
        through = [dot_tn(left, right) for left, right in zip(prob, upstream)]
        both = []
        for head in heads:
            prob_wide = prob[head].astype(F32)
            inner_sum = jnp.sum(back_prob[head] * prob_wide, axis=1, keepdims=True)
            back_score = prob_wide * (back_prob[head] - inner_sum) * (1.0 / HD)
            both.append((back_score + back_score.T).astype(BF))
        back_normed = [
            (through[head] + dot(both[head], normed[head])).astype(BF).astype(F32) for head in heads
        ]
        norm_dot = jnp.zeros((size, HD), F32)
        for head in heads:
            term = jnp.sum(back_normed[head] * unit[head], axis=0, keepdims=True)
            gain_sums[head] = term if gain_sums[head] is None else gain_sums[head] + term
            if carried is not None:
                scaled = back_normed[head] * gains[head]
                norm_dot = norm_dot + scaled * wide[head]
                carried[span, parts[head]] = (onward[head] + scaled * scale).astype(BF)
        if carried is not None:
            column = jnp.broadcast_to(jnp.sum(norm_dot, axis=1, keepdims=True), (size, size))
            line = column.T[0:1, :]
            high, low = two_parts(line)
            base = rows + 16 * block
            pay[base : base + 16, :] = jnp.concatenate(
                (high.astype(F32), low.astype(F32), jnp.zeros((14, size), F32)), axis=0
            ).astype(BF)
    zeros = jnp.zeros((15, HD), F32)
    for head in heads:
        gain_row[:, head * HD : (head + 1) * HD] = jnp.concatenate(
            (gain_sums[head], zeros), axis=0
        ).astype(BF)
    if carried is not None:
        pay[0:rows, :] = to_rank(carried[...], weights_before, own).astype(BF)


def turn_kernel(count, layer, width, *refs):
    pays, sides, refs = refs[:count], refs[count : 2 * count], refs[2 * count :]
    x_before, mean_before, mask, weights, cot = refs[:5]
    x, mean, reduced, cross, mixed, dred_out, gain_row, carried, pay, probs = refs[5:]
    rows = x.shape[0]
    weights_before, weights = layer_of(weights, layer - 1), layer_of(weights, layer)
    receive_forward(
        pays, gram_of(sides, layer - 1, layer, rows), x_before, mean_before, weights_before,
        width, x, mean, reduced, cross,
    )
    attend(x, mean[:, 0:1], weights, mask, probs, mixed)
    dred = total_of(sides, 0, rows).astype(BF)
    dred_out[...] = dred
    layer_backward(
        cot[...], dred, x, mean[:, 0:1], weights, weights_before, probs, gain_row, carried, pay
    )
    pay[pay.shape[0] - rows :, :] = to_rank(mixed[...], weights, 0).astype(BF)


def receive_backward(pays, carried_after, x_after, mean_after, cross_after, width):
    rows = x_after.shape[0]
    size = block_size(rows)
    douts, dreds = [], []
    for block in range(rows // size):
        span = slice(block * size, (block + 1) * size)
        base = rows + 16 * block
        lines = total_of(pays, base, base + 16)
        column = jnp.broadcast_to(lines[0:1] + lines[1:2], (size, size)).T
        factor = lax.rsqrt(mean_after[span, 0:1] + EPS)
        pull = column[:, 0:1] * (factor * factor * factor / width)
        own_total = total_of(pays, block * size, (block + 1) * size)
        dreds.append((own_total - cross_after[span, :] * pull).astype(BF))
        douts.append(
            (carried_after[span, :].astype(F32) - x_after[span, :].astype(F32) * pull).astype(BF)
        )
    if len(douts) == 1:
        return douts[0], dreds[0]
    return jnp.concatenate(douts, axis=0), jnp.concatenate(dreds, axis=0)


def back_kernel(count, layer, width, *refs):
    pays, refs = refs[:count], refs[count:]
    carried_after, x_after, mean_after, cross_after, x, mean, weights, probs = refs[:8]
    carried, pay, dout_out, dred_out, gain_row = refs[8:]
    dout, dred = receive_backward(pays, carried_after, x_after, mean_after, cross_after, width)
    layer_backward(
        dout, dred, x, mean[:, 0:1], layer_of(weights, layer), layer_of(weights, layer - 1), probs,
        gain_row, carried, pay,
    )
    dout_out[...] = dout
    dred_out[...] = dred


def split_grads(dred, mixed, second, gain_row, wide, keep, send):
    rank = second.shape[0]
    own = keep.shape[1]
    core = lax.axis_index("core")
    for head in range(mixed.shape[1] // HD):
        part = slice(head * HD, (head + 1) * HD)
        wide[0:HD, head * rank : (head + 1) * rank] = dot_tn(mixed[:, part], dred).astype(BF)
    wide[rank : 2 * rank, :] = second.astype(BF)
    if gain_row is not None:
        wide[2 * rank :, :] = gain_row[...]
    keep[...] = wide[:, pl.ds(pl.multiple_of(core * own, own), own)]
    send[...] = wide[:, pl.ds(pl.multiple_of((1 - core) * own, own), own)]


def grads_kernel(count, *refs):
    sources, refs = refs[:count], refs[count:]
    dout, dred, mixed, gain_row, keep, send, wide = refs
    rows = dout.shape[0]
    height = sources[0].shape[0]
    reduced = total_of(sources, height - rows, height).astype(BF)
    second = dot_tn(reduced, dout[...])
    split_grads(dred[...], mixed, second, gain_row, wide, keep, send)


def back_first_kernel(count, width, *refs):
    pays, refs = refs[:count], refs[count:]
    carried_after, x_after, mean_after, cross_after, x, mean, weights, probs, mixed = refs[:9]
    reduced, keep, send, wide = refs[9:]
    rank = reduced.shape[1]
    dout, dred = receive_backward(pays, carried_after, x_after, mean_after, cross_after, width)
    second = dot_tn(reduced[...], dout)
    layer_backward(
        dout, dred, x, mean[:, 0:1], layer_of(weights, 0), None, probs, wide.at[pl.ds(2 * rank, 16)],
        None, None,
    )
    split_grads(dred, mixed, second, None, wide, keep, send)


def combine_kernel(sections, *refs):
    kept, swapped = refs[:sections], refs[sections : 2 * sections]
    outs = refs[2 * sections :]
    section = lax.axis_index("pipe")
    for distance in range(sections):
        for layer in range(sections):

            @pl.when(section == layer ^ distance)
            def _(distance=distance, layer=layer):
                total = kept[layer][...].astype(F32) + swapped[layer][...].astype(F32)
                outs[distance][...] = total.astype(BF)


def combine_halves_kernel(*refs):
    kept, swapped = refs[:4], refs[4:8]
    mine, by_x, by_y, later_x, later_y = refs[8:]
    rows = mine.shape[0]
    half = mine.shape[1] // 2
    section = lax.axis_index("pipe")
    for distance in range(4):
        for layer in range(4):

            @pl.when(section == layer ^ distance)
            def _(distance=distance, layer=layer):
                total = kept[layer][...].astype(F32) + swapped[layer][...].astype(F32)
                total = total.astype(BF)
                left, right = total[:, :half], total[:, half:]
                if distance == 0:
                    mine[...] = total
                elif distance == 1:
                    by_x[0:rows, :] = right
                    later_x[...] = left
                elif distance == 2:
                    by_y[0:rows, :] = left
                    later_y[...] = right
                else:
                    by_x[rows:, :] = right
                    by_y[rows:, :] = left


def relay_kernel(later_x, later_y, from_x, from_y, to_x, to_y):
    rows = later_x.shape[0]
    to_x[...] = (later_x[...].astype(F32) + from_y[rows:, :].astype(F32)).astype(BF)
    to_y[...] = (later_y[...].astype(F32) + from_x[rows:, :].astype(F32)).astype(BF)


def finish_halves_kernel(mine, from_x, from_y, last_x, last_y, gain, first, second):
    rank = second.shape[1]
    rows = mine.shape[0]
    half = mine.shape[1] // 2
    for side, (direct, relayed) in enumerate(((from_y, last_x), (from_x, last_y))):
        span = slice(side * half, (side + 1) * half)
        total = mine[:, span].astype(F32) + direct[0:rows, :].astype(F32)
        total = total + relayed[...].astype(F32)
        for block in range(half // rank):
            base = side * half + block * HD
            first[0, base : base + HD, :] = total[0:HD, block * rank : (block + 1) * rank]
        second[0, :, span] = total[rank : 2 * rank]
        gain[:, span] = total[2 * rank : 2 * rank + 1]


def finish_kernel(sections, *refs):
    parts = refs[:sections]
    gain, first, second = refs[sections:]
    rank = second.shape[1]
    total = parts[0][...].astype(F32)
    for part in parts[1:]:
        total = total + part[...].astype(F32)
    for block in range(first.shape[1] // HD):
        first[0, block * HD : (block + 1) * HD, :] = total[0:HD, block * rank : (block + 1) * rank]
    second[0] = total[rank : 2 * rank]
    gain[...] = total[2 * rank : 2 * rank + 1]


def per_device(tokens, cotangents, starts, counts, layer_gains, first_map, second_map):
    sections = lax.axis_size("pipe")
    groups = lax.axis_size("z")
    directions, micro_count, length, width = tokens.shape
    micro_local = -(-directions * micro_count // sections)
    rows = groups * micro_local * length
    local = width // groups
    own = first_map.shape[1]
    rank = first_map.shape[2]
    heads = local // HD
    size = block_size(rows)
    blocks = rows // size
    sides = lax.axis_size("core")
    top = sections - 1

    def shifted(value, shift):
        return lax.ppermute(value, "z", [(i, i ^ shift) for i in range(groups)])

    def across(value, distance):
        return lax.ppermute(value, "pipe", [(i, i ^ distance) for i in range(sections)])

    def swapped(value):
        return lax.ppermute(value, "core", [(i, 1 - i) for i in range(sides)])

    def exchange(pay):
        return [pay] + [
            shifted(pay, place)
            for place in sorted(range(1, groups), key=lambda place: (place > 2, -place))
        ]

    token_parts, packed = pack(
        tokens, cotangents, starts, counts, layer_gains, first_map, second_map, groups, micro_local
    )
    mine = [packed] + [across(packed, distance) for distance in range(1, sections)]
    order = [0] + list(range(groups - 1, 0, -1))
    received = [token_parts[0]] + [shifted(token_parts[place], place) for place in order[1:]]
    def shaped(shape, kind=BF):
        return jax.ShapeDtypeStruct(shape, kind)

    def call(kernel, operands, specs, outs, name, **more):
        return pl.pallas_call(
            kernel,
            in_specs=specs,
            out_specs=vmem_specs(len(outs)),
            out_shape=outs,
            compiler_params=PARAMS,
            name=name,
            **more,
        )(*operands)

    received[0], mine[0], mine[1] = call(
        own_kernel,
        (received[0], packed, mine[1]),
        vmem_specs(3),
        [shaped(received[0].shape), shaped(packed.shape), shaped(packed.shape)],
        "own_parts",
    )
    received, mine = lax.optimization_barrier((received, mine))
    theirs = [swapped(part) for part in mine]

    wide_shape = shaped((rows, local))
    mean_shape = shaped((rows, HD), F32)
    rank_shape = shaped((rows, rank))
    cross_shape = shaped((rows, rank), F32)
    probs_shape = shaped((blocks, heads, size, size))
    grads_shape = (sides, 2 * rank + 16, own)
    half_shape = shaped(grads_shape[1:])
    weights_shape = shaped((sections, sides, slice_rows(own), HD))

    x, cot, mask, mean = call(
        functools.partial(arrange_kernel, length, order),
        received,
        vmem_specs(groups),
        [wide_shape, wide_shape, shaped((blocks, size, size)), mean_shape],
        "arrange",
        scratch_shapes=[pltpu.VMEM((rows, HD), BF)],
    )
    last_gram = gram_place(top - 1, top, rows)
    side_rows = last_gram[0] + last_gram[1]
    probs, mixed, pay, weights = call(
        functools.partial(first_kernel, sections),
        (*mine, *theirs, x, mask, mean),
        vmem_specs(2 * sections + 3),
        [probs_shape, wide_shape, shaped((2 * rows + FOLDED, HD)), weights_shape],
        "forward_first",
        scratch_shapes=[pltpu.SemaphoreType.DMA((sections, sides))],
    )
    xs, means, reduceds, crosses = [x], [mean], [], [None]
    all_probs, all_mixed = [probs], [mixed]
    first_pays = pays = exchange(pay)
    side = call(side_kernel, (weights, cot), vmem_specs(2), [shaped((side_rows, HD))], "side")[0]
    arrived = exchange(side)
    for layer in range(1, top):
        operands = (*pays, *((), first_pays, arrived)[min(layer, 3) - 1])
        specs = vmem_specs(len(operands) + 4)
        x, mean, reduced, cross, probs, mixed, pay = call(
            functools.partial(middle_kernel, groups, layer, top, float(width)),
            (*operands, xs[-1], means[-1], mask, weights),
            specs,
            [
                wide_shape,
                mean_shape,
                rank_shape,
                cross_shape,
                probs_shape,
                wide_shape,
                shaped((2 * rows, HD)),
            ],
            "forward_middle",
        )
        xs.append(x)
        means.append(mean)
        reduceds.append(reduced)
        crosses.append(cross)
        all_probs.append(probs)
        all_mixed.append(mixed)
        pays = exchange(pay)

    back_rows = rows + 16 * blocks
    gain_shape = shaped((16, local))
    wide_scratch = [pltpu.VMEM((2 * rank + 16, local), BF)]
    x, mean, reduced, cross, mixed, dred, gain_row, carried, pay = call(
        functools.partial(turn_kernel, groups, top, float(width)),
        (*pays, *arrived, xs[-1], means[-1], mask, weights, cot),
        vmem_specs(2 * groups + 5),
        [
            wide_shape,
            mean_shape,
            rank_shape,
            cross_shape,
            wide_shape,
            rank_shape,
            gain_shape,
            wide_shape,
            shaped((back_rows + rows, HD)),
        ],
        "turn",
        scratch_shapes=[pltpu.VMEM(probs_shape.shape, BF)],
    )
    xs.append(x)
    means.append(mean)
    reduceds.append(reduced)
    crosses.append(cross)
    all_mixed.append(mixed)

    def gradients(layer, sources, dout, dred, gain_row):
        operands = (*sources, dout, dred, all_mixed[layer], gain_row)
        keep, send = call(
            functools.partial(grads_kernel, len(sources)),
            operands,
            vmem_specs(len(operands)),
            [half_shape] * 2,
            "weight_grads",
            scratch_shapes=wide_scratch,
        )
        return keep, send

    pays = exchange(pay)
    halves = [None] * sections
    waiting = [(top, pays, cot, dred, gain_row)]
    for layer in range(top - 1, 0, -1):
        operands = (
            *pays, carried, xs[layer + 1], means[layer + 1], crosses[layer + 1],
            xs[layer], means[layer], weights, all_probs[layer],
        )
        carried, pay, dout, dred, gain_row = call(
            functools.partial(back_kernel, groups, layer, float(width)),
            operands,
            vmem_specs(len(operands)),
            [wide_shape, shaped((back_rows, HD)), wide_shape, rank_shape, gain_shape],
            "backward",
        )
        pays = exchange(pay)
        waiting.append((layer, [reduceds[layer]], dout, dred, gain_row))
        done = [gradients(*item) for item in waiting]
        if layer > 1:
            pays, done = lax.optimization_barrier((pays, done))
        for item, (keep, send) in zip(waiting, done):
            halves[item[0]] = (keep, swapped(send))
        waiting = []
    operands = (
        *pays, carried, xs[1], means[1], crosses[1], xs[0], means[0], weights, all_probs[0],
        all_mixed[0], reduceds[0],
    )
    keep, send = call(
        functools.partial(back_first_kernel, groups, float(width)),
        operands,
        vmem_specs(len(operands)),
        [half_shape] * 2,
        "backward_first",
        scratch_shapes=wide_scratch,
    )
    halves[0] = (keep, swapped(send))

    gradients_of = [
        shaped((1, own), F32),
        shaped((1, own, rank), F32),
        shaped((1, rank, own), F32),
    ]
    pieces = [pair[side] for side in range(2) for pair in halves]
    if sections == 4 and own % (2 * HD) == 0:
        height = half_shape.shape[0]
        double = shaped((2 * height, own // 2))
        single = shaped((height, own // 2))
        whole, by_x, by_y, later_x, later_y = call(
            combine_halves_kernel,
            pieces,
            vmem_specs(8),
            [half_shape, double, double, single, single],
            "combine",
        )
        from_x, from_y = across(by_x, 1), across(by_y, 2)
        to_x, to_y = call(
            relay_kernel,
            (later_x, later_y, from_x, from_y),
            vmem_specs(4),
            [single, single],
            "relay",
        )
        return tuple(
            call(
                finish_halves_kernel,
                (whole, from_x, from_y, across(to_x, 1), across(to_y, 2)),
                vmem_specs(5),
                gradients_of,
                "finish",
            )
        )
    parts = call(
        functools.partial(combine_kernel, sections),
        pieces,
        vmem_specs(2 * sections),
        [half_shape] * sections,
        "combine",
    )
    arrived = [parts[0]] + [across(parts[distance], distance) for distance in range(1, sections)]
    gain_grad, first_grad, second_grad = call(
        functools.partial(finish_kernel, sections),
        arrived,
        vmem_specs(sections),
        gradients_of,
        "finish",
    )
    return (gain_grad, first_grad, second_grad)


def solution(mesh):
    fine = Mesh(
        mesh.devices.reshape(mesh.shape["pipe"], mesh.shape["dp"] // 2, 2), ("pipe", "z", "core")
    )
    data = ("z", "core")
    in_specs = (
        P(None, data, None, None),
        P(None, data, None, None),
        P(None, data, None),
        P(None, data),
        P("pipe", data),
        P("pipe", data, None),
        P("pipe", None, data),
    )
    out_specs = (P("pipe", data), P("pipe", data, None), P("pipe", None, data))
    mapped = jax.shard_map(
        per_device, mesh=fine, in_specs=in_specs, out_specs=out_specs, check_vma=False
    )

    return mapped
```
